32 devices in a mesh: section: 2 (over core), dp: 4 (over z), seq: 4 (over y, x).
Axes of the slice: x: 2, y: 2, z: 4, core: 2. Of those that a mesh axis runs over, the one named last changes fastest.
Arguments:
- clip_ids: int32 [4, 4], P('dp'), may hold values from 0 to 3, as said below
- tokens: bfloat16 [2, 16, 196, 768], P(None, ('dp', 'seq')), may hold values from -6 to 6
- time_qkv: bfloat16 [2, 768, 2304], P('section'), may hold values from -0.21875 to 0.21875
- time_out: bfloat16 [2, 768, 768], P('section'), may hold values from -0.4375 to 0.4375
- time_fc: bfloat16 [2, 768, 768], P('section'), may hold values from -0.21875 to 0.21875
- space_qkv: bfloat16 [2, 768, 2304], P('section'), may hold values from -0.21875 to 0.21875
- space_out: bfloat16 [2, 768, 768], P('section'), may hold values from -1.75 to 1.75
- up_weight: bfloat16 [2, 768, 3072], P('section'), may hold values from -0.21875 to 0.21875
- down_weight: bfloat16 [2, 3072, 768], P('section'), may hold values from -0.109375 to 0.109375
- norm_gains: float32 [2, 3, 768], P('section'), may hold values from 0.5 to 1.5
- bias_rows: float32 [2, 11, 768], P('section'), may hold values from -3 to 3
- up_bias: float32 [2, 3072], P('section'), may hold values from -3 to 3
- cotangent: bfloat16 [2, 16, 196, 768], P(None, ('dp', 'seq')), may hold values from -6 to 6
Outputs:
- layer_outputs: bfloat16 [2, 2, 16, 196, 768], P('section', None, ('dp', 'seq'))
- input_grads: bfloat16 [2, 2, 16, 196, 768], P('section', None, ('dp', 'seq'))
- grad_time_qkv: float32 [2, 1769472], P('section', ('dp', 'seq'))
- grad_time_out: float32 [2, 589824], P('section', ('dp', 'seq'))
- grad_time_fc: float32 [2, 589824], P('section', ('dp', 'seq'))
- grad_space_qkv: float32 [2, 1769472], P('section', ('dp', 'seq'))
- grad_space_out: float32 [2, 589824], P('section', ('dp', 'seq'))
- grad_up_weight: float32 [2, 2359296], P('section', ('dp', 'seq'))
- grad_down_weight: float32 [2, 2359296], P('section', ('dp', 'seq'))
- grad_norm_gains: float32 [2, 2304], P('section', ('dp', 'seq'))
- grad_bias_rows: float32 [2, 8448], P('section', ('dp', 'seq'))
- grad_up_bias: float32 [2, 3072], P('section', ('dp', 'seq'))
The draws below stay inside these ranges and needn't reach their ends.
Inputs may be any that keep to these rules, and one draw needn't show every extreme that they name: `clip_ids`: frames of one group with equal ids form one clip; every frame attends to the frames of its own clip.
All inputs are finite; a program needn't handle non-finite values.
Results may differ from the reference program's by a relative error of at most 0.02.
Values may be sent and summed in bfloat16 or wider, within the bound.
A program may use at most 320 MiB of HBM per device.

```python
import jax
import jax.numpy as jnp
from jax import lax

H = 12
HD = 64
D = 768
FF = 3072
P_SIZE = 196
MB = 2
NCLIP = 4
GF = 4
NF = 16
N_DP = 4


def draw_clip_ids(key, part):
    key = jax.random.fold_in(key, 11)
    labels = jax.random.randint(key, (N_DP, GF), 0, NCLIP)
    labels = labels.at[:, 1].set(NCLIP - 1)
    labels = labels.at[:, 2].set(0)
    labels = labels.at[:, GF - 1].set(labels[:, 0])
    return labels.astype(jnp.int32)


def block_levels(own_key, shape, split, least, largest):
    level = 1.0
    for axis_at, blocks in split:
        steps = jax.random.uniform(jax.random.fold_in(jax.random.fold_in(own_key, 6), axis_at), (blocks,), jnp.float32, least / len(split), largest / len(split))
        level = level * jnp.repeat(jnp.exp(steps), shape[axis_at] // blocks).reshape((-1,) + (1,) * (len(shape) - 1 - axis_at))
    return level


def gaussian(own_key, shape, scale, reach, cuts=(), held_as=jnp.bfloat16):
    values = scale * jax.random.normal(own_key, shape, jnp.float32)
    if cuts:
        values = values * block_levels(own_key, shape, cuts, -0.22, 0.18)
    return jnp.clip(values, -reach, reach).astype(held_as)


def setup_inputs(seed: int = 0) -> dict:
    keys = jax.random.split(jax.random.key(seed), 14)
    return {
        "clip_ids": draw_clip_ids(jax.random.fold_in(keys[13], 71), 0),
        "tokens": gaussian(keys[1], (MB, NF, P_SIZE, D), 1.0, 6.0, ((1, 16),)),
        "time_qkv": gaussian(keys[2], (2, D, 3 * D), D ** -0.5, 0.21875, ((0, 2),)),
        "time_out": gaussian(keys[3], (2, D, D), (D // 4) ** -0.5, 0.4375, ((0, 2),)),
        "time_fc": gaussian(keys[4], (2, D, D), D ** -0.5, 0.21875, ((0, 2),)),
        "space_qkv": gaussian(keys[5], (2, D, 3 * D), D ** -0.5, 0.21875, ((0, 2),)),
        "space_out": gaussian(keys[6], (2, D, D), (D // 64) ** -0.5, 1.75, ((0, 2),)),
        "up_weight": gaussian(keys[7], (2, D, FF), D ** -0.5, 0.21875, ((0, 2),)),
        "down_weight": gaussian(keys[8], (2, FF, D), FF ** -0.5, 0.109375, ((0, 2),)),
        "norm_gains": jnp.clip(1.0 + 0.1 * jax.random.normal(keys[9], (2, 3, D), jnp.float32), 0.5, 1.5),
        "bias_rows": gaussian(keys[10], (2, 11, D), 0.5, 3.0, ((0, 2),), jnp.float32),
        "up_bias": gaussian(keys[11], (2, FF), 0.5, 3.0, ((0, 2),), jnp.float32),
        "cotangent": gaussian(keys[12], (MB, NF, P_SIZE, D), 1.0, 6.0, ((1, 16),)),
    }


@jax.custom_vjp
def low(v):
    return lax.optimization_barrier(v.astype(jnp.bfloat16)).astype(jnp.float32)

@jax.custom_vjp
def low_back(v):
    return v

def low_keep(v):
    return (low(v), None)

def low_pass(kept, grad):
    return (grad,)

def back_keep(v):
    return (v, None)

def back_low(kept, grad):
    return (low(grad),)
low.defvjp(low_keep, low_pass)
low_back.defvjp(back_keep, back_low)

def norm_rows(values, gain, shift):
    centre = values - lax.optimization_barrier(jnp.mean(values, axis=-1, keepdims=True))
    spread = lax.optimization_barrier(jnp.mean(centre * centre, axis=-1, keepdims=True))
    return centre * lax.rsqrt(spread + 1e-06) * gain + shift

def project(left, right):
    return jnp.einsum('fpd,de->fpe', left, right, precision=lax.Precision.HIGHEST)

def spatial_frame(block_rows):
    queries = block_rows[:, 0]
    key_rows = block_rows[:, 1]
    values = block_rows[:, 2]
    scores = jnp.einsum('inc,jnc->nij', queries, key_rows, precision=lax.Precision.HIGHEST) * HD ** (-0.5)
    scores = low_back(scores)
    weights_soft = jax.nn.softmax(scores, axis=-1)
    mixed = jnp.einsum('nij,jnc->inc', low(weights_soft), values, precision=lax.Precision.HIGHEST)
    return low_back(low(mixed)).reshape(P_SIZE, H * HD)

def block_forward(inputs, params, same_clip):
    time_qkv, time_out, time_fc, space_qkv, space_out, up_weight, down_weight, norm_gains, bias_rows, up_bias = params
    zero_row = jnp.zeros_like(bias_rows[0])
    normed_time = low(norm_rows(inputs, norm_gains[0], bias_rows[0]))
    qkv_time = project(normed_time, time_qkv) + jnp.concatenate([bias_rows[1], zero_row, bias_rows[2]])
    qkv_time = low_back(low(qkv_time))
    grouped = qkv_time.reshape(N_DP, GF, P_SIZE, 3, H, HD)
    queries = grouped[:, :, :, 0]
    key_rows = grouped[:, :, :, 1]
    values = grouped[:, :, :, 2]
    scores = jnp.einsum('gipnc,gjpnc->gpnij', queries, key_rows, precision=lax.Precision.HIGHEST) * HD ** (-0.5)
    scores = low_back(scores)
    scores = jnp.where(same_clip[:, None, None], scores, -1000000000.0)
    weights_soft = jax.nn.softmax(scores, axis=-1)
    attn_time = jnp.einsum('gpnij,gjpnc->gipnc', low(weights_soft), values, precision=lax.Precision.HIGHEST)
    attn_time = low_back(low(attn_time)).reshape(inputs.shape)
    proj_out = low_back(low(project(attn_time, time_out) + bias_rows[3]))
    after_time = inputs + low_back(project(proj_out, time_fc) + bias_rows[4])
    normed_space = low(norm_rows(after_time, norm_gains[1], bias_rows[5]))
    qkv_space = project(normed_space, space_qkv) + jnp.concatenate([bias_rows[6], zero_row, bias_rows[7]])
    qkv_space = low_back(low(qkv_space))
    attn_space = lax.map(jax.checkpoint(spatial_frame), qkv_space.reshape(NF, P_SIZE, 3, H, HD))
    after_space = after_time + low_back(project(attn_space, space_out) + bias_rows[8])
    normed_mlp = low(norm_rows(after_space, norm_gains[2], bias_rows[9]))
    hidden_pre = low_back(project(normed_mlp, up_weight) + up_bias)
    hidden_act = low(jax.nn.gelu(hidden_pre))
    return after_space + low_back(project(hidden_act, down_weight) + bias_rows[10])

def reference(clip_ids, tokens, time_qkv, time_out, time_fc, space_qkv, space_out, up_weight, down_weight, norm_gains, bias_rows, up_bias, cotangent):
    same_clip = clip_ids[:, :, None] == clip_ids[:, None, :]
    stacked = tuple((array.astype(jnp.float32) for array in (time_qkv, time_out, time_fc, space_qkv, space_out, up_weight, down_weight, norm_gains, bias_rows, up_bias)))
    first_layer = tuple((array[0] for array in stacked))
    second_layer = tuple((array[1] for array in stacked))
    source = tokens.astype(jnp.float32)
    probes = jnp.zeros_like(source)

    def forward(source, probes, first_layer, second_layer):
        middle = []
        finals = []
        for micro_index in range(MB):
            handed = low_back(low(block_forward(source[micro_index], first_layer, same_clip))) + probes[micro_index]
            middle.append(handed)
            finals.append(block_forward(handed, second_layer, same_clip))
        return (jnp.stack(middle), jnp.stack(finals))
    (middle, finals), pullback = jax.vjp(forward, source, probes, first_layer, second_layer)
    grad_source, grad_probes, grad_first, grad_second = pullback((jnp.zeros_like(middle), cotangent.astype(jnp.float32)))
    layer_outputs = jnp.stack([middle, finals]).astype(jnp.bfloat16)
    input_grads = jnp.stack([grad_source, grad_probes]).astype(jnp.bfloat16)
    weight_grads = [jnp.stack([left.reshape(-1), right.reshape(-1)]) for left, right in zip(grad_first, grad_second)]
    return (layer_outputs, input_grads, weight_grads[0], weight_grads[1], weight_grads[2], weight_grads[3], weight_grads[4], weight_grads[5], weight_grads[6], weight_grads[7], weight_grads[8], weight_grads[9])
```

```python
import jax
import jax.numpy as jnp
from jax import lax
from jax.sharding import PartitionSpec as P

H = 12
HD = 64

eps_norm = 1e-06
far_below = -1000000000.0
names = ("time_qkv", "time_out", "time_fc", "space_qkv", "space_out", "up_weight", "down_weight")


def norm_rows(values, gain, shift):
    centre = values - jnp.mean(values, axis=-1, keepdims=True)
    spread = jnp.mean(centre * centre, axis=-1, keepdims=True)
    return centre * lax.rsqrt(spread + eps_norm) * gain + shift


def dot(left, right):
    return jnp.einsum("tk,kn->tn", left, right, preferred_element_type=jnp.float32)


def dot_t(left, right):
    return jnp.einsum("tn,kn->tk", left, right, preferred_element_type=jnp.float32)


def grad_dot(left, right):
    return jnp.einsum("tk,tn->kn", left, right, preferred_element_type=jnp.float32)


def column_sum(rows):
    return jnp.sum(rows.astype(jnp.float32), axis=0)


def head_map(width):
    lane = lax.broadcasted_iota(jnp.int32, (width, H), 0) // HD
    head = lax.broadcasted_iota(jnp.int32, (width, H), 1)
    return (lane == head).astype(jnp.float32)


def head_sum(rows):
    return jnp.einsum("...w,wh->...h", rows, head_map(rows.shape[-1]), precision=lax.Precision.HIGHEST)


def head_spread(rows):
    return jnp.einsum("...h,wh->...w", rows, head_map(H * HD), precision=lax.Precision.HIGHEST)


def time_probs(query, key, allowed):
    scores = head_sum(query[:, None] * key[None]) * HD ** (-0.5)
    scores = jnp.where(allowed[:, :, None, None], scores, far_below)
    return jax.nn.softmax(scores, axis=1)


def time_attend(query, key, value, allowed):
    query, key, value = (part.astype(jnp.float32) for part in (query, key, value))
    probs = time_probs(query, key, allowed).astype(jnp.bfloat16).astype(jnp.float32)
    return jnp.sum(head_spread(probs) * value[None], axis=1).astype(jnp.bfloat16)


def time_attend_back(query, key, value, allowed, grad):
    query, key, value, grad = (part.astype(jnp.float32) for part in (query, key, value, grad))
    probs = time_probs(query, key, allowed)
    wide = head_spread(probs.astype(jnp.bfloat16).astype(jnp.float32))
    grad_value = jnp.sum(wide * grad[:, None], axis=0)
    grad_probs = head_sum(grad[:, None] * value[None])
    total = jnp.sum(grad_probs * probs, axis=1, keepdims=True)
    grad_scores = (probs * (grad_probs - total)).astype(jnp.bfloat16).astype(jnp.float32)
    wide = head_spread(grad_scores) * HD ** (-0.5)
    grad_query = jnp.sum(wide * key[None], axis=1)
    grad_key = jnp.sum(wide * query[:, None], axis=0)
    return grad_query, grad_key, grad_value


def space_scores(query, key):
    return jnp.einsum("fihc,fjhc->fhij", query, key, preferred_element_type=jnp.float32) * HD ** (-0.5)


def space_attend(query, key, value):
    probs = jax.nn.softmax(space_scores(query, key), axis=-1).astype(jnp.bfloat16)
    return jnp.einsum("fhij,fjhc->fihc", probs, value, preferred_element_type=jnp.float32).astype(
        jnp.bfloat16
    )


def space_attend_back(query, key, value, grad):
    probs = jax.nn.softmax(space_scores(query, key), axis=-1)
    grad_value = jnp.einsum(
        "fhij,fihc->fjhc", probs.astype(jnp.bfloat16), grad, preferred_element_type=jnp.float32
    )
    grad_probs = jnp.einsum("fihc,fjhc->fhij", grad, value, preferred_element_type=jnp.float32)
    total = jnp.sum(grad_probs * probs, axis=-1, keepdims=True)
    grad_scores = (probs * (grad_probs - total)).astype(jnp.bfloat16)
    grad_query = jnp.einsum("fhij,fjhc->fihc", grad_scores, key, preferred_element_type=jnp.float32)
    grad_key = jnp.einsum("fhij,fihc->fjhc", grad_scores, query, preferred_element_type=jnp.float32)
    scale = HD ** (-0.5)
    return grad_query * scale, grad_key * scale, grad_value


def layer_forward(inputs, params, small, allowed, frames):
    time_qkv, time_out, time_fc, space_qkv, space_out, up_weight, down_weight = params
    gains, biases, up_bias = small
    tokens, width = inputs.shape
    by_frame = (frames, tokens // frames, width)
    by_head = (frames, tokens // frames, H, HD)
    zero_row = jnp.zeros((width,), jnp.float32)
    normed_time = norm_rows(inputs, gains[0], biases[0]).astype(jnp.bfloat16)
    bias = jnp.concatenate([biases[1], zero_row, biases[2]])
    qkv_time = (dot(normed_time, time_qkv) + bias).astype(jnp.bfloat16)
    parts = [part.reshape(by_frame) for part in jnp.split(qkv_time, 3, axis=1)]
    attn_time = time_attend(*parts, allowed).reshape(tokens, width)
    proj = (dot(attn_time, time_out) + biases[3]).astype(jnp.bfloat16)
    after_time = inputs + (dot(proj, time_fc) + biases[4])
    normed_space = norm_rows(after_time, gains[1], biases[5]).astype(jnp.bfloat16)
    bias = jnp.concatenate([biases[6], zero_row, biases[7]])
    qkv_space = (dot(normed_space, space_qkv) + bias).astype(jnp.bfloat16)
    parts = [part.reshape(by_head) for part in jnp.split(qkv_space, 3, axis=1)]
    attn_space = space_attend(*parts).reshape(tokens, width)
    after_space = after_time + (dot(attn_space, space_out) + biases[8])
    normed_mlp = norm_rows(after_space, gains[2], biases[9]).astype(jnp.bfloat16)
    hidden_pre = dot(normed_mlp, up_weight) + up_bias
    hidden_act = jax.nn.gelu(hidden_pre).astype(jnp.bfloat16)
    outputs = after_space + (dot(hidden_act, down_weight) + biases[10])
    kept = (
        inputs,
        normed_time,
        qkv_time,
        attn_time,
        proj,
        after_time,
        normed_space,
        qkv_space,
        attn_space,
        after_space,
        normed_mlp,
        hidden_pre,
        hidden_act,
    )
    return outputs, kept


def layer_backward(grad_top, params, small, kept, allowed, frames, pick):
    time_qkv, time_out, time_fc, space_qkv, space_out, up_weight, down_weight = params
    gains, biases, up_bias = small
    (
        inputs,
        normed_time,
        qkv_time,
        attn_time,
        proj,
        after_time,
        normed_space,
        qkv_space,
        attn_space,
        after_space,
        normed_mlp,
        hidden_pre,
        hidden_act,
    ) = kept
    tokens, width = inputs.shape
    by_frame = (frames, tokens // frames, width)
    by_head = (frames, tokens // frames, H, HD)
    grad_mlp = grad_top.astype(jnp.bfloat16)
    grad_down = grad_dot(pick(hidden_act), grad_mlp)
    grad_act = dot_t(grad_mlp, down_weight)
    grad_pre = jax.vjp(jax.nn.gelu, hidden_pre)[1](grad_act)[0].astype(jnp.bfloat16)
    grad_up = grad_dot(pick(normed_mlp), grad_pre)
    norm_back = jax.vjp(norm_rows, after_space, gains[2], biases[9])[1]
    grad_into, gain_mlp, shift_mlp = norm_back(dot_t(grad_pre, up_weight))
    grad_space = grad_top + grad_into
    grad_branch = grad_space.astype(jnp.bfloat16)
    grad_space_out = grad_dot(pick(attn_space), grad_branch)
    grad_attn = dot_t(grad_branch, space_out).astype(jnp.bfloat16)
    parts = [part.reshape(by_head) for part in jnp.split(qkv_space, 3, axis=1)]
    parts = space_attend_back(*parts, grad_attn.reshape(by_head))
    grad_qkv_space = jnp.concatenate([part.reshape(tokens, width) for part in parts], axis=1)
    grad_qkv_space = grad_qkv_space.astype(jnp.bfloat16)
    grad_space_qkv = grad_dot(pick(normed_space), grad_qkv_space)
    norm_back = jax.vjp(norm_rows, after_time, gains[1], biases[5])[1]
    grad_into, gain_space, shift_space = norm_back(dot_t(grad_qkv_space, space_qkv))
    grad_time = grad_space + grad_into
    grad_fc = grad_time.astype(jnp.bfloat16)
    grad_time_fc = grad_dot(pick(proj), grad_fc)
    grad_proj = dot_t(grad_fc, time_fc).astype(jnp.bfloat16)
    grad_time_out = grad_dot(pick(attn_time), grad_proj)
    grad_attn = dot_t(grad_proj, time_out).astype(jnp.bfloat16)
    parts = [part.reshape(by_frame) for part in jnp.split(qkv_time, 3, axis=1)]
    parts = time_attend_back(*parts, allowed, grad_attn.reshape(by_frame))
    grad_qkv_time = jnp.concatenate([part.reshape(tokens, width) for part in parts], axis=1)
    grad_qkv_time = grad_qkv_time.astype(jnp.bfloat16)
    grad_time_qkv = grad_dot(pick(normed_time), grad_qkv_time)
    norm_back = jax.vjp(norm_rows, inputs, gains[0], biases[0])[1]
    grad_into, gain_time, shift_time = norm_back(dot_t(grad_qkv_time, time_qkv))
    bias_qkv_time = column_sum(grad_qkv_time)
    bias_qkv_space = column_sum(grad_qkv_space)
    gain_grads = jnp.concatenate([gain_time, gain_space, gain_mlp])
    bias_grads = jnp.concatenate(
        [
            shift_time,
            bias_qkv_time[:width],
            bias_qkv_time[2 * width :],
            column_sum(grad_proj),
            column_sum(grad_fc),
            shift_space,
            bias_qkv_space[:width],
            bias_qkv_space[2 * width :],
            column_sum(grad_branch),
            shift_mlp,
            column_sum(grad_mlp),
        ]
    )
    weights = (
        grad_time_qkv,
        grad_time_out,
        grad_time_fc,
        grad_space_qkv,
        grad_space_out,
        grad_up,
        grad_down,
    )
    return grad_time + grad_into, weights, (gain_grads, bias_grads, column_sum(grad_pre))


def shards(clip_ids, tokens, *rest):
    weights, small, cotangent = rest[:7], rest[7:10], rest[10]
    section = lax.axis_index("section")
    place = lax.axis_index("seq")
    n_dp, n_seq = lax.axis_size("dp"), lax.axis_size("seq")
    first = section == 0
    micro, own_frames, patches, width = tokens.shape
    swap = [(0, 1), (1, 0)]

    def both_blocks(own):
        other = lax.ppermute(own, "section", swap)
        return jnp.where(first, own, other), jnp.where(first, other, own)

    params = [both_blocks(array[0]) for array in weights]
    smalls = [both_blocks(array[0]) for array in small]
    params = [[pair[block] for pair in params] for block in range(2)]
    smalls = [[pair[block] for pair in smalls] for block in range(2)]
    allowed = clip_ids[0][:, None] == clip_ids[0][None, :]

    def clip_of(array):
        own = jnp.where(first, array[0], array[1])
        rows = lax.all_gather(own, "seq", axis=0, tiled=True)
        return rows.reshape(-1, width)

    frames = own_frames * n_seq
    inputs = clip_of(tokens)
    grad_top = clip_of(cotangent)

    def pick(rows):
        count = rows.shape[1] // (n_dp * n_seq)
        split = rows.reshape(rows.shape[0], n_dp, n_seq, count)
        return lax.dynamic_index_in_dim(split, place, 2, keepdims=False).reshape(rows.shape[0], -1)

    outputs, kepts = [], []
    for block in range(2):
        result, kept = layer_forward(
            inputs.astype(jnp.float32), params[block], smalls[block], allowed, frames
        )
        inputs = result.astype(jnp.bfloat16)
        outputs.append(inputs)
        kepts.append(kept)
    input_grads, grads, smallg = [None] * 2, [None] * 2, [None] * 2
    for block in (1, 0):
        result, grads[block], smallg[block] = layer_backward(
            grad_top.astype(jnp.float32),
            params[block],
            smalls[block],
            kepts[block],
            allowed,
            frames,
            pick,
        )
        grad_top = result.astype(jnp.bfloat16)
        input_grads[block] = grad_top

    def home(pair):
        frame = [
            lax.dynamic_slice_in_dim(array, place * own_frames * patches, own_frames * patches)
            for array in pair
        ]
        mine = jnp.where(first, frame[0], frame[1])
        other = lax.ppermute(jnp.where(first, frame[1], frame[0]), "section", swap)
        both = [jnp.where(first, mine, other), jnp.where(first, other, mine)]
        return jnp.stack(both).reshape(1, micro, own_frames, patches, width)

    def flat(block):
        return jnp.concatenate(
            [grad.astype(jnp.bfloat16).reshape(n_dp, -1) for grad in grads[block]], axis=1
        )

    def small_flat(block):
        parts = []
        for term in smallg[block]:
            split = term.reshape(n_dp, n_seq, -1)
            parts.append(lax.dynamic_index_in_dim(split, place, 1, keepdims=False))
        return jnp.concatenate(parts, axis=1)

    def summed(pair):
        mine = jnp.where(first, pair[0], pair[1])
        other = lax.ppermute(jnp.where(first, pair[1], pair[0]), "section", swap)
        total = (mine.astype(jnp.float32) + other.astype(jnp.float32)).astype(mine.dtype)
        return lax.psum_scatter(total, "dp", scatter_dimension=0, tiled=True)[0]

    big = summed([flat(0), flat(1)]).astype(jnp.float32)
    low = summed([small_flat(0), small_flat(1)])
    shares = []
    for source, arrays in ((big, weights), (low, small)):
        at = 0
        for array in arrays:
            size = array[0].size // (n_dp * n_seq)
            shares.append(source[at : at + size][None])
            at += size
    return (home(outputs), home(input_grads), *shares)


def relay_from_behind(value, axis, steps):
    count = lax.axis_size(axis)
    leading, last = (max(0, -steps), min(count, count - steps))
    return lax.ppermute(value, axis, [(source, source + steps) for source in range(leading, last)])


def relay_norm_rows(values, gain, shift):
    centre = values - jnp.mean(values, axis=-1, keepdims=True)
    spread = jnp.mean(centre * centre, axis=-1, keepdims=True)
    return centre * lax.rsqrt(spread + eps_norm) * gain + shift


def relay_mixed_dot(left, right, form):
    return jnp.einsum(form, left, right, preferred_element_type=jnp.float32)


def relay_column_sum(grad_rows):
    return jnp.sum(grad_rows.astype(jnp.float32), axis=(0, 1))


def relay_flat_terms(terms):
    return tuple((term.reshape(-1) for term in terms))


def relay_masked_scores(queries, key_rows, allowed):
    scores = relay_mixed_dot(queries, key_rows, "bic,bjc->bij") * queries.shape[-1] ** (-0.5)
    if allowed is None:
        return scores
    return jnp.where(allowed[None], scores, far_below)


def relay_attend(queries, key_rows, values, allowed):
    scores = relay_masked_scores(queries, key_rows, allowed)
    top_score = jnp.max(scores, axis=-1, keepdims=True)
    total_exp = jnp.sum(jnp.exp(scores - top_score), axis=-1, keepdims=True)
    log_total = top_score + jnp.log(total_exp)
    weights_soft = jnp.exp(scores - log_total).astype(jnp.bfloat16)
    mixed = relay_mixed_dot(weights_soft, values, "bij,bjc->bic").astype(jnp.bfloat16)
    return (mixed, log_total)


def relay_attend_back(queries, key_rows, values, log_total, allowed, grad_out):
    scale = queries.shape[-1] ** (-0.5)
    weights_soft = jnp.exp(relay_masked_scores(queries, key_rows, allowed) - log_total)
    grad_values = relay_mixed_dot(weights_soft.astype(jnp.bfloat16), grad_out, "bij,bic->bjc")
    grad_soft = relay_mixed_dot(grad_out, values, "bic,bjc->bij")
    row_total = jnp.sum(grad_soft * weights_soft, axis=-1, keepdims=True)
    grad_scores = (weights_soft * (grad_soft - row_total)).astype(jnp.bfloat16)
    grad_queries = relay_mixed_dot(grad_scores, key_rows, "bij,bjc->bic") * scale
    grad_keys = relay_mixed_dot(grad_scores, queries, "bij,bic->bjc") * scale
    return (grad_queries, grad_keys, grad_values)


def relay_heads_first(rows):
    frames, patches, width = rows.shape
    return (
        rows.reshape(frames, patches, H, width // H)
        .transpose(0, 2, 1, 3)
        .reshape(frames * H, patches, width // H)
    )


def relay_heads_last(rows, frames):
    batch, patches, head_size = rows.shape
    return (
        rows.reshape(frames, batch // frames, patches, head_size)
        .transpose(0, 2, 1, 3)
        .reshape(frames, patches, batch // frames * head_size)
    )


def relay_time_mix(normed_time, time_qkv, time_out, bias_rows, allowed):
    frames, patches, width = normed_time.shape
    zero_row = jnp.zeros((width,), jnp.float32)
    bias_time = jnp.stack([bias_rows[1], zero_row, bias_rows[2]])
    proj_time = relay_mixed_dot(normed_time, time_qkv.reshape(width, 3, width), "fpd,dke->fkpe")
    proj_time = (proj_time + bias_time[None, :, None, :]).astype(jnp.bfloat16)
    proj_time = proj_time.reshape(frames, 3, patches * H, HD)
    by_patch = lax.all_to_all(proj_time, "seq", split_axis=2, concat_axis=0, tiled=True)
    query_time = by_patch[:, 0].transpose(1, 0, 2)
    key_time = by_patch[:, 1].transpose(1, 0, 2)
    value_time = by_patch[:, 2].transpose(1, 0, 2)
    mixed_time, total_time = relay_attend(query_time, key_time, value_time, allowed)
    back_frames = lax.all_to_all(
        mixed_time.transpose(1, 0, 2), "seq", split_axis=0, concat_axis=1, tiled=True
    )
    attn_time = back_frames.reshape(frames, patches, width)
    proj_out = (relay_mixed_dot(attn_time, time_out, "fpd,de->fpe") + bias_rows[3]).astype(jnp.bfloat16)
    return (proj_out, (normed_time, query_time, key_time, value_time, total_time, attn_time))


def relay_time_mix_back(grad_proj_out, time_qkv, time_out, time_kept, allowed):
    normed_rows, query_time, key_time, value_time, total_time, attn_time = time_kept
    frames, patches, width = grad_proj_out.shape
    grad_time_out = relay_mixed_dot(attn_time, grad_proj_out, "fpd,fpe->de")
    grad_attn_time = relay_mixed_dot(grad_proj_out, time_out, "fpe,de->fpd").astype(jnp.bfloat16)
    grad_attn_time = grad_attn_time.reshape(frames, patches * H, HD)
    grad_by_patch = lax.all_to_all(
        grad_attn_time, "seq", split_axis=1, concat_axis=0, tiled=True
    ).transpose(1, 0, 2)
    grads_time = relay_attend_back(query_time, key_time, value_time, total_time, allowed, grad_by_patch)
    grad_mixed = jnp.stack(grads_time, axis=0).transpose(2, 0, 1, 3).astype(jnp.bfloat16)
    grad_frames = lax.all_to_all(
        grad_mixed, "seq", split_axis=0, concat_axis=2, tiled=True
    ).reshape(frames, 3, patches, width)
    grad_time_qkv = relay_mixed_dot(normed_rows, grad_frames, "fpd,fkpe->dke").reshape(width, 3 * width)
    grad_normed = relay_mixed_dot(grad_frames, time_qkv.reshape(width, 3, width), "fkpe,dke->fpd")
    return (
        grad_normed,
        grad_time_qkv,
        grad_time_out,
        relay_column_sum(grad_frames[:, 0]),
        relay_column_sum(grad_frames[:, 2]),
        relay_column_sum(grad_proj_out),
    )


def relay_layer_forward(inputs, params, allowed):
    (
        time_qkv,
        time_out,
        time_fc,
        space_qkv,
        space_out,
        up_weight,
        down_weight,
        norm_gains,
        bias_rows,
        up_bias,
    ) = params
    frames, patches, width = inputs.shape
    zero_row = jnp.zeros((width,), jnp.float32)
    normed_time = relay_norm_rows(inputs, norm_gains[0], bias_rows[0]).astype(jnp.bfloat16)
    proj_out, time_kept = relay_time_mix(normed_time, time_qkv, time_out, bias_rows, allowed)
    after_time = inputs + (relay_mixed_dot(proj_out, time_fc, "fpd,de->fpe") + bias_rows[4])
    normed_space = relay_norm_rows(after_time, norm_gains[1], bias_rows[5]).astype(jnp.bfloat16)
    bias_space = jnp.stack([bias_rows[6], zero_row, bias_rows[7]])
    proj_space = relay_mixed_dot(normed_space, space_qkv.reshape(width, 3, width), "fpd,dke->fkpe")
    proj_space = (proj_space + bias_space[None, :, None, :]).astype(jnp.bfloat16)
    query_space = relay_heads_first(proj_space[:, 0])
    key_space = relay_heads_first(proj_space[:, 1])
    value_space = relay_heads_first(proj_space[:, 2])
    mixed_space, total_space = relay_attend(query_space, key_space, value_space, None)
    attn_space = relay_heads_last(mixed_space, frames)
    after_space = after_time + (relay_mixed_dot(attn_space, space_out, "fpd,de->fpe") + bias_rows[8])
    normed_mlp = relay_norm_rows(after_space, norm_gains[2], bias_rows[9]).astype(jnp.bfloat16)
    hidden_pre = relay_mixed_dot(normed_mlp, up_weight, "fpd,de->fpe") + up_bias
    hidden_act = jax.nn.gelu(hidden_pre).astype(jnp.bfloat16)
    outputs = after_space + (relay_mixed_dot(hidden_act, down_weight, "fpe,ed->fpd") + bias_rows[10])
    kept = (
        inputs,
        time_kept,
        proj_out,
        after_time,
        normed_space,
        query_space,
        key_space,
        value_space,
        total_space,
        attn_space,
        after_space,
        normed_mlp,
        hidden_pre,
        hidden_act,
    )
    return (outputs, kept)


def relay_layer_backward(grad_top, params, kept, allowed):
    (
        time_qkv,
        time_out,
        time_fc,
        space_qkv,
        space_out,
        up_weight,
        down_weight,
        norm_gains,
        bias_rows,
        up_bias,
    ) = params
    (
        inputs,
        time_kept,
        proj_out,
        after_time,
        normed_space,
        query_space,
        key_space,
        value_space,
        total_space,
        attn_space,
        after_space,
        normed_mlp,
        hidden_pre,
        hidden_act,
    ) = kept
    frames, patches, width = inputs.shape
    grad_mlp = grad_top.astype(jnp.bfloat16)
    grad_down = relay_mixed_dot(hidden_act, grad_mlp, "fpe,fpd->ed")
    grad_act = relay_mixed_dot(grad_mlp, down_weight, "fpd,ed->fpe")
    gelu_back = jax.vjp(jax.nn.gelu, hidden_pre)[1]
    grad_pre = gelu_back(grad_act)[0].astype(jnp.bfloat16)
    grad_up = relay_mixed_dot(normed_mlp, grad_pre, "fpd,fpe->de")
    grad_normed = relay_mixed_dot(grad_pre, up_weight, "fpe,de->fpd")
    norm_back = jax.vjp(relay_norm_rows, after_space, norm_gains[2], bias_rows[9])[1]
    grad_into, gain_mlp, shift_mlp = norm_back(grad_normed)
    grad_space = grad_top + grad_into
    grad_branch = grad_space.astype(jnp.bfloat16)
    grad_space_out = relay_mixed_dot(attn_space, grad_branch, "fpd,fpe->de")
    grad_attn = relay_heads_first(relay_mixed_dot(grad_branch, space_out, "fpe,de->fpd").astype(jnp.bfloat16))
    grads_space = relay_attend_back(query_space, key_space, value_space, total_space, None, grad_attn)
    grad_proj = jnp.stack([relay_heads_last(piece, frames) for piece in grads_space], axis=1).astype(
        jnp.bfloat16
    )
    grad_space_qkv = relay_mixed_dot(normed_space, grad_proj, "fpd,fkpe->dke").reshape(width, 3 * width)
    grad_normed = relay_mixed_dot(grad_proj, space_qkv.reshape(width, 3, width), "fkpe,dke->fpd")
    norm_back = jax.vjp(relay_norm_rows, after_time, norm_gains[1], bias_rows[5])[1]
    grad_into, gain_space, shift_space = norm_back(grad_normed)
    grad_time = grad_space + grad_into
    grad_branch_time = grad_time.astype(jnp.bfloat16)
    grad_time_fc = relay_mixed_dot(proj_out, grad_branch_time, "fpd,fpe->de")
    grad_proj_out = relay_mixed_dot(grad_branch_time, time_fc, "fpe,de->fpd").astype(jnp.bfloat16)
    grad_normed, grad_time_qkv, grad_time_out, query_bias, value_bias, out_bias = relay_time_mix_back(
        grad_proj_out, time_qkv, time_out, time_kept, allowed
    )
    norm_back = jax.vjp(relay_norm_rows, inputs, norm_gains[0], bias_rows[0])[1]
    grad_into, gain_time, shift_time = norm_back(grad_normed)
    grad_inputs = grad_time + grad_into
    gain_grads = jnp.stack([gain_time, gain_space, gain_mlp])
    bias_grads = jnp.stack(
        [
            shift_time,
            query_bias,
            value_bias,
            out_bias,
            relay_column_sum(grad_branch_time),
            shift_space,
            relay_column_sum(grad_proj[:, 0]),
            relay_column_sum(grad_proj[:, 2]),
            relay_column_sum(grad_branch),
            shift_mlp,
            relay_column_sum(grad_mlp),
        ]
    )
    up_grad = relay_column_sum(grad_pre)
    return (
        grad_inputs,
        (
            grad_time_qkv,
            grad_time_out,
            grad_time_fc,
            grad_space_qkv,
            grad_space_out,
            grad_up,
            grad_down,
            gain_grads,
            bias_grads,
            up_grad,
        ),
    )


def relay_shards(
    clip_ids,
    tokens,
    time_qkv,
    time_out,
    time_fc,
    space_qkv,
    space_out,
    up_weight,
    down_weight,
    norm_gains,
    bias_rows,
    up_bias,
    cotangent,
):
    params = (
        time_qkv[0],
        time_out[0],
        time_fc[0],
        space_qkv[0],
        space_out[0],
        up_weight[0],
        down_weight[0],
        norm_gains[0],
        bias_rows[0],
        up_bias[0],
    )
    allowed = clip_ids[0][:, None] == clip_ids[0][None, :]
    first_section = lax.axis_index("section") == 0
    micro = tokens.shape[0]
    arriving = jnp.zeros_like(tokens[0])
    section_inputs = []
    section_outputs = []
    for moment in range(micro + 1):
        taken_rows = jnp.where(first_section, tokens[min(moment, micro - 1)], arriving)
        result = relay_layer_forward(taken_rows.astype(jnp.float32), params, allowed)[0].astype(
            jnp.bfloat16
        )
        section_inputs.append(taken_rows)
        section_outputs.append(result)
        if moment < micro:
            arriving = relay_from_behind(result, "section", 1)
    saved_inputs = [
        jnp.where(first_section, section_inputs[number], section_inputs[number + 1])
        for number in range(micro)
    ]
    layer_outputs = jnp.stack(
        [
            jnp.where(first_section, section_outputs[number], section_outputs[number + 1])
            for number in range(micro)
        ]
    )
    returning = jnp.zeros_like(tokens[0])
    back_results = []
    totals = None
    for moment in range(micro + 1):
        grad_given = jnp.where(first_section, returning, cotangent[min(moment, micro - 1)]).astype(
            jnp.float32
        )
        source_rows = jnp.where(
            first_section, saved_inputs[max(moment - 1, 0)], saved_inputs[min(moment, micro - 1)]
        )
        live_share = jnp.where(
            first_section, 1.0 if moment >= 1 else 0.0, 1.0 if moment < micro else 0.0
        )
        kept = relay_layer_forward(source_rows.astype(jnp.float32), params, allowed)[1]
        grad_inputs, weight_terms = relay_layer_backward(grad_given, params, kept, allowed)
        grad_inputs = grad_inputs.astype(jnp.bfloat16)
        back_results.append(grad_inputs)
        weight_terms = relay_flat_terms(jax.tree.map(lambda term: term * live_share, weight_terms))
        if totals is None:
            totals = tuple(weight_terms)
        else:
            totals = tuple((left + right for left, right in zip(totals, weight_terms)))
        if moment < micro:
            returning = relay_from_behind(grad_inputs, "section", -1)
    input_grads = jnp.stack(
        [
            jnp.where(first_section, back_results[number + 1], back_results[number])
            for number in range(micro)
        ]
    )
    shares = (
        lax.psum_scatter(totals[0], ("dp", "seq"), scatter_dimension=0, tiled=True),
        lax.psum_scatter(totals[1], ("dp", "seq"), scatter_dimension=0, tiled=True),
        lax.psum_scatter(totals[2], ("dp", "seq"), scatter_dimension=0, tiled=True),
        lax.psum_scatter(totals[3], ("dp", "seq"), scatter_dimension=0, tiled=True),
        lax.psum_scatter(totals[4], ("dp", "seq"), scatter_dimension=0, tiled=True),
        lax.psum_scatter(totals[5], ("dp", "seq"), scatter_dimension=0, tiled=True),
        lax.psum_scatter(totals[6], ("dp", "seq"), scatter_dimension=0, tiled=True),
        lax.psum_scatter(totals[7], ("dp", "seq"), scatter_dimension=0, tiled=True),
        lax.psum_scatter(totals[8], ("dp", "seq"), scatter_dimension=0, tiled=True),
        lax.psum_scatter(totals[9], ("dp", "seq"), scatter_dimension=0, tiled=True),
    )
    return (
        layer_outputs[None],
        input_grads[None],
        shares[0][None],
        shares[1][None],
        shares[2][None],
        shares[3][None],
        shares[4][None],
        shares[5][None],
        shares[6][None],
        shares[7][None],
        shares[8][None],
        shares[9][None],
    )


def solution(mesh):
    stacked = P("section", None, None)
    spread = P(None, ("dp", "seq"), None, None)
    in_specs = (P("dp", None), spread, *[stacked] * 9, P("section", None), spread)
    flat = P("section", ("dp", "seq"))
    out = P("section", None, ("dp", "seq"), None, None)
    relay = mesh.shape["seq"] > 4 or mesh.shape["section"] != 2
    return jax.shard_map(
        relay_shards if relay else shards, mesh=mesh, in_specs=in_specs, out_specs=(out, out, *[flat] * 10), check_vma=False
    )
```

```python
import functools

import jax
import jax.numpy as jnp
from jax import lax
from jax.experimental import pallas as pl
from jax.experimental.pallas import tpu as pltpu
from jax.sharding import PartitionSpec as P

H = 12
HD = 64
PAIR = 2 * HD
eps_norm = 1e-06
far_below = -1000000000.0
BF = jnp.bfloat16
F32 = jnp.float32
VMEM_BYTES = 62 << 20
NEXT_ID = [1]


def nn(left, right):
    return lax.dot_general(left, right, (((1,), (0,)), ((), ())), preferred_element_type=F32)


def nt(left, right):
    return lax.dot_general(left, right, (((1,), (1,)), ((), ())), preferred_element_type=F32)


def norm_stats(values):
    centre = values - jnp.mean(values, axis=-1, keepdims=True)
    scale = lax.rsqrt(jnp.mean(centre * centre, axis=-1, keepdims=True) + eps_norm)
    return centre * scale, scale


def rows_at(index, count):
    return pl.ds(pl.multiple_of(index * count, count), count)


def norm_into(source, target, gain, shift, chunk):
    @pl.loop(0, source.shape[0] // chunk)
    def _(step):
        at = rows_at(step, chunk)
        hat, _ = norm_stats(source[at, :].astype(F32))
        target[at, :] = (hat * gain[...] + shift[...]).astype(BF)


def gelu_both(pre):
    rate, cube = 0.7978845608028654, 0.044715
    square = pre * pre
    tanh = jnp.tanh(pre * (rate + rate * cube * square))
    half = 0.5 + 0.5 * tanh
    act = pre * half
    slope = half + act * (1.0 - tanh) * (rate + 3.0 * rate * cube * square)
    return act, slope


class Copies:
    def __init__(self, sems):
        self.sems, self.used, self.open = sems, 0, []

    def fetch(self, own, other, target, mine):
        sem = self.sems.at[self.used]
        self.used += 1

        @pl.when(mine)
        def _():
            pltpu.make_async_copy(own, target, sem).start()

        @pl.when(jnp.logical_not(mine))
        def _():
            pltpu.make_async_copy(other, target, sem).start()

        return pltpu.make_async_copy(own, target, sem)

    def start(self, source, target):
        copy = pltpu.make_async_copy(source, target, self.sems.at[self.used])
        self.used += 1
        copy.start()
        return copy

    def store(self, source, target):
        self.open.append(self.start(source, target))

    def finish(self):
        for copy in self.open:
            copy.wait()


def time_attention(qkv, attn, probs, stage, soft, heads, heads_t, clips, frames, rows, width):
    @pl.loop(0, frames)
    def _(i):
        own = rows_at(i, rows)
        for j in range(frames):
            stage[pl.ds(j * rows, rows), :] = qkv[own, 0:width] * qkv[pl.ds(j * rows, rows), width : 2 * width]
        scores = nn(stage[...], heads[...])
        parts = []
        for j in range(frames):
            open_pair = clips[0, i] == clips[0, j]
            parts.append(scores[j * rows : (j + 1) * rows] + jnp.where(open_pair, 0.0, far_below))
        top = functools.reduce(jnp.maximum, parts)
        parts = [jnp.exp(part - top) for part in parts]
        inverse = 1.0 / sum(parts)
        for j in range(frames):
            prob = parts[j] * inverse
            probs[i, pl.ds(j * rows, rows), :] = prob
            soft[pl.ds(j * rows, rows), :] = prob.astype(BF)
        total = None
        for j in range(frames):
            at = pl.ds(j * rows, rows)
            term = nn(soft[at, :], heads_t[...]) * qkv[at, 2 * width : 3 * width].astype(F32)
            total = term if total is None else total + term
        attn[own, :] = total.astype(BF)


def space_attention(qkv, attn, frames, rows, patches, width):
    lane = lax.broadcasted_iota(jnp.int32, (rows, PAIR), 1)
    column = lax.broadcasted_iota(jnp.int32, (rows, rows), 1)

    @pl.loop(0, frames)
    def _(f):
        at = rows_at(f, rows)

        @pl.loop(0, width // PAIR)
        def _(pair):
            def part(which):
                return qkv[at, pl.ds(pl.multiple_of(which * width + pair * PAIR, PAIR), PAIR)]

            query, key, value = part(0) * BF(HD**-0.5), part(1), part(2)
            mixed = []
            for half in range(2):
                mine = jnp.where(lane // HD == half, query, BF(0))
                scores = jnp.where(column < patches, nt(mine, key), far_below)
                expo = jnp.exp(scores - jnp.max(scores, axis=-1, keepdims=True))
                soft = expo * (1.0 / jnp.sum(expo, axis=-1, keepdims=True))
                mixed.append(nn(soft.astype(BF), value))
            both = jnp.where(lane < HD, mixed[0], mixed[1])
            attn[at, pl.ds(pl.multiple_of(pair * PAIR, PAIR), PAIR)] = both.astype(BF)


class Smalls:
    def __init__(self, own, other, held, mine):
        for which, refs in ((mine, own), (jnp.logical_not(mine), other)):

            @pl.when(which)
            def _(refs=refs):
                for source, target in zip(refs, held):
                    target[...] = source[...].reshape(target.shape)

        self.gains, self.biases, self.up_bias = held

    def gain(self, row):
        return self.gains.at[row : row + 1]

    def bias(self, row):
        return self.biases.at[row : row + 1]


def fill_heads(heads, heads_t):
    lane = lax.broadcasted_iota(jnp.int32, heads.shape, 0) // HD
    head = lax.broadcasted_iota(jnp.int32, heads.shape, 1)
    heads[...] = jnp.where(lane == head, HD**-0.5, 0.0).astype(BF)
    lane = lax.broadcasted_iota(jnp.int32, heads_t.shape, 1) // HD
    head = lax.broadcasted_iota(jnp.int32, heads_t.shape, 0)
    heads_t[...] = jnp.where(lane == head, 1.0, 0.0).astype(BF)


def fill_pick(pick, outer, place, count):
    each = pick.shape[0] // outer
    row = lax.broadcasted_iota(jnp.int32, pick.shape, 0)
    column = lax.broadcasted_iota(jnp.int32, pick.shape, 1)
    pick[...] = jnp.where(column == (row // each * count + place) * each + row % each, 1.0, 0.0).astype(BF)


def project(source, weight, biases, target):
    width = source.shape[1]
    for part in range(3):
        at = slice(part * width, (part + 1) * width)
        result = nn(source[...], weight[:, at])
        if biases[part] is not None:
            result = result + biases[part][...]
        target[:, at] = result.astype(BF)


def forward_time_kernel(block, frames, x, where, clips, *refs):
    small, small_other, own, other, refs = refs[:3], refs[3:6], refs[6:9], refs[9:12], refs[12:]
    (qkv_out, attn_out, proj_out, x1_out, probs_out), refs = refs[:5], refs[5:]
    (time_qkv, time_out, time_fc), small_held, refs = refs[:3], refs[3:6], refs[6:]
    (normed, qkv, attn, proj, x1, probs, soft, heads, heads_t, sems) = refs
    total, width = x.shape
    copies = Copies(sems)
    mine = where[0] == block
    loads = [copies.fetch(a, b, c, mine) for a, b, c in zip(own, other, (time_qkv, time_out, time_fc))]
    smalls = Smalls(small, small_other, small_held, mine)
    fill_heads(heads, heads_t)
    norm_into(x, normed, smalls.gain(0), smalls.bias(0), 64)
    loads[0].wait()
    project(normed, time_qkv, (smalls.bias(1), None, smalls.bias(2)), qkv)
    copies.store(qkv, qkv_out)
    time_attention(qkv, attn, probs, normed, soft, heads, heads_t, clips, frames, total // frames, width)
    copies.store(attn, attn_out)
    copies.store(probs, probs_out)
    loads[1].wait()
    proj[...] = (nn(attn[...], time_out[...]) + smalls.bias(3)[...]).astype(BF)
    copies.store(proj, proj_out)
    loads[2].wait()
    x1[...] = x[...].astype(F32) + nn(proj[...], time_fc[...]) + smalls.bias(4)[...]
    copies.store(x1, x1_out)
    copies.finish()


def forward_rest_kernel(block, frames, patches, x1, where, *refs):
    small, small_other, own, other, refs = refs[:3], refs[3:6], refs[6:10], refs[10:14], refs[14:]
    (y_out, qkv_out, attn_out, x2_out, act_out, slope_out), refs = refs[:6], refs[6:]
    (space_qkv, space_out, up_weight, down_weight), small_held, refs = refs[:4], refs[4:7], refs[7:]
    (normed, y, qkv, attn, x2, act, slope, sems) = refs
    total, width = x1.shape
    copies = Copies(sems)
    mine = where[0] == block
    held = (space_qkv, space_out, up_weight, down_weight)
    loads = [copies.fetch(a, b, c, mine) for a, b, c in zip(own, other, held)]
    smalls = Smalls(small, small_other, small_held, mine)
    norm_into(x1, normed, smalls.gain(1), smalls.bias(5), 64)
    loads[0].wait()
    project(normed, space_qkv, (smalls.bias(6), None, smalls.bias(7)), qkv)
    copies.store(qkv, qkv_out)
    space_attention(qkv, attn, frames, total // frames, patches, width)
    copies.store(attn, attn_out)
    loads[1].wait()
    x2[...] = x1[...] + nn(attn[...], space_out[...]) + smalls.bias(8)[...]
    copies.store(x2, x2_out)
    norm_into(x2, normed, smalls.gain(2), smalls.bias(9), 64)
    loads[2].wait()

    @pl.loop(0, up_weight.shape[1] // width)
    def _(tile):
        at = rows_at(tile, width)
        pre = nn(normed[...], up_weight[:, at]) + smalls.up_bias[:, at]
        both = gelu_both(pre)
        act[:, at] = both[0].astype(BF)
        slope[:, at] = both[1].astype(BF)

    copies.store(act, act_out)
    copies.store(slope, slope_out)
    loads[3].wait()

    @pl.loop(0, 3)
    def _(tile):
        at = rows_at(tile, width // 3)
        y_at = nn(act[...], down_weight[:, at]) + smalls.biases[10:11, at] + x2[:, at]
        y[:, at] = y_at.astype(BF)

    copies.store(y, y_out)
    copies.finish()


def struct(shape, dtype=BF):
    return jax.ShapeDtypeStruct(shape, dtype)


def held(*structs):
    return [pltpu.VMEM(s.shape, s.dtype) for s in structs]


IN_VMEM = pl.BlockSpec(memory_space=pltpu.VMEM)
IN_SMEM = pl.BlockSpec(memory_space=pltpu.SMEM)
IN_HBM = pl.BlockSpec(memory_space=pl.ANY)


def small_held(small):
    return held(*[struct((array.size // array.shape[-1], array.shape[-1]), F32) for array in small])


def call(kernel, name, flops, specs, args, outs, out_specs, scratch, carried=None, partial=None):
    more_args, more_outs, more_scratch = relay_args(partial)
    specs, args = specs + [IN_HBM] * len(more_args), (*args, *more_args)
    outs, out_specs, scratch = outs + more_outs, out_specs + [IN_VMEM] * len(more_outs), scratch + more_scratch
    remote = {}
    if partial is not None:
        NEXT_ID.append(NEXT_ID[-1] + 1)
        remote = dict(collective_id=NEXT_ID[-1], has_side_effects=True)
    return pl.pallas_call(
        kernel,
        out_shape=outs,
        in_specs=specs,
        out_specs=out_specs,
        scratch_shapes=scratch,
        compiler_params=pltpu.CompilerParams(vmem_limit_bytes=VMEM_BYTES, **remote),
        cost_estimate=pl.CostEstimate(flops=flops, bytes_accessed=30 << 20, transcendentals=0),
        name=name,
    )(*args)


def forward_time(block, frames, x, where, clips, small, small_other, own, other):
    total, width = x.shape
    wide, full, triple = struct((total, width)), struct((total, width), F32), struct((total, 3 * width))
    probs = struct((frames, total, PAIR), F32)
    scratch = held(*own) + small_held(small)
    scratch += held(wide, triple, wide, wide, full, probs, struct((total, PAIR)), struct((width, PAIR)), struct((PAIR, width)))
    return call(
        functools.partial(forward_time_kernel, block, frames),
        f"block{block}_forward_time",
        10 * total * width * width,
        [IN_VMEM, IN_SMEM, IN_SMEM] + [IN_VMEM] * 6 + [IN_HBM] * 6,
        (x, where, clips, *small, *small_other, *own, *other),
        [triple, wide, wide, full, probs],
        [IN_HBM] * 5,
        scratch + [pltpu.SemaphoreType.DMA((8,))],
    )


def forward_rest(block, frames, patches, x1, where, small, small_other, own, other):
    total, width = x1.shape
    wide, full, triple = struct((total, width)), struct((total, width), F32), struct((total, 3 * width))
    deep = struct((total, own[2].shape[1]))
    scratch = held(*own) + small_held(small) + held(wide, wide, triple, wide, full, deep, deep)
    return call(
        functools.partial(forward_rest_kernel, block, frames, patches),
        f"block{block}_forward_rest",
        24 * total * width * width,
        [IN_VMEM, IN_SMEM] + [IN_VMEM] * 6 + [IN_HBM] * 8,
        (x1, where, *small, *small_other, *own, *other),
        [wide, triple, wide, full, deep, deep],
        [IN_HBM] * 6,
        scratch + [pltpu.SemaphoreType.DMA((10,))],
    )

MESH = pl.DeviceIdType.MESH


class Relay:
    def __init__(self, block, refs):
        self.on = block is not None
        self.block = block
        if not self.on:
            return
        self.partial, self.out, self.mine, self.mates, self.taken, self.send, self.recv = refs
        self.count = self.mates.shape[0]
        self.z = lax.axis_index("dp")
        self.section = lax.axis_index("section")
        self.home = self.section == block
        self.away = self.section != block

    def over(self):
        return pltpu.make_async_remote_copy(
            self.partial,
            self.mates,
            self.send.at[0],
            self.recv.at[0],
            device_id={"section": 1 - self.section},
            device_id_type=MESH,
        )

    def local(self):
        return pltpu.make_async_copy(self.partial, self.mine, self.send.at[self.count])

    def target(self, step):
        return lax.rem(self.z + step, self.count)

    def along(self, step):
        return pltpu.make_async_remote_copy(
            self.mine.at[self.target(step)],
            self.taken.at[step - 1],
            self.send.at[step],
            self.recv.at[step],
            device_id={"dp": self.target(step)},
            device_id_type=MESH,
        )

    def begin(self):
        if not self.on:
            return
        barrier = pltpu.get_barrier_semaphore()
        pl.semaphore_signal(barrier, inc=1, device_id={"section": 1 - self.section}, device_id_type=MESH)
        for step in range(1, self.count):
            pl.semaphore_signal(barrier, inc=1, device_id={"dp": self.target(step)}, device_id_type=MESH)
        pl.semaphore_wait(barrier, self.count)

        @pl.when(self.away)
        def _():
            self.over().start()

        @pl.when(self.home)
        def _():
            self.local().start()

    def middle(self):
        if not self.on:
            return

        @pl.when(self.home)
        def _():
            self.local().wait()
            self.over().wait_recv()
            for step in range(1, self.count):
                at = self.target(step)
                self.mine[at] = (self.mine[at].astype(F32) + self.mates[at].astype(F32)).astype(BF)
                self.along(step).start()

        @pl.when(self.away)
        def _():
            self.over().wait_send()

    def end(self):
        if not self.on:
            return

        @pl.when(self.home)
        def _():
            for step in range(1, self.count):
                self.along(step).wait()
            total = self.mine[self.z].astype(F32) + self.mates[self.z].astype(F32)
            for step in range(1, self.count):
                total = total + self.taken[step - 1].astype(F32)
            self.out[...] = total

        @pl.when(self.away)
        def _():
            self.out[...] = jnp.zeros_like(self.out)


def split_relay(block, refs, outs):
    if block is None:
        return refs[:outs], Relay(None, ()), refs[outs:]
    partial, results, out, refs = refs[0], refs[1 : 1 + outs], refs[1 + outs], refs[2 + outs :]
    return results, Relay(block, (partial, out, *refs[-5:])), refs[:-5]


def relay_args(partial):
    if partial is None:
        return [], [], []
    count, rows, width = partial.shape
    dma = pltpu.SemaphoreType.DMA
    scratch = held(struct(partial.shape), struct(partial.shape), struct((count - 1, rows, width)))
    return [partial], [struct((rows, width), F32)], scratch + [dma((count + 1,)), dma((count,))]


BIAS, UP, LOW = 3, 14, 24


def norm_back(hidden, grads, gain, above, target, sums, chunk):
    width = hidden.shape[1]
    sums[...] = jnp.zeros_like(sums)

    def fold(rows):
        return jnp.sum(rows.reshape(chunk // 8, 8, width), axis=0)

    @pl.loop(0, hidden.shape[0] // chunk)
    def _(step):
        at = rows_at(step, chunk)
        hat, scale = norm_stats(hidden[at, :].astype(F32))
        grad = grads[at, :]
        sums[0:8, :] += fold(grad * hat)
        sums[8:16, :] += fold(grad)
        inner = grad * gain[...]
        mean = jnp.mean(inner, axis=-1, keepdims=True)
        slant = jnp.mean(inner * hat, axis=-1, keepdims=True)
        result = above[at, :].astype(F32) + scale * (inner - mean - hat * slant)
        target[at, :] = result.astype(target.dtype)


def norm_sums(sums, low, gain_row, bias_row):
    low[gain_row : gain_row + 1, :] = jnp.sum(sums[0:8, :], axis=0, keepdims=True)
    low[BIAS + bias_row : BIAS + bias_row + 1, :] = jnp.sum(sums[8:16, :], axis=0, keepdims=True)


def fill_ones(turned, count):
    turned[pl.ds(count, 16), :] = jnp.ones((16, turned.shape[1]), BF)


def weight_grad(turned, count, grads, result, row, low, *low_rows):
    width = low.shape[1]
    parts = result.shape[0]
    each = count // parts

    for step, low_row in enumerate(low_rows):
        both = nn(turned[0 : count + 16, :], grads[:, step * width : (step + 1) * width])
        at = slice(row + step * each, row + (step + 1) * each)
        for part in range(parts):
            result[part, at, :] = both[part * each : (part + 1) * each].astype(BF)
        if low_row is not None:
            low[low_row : low_row + 1, :] = both[count : count + 1, :]


def tiled_nt(left, right, target, tile):
    @pl.loop(0, right.shape[0] // tile)
    def _(step):
        at = rows_at(step, tile)
        target[:, at] = nt(left[...], right[at, :])


def back_mlp_kernel(block, carried, places, gy, *refs):
    small, small_other, own, other, refs = refs[:3], refs[3:6], refs[6:8], refs[8:10], refs[10:]
    act_in, slope_in, x2_in, refs = refs[0], refs[1], refs[2], refs[3:]
    (g2_out, grads_out, low), relay, refs = split_relay(carried, refs, 3)
    (up_weight, down_weight), small_held, refs = refs[:2], refs[2:5], refs[5:]
    (act, slope, x2, normed, gpre, gnm, g2, turned, result, sums, pick, pick_wide, sems) = refs
    total, width = gy.shape
    chunk = 64
    copies = Copies(sems)
    relay.begin()
    mine = lax.axis_index("section") == block
    load_down = copies.fetch(own[1], other[1], down_weight, mine)
    load_slope = copies.start(slope_in, slope)
    load_up = copies.fetch(own[0], other[0], up_weight, mine)
    load_act = copies.start(act_in, act)
    load_x2 = copies.start(x2_in, x2)
    smalls = Smalls(small, small_other, small_held, mine)
    fill_pick(pick, result.shape[0], lax.axis_index("seq"), places)
    fill_pick(pick_wide, 1, lax.axis_index("seq"), places)
    low[...] = jnp.zeros_like(low)
    load_down.wait()
    load_slope.wait()

    @pl.loop(0, down_weight.shape[0] // width)
    def _(tile):
        at = rows_at(tile, width)
        gpre[:, at] = (nt(gy[...], down_weight[at, :]) * slope[:, at].astype(F32)).astype(BF)

    relay.middle()
    load_up.wait()
    tiled_nt(gpre, up_weight, gnm, width // 3)
    load_x2.wait()
    norm_back(x2, gnm, smalls.gain(2), gy, g2, sums, chunk)
    copies.store(g2, g2_out)
    norm_sums(sums, low, 2, 9)
    norm_into(x2, normed, smalls.gain(2), smalls.bias(9), chunk)
    count = pick.shape[0]
    turned[0:count, :] = nt(pick[...], normed[...]).astype(BF)
    fill_ones(turned, count)
    weight_grad(turned, count, gpre, result, 0, low, *range(UP, UP + gpre.shape[1] // width))
    load_act.wait()
    wide = pick_wide.shape[0]
    parts = act.shape[1] // pick_wide.shape[1]

    @pl.loop(0, parts)
    def _(part):
        turned[rows_at(part, wide), :] = nt(pick_wide[...], act[:, rows_at(part, pick_wide.shape[1])]).astype(BF)

    fill_ones(turned, parts * wide)
    weight_grad(turned, parts * wide, gy, result, result.shape[1] - parts * wide // result.shape[0], low, BIAS + 10)
    copies.store(result, grads_out)
    relay.end()
    copies.finish()


def space_attention_back(qkv, grads, result, frames, rows, patches, width):
    lane = lax.broadcasted_iota(jnp.int32, (rows, PAIR), 1)
    key_row = lax.broadcasted_iota(jnp.int32, (rows, rows), 0)
    unit = (
        lax.broadcasted_iota(jnp.int32, (rows, rows), 0) == lax.broadcasted_iota(jnp.int32, (rows, rows), 1)
    ).astype(BF)
    scaled_unit = jnp.where(
        lax.broadcasted_iota(jnp.int32, (PAIR, PAIR), 0) == lax.broadcasted_iota(jnp.int32, (PAIR, PAIR), 1),
        HD**-0.5,
        0.0,
    ).astype(BF)

    @pl.loop(0, frames)
    def _(f):
        at = rows_at(f, rows)

        @pl.loop(0, width // PAIR)
        def _(pair):
            def lanes(which):
                return pl.ds(pl.multiple_of(which * width + pair * PAIR, PAIR), PAIR)

            query = qkv[at, lanes(0)] * BF(HD**-0.5)
            key, value, grad = qkv[at, lanes(1)], qkv[at, lanes(2)], grads[at, lanes(0)]
            key_t = nt(scaled_unit, key).astype(BF)
            turned_query, grad_key, grad_value = [], [], []
            for half in range(2):
                mine = lane // HD == half
                scores = nt(jnp.where(mine, key, BF(0)), query)
                scores = jnp.where(key_row < patches, scores, far_below)
                expo = jnp.exp(scores - jnp.max(scores, axis=0, keepdims=True))
                soft = expo * (1.0 / jnp.sum(expo, axis=0, keepdims=True))
                grad_soft = nt(jnp.where(mine, value, BF(0)), grad)
                total = jnp.sum(soft * grad_soft, axis=0, keepdims=True)
                grad_scores = (soft * (grad_soft - total)).astype(BF)
                grad_value.append(nn(soft.astype(BF), grad))
                grad_key.append(nn(grad_scores, query))
                turned_query.append(nn(key_t[half * HD : (half + 1) * HD], grad_scores))
            turned = jnp.concatenate(turned_query, axis=0).astype(BF)
            result[at, lanes(0)] = nt(unit, turned).astype(BF)
            result[at, lanes(1)] = jnp.where(lane < HD, grad_key[0], grad_key[1]).astype(BF)
            result[at, lanes(2)] = jnp.where(lane < HD, grad_value[0], grad_value[1]).astype(BF)


def back_space_kernel(block, carried, places, frames, patches, *refs):
    small, small_other, own, other, refs = refs[:3], refs[3:6], refs[6:8], refs[8:10], refs[10:]
    g2_in, qkv_in, attn_in, x1_in, refs = refs[0], refs[1], refs[2], refs[3], refs[4:]
    (g1_out, grads_out, low), relay, refs = split_relay(carried, refs, 3)
    (space_qkv, space_out), small_held, refs = refs[:2], refs[2:5], refs[5:]
    (g2, qkv, attn, x1, g2_low, gattn, gqkv, gnorm, g1, turned, result, sums, pick, sems) = refs
    total, width = g2.shape
    chunk = 64
    copies = Copies(sems)
    relay.begin()
    mine = lax.axis_index("section") == block
    load_g2 = copies.start(g2_in, g2)
    load_out = copies.fetch(own[1], other[1], space_out, mine)
    load_qkv = copies.start(qkv_in, qkv)
    load_weight = copies.fetch(own[0], other[0], space_qkv, mine)
    load_attn = copies.start(attn_in, attn)
    load_x1 = copies.start(x1_in, x1)
    smalls = Smalls(small, small_other, small_held, mine)
    fill_pick(pick, result.shape[0], lax.axis_index("seq"), places)
    low[...] = jnp.zeros_like(low)
    load_g2.wait()
    g2_low[...] = g2[...].astype(BF)
    load_out.wait()
    gattn[...] = nt(g2_low[...], space_out[...]).astype(BF)
    relay.middle()
    load_qkv.wait()
    space_attention_back(qkv, gattn, gqkv, frames, total // frames, patches, width)
    load_weight.wait()
    tiled_nt(gqkv, space_qkv, gnorm, width // 3)
    load_x1.wait()
    norm_back(x1, gnorm, smalls.gain(1), g2, g1, sums, chunk)
    copies.store(g1, g1_out)
    norm_sums(sums, low, 1, 5)
    load_attn.wait()
    count = pick.shape[0]
    turned[0:count, :] = nt(pick[...], attn[...]).astype(BF)
    fill_ones(turned, count)
    each = count // result.shape[0]
    weight_grad(turned, count, g2_low, result, 3 * each, low, BIAS + 8)
    norm_into(x1, attn, smalls.gain(1), smalls.bias(5), chunk)
    turned[0:count, :] = nt(pick[...], attn[...]).astype(BF)
    weight_grad(turned, count, gqkv, result, 0, low, BIAS + 6, None, BIAS + 7)
    copies.store(result, grads_out)
    relay.end()
    copies.finish()


def time_attention_back(qkv, grads, probs, result, stage, soft, soft_grad, grad_key, grad_value, heads, heads_t, frames, rows, width):
    grad_key[...] = jnp.zeros_like(grad_key)
    grad_value[...] = jnp.zeros_like(grad_value)

    @pl.loop(0, frames)
    def _(i):
        own = rows_at(i, rows)
        for j in range(frames):
            stage[pl.ds(j * rows, rows), :] = grads[own, :] * qkv[pl.ds(j * rows, rows), 2 * width : 3 * width]
        grad_soft = nn(stage[...], heads[...]) * HD**0.5
        parts = [probs[i, pl.ds(j * rows, rows), :] for j in range(frames)]
        changes = [grad_soft[j * rows : (j + 1) * rows] for j in range(frames)]
        total = sum(part * change for part, change in zip(parts, changes))
        for j in range(frames):
            at = pl.ds(j * rows, rows)
            soft[at, :] = parts[j].astype(BF)
            soft_grad[at, :] = (parts[j] * (changes[j] - total)).astype(BF)
        grad_query = None
        for j in range(frames):
            at = pl.ds(j * rows, rows)
            wide = nn(soft_grad[at, :], heads_t[...])
            term = wide * qkv[at, width : 2 * width].astype(F32)
            grad_query = term if grad_query is None else grad_query + term
            grad_key[at, :] += wide * qkv[own, 0:width].astype(F32)
            grad_value[at, :] += nn(soft[at, :], heads_t[...]) * grads[own, :].astype(F32)
        result[own, 0:width] = (grad_query * HD**-0.5).astype(BF)

    result[:, width : 2 * width] = (grad_key[...] * HD**-0.5).astype(BF)
    result[:, 2 * width : 3 * width] = grad_value[...].astype(BF)


def back_time_kernel(block, carried, places, frames, x, *refs):
    small, small_other, own, other, refs = refs[:3], refs[3:6], refs[6:9], refs[9:12], refs[12:]
    g1_in, qkv_in, attn_in, proj_in, probs_in, refs = refs[0], refs[1], refs[2], refs[3], refs[4], refs[5:]
    (gx_out, grads_out, low), relay, refs = split_relay(carried, refs, 3)
    (time_qkv, time_out, time_fc), small_held, refs = refs[:3], refs[3:6], refs[6:]
    (g1, qkv, attn, proj, probs, g1_low, gproj, gattn, gqkv, stage, soft, soft_grad), refs = refs[:12], refs[12:]
    (grad_key, grad_value, turned, result, sums, pick, heads, heads_t, sems) = refs
    total, width = x.shape
    chunk = 64
    copies = Copies(sems)
    relay.begin()
    mine = lax.axis_index("section") == block
    load_g1 = copies.start(g1_in, g1)
    load_fc = copies.fetch(own[2], other[2], time_fc, mine)
    load_out = copies.fetch(own[1], other[1], time_out, mine)
    load_qkv = copies.start(qkv_in, qkv)
    load_probs = copies.start(probs_in, probs)
    load_weight = copies.fetch(own[0], other[0], time_qkv, mine)
    load_proj = copies.start(proj_in, proj)
    load_attn = copies.start(attn_in, attn)
    smalls = Smalls(small, small_other, small_held, mine)
    fill_pick(pick, result.shape[0], lax.axis_index("seq"), places)
    fill_heads(heads, heads_t)
    low[...] = jnp.zeros_like(low)
    load_g1.wait()
    g1_low[...] = g1[...].astype(BF)
    load_fc.wait()
    gproj[...] = nt(g1_low[...], time_fc[...]).astype(BF)
    load_out.wait()
    gattn[...] = nt(gproj[...], time_out[...]).astype(BF)
    relay.middle()
    load_qkv.wait()
    load_probs.wait()
    time_attention_back(
        qkv, gattn, probs, gqkv, stage, soft, soft_grad, grad_key, grad_value, heads, heads_t, frames, total // frames, width
    )
    load_weight.wait()
    gnorm = grad_key
    tiled_nt(gqkv, time_qkv, gnorm, width // 3)
    norm_back(x, gnorm, smalls.gain(0), g1, gattn, sums, chunk)
    copies.store(gattn, gx_out)
    norm_sums(sums, low, 0, 0)
    count = pick.shape[0]
    load_proj.wait()
    turned[0:count, :] = nt(pick[...], proj[...]).astype(BF)
    fill_ones(turned, count)
    each = count // result.shape[0]
    weight_grad(turned, count, g1_low, result, 4 * each, low, BIAS + 4)
    load_attn.wait()
    turned[0:count, :] = nt(pick[...], attn[...]).astype(BF)
    weight_grad(turned, count, gproj, result, 3 * each, low, BIAS + 3)
    norm_into(x, stage, smalls.gain(0), smalls.bias(0), chunk)
    turned[0:count, :] = nt(pick[...], stage[...]).astype(BF)
    weight_grad(turned, count, gqkv, result, 0, low, BIAS + 1, None, BIAS + 2)
    copies.store(result, grads_out)
    relay.end()
    copies.finish()


def back_mlp(block, carried, partial, parts, places, gy, small, small_other, own, other, act, slope, x2):
    total, width = gy.shape
    hidden = act.shape[1]
    count, many = width // places, hidden // places
    wide, full, low = struct((total, width)), struct((total, width), F32), struct((LOW, width), F32)
    result = struct((parts, (count * (hidden // width) + many) // parts, width))
    deep = struct((total, hidden))
    scratch = held(*own) + small_held(small)
    scratch += held(deep, deep, full, wide, deep, full, full, struct((many + 16, total)), result, struct((16, width), F32))
    scratch += held(struct((count, width)), struct((hidden // parts // places, hidden // parts)))
    return call(
        functools.partial(back_mlp_kernel, block, carried, places),
        f"block{block}_mlp_backward",
        24 * total * width * width,
        [IN_VMEM] * 7 + [IN_HBM] * 7,
        (gy, *small, *small_other, *own, *other, act, slope, x2),
        [full, result, low],
        [IN_HBM] * 2 + [IN_VMEM],
        scratch + [pltpu.SemaphoreType.DMA((8,))],
        carried,
        partial,
    )


def back_space(block, carried, partial, parts, places, frames, patches, small, small_other, own, other, g2, qkv, attn, x1):
    total, width = g2.shape
    count = width // places
    wide, full, triple = struct((total, width)), struct((total, width), F32), struct((total, 3 * width))
    result, low = struct((parts, 4 * count // parts, width)), struct((LOW, width), F32)
    scratch = held(*own) + small_held(small) + held(full, triple, wide, full, wide, wide, triple, full, full)
    scratch += held(struct((count + 16, total)), result, struct((16, width), F32), struct((count, width)))
    return call(
        functools.partial(back_space_kernel, block, carried, places, frames, patches),
        f"block{block}_space_backward",
        30 * total * width * width,
        [IN_VMEM] * 6 + [IN_HBM] * 8,
        (*small, *small_other, *own, *other, g2, qkv, attn, x1),
        [full, result, low],
        [IN_HBM] * 2 + [IN_VMEM],
        scratch + [pltpu.SemaphoreType.DMA((9,))],
        carried,
        partial,
    )


def back_time(block, carried, partial, parts, places, frames, x, small, small_other, own, other, g1, qkv, attn, proj, probs):
    total, width = x.shape
    count = width // places
    wide, full, triple = struct((total, width)), struct((total, width), F32), struct((total, 3 * width))
    few = struct((total, PAIR))
    result, low = struct((parts, 5 * count // parts, width)), struct((LOW, width), F32)
    scratch = held(*own) + small_held(small)
    scratch += held(full, triple, wide, wide, probs, wide, wide, wide, triple, wide, few, few, full, full)
    scratch += held(struct((count + 16, total)), result, struct((16, width), F32), struct((count, width)))
    scratch += held(struct((width, PAIR)), struct((PAIR, width)))
    return call(
        functools.partial(back_time_kernel, block, carried, places, frames),
        f"block{block}_time_backward",
        24 * total * width * width,
        [IN_VMEM] * 7 + [IN_HBM] * 11,
        (x, *small, *small_other, *own, *other, g1, qkv, attn, proj, probs),
        [wide, result, low],
        [IN_HBM] * 2 + [IN_VMEM],
        scratch + [pltpu.SemaphoreType.DMA((12,))],
        carried,
        partial,
    )


def begin_kernel(tokens, cotangent, *refs):
    own, refs = refs[:6], refs[6:]
    x_out, cot_out, refs = refs[0], refs[1], refs[2:]
    other, refs = refs[:6], refs[6:]
    frame, cot, send, recv, local = refs
    count = lax.axis_size("seq")
    me = lax.axis_index("seq")
    section = lax.axis_index("section")
    first = section == 0
    patches = tokens.shape[2]
    whole = patches // 16 * 16

    def pad_into(source, target):
        mine = jnp.where(first, source[0, 0], source[1, 0])
        target[0:whole, :] = mine[:whole]
        if target.shape[0] > whole:
            rest = jnp.zeros((target.shape[0] - patches, mine.shape[1]), BF)
            target[whole:, :] = jnp.concatenate([mine[whole:], rest], axis=0)

    pad_into(tokens, frame)
    barrier = pltpu.get_barrier_semaphore()
    mate = {"section": 1 - section}
    pl.semaphore_signal(barrier, inc=1, device_id=mate, device_id_type=MESH)
    for step in range(1, count):
        pl.semaphore_signal(barrier, inc=1, device_id={"seq": lax.rem(me + step, count)}, device_id_type=MESH)
    pl.semaphore_wait(barrier, count)
    copies = [pltpu.make_async_copy(frame, x_out.at[me], local.at[0])]
    for step in range(1, count):
        copies.append(
            pltpu.make_async_remote_copy(
                frame,
                x_out.at[me],
                send.at[step - 1],
                recv.at[step - 1],
                device_id={"seq": lax.rem(me + step, count)},
                device_id_type=MESH,
            )
        )
    for at, (source, target) in enumerate(zip(own, other)):
        copies.append(
            pltpu.make_async_remote_copy(
                source, target, send.at[count - 1 + at], recv.at[count - 1 + at], device_id=mate, device_id_type=MESH
            )
        )
    for copy in copies:
        copy.start()
    pad_into(cotangent, cot)
    last = pltpu.make_async_copy(cot, cot_out, local.at[1])
    last.start()
    for copy in copies:
        copy.wait()
    last.wait()


def begin(tokens, cotangent, own, rows):
    count = lax.axis_size("seq")
    width = tokens.shape[-1]
    pad = struct((rows, width))
    outs = [struct((count, rows, width)), pad] + [struct(a.shape, a.dtype) for a in own]
    copies = count - 1 + len(own)
    return pl.pallas_call(
        begin_kernel,
        out_shape=outs,
        in_specs=[IN_VMEM] * 2 + [IN_HBM] * len(own),
        out_specs=[IN_HBM] * len(outs),
        scratch_shapes=held(pad, pad)
        + [pltpu.SemaphoreType.DMA((copies,)), pltpu.SemaphoreType.DMA((copies,)), pltpu.SemaphoreType.DMA((2,))],
        compiler_params=pltpu.CompilerParams(collective_id=0, has_side_effects=True, vmem_limit_bytes=VMEM_BYTES),
        name="gather_frames",
    )(tokens, cotangent, *own)


def finish_kernel(partial, low, total_out, low_out, mates, taken, lows, send, recv, send_low, recv_low):
    count = lax.axis_size("dp")
    z = lax.axis_index("dp")
    section = lax.axis_index("section")
    mate = 1 - section
    spots = [(section, lax.rem(z + step, count)) for step in range(1, count)]
    spots += [(mate, lax.rem(z + step, count)) for step in range(count)]
    barrier = pltpu.get_barrier_semaphore()
    for s, d in spots:
        pl.semaphore_signal(barrier, inc=1, device_id={"section": s, "dp": d}, device_id_type=MESH)
    pl.semaphore_wait(barrier, len(spots))

    def over(step):
        target = lax.rem(z + step, count)
        return target, pltpu.make_async_remote_copy(
            partial.at[target],
            mates.at[step],
            send.at[step],
            recv.at[step],
            device_id={"section": mate},
            device_id_type=MESH,
        )

    def along(step):
        target = lax.rem(z + step, count)
        return pltpu.make_async_remote_copy(
            mates.at[step],
            taken.at[step - 1],
            send.at[count + step],
            recv.at[count + step],
            device_id={"dp": target},
            device_id_type=MESH,
        )

    order = list(range(1, count)) + [0]

    @pl.when(section == 1)
    def _():
        for step in order:
            over(step)[1].start()

    small = []
    for at, (s, d) in enumerate(spots):
        small.append(
            pltpu.make_async_remote_copy(
                low.at[s],
                lows.at[at],
                send_low.at[at],
                recv_low.at[at],
                device_id={"section": s, "dp": d},
                device_id_type=MESH,
            )
        )
    for copy in small:
        copy.start()

    @pl.when(section == 0)
    def _():
        for step in range(1, count):
            target, copy = over(step)
            copy.wait_recv()
            mates[step] = (mates[step].astype(F32) + partial[target].astype(F32)).astype(BF)
            along(step).start()
        target, copy = over(0)
        copy.wait_recv()
        total_out[...] = mates[0].astype(F32) + partial[z].astype(F32)
        for step in range(1, count):
            along(step).wait()
            total_out[...] += taken[step - 1].astype(F32)

    @pl.when(section == 1)
    def _():
        total_out[...] = jnp.zeros_like(total_out)
        for step in order:
            over(step)[1].wait_send()

    for copy in small:
        copy.wait()
    result = jnp.where(section == 0, low[0], low[1])
    for at in range(len(spots)):
        result = result + lows[at]
    low_out[...] = result


def finish(partial, low):
    count, rows, width = partial.shape
    others = 2 * count - 1
    dma = pltpu.SemaphoreType.DMA
    return pl.pallas_call(
        finish_kernel,
        out_shape=[struct((rows, width), F32), struct(low.shape[1:], F32)],
        in_specs=[IN_VMEM] * 2,
        out_specs=[IN_VMEM] * 2,
        scratch_shapes=held(
            struct((count, rows, width)), struct((count - 1, rows, width)), struct((others, *low.shape[1:]), F32)
        )
        + [dma((2 * count,)), dma((2 * count,)), dma((others,)), dma((others,))],
        compiler_params=pltpu.CompilerParams(collective_id=1, has_side_effects=True, vmem_limit_bytes=VMEM_BYTES),
        name="finish_sums",
    )(partial, low)


def after(first, then):
    return lax.optimization_barrier((first, then))[1]


def shards(clip_ids, tokens, *rest):
    weights, small, cotangent = rest[:7], list(rest[7:10]), rest[10]
    NEXT_ID[:] = [1]
    section = lax.axis_index("section")
    place = lax.axis_index("seq")
    z = lax.axis_index("dp")
    n_dp, n_seq = lax.axis_size("dp"), lax.axis_size("seq")
    first = section == 0
    micro, own_frames, patches, width = tokens.shape
    hidden = weights[5].shape[2]
    frames = own_frames * n_seq
    places = n_dp * n_seq
    rows = -(-patches // 16) * 16
    swap = [(0, 1), (1, 0)]
    small[2] = small[2].reshape(1, 1, hidden)

    own = [array[0] for array in weights]
    inputs, cot, *swapped = begin(tokens, cotangent, own[:3] + small, rows)
    small_other = swapped[3:]
    later = after(inputs, own[3:])
    other = swapped[:3] + [lax.ppermute(array, "section", swap) for array in later]
    inputs = inputs.reshape(frames * rows, width)
    grad_top = lax.all_gather(after(inputs, cot), "seq", axis=0, tiled=True)
    where = jnp.stack([section, place])
    params = (small, small_other)

    kept, outputs = [], []
    for block in range(2):
        time = forward_time(block, frames, inputs, where, clip_ids, small, small_other, own[:3], other[:3])
        rest = forward_rest(block, frames, patches, time[3], where, small, small_other, own[3:], other[3:])
        kept.append((inputs, time, rest))
        inputs = rest[0]
        outputs.append(inputs)

    def home(pair):
        frame = [lax.dynamic_slice_in_dim(array, place * own_frames * rows, own_frames * rows) for array in pair]
        mine = jnp.where(first, frame[0], frame[1])
        mate = lax.ppermute(jnp.where(first, frame[1], frame[0]), "section", swap)
        both = jnp.stack([jnp.where(first, mine, mate), jnp.where(first, mate, mine)])
        return both.reshape(1, micro, own_frames, rows, width)[:, :, :, :patches]

    input_grads, lows, sums = [None] * 2, [None] * 2, []
    carried = partial = None
    sizes = (n_dp, n_seq)
    for block in (1, 0):
        x, (qkv_t, attn_t, proj, x1, probs), (_, qkv_s, attn_s, x2, act, slope) = kept[block]
        g2, mlp, low_mlp, *total = back_mlp(
            block, carried, partial, *sizes, grad_top, *params, own[5:], other[5:], act, slope, x2
        )
        sums += total
        g1, space, low_space, *total = back_space(
            block, block, mlp, *sizes, frames, patches, *params, own[3:5], other[3:5], g2, qkv_s, attn_s, x1
        )
        sums += total
        grad_top, time, low_time, *total = back_time(
            block, block, space, *sizes, frames, x, *params, own[:3], other[:3], g1, qkv_t, attn_t, proj, probs
        )
        sums += total
        carried, partial = block, time
        input_grads[block] = grad_top
        lows[block] = low_time + low_space + low_mlp
    total, low = finish(partial, jnp.stack(lows))
    mlp1, space1, time1, mlp0, space0 = sums
    sums = ((total, time1), (space0, space1), (mlp0, mlp1))
    time, space, mlp = (jnp.where(first, *pair) for pair in sums)
    each = width // places
    deep = hidden // width

    def turn(part, count):
        return part.reshape(count, each, width).transpose(1, 0, 2).reshape(1, -1)

    shares = [
        turn(time[: 3 * each], 3),
        time[3 * each : 4 * each].reshape(1, -1),
        time[4 * each :].reshape(1, -1),
        turn(space[: 3 * each], 3),
        space[3 * each :].reshape(1, -1),
        turn(mlp[: deep * each], deep),
        mlp[deep * each :].reshape(1, -1),
    ]
    low = low.reshape(-1)
    for start, end in ((0, BIAS), (BIAS, UP), (UP, UP + deep)):
        size = (end - start) * width // places
        shares.append(lax.dynamic_slice_in_dim(low, start * width + (z * n_seq + place) * size, size)[None])
    return (home(outputs), home(input_grads), *shares)


def relay_from_behind(value, axis, steps):
    count = lax.axis_size(axis)
    leading, last = (max(0, -steps), min(count, count - steps))
    return lax.ppermute(value, axis, [(source, source + steps) for source in range(leading, last)])


def relay_norm_rows(values, gain, shift):
    centre = values - jnp.mean(values, axis=-1, keepdims=True)
    spread = jnp.mean(centre * centre, axis=-1, keepdims=True)
    return centre * lax.rsqrt(spread + eps_norm) * gain + shift


def relay_mixed_dot(left, right, form):
    return jnp.einsum(form, left, right, preferred_element_type=jnp.float32)


def relay_column_sum(grad_rows):
    return jnp.sum(grad_rows.astype(jnp.float32), axis=(0, 1))


def relay_flat_terms(terms):
    return tuple((term.reshape(-1) for term in terms))


def relay_masked_scores(queries, key_rows, allowed):
    scores = relay_mixed_dot(queries, key_rows, "bic,bjc->bij") * queries.shape[-1] ** (-0.5)
    if allowed is None:
        return scores
    return jnp.where(allowed[None], scores, far_below)


def relay_attend(queries, key_rows, values, allowed):
    scores = relay_masked_scores(queries, key_rows, allowed)
    top_score = jnp.max(scores, axis=-1, keepdims=True)
    total_exp = jnp.sum(jnp.exp(scores - top_score), axis=-1, keepdims=True)
    log_total = top_score + jnp.log(total_exp)
    weights_soft = jnp.exp(scores - log_total).astype(jnp.bfloat16)
    mixed = relay_mixed_dot(weights_soft, values, "bij,bjc->bic").astype(jnp.bfloat16)
    return (mixed, log_total)


def relay_attend_back(queries, key_rows, values, log_total, allowed, grad_out):
    scale = queries.shape[-1] ** (-0.5)
    weights_soft = jnp.exp(relay_masked_scores(queries, key_rows, allowed) - log_total)
    grad_values = relay_mixed_dot(weights_soft.astype(jnp.bfloat16), grad_out, "bij,bic->bjc")
    grad_soft = relay_mixed_dot(grad_out, values, "bic,bjc->bij")
    row_total = jnp.sum(grad_soft * weights_soft, axis=-1, keepdims=True)
    grad_scores = (weights_soft * (grad_soft - row_total)).astype(jnp.bfloat16)
    grad_queries = relay_mixed_dot(grad_scores, key_rows, "bij,bjc->bic") * scale
    grad_keys = relay_mixed_dot(grad_scores, queries, "bij,bic->bjc") * scale
    return (grad_queries, grad_keys, grad_values)


def relay_heads_first(rows):
    frames, patches, width = rows.shape
    return (
        rows.reshape(frames, patches, H, width // H)
        .transpose(0, 2, 1, 3)
        .reshape(frames * H, patches, width // H)
    )


def relay_heads_last(rows, frames):
    batch, patches, head_size = rows.shape
    return (
        rows.reshape(frames, batch // frames, patches, head_size)
        .transpose(0, 2, 1, 3)
        .reshape(frames, patches, batch // frames * head_size)
    )


def relay_time_mix(normed_time, time_qkv, time_out, bias_rows, allowed):
    frames, patches, width = normed_time.shape
    zero_row = jnp.zeros((width,), jnp.float32)
    bias_time = jnp.stack([bias_rows[1], zero_row, bias_rows[2]])
    proj_time = relay_mixed_dot(normed_time, time_qkv.reshape(width, 3, width), "fpd,dke->fkpe")
    proj_time = (proj_time + bias_time[None, :, None, :]).astype(jnp.bfloat16)
    proj_time = proj_time.reshape(frames, 3, patches * H, HD)
    by_patch = lax.all_to_all(proj_time, "seq", split_axis=2, concat_axis=0, tiled=True)
    query_time = by_patch[:, 0].transpose(1, 0, 2)
    key_time = by_patch[:, 1].transpose(1, 0, 2)
    value_time = by_patch[:, 2].transpose(1, 0, 2)
    mixed_time, total_time = relay_attend(query_time, key_time, value_time, allowed)
    back_frames = lax.all_to_all(
        mixed_time.transpose(1, 0, 2), "seq", split_axis=0, concat_axis=1, tiled=True
    )
    attn_time = back_frames.reshape(frames, patches, width)
    proj_out = (relay_mixed_dot(attn_time, time_out, "fpd,de->fpe") + bias_rows[3]).astype(jnp.bfloat16)
    return (proj_out, (normed_time, query_time, key_time, value_time, total_time, attn_time))


def relay_time_mix_back(grad_proj_out, time_qkv, time_out, time_kept, allowed):
    normed_rows, query_time, key_time, value_time, total_time, attn_time = time_kept
    frames, patches, width = grad_proj_out.shape
    grad_time_out = relay_mixed_dot(attn_time, grad_proj_out, "fpd,fpe->de")
    grad_attn_time = relay_mixed_dot(grad_proj_out, time_out, "fpe,de->fpd").astype(jnp.bfloat16)
    grad_attn_time = grad_attn_time.reshape(frames, patches * H, HD)
    grad_by_patch = lax.all_to_all(
        grad_attn_time, "seq", split_axis=1, concat_axis=0, tiled=True
    ).transpose(1, 0, 2)
    grads_time = relay_attend_back(query_time, key_time, value_time, total_time, allowed, grad_by_patch)
    grad_mixed = jnp.stack(grads_time, axis=0).transpose(2, 0, 1, 3).astype(jnp.bfloat16)
    grad_frames = lax.all_to_all(
        grad_mixed, "seq", split_axis=0, concat_axis=2, tiled=True
    ).reshape(frames, 3, patches, width)
    grad_time_qkv = relay_mixed_dot(normed_rows, grad_frames, "fpd,fkpe->dke").reshape(width, 3 * width)
    grad_normed = relay_mixed_dot(grad_frames, time_qkv.reshape(width, 3, width), "fkpe,dke->fpd")
    return (
        grad_normed,
        grad_time_qkv,
        grad_time_out,
        relay_column_sum(grad_frames[:, 0]),
        relay_column_sum(grad_frames[:, 2]),
        relay_column_sum(grad_proj_out),
    )


def relay_layer_forward(inputs, params, allowed):
    (
        time_qkv,
        time_out,
        time_fc,
        space_qkv,
        space_out,
        up_weight,
        down_weight,
        norm_gains,
        bias_rows,
        up_bias,
    ) = params
    frames, patches, width = inputs.shape
    zero_row = jnp.zeros((width,), jnp.float32)
    normed_time = relay_norm_rows(inputs, norm_gains[0], bias_rows[0]).astype(jnp.bfloat16)
    proj_out, time_kept = relay_time_mix(normed_time, time_qkv, time_out, bias_rows, allowed)
    after_time = inputs + (relay_mixed_dot(proj_out, time_fc, "fpd,de->fpe") + bias_rows[4])
    normed_space = relay_norm_rows(after_time, norm_gains[1], bias_rows[5]).astype(jnp.bfloat16)
    bias_space = jnp.stack([bias_rows[6], zero_row, bias_rows[7]])
    proj_space = relay_mixed_dot(normed_space, space_qkv.reshape(width, 3, width), "fpd,dke->fkpe")
    proj_space = (proj_space + bias_space[None, :, None, :]).astype(jnp.bfloat16)
    query_space = relay_heads_first(proj_space[:, 0])
    key_space = relay_heads_first(proj_space[:, 1])
    value_space = relay_heads_first(proj_space[:, 2])
    mixed_space, total_space = relay_attend(query_space, key_space, value_space, None)
    attn_space = relay_heads_last(mixed_space, frames)
    after_space = after_time + (relay_mixed_dot(attn_space, space_out, "fpd,de->fpe") + bias_rows[8])
    normed_mlp = relay_norm_rows(after_space, norm_gains[2], bias_rows[9]).astype(jnp.bfloat16)
    hidden_pre = relay_mixed_dot(normed_mlp, up_weight, "fpd,de->fpe") + up_bias
    hidden_act = jax.nn.gelu(hidden_pre).astype(jnp.bfloat16)
    outputs = after_space + (relay_mixed_dot(hidden_act, down_weight, "fpe,ed->fpd") + bias_rows[10])
    kept = (
        inputs,
        time_kept,
        proj_out,
        after_time,
        normed_space,
        query_space,
        key_space,
        value_space,
        total_space,
        attn_space,
        after_space,
        normed_mlp,
        hidden_pre,
        hidden_act,
    )
    return (outputs, kept)


def relay_layer_backward(grad_top, params, kept, allowed):
    (
        time_qkv,
        time_out,
        time_fc,
        space_qkv,
        space_out,
        up_weight,
        down_weight,
        norm_gains,
        bias_rows,
        up_bias,
    ) = params
    (
        inputs,
        time_kept,
        proj_out,
        after_time,
        normed_space,
        query_space,
        key_space,
        value_space,
        total_space,
        attn_space,
        after_space,
        normed_mlp,
        hidden_pre,
        hidden_act,
    ) = kept
    frames, patches, width = inputs.shape
    grad_mlp = grad_top.astype(jnp.bfloat16)
    grad_down = relay_mixed_dot(hidden_act, grad_mlp, "fpe,fpd->ed")
    grad_act = relay_mixed_dot(grad_mlp, down_weight, "fpd,ed->fpe")
    gelu_back = jax.vjp(jax.nn.gelu, hidden_pre)[1]
    grad_pre = gelu_back(grad_act)[0].astype(jnp.bfloat16)
    grad_up = relay_mixed_dot(normed_mlp, grad_pre, "fpd,fpe->de")
    grad_normed = relay_mixed_dot(grad_pre, up_weight, "fpe,de->fpd")
    norm_back = jax.vjp(relay_norm_rows, after_space, norm_gains[2], bias_rows[9])[1]
    grad_into, gain_mlp, shift_mlp = norm_back(grad_normed)
    grad_space = grad_top + grad_into
    grad_branch = grad_space.astype(jnp.bfloat16)
    grad_space_out = relay_mixed_dot(attn_space, grad_branch, "fpd,fpe->de")
    grad_attn = relay_heads_first(relay_mixed_dot(grad_branch, space_out, "fpe,de->fpd").astype(jnp.bfloat16))
    grads_space = relay_attend_back(query_space, key_space, value_space, total_space, None, grad_attn)
    grad_proj = jnp.stack([relay_heads_last(piece, frames) for piece in grads_space], axis=1).astype(
        jnp.bfloat16
    )
    grad_space_qkv = relay_mixed_dot(normed_space, grad_proj, "fpd,fkpe->dke").reshape(width, 3 * width)
    grad_normed = relay_mixed_dot(grad_proj, space_qkv.reshape(width, 3, width), "fkpe,dke->fpd")
    norm_back = jax.vjp(relay_norm_rows, after_time, norm_gains[1], bias_rows[5])[1]
    grad_into, gain_space, shift_space = norm_back(grad_normed)
    grad_time = grad_space + grad_into
    grad_branch_time = grad_time.astype(jnp.bfloat16)
    grad_time_fc = relay_mixed_dot(proj_out, grad_branch_time, "fpd,fpe->de")
    grad_proj_out = relay_mixed_dot(grad_branch_time, time_fc, "fpe,de->fpd").astype(jnp.bfloat16)
    grad_normed, grad_time_qkv, grad_time_out, query_bias, value_bias, out_bias = relay_time_mix_back(
        grad_proj_out, time_qkv, time_out, time_kept, allowed
    )
    norm_back = jax.vjp(relay_norm_rows, inputs, norm_gains[0], bias_rows[0])[1]
    grad_into, gain_time, shift_time = norm_back(grad_normed)
    grad_inputs = grad_time + grad_into
    gain_grads = jnp.stack([gain_time, gain_space, gain_mlp])
    bias_grads = jnp.stack(
        [
            shift_time,
            query_bias,
            value_bias,
            out_bias,
            relay_column_sum(grad_branch_time),
            shift_space,
            relay_column_sum(grad_proj[:, 0]),
            relay_column_sum(grad_proj[:, 2]),
            relay_column_sum(grad_branch),
            shift_mlp,
            relay_column_sum(grad_mlp),
        ]
    )
    up_grad = relay_column_sum(grad_pre)
    return (
        grad_inputs,
        (
            grad_time_qkv,
            grad_time_out,
            grad_time_fc,
            grad_space_qkv,
            grad_space_out,
            grad_up,
            grad_down,
            gain_grads,
            bias_grads,
            up_grad,
        ),
    )


def relay_shards(
    clip_ids,
    tokens,
    time_qkv,
    time_out,
    time_fc,
    space_qkv,
    space_out,
    up_weight,
    down_weight,
    norm_gains,
    bias_rows,
    up_bias,
    cotangent,
):
    params = (
        time_qkv[0],
        time_out[0],
        time_fc[0],
        space_qkv[0],
        space_out[0],
        up_weight[0],
        down_weight[0],
        norm_gains[0],
        bias_rows[0],
        up_bias[0],
    )
    allowed = clip_ids[0][:, None] == clip_ids[0][None, :]
    first_section = lax.axis_index("section") == 0
    micro = tokens.shape[0]
    arriving = jnp.zeros_like(tokens[0])
    section_inputs = []
    section_outputs = []
    for moment in range(micro + 1):
        taken_rows = jnp.where(first_section, tokens[min(moment, micro - 1)], arriving)
        result = relay_layer_forward(taken_rows.astype(jnp.float32), params, allowed)[0].astype(
            jnp.bfloat16
        )
        section_inputs.append(taken_rows)
        section_outputs.append(result)
        if moment < micro:
            arriving = relay_from_behind(result, "section", 1)
    saved_inputs = [
        jnp.where(first_section, section_inputs[number], section_inputs[number + 1])
        for number in range(micro)
    ]
    layer_outputs = jnp.stack(
        [
            jnp.where(first_section, section_outputs[number], section_outputs[number + 1])
            for number in range(micro)
        ]
    )
    returning = jnp.zeros_like(tokens[0])
    back_results = []
    totals = None
    for moment in range(micro + 1):
        grad_given = jnp.where(first_section, returning, cotangent[min(moment, micro - 1)]).astype(
            jnp.float32
        )
        source_rows = jnp.where(
            first_section, saved_inputs[max(moment - 1, 0)], saved_inputs[min(moment, micro - 1)]
        )
        live_share = jnp.where(
            first_section, 1.0 if moment >= 1 else 0.0, 1.0 if moment < micro else 0.0
        )
        kept = relay_layer_forward(source_rows.astype(jnp.float32), params, allowed)[1]
        grad_inputs, weight_terms = relay_layer_backward(grad_given, params, kept, allowed)
        grad_inputs = grad_inputs.astype(jnp.bfloat16)
        back_results.append(grad_inputs)
        weight_terms = relay_flat_terms(jax.tree.map(lambda term: term * live_share, weight_terms))
        if totals is None:
            totals = tuple(weight_terms)
        else:
            totals = tuple((left + right for left, right in zip(totals, weight_terms)))
        if moment < micro:
            returning = relay_from_behind(grad_inputs, "section", -1)
    input_grads = jnp.stack(
        [
            jnp.where(first_section, back_results[number + 1], back_results[number])
            for number in range(micro)
        ]
    )
    shares = (
        lax.psum_scatter(totals[0], ("dp", "seq"), scatter_dimension=0, tiled=True),
        lax.psum_scatter(totals[1], ("dp", "seq"), scatter_dimension=0, tiled=True),
        lax.psum_scatter(totals[2], ("dp", "seq"), scatter_dimension=0, tiled=True),
        lax.psum_scatter(totals[3], ("dp", "seq"), scatter_dimension=0, tiled=True),
        lax.psum_scatter(totals[4], ("dp", "seq"), scatter_dimension=0, tiled=True),
        lax.psum_scatter(totals[5], ("dp", "seq"), scatter_dimension=0, tiled=True),
        lax.psum_scatter(totals[6], ("dp", "seq"), scatter_dimension=0, tiled=True),
        lax.psum_scatter(totals[7], ("dp", "seq"), scatter_dimension=0, tiled=True),
        lax.psum_scatter(totals[8], ("dp", "seq"), scatter_dimension=0, tiled=True),
        lax.psum_scatter(totals[9], ("dp", "seq"), scatter_dimension=0, tiled=True),
    )
    return (
        layer_outputs[None],
        input_grads[None],
        shares[0][None],
        shares[1][None],
        shares[2][None],
        shares[3][None],
        shares[4][None],
        shares[5][None],
        shares[6][None],
        shares[7][None],
        shares[8][None],
        shares[9][None],
    )


def solution(mesh):
    stacked = P("section", None, None)
    spread = P(None, ("dp", "seq"), None, None)
    in_specs = (P("dp", None), spread, *[stacked] * 9, P("section", None), spread)
    flat = P("section", ("dp", "seq"))
    out = P("section", None, ("dp", "seq"), None, None)
    relay = mesh.shape["seq"] > 4 or mesh.shape["section"] != 2
    return jax.shard_map(
        relay_shards if relay else shards, mesh=mesh, in_specs=in_specs, out_specs=(out, out, *[flat] * 10), check_vma=False
    )
```

```python
import functools

import jax
import jax.numpy as jnp
from jax import lax
from jax.experimental import pallas as pl
from jax.experimental.pallas import tpu as pltpu
from jax.sharding import PartitionSpec as P

H = 12
HD = 64
PAIR = 2 * HD
eps_norm = 1e-06
far_below = -1000000000.0
BF = jnp.bfloat16
F32 = jnp.float32
VMEM_BYTES = 62 << 20
NEXT_ID = [1]
GROUP = 6
GROUP_BACK = 6
CHUNK = 208


def nn(left, right):
    return lax.dot_general(left, right, (((1,), (0,)), ((), ())), preferred_element_type=F32)


def nt(left, right):
    return lax.dot_general(left, right, (((1,), (1,)), ((), ())), preferred_element_type=F32)


def norm_stats(values):
    centre = values - jnp.mean(values, axis=-1, keepdims=True)
    scale = lax.rsqrt(jnp.mean(centre * centre, axis=-1, keepdims=True) + eps_norm)
    return centre * scale, scale


def rows_at(index, count):
    return pl.ds(pl.multiple_of(index * count, count), count)


def norm_into(source, target, gain, shift, chunk):
    @pl.loop(0, source.shape[0] // chunk)
    def _(step):
        at = rows_at(step, chunk)
        hat, _ = norm_stats(source[at, :].astype(F32))
        target[at, :] = (hat * gain[...] + shift[...]).astype(BF)


def gelu_both(pre):
    rate, cube = 0.7978845608028654, 0.044715
    square = pre * pre
    tanh = jnp.tanh(pre * (rate + rate * cube * square))
    half = 0.5 + 0.5 * tanh
    act = pre * half
    slope = half + act * (1.0 - tanh) * (rate + 3.0 * rate * cube * square)
    return act, slope


class Copies:
    def __init__(self, sems):
        self.sems, self.used, self.open = sems, 0, []

    def fetch(self, own, other, target, mine):
        sem = self.sems.at[self.used]
        self.used += 1

        @pl.when(mine)
        def _():
            pltpu.make_async_copy(own, target, sem).start()

        @pl.when(jnp.logical_not(mine))
        def _():
            pltpu.make_async_copy(other, target, sem).start()

        return pltpu.make_async_copy(own, target, sem)

    def start(self, source, target):
        copy = pltpu.make_async_copy(source, target, self.sems.at[self.used])
        self.used += 1
        copy.start()
        return copy

    def store(self, source, target):
        self.open.append(self.start(source, target))

    def finish(self):
        for copy in self.open:
            copy.wait()


def time_attention(qkv, attn, probs, stage, soft, heads, heads_t, clips, frames, rows, width):
    @pl.loop(0, frames)
    def _(i):
        own = rows_at(i, rows)
        for j in range(frames):
            stage[pl.ds(j * rows, rows), :] = qkv[own, 0:width] * qkv[pl.ds(j * rows, rows), width : 2 * width]
        scores = nn(stage[...], heads[...])
        parts = []
        for j in range(frames):
            open_pair = clips[0, i] == clips[0, j]
            parts.append(scores[j * rows : (j + 1) * rows] + jnp.where(open_pair, 0.0, far_below))
        top = functools.reduce(jnp.maximum, parts)
        parts = [jnp.exp(part - top) for part in parts]
        inverse = 1.0 / sum(parts)
        for j in range(frames):
            prob = parts[j] * inverse
            probs[i, pl.ds(j * rows, rows), :] = prob
            soft[pl.ds(j * rows, rows), :] = prob.astype(BF)
        total = None
        for j in range(frames):
            at = pl.ds(j * rows, rows)
            term = nn(soft[at, :], heads_t[...]) * qkv[at, 2 * width : 3 * width].astype(F32)
            total = term if total is None else total + term
        attn[own, :] = total.astype(BF)


def fill_units(unit, pair_unit):
    for target in (unit, pair_unit):
        row = lax.broadcasted_iota(jnp.int32, target.shape, 0)
        column = lax.broadcasted_iota(jnp.int32, target.shape, 1)
        target[...] = jnp.where(row == column, 1.0, 0.0).astype(BF)


def split_patches(scores, patches):
    whole = patches // 16 * 16
    if whole == scores.shape[0]:
        return [scores]
    rest = scores[whole:]
    row = lax.broadcasted_iota(jnp.int32, rest.shape, 0)
    return [scores[:whole], jnp.where(row < patches - whole, rest, far_below)]


def space_attention(qkv, attn, logs, values_t, mixed_t, unit, pair_unit, frames, rows, patches, width):
    low_lane = lax.broadcasted_iota(jnp.int32, (rows, PAIR), 1) < HD
    deep = HD + 16
    values_t[...] = jnp.ones_like(values_t)

    @pl.loop(0, frames)
    def _(f):
        at = rows_at(f, rows)
        for pair in range(width // PAIR):
            turned = nt(pair_unit[...], qkv[at, 2 * width + pair * PAIR : 2 * width + (pair + 1) * PAIR]).astype(BF)
            for half in range(2):
                head = 2 * pair + half
                values_t[head * deep : head * deep + HD, :] = turned[half * HD : (half + 1) * HD]

        @pl.loop(0, width // PAIR // GROUP)
        def _(group):
            scores = []
            for member in range(GROUP):
                pair = group * GROUP + member

                def lanes(which):
                    return pl.ds(pl.multiple_of(which * width + pair * PAIR, PAIR), PAIR)

                query, key = qkv[at, lanes(0)] * BF(HD**-0.5), qkv[at, lanes(1)]
                for half in range(2):
                    scores.append(nt(jnp.where(low_lane if half == 0 else ~low_lane, key, BF(0)), query))
            expos, tops = [], []
            for score in scores:
                parts = split_patches(score, patches)
                top = functools.reduce(jnp.maximum, [jnp.max(part, axis=0, keepdims=True) for part in parts])
                expos.append(jnp.concatenate([jnp.exp(part - top).astype(BF) for part in parts], axis=0))
                tops.append(top)
            for member, (expo, top) in enumerate(zip(expos, tops)):
                head = group * (2 * GROUP) + member
                both = nn(values_t[pl.ds(pl.multiple_of(head * deep, 16), deep), :], expo)
                total = both[HD : HD + 1]
                logs[pl.ds(f * H + head, 1), :] = top + jnp.log(total)
                mixed_t[pl.ds(pl.multiple_of(head * HD, HD), HD), :] = (both[:HD] * (1.0 / total)).astype(BF)

        attn[at, :] = nt(unit[...], mixed_t[...]).astype(BF)


class Smalls:
    def __init__(self, own, other, held, mine):
        for which, refs in ((mine, own), (jnp.logical_not(mine), other)):

            @pl.when(which)
            def _(refs=refs):
                for source, target in zip(refs, held):
                    target[...] = source[...].reshape(target.shape)

        self.gains, self.biases, self.up_bias = held

    def gain(self, row):
        return self.gains.at[row : row + 1]

    def bias(self, row):
        return self.biases.at[row : row + 1]


def fill_heads(heads, heads_t):
    lane = lax.broadcasted_iota(jnp.int32, heads.shape, 0) // HD
    head = lax.broadcasted_iota(jnp.int32, heads.shape, 1)
    heads[...] = jnp.where(lane == head, HD**-0.5, 0.0).astype(BF)
    lane = lax.broadcasted_iota(jnp.int32, heads_t.shape, 1) // HD
    head = lax.broadcasted_iota(jnp.int32, heads_t.shape, 0)
    heads_t[...] = jnp.where(lane == head, 1.0, 0.0).astype(BF)


def fill_pick(pick, outer, place, count):
    each = pick.shape[0] // outer
    row = lax.broadcasted_iota(jnp.int32, pick.shape, 0)
    column = lax.broadcasted_iota(jnp.int32, pick.shape, 1)
    pick[...] = jnp.where(column == (row // each * count + place) * each + row % each, 1.0, 0.0).astype(BF)


def project(source, weight, biases, target):
    width = source.shape[1]
    for part in range(3):
        at = slice(part * width, (part + 1) * width)
        result = nn(source[...], weight[:, at])
        if biases[part] is not None:
            result = result + biases[part][...]
        target[:, at] = result.astype(BF)


def forward_time_kernel(block, frames, x, where, clips, *refs):
    small, small_other, own, other, refs = refs[:3], refs[3:6], refs[6:9], refs[9:12], refs[12:]
    (qkv_out, attn_out, proj_out, x1_out, probs_out, normed_out), refs = refs[:6], refs[6:]
    (time_qkv, time_out, time_fc), small_held, refs = refs[:3], refs[3:6], refs[6:]
    (normed, stage, qkv, attn, proj, x1, probs, soft, heads, heads_t, sems) = refs
    total, width = x.shape
    copies = Copies(sems)
    mine = where[0] == block
    loads = [copies.fetch(a, b, c, mine) for a, b, c in zip(own, other, (time_qkv, time_out, time_fc))]
    smalls = Smalls(small, small_other, small_held, mine)
    fill_heads(heads, heads_t)
    norm_into(x, normed, smalls.gain(0), smalls.bias(0), CHUNK)
    copies.store(normed, normed_out)
    loads[0].wait()
    project(normed, time_qkv, (smalls.bias(1), None, smalls.bias(2)), qkv)
    copies.store(qkv, qkv_out)
    time_attention(qkv, attn, probs, stage, soft, heads, heads_t, clips, frames, total // frames, width)
    copies.store(attn, attn_out)
    copies.store(probs, probs_out)
    loads[1].wait()
    proj[...] = (nn(attn[...], time_out[...]) + smalls.bias(3)[...]).astype(BF)
    copies.store(proj, proj_out)
    loads[2].wait()
    x1[...] = x[...].astype(F32) + nn(proj[...], time_fc[...]) + smalls.bias(4)[...]
    copies.store(x1, x1_out)
    copies.finish()


def forward_rest_kernel(block, frames, patches, x1, where, *refs):
    small, small_other, own, other, refs = refs[:3], refs[3:6], refs[6:10], refs[10:14], refs[14:]
    (y_out, qkv_out, attn_out, x2_out, act_out, slope_out, normed_out, normed_mlp_out, logs_out), refs = refs[:9], refs[9:]
    (space_qkv, space_out, up_weight, down_weight), small_held, refs = refs[:4], refs[4:7], refs[7:]
    (normed, normed_mlp, y, qkv, attn, x2, act, slope, logs, values_t, mixed_t, unit, pair_unit, sems) = refs
    total, width = x1.shape
    copies = Copies(sems)
    mine = where[0] == block
    held = (space_qkv, space_out, up_weight, down_weight)
    loads = [copies.fetch(a, b, c, mine) for a, b, c in zip(own, other, held)]
    smalls = Smalls(small, small_other, small_held, mine)
    fill_units(unit, pair_unit)
    norm_into(x1, normed, smalls.gain(1), smalls.bias(5), CHUNK)
    copies.store(normed, normed_out)
    loads[0].wait()
    project(normed, space_qkv, (smalls.bias(6), None, smalls.bias(7)), qkv)
    copies.store(qkv, qkv_out)
    space_attention(
        qkv, attn, logs, values_t, mixed_t, unit, pair_unit, frames, total // frames, patches, width
    )
    copies.store(attn, attn_out)
    copies.store(logs, logs_out)
    loads[1].wait()
    x2[...] = x1[...] + nn(attn[...], space_out[...]) + smalls.bias(8)[...]
    copies.store(x2, x2_out)
    norm_into(x2, normed_mlp, smalls.gain(2), smalls.bias(9), CHUNK)
    copies.store(normed_mlp, normed_mlp_out)
    loads[2].wait()

    @pl.loop(0, up_weight.shape[1] // width)
    def _(tile):
        at = rows_at(tile, width)
        pre = nn(normed_mlp[...], up_weight[:, at]) + smalls.up_bias[:, at]
        both = gelu_both(pre)
        act[:, at] = both[0].astype(BF)
        slope[:, at] = both[1].astype(BF)

    copies.store(act, act_out)
    copies.store(slope, slope_out)
    loads[3].wait()

    @pl.loop(0, 3)
    def _(tile):
        at = rows_at(tile, width // 3)
        y_at = nn(act[...], down_weight[:, at]) + smalls.biases[10:11, at] + x2[:, at]
        y[:, at] = y_at.astype(BF)

    copies.store(y, y_out)
    copies.finish()


def struct(shape, dtype=BF):
    return jax.ShapeDtypeStruct(shape, dtype)


def held(*structs):
    return [pltpu.VMEM(s.shape, s.dtype) for s in structs]


IN_VMEM = pl.BlockSpec(memory_space=pltpu.VMEM)
IN_SMEM = pl.BlockSpec(memory_space=pltpu.SMEM)
IN_HBM = pl.BlockSpec(memory_space=pl.ANY)


def small_held(small):
    return held(*[struct((array.size // array.shape[-1], array.shape[-1]), F32) for array in small])


def call(kernel, name, flops, specs, args, outs, out_specs, scratch, carried=None, partial=None):
    more_args, more_outs, more_scratch = relay_args(partial)
    specs, args = specs + [IN_HBM] * len(more_args), (*args, *more_args)
    outs, out_specs, scratch = outs + more_outs, out_specs + [IN_VMEM] * len(more_outs), scratch + more_scratch
    remote = {}
    if partial is not None:
        NEXT_ID.append(NEXT_ID[-1] + 1)
        remote = dict(collective_id=NEXT_ID[-1], has_side_effects=True)
    return pl.pallas_call(
        kernel,
        out_shape=outs,
        in_specs=specs,
        out_specs=out_specs,
        scratch_shapes=scratch,
        compiler_params=pltpu.CompilerParams(vmem_limit_bytes=VMEM_BYTES, **remote),
        cost_estimate=pl.CostEstimate(flops=flops, bytes_accessed=30 << 20, transcendentals=0),
        name=name,
    )(*args)


def forward_time(block, frames, x, where, clips, small, small_other, own, other):
    total, width = x.shape
    wide, full, triple = struct((total, width)), struct((total, width), F32), struct((total, 3 * width))
    probs = struct((frames, total, PAIR), F32)
    scratch = held(*own) + small_held(small)
    scratch += held(wide, wide, triple, wide, wide, full, probs, struct((total, PAIR)), struct((width, PAIR)), struct((PAIR, width)))
    return call(
        functools.partial(forward_time_kernel, block, frames),
        f"block{block}_forward_time",
        10 * total * width * width,
        [IN_VMEM, IN_SMEM, IN_SMEM] + [IN_VMEM] * 6 + [IN_HBM] * 6,
        (x, where, clips, *small, *small_other, *own, *other),
        [triple, wide, wide, full, probs, wide],
        [IN_HBM] * 6,
        scratch + [pltpu.SemaphoreType.DMA((9,))],
    )


def forward_rest(block, frames, patches, x1, where, small, small_other, own, other):
    total, width = x1.shape
    wide, full, triple = struct((total, width)), struct((total, width), F32), struct((total, 3 * width))
    deep = struct((total, own[2].shape[1]))
    rows = total // frames
    logs = struct((frames * H, rows), F32)
    scratch = held(*own) + small_held(small) + held(wide, wide, wide, triple, wide, full, deep, deep, logs)
    scratch += held(struct((H * (HD + 16), rows)), struct((width, rows)), struct((rows, rows)), struct((PAIR, PAIR)))
    return call(
        functools.partial(forward_rest_kernel, block, frames, patches),
        f"block{block}_forward_rest",
        24 * total * width * width,
        [IN_VMEM, IN_SMEM] + [IN_VMEM] * 6 + [IN_HBM] * 8,
        (x1, where, *small, *small_other, *own, *other),
        [wide, triple, wide, full, deep, deep, wide, wide, logs],
        [IN_HBM] * 9,
        scratch + [pltpu.SemaphoreType.DMA((13,))],
    )

MESH = pl.DeviceIdType.MESH


class Relay:
    def __init__(self, block, refs):
        self.on = block is not None
        self.block = block
        if not self.on:
            return
        self.partial, self.out, self.mine, self.mates, self.taken, self.send, self.recv = refs
        self.count = self.mates.shape[0]
        self.z = lax.axis_index("dp")
        self.section = lax.axis_index("section")
        self.home = self.section == block
        self.away = self.section != block

    def over(self):
        return pltpu.make_async_remote_copy(
            self.partial,
            self.mates,
            self.send.at[0],
            self.recv.at[0],
            device_id={"section": 1 - self.section},
            device_id_type=MESH,
        )

    def local(self):
        return pltpu.make_async_copy(self.partial, self.mine, self.send.at[self.count])

    def target(self, step):
        return lax.rem(self.z + step, self.count)

    def along(self, step):
        return pltpu.make_async_remote_copy(
            self.mine.at[self.target(step)],
            self.taken.at[step - 1],
            self.send.at[step],
            self.recv.at[step],
            device_id={"dp": self.target(step)},
            device_id_type=MESH,
        )

    def begin(self):
        if not self.on:
            return
        barrier = pltpu.get_barrier_semaphore()
        pl.semaphore_signal(barrier, inc=1, device_id={"section": 1 - self.section}, device_id_type=MESH)
        for step in range(1, self.count):
            pl.semaphore_signal(barrier, inc=1, device_id={"dp": self.target(step)}, device_id_type=MESH)
        pl.semaphore_wait(barrier, self.count)

        @pl.when(self.away)
        def _():
            self.over().start()

        @pl.when(self.home)
        def _():
            self.local().start()

    def middle(self):
        if not self.on:
            return

        @pl.when(self.home)
        def _():
            self.local().wait()
            self.over().wait_recv()
            for step in range(1, self.count):
                at = self.target(step)
                self.mine[at] = (self.mine[at].astype(F32) + self.mates[at].astype(F32)).astype(BF)
                self.along(step).start()

        @pl.when(self.away)
        def _():
            self.over().wait_send()

    def end(self):
        if not self.on:
            return

        @pl.when(self.home)
        def _():
            for step in range(1, self.count):
                self.along(step).wait()
            total = self.mine[self.z].astype(F32) + self.mates[self.z].astype(F32)
            for step in range(1, self.count):
                total = total + self.taken[step - 1].astype(F32)
            self.out[...] = total

        @pl.when(self.away)
        def _():
            self.out[...] = jnp.zeros_like(self.out)


def split_relay(block, refs, outs):
    if block is None:
        return refs[:outs], Relay(None, ()), refs[outs:]
    partial, results, out, refs = refs[0], refs[1 : 1 + outs], refs[1 + outs], refs[2 + outs :]
    return results, Relay(block, (partial, out, *refs[-5:])), refs[:-5]


def relay_args(partial):
    if partial is None:
        return [], [], []
    count, rows, width = partial.shape
    dma = pltpu.SemaphoreType.DMA
    scratch = held(struct(partial.shape), struct(partial.shape), struct((count - 1, rows, width)))
    return [partial], [struct((rows, width), F32)], scratch + [dma((count + 1,)), dma((count,))]


BIAS, UP, LOW = 3, 14, 24


def norm_back(hidden, grads, gain, above, target, sums, chunk):
    width = hidden.shape[1]
    sums[...] = jnp.zeros_like(sums)

    def fold(rows):
        return jnp.sum(rows.reshape(chunk // 8, 8, width), axis=0)

    @pl.loop(0, hidden.shape[0] // chunk)
    def _(step):
        at = rows_at(step, chunk)
        hat, scale = norm_stats(hidden[at, :].astype(F32))
        grad = grads[at, :]
        sums[0:8, :] += fold(grad * hat)
        sums[8:16, :] += fold(grad)
        inner = grad * gain[...]
        mean = jnp.mean(inner, axis=-1, keepdims=True)
        slant = jnp.mean(inner * hat, axis=-1, keepdims=True)
        result = above[at, :].astype(F32) + scale * (inner - mean - hat * slant)
        target[at, :] = result.astype(target.dtype)


def norm_sums(sums, low, gain_row, bias_row):
    low[gain_row : gain_row + 1, :] = jnp.sum(sums[0:8, :], axis=0, keepdims=True)
    low[BIAS + bias_row : BIAS + bias_row + 1, :] = jnp.sum(sums[8:16, :], axis=0, keepdims=True)


def fill_ones(turned, count):
    turned[pl.ds(count, 16), :] = jnp.ones((16, turned.shape[1]), BF)


def weight_grad(turned, count, grads, result, row, low, *low_rows):
    width = low.shape[1]
    parts = result.shape[0]
    each = count // parts

    for step, low_row in enumerate(low_rows):
        both = nn(turned[0 : count + 16, :], grads[:, step * width : (step + 1) * width])
        at = slice(row + step * each, row + (step + 1) * each)
        for part in range(parts):
            result[part, at, :] = both[part * each : (part + 1) * each].astype(BF)
        if low_row is not None:
            low[low_row : low_row + 1, :] = both[count : count + 1, :]


def tiled_nt(left, right, target, tile):
    @pl.loop(0, right.shape[0] // tile)
    def _(step):
        at = rows_at(step, tile)
        target[:, at] = nt(left[...], right[at, :])


def back_mlp_kernel(block, carried, places, gy, *refs):
    small, small_other, own, other, refs = refs[:3], refs[3:6], refs[6:8], refs[8:10], refs[10:]
    act_in, slope_in, x2_in, normed_in, refs = refs[0], refs[1], refs[2], refs[3], refs[4:]
    (g2_out, grads_out, low), relay, refs = split_relay(carried, refs, 3)
    (up_weight, down_weight), small_held, refs = refs[:2], refs[2:5], refs[5:]
    (act, slope, x2, normed, gpre, gnm, g2, turned, result, sums, pick, pick_wide, sems) = refs
    total, width = gy.shape
    chunk = CHUNK
    copies = Copies(sems)
    relay.begin()
    mine = lax.axis_index("section") == block
    load_down = copies.fetch(own[1], other[1], down_weight, mine)
    load_slope = copies.start(slope_in, slope)
    load_up = copies.fetch(own[0], other[0], up_weight, mine)
    load_act = copies.start(act_in, act)
    load_x2 = copies.start(x2_in, x2)
    load_normed = copies.start(normed_in, normed)
    smalls = Smalls(small, small_other, small_held, mine)
    fill_pick(pick, result.shape[0], lax.axis_index("seq"), places)
    fill_pick(pick_wide, 1, lax.axis_index("seq"), places)
    low[...] = jnp.zeros_like(low)
    load_down.wait()
    load_slope.wait()

    @pl.loop(0, down_weight.shape[0] // width)
    def _(tile):
        at = rows_at(tile, width)
        gpre[:, at] = (nt(gy[...], down_weight[at, :]) * slope[:, at].astype(F32)).astype(BF)

    relay.middle()
    load_up.wait()
    tiled_nt(gpre, up_weight, gnm, width // 3)
    load_x2.wait()
    norm_back(x2, gnm, smalls.gain(2), gy, g2, sums, chunk)
    copies.store(g2, g2_out)
    norm_sums(sums, low, 2, 9)
    load_normed.wait()
    count = pick.shape[0]
    turned[0:count, :] = nt(pick[...], normed[...]).astype(BF)
    fill_ones(turned, count)
    weight_grad(turned, count, gpre, result, 0, low, *range(UP, UP + gpre.shape[1] // width))
    load_act.wait()
    wide = pick_wide.shape[0]
    parts = act.shape[1] // pick_wide.shape[1]

    @pl.loop(0, parts)
    def _(part):
        turned[rows_at(part, wide), :] = nt(pick_wide[...], act[:, rows_at(part, pick_wide.shape[1])]).astype(BF)

    fill_ones(turned, parts * wide)
    weight_grad(turned, parts * wide, gy, result, result.shape[1] - parts * wide // result.shape[0], low, BIAS + 10)
    copies.store(result, grads_out)
    relay.end()
    copies.finish()


def space_attention_back(
    qkv, grads, logs, result, keys_t, turned_t, unit, pair_unit, frames, rows, patches, width
):
    low_lane = lax.broadcasted_iota(jnp.int32, (rows, PAIR), 1) < HD

    @pl.loop(0, frames)
    def _(f):
        at = rows_at(f, rows)
        for pair in range(width // PAIR):
            lanes = slice(width + pair * PAIR, width + (pair + 1) * PAIR)
            keys_t[pair * PAIR : (pair + 1) * PAIR, :] = nt(pair_unit[...], qkv[at, lanes]).astype(BF)

        @pl.loop(0, width // PAIR // GROUP_BACK)
        def _(group):
            def lanes(which, member):
                pair = group * GROUP_BACK + member
                return pl.ds(pl.multiple_of(which * width + pair * PAIR, PAIR), PAIR)

            scores, grad_softs = [], []
            for member in range(GROUP_BACK):
                query = qkv[at, lanes(0, member)] * BF(HD**-0.5)
                key, value, grad = qkv[at, lanes(1, member)], qkv[at, lanes(2, member)], grads[at, lanes(0, member)]
                for half in range(2):
                    mine = low_lane if half == 0 else ~low_lane
                    scores.append(nt(jnp.where(mine, key, BF(0)), query))
                    grad_softs.append(nt(jnp.where(mine, value, BF(0)), grad))
            softs, grad_scores = [], []
            for member, (score, grad_soft) in enumerate(zip(scores, grad_softs)):
                head = group * (2 * GROUP_BACK) + member
                log = logs[pl.ds(f * H + head, 1), :]
                soft = [jnp.exp(part - log) for part in split_patches(score, patches)]
                cut = soft[0].shape[0]
                changes = [grad_soft[:cut], grad_soft[cut:]][: len(soft)]
                slant = sum(jnp.sum(part * change, axis=0, keepdims=True) for part, change in zip(soft, changes))
                changes = [change - slant for change in changes]
                softs.append(jnp.concatenate([part.astype(BF) for part in soft], axis=0))
                grad_scores.append(
                    jnp.concatenate([(part * change).astype(BF) for part, change in zip(soft, changes)], axis=0)
                )
            for member in range(GROUP_BACK):
                query = qkv[at, lanes(0, member)] * BF(HD**-0.5)
                grad = grads[at, lanes(0, member)]
                pair = 2 * member
                grad_key = [nn(grad_scores[pair + half], query) for half in range(2)]
                grad_value = [nn(softs[pair + half], grad) for half in range(2)]
                result[at, lanes(1, member)] = jnp.where(low_lane, *grad_key).astype(BF)
                result[at, lanes(2, member)] = jnp.where(low_lane, *grad_value).astype(BF)
                for half in range(2):
                    head = group * (2 * GROUP_BACK) + pair + half
                    own = pl.ds(pl.multiple_of(head * HD, HD), HD)
                    turned_t[own, :] = (nn(keys_t[own, :], grad_scores[pair + half]) * HD**-0.5).astype(BF)

        result[at, 0:width] = nt(unit[...], turned_t[...]).astype(BF)


def back_space_kernel(block, carried, places, frames, patches, *refs):
    small, small_other, own, other, refs = refs[:3], refs[3:6], refs[6:8], refs[8:10], refs[10:]
    (g2_in, qkv_in, attn_in, x1_in, normed_in, logs_in), refs = refs[:6], refs[6:]
    (g1_out, grads_out, low), relay, refs = split_relay(carried, refs, 3)
    (space_qkv, space_out), small_held, refs = refs[:2], refs[2:5], refs[5:]
    (g2, qkv, attn, x1, normed, logs, g2_low, gattn, gqkv, gnorm, g1, turned, result, sums, pick), refs = refs[:15], refs[15:]
    (keys_t, turned_t, unit, pair_unit, sems) = refs
    total, width = g2.shape
    chunk = CHUNK
    copies = Copies(sems)
    relay.begin()
    mine = lax.axis_index("section") == block
    load_g2 = copies.start(g2_in, g2)
    load_out = copies.fetch(own[1], other[1], space_out, mine)
    load_qkv = copies.start(qkv_in, qkv)
    load_attn = copies.start(attn_in, attn)
    load_logs = copies.start(logs_in, logs)
    load_weight = copies.fetch(own[0], other[0], space_qkv, mine)
    load_x1 = copies.start(x1_in, x1)
    load_normed = copies.start(normed_in, normed)
    smalls = Smalls(small, small_other, small_held, mine)
    fill_pick(pick, result.shape[0], lax.axis_index("seq"), places)
    fill_units(unit, pair_unit)
    low[...] = jnp.zeros_like(low)
    load_g2.wait()
    g2_low[...] = g2[...].astype(BF)
    load_out.wait()
    gattn[...] = nt(g2_low[...], space_out[...]).astype(BF)
    relay.middle()
    load_qkv.wait()
    load_logs.wait()
    space_attention_back(
        qkv, gattn, logs, gqkv, keys_t, turned_t, unit, pair_unit, frames, total // frames, patches, width
    )
    load_weight.wait()
    tiled_nt(gqkv, space_qkv, gnorm, width // 3)
    load_x1.wait()
    norm_back(x1, gnorm, smalls.gain(1), g2, g1, sums, chunk)
    copies.store(g1, g1_out)
    norm_sums(sums, low, 1, 5)
    load_attn.wait()
    count = pick.shape[0]
    turned[0:count, :] = nt(pick[...], attn[...]).astype(BF)
    fill_ones(turned, count)
    each = count // result.shape[0]
    weight_grad(turned, count, g2_low, result, 3 * each, low, BIAS + 8)
    load_normed.wait()
    turned[0:count, :] = nt(pick[...], normed[...]).astype(BF)
    weight_grad(turned, count, gqkv, result, 0, low, BIAS + 6, None, BIAS + 7)
    copies.store(result, grads_out)
    relay.end()
    copies.finish()


def time_attention_back(qkv, grads, probs, result, stage, soft, soft_grad, grad_key, grad_value, heads, heads_t, frames, rows, width):
    grad_key[...] = jnp.zeros_like(grad_key)
    grad_value[...] = jnp.zeros_like(grad_value)

    @pl.loop(0, frames)
    def _(i):
        own = rows_at(i, rows)
        for j in range(frames):
            stage[pl.ds(j * rows, rows), :] = grads[own, :] * qkv[pl.ds(j * rows, rows), 2 * width : 3 * width]
        grad_soft = nn(stage[...], heads[...]) * HD**0.5
        parts = [probs[i, pl.ds(j * rows, rows), :] for j in range(frames)]
        changes = [grad_soft[j * rows : (j + 1) * rows] for j in range(frames)]
        total = sum(part * change for part, change in zip(parts, changes))
        for j in range(frames):
            at = pl.ds(j * rows, rows)
            soft[at, :] = parts[j].astype(BF)
            soft_grad[at, :] = (parts[j] * (changes[j] - total)).astype(BF)
        grad_query = None
        for j in range(frames):
            at = pl.ds(j * rows, rows)
            wide = nn(soft_grad[at, :], heads_t[...])
            term = wide * qkv[at, width : 2 * width].astype(F32)
            grad_query = term if grad_query is None else grad_query + term
            grad_key[at, :] += wide * qkv[own, 0:width].astype(F32)
            grad_value[at, :] += nn(soft[at, :], heads_t[...]) * grads[own, :].astype(F32)
        result[own, 0:width] = (grad_query * HD**-0.5).astype(BF)

    result[:, width : 2 * width] = (grad_key[...] * HD**-0.5).astype(BF)
    result[:, 2 * width : 3 * width] = grad_value[...].astype(BF)


def back_time_kernel(block, carried, places, frames, x, *refs):
    small, small_other, own, other, refs = refs[:3], refs[3:6], refs[6:9], refs[9:12], refs[12:]
    (g1_in, qkv_in, attn_in, proj_in, probs_in, normed_in), refs = refs[:6], refs[6:]
    (gx_out, grads_out, low), relay, refs = split_relay(carried, refs, 3)
    (time_qkv, time_out, time_fc), small_held, refs = refs[:3], refs[3:6], refs[6:]
    (g1, qkv, attn, proj, probs, normed, g1_low, gproj, gattn, gqkv, stage, soft, soft_grad), refs = refs[:13], refs[13:]
    (grad_key, grad_value, turned, result, sums, pick, heads, heads_t, sems) = refs
    total, width = x.shape
    chunk = CHUNK
    copies = Copies(sems)
    relay.begin()
    mine = lax.axis_index("section") == block
    load_g1 = copies.start(g1_in, g1)
    load_fc = copies.fetch(own[2], other[2], time_fc, mine)
    load_out = copies.fetch(own[1], other[1], time_out, mine)
    load_qkv = copies.start(qkv_in, qkv)
    load_probs = copies.start(probs_in, probs)
    load_weight = copies.fetch(own[0], other[0], time_qkv, mine)
    load_proj = copies.start(proj_in, proj)
    load_attn = copies.start(attn_in, attn)
    load_normed = copies.start(normed_in, normed)
    smalls = Smalls(small, small_other, small_held, mine)
    fill_pick(pick, result.shape[0], lax.axis_index("seq"), places)
    fill_heads(heads, heads_t)
    low[...] = jnp.zeros_like(low)
    load_g1.wait()
    g1_low[...] = g1[...].astype(BF)
    load_fc.wait()
    gproj[...] = nt(g1_low[...], time_fc[...]).astype(BF)
    load_out.wait()
    gattn[...] = nt(gproj[...], time_out[...]).astype(BF)
    relay.middle()
    load_qkv.wait()
    load_probs.wait()
    time_attention_back(
        qkv, gattn, probs, gqkv, stage, soft, soft_grad, grad_key, grad_value, heads, heads_t, frames, total // frames, width
    )
    load_weight.wait()
    gnorm = grad_key
    tiled_nt(gqkv, time_qkv, gnorm, width // 3)
    norm_back(x, gnorm, smalls.gain(0), g1, gattn, sums, chunk)
    copies.store(gattn, gx_out)
    norm_sums(sums, low, 0, 0)
    count = pick.shape[0]
    load_proj.wait()
    turned[0:count, :] = nt(pick[...], proj[...]).astype(BF)
    fill_ones(turned, count)
    each = count // result.shape[0]
    weight_grad(turned, count, g1_low, result, 4 * each, low, BIAS + 4)
    load_attn.wait()
    turned[0:count, :] = nt(pick[...], attn[...]).astype(BF)
    weight_grad(turned, count, gproj, result, 3 * each, low, BIAS + 3)
    load_normed.wait()
    turned[0:count, :] = nt(pick[...], normed[...]).astype(BF)
    weight_grad(turned, count, gqkv, result, 0, low, BIAS + 1, None, BIAS + 2)
    copies.store(result, grads_out)
    relay.end()
    copies.finish()


def back_mlp(block, carried, partial, parts, places, gy, small, small_other, own, other, act, slope, x2, normed):
    total, width = gy.shape
    hidden = act.shape[1]
    count, many = width // places, hidden // places
    wide, full, low = struct((total, width)), struct((total, width), F32), struct((LOW, width), F32)
    result = struct((parts, (count * (hidden // width) + many) // parts, width))
    deep = struct((total, hidden))
    scratch = held(*own) + small_held(small)
    scratch += held(deep, deep, full, wide, deep, full, full, struct((many + 16, total)), result, struct((16, width), F32))
    scratch += held(struct((count, width)), struct((hidden // parts // places, hidden // parts)))
    return call(
        functools.partial(back_mlp_kernel, block, carried, places),
        f"block{block}_mlp_backward",
        24 * total * width * width,
        [IN_VMEM] * 7 + [IN_HBM] * 8,
        (gy, *small, *small_other, *own, *other, act, slope, x2, normed),
        [full, result, low],
        [IN_HBM] * 2 + [IN_VMEM],
        scratch + [pltpu.SemaphoreType.DMA((9,))],
        carried,
        partial,
    )


def back_space(block, carried, partial, parts, places, frames, patches, small, small_other, own, other, g2, qkv, attn, x1, normed, logs):
    total, width = g2.shape
    count = width // places
    wide, full, triple = struct((total, width)), struct((total, width), F32), struct((total, 3 * width))
    result, low = struct((parts, 4 * count // parts, width)), struct((LOW, width), F32)
    scratch = held(*own) + small_held(small) + held(full, triple, wide, full, wide, logs, wide, wide, triple, full, full)
    scratch += held(struct((count + 16, total)), result, struct((16, width), F32), struct((count, width)))
    rows = total // frames
    scratch += held(struct((width, rows)), struct((width, rows)), struct((rows, rows)), struct((PAIR, PAIR)))
    return call(
        functools.partial(back_space_kernel, block, carried, places, frames, patches),
        f"block{block}_space_backward",
        30 * total * width * width,
        [IN_VMEM] * 6 + [IN_HBM] * 10,
        (*small, *small_other, *own, *other, g2, qkv, attn, x1, normed, logs),
        [full, result, low],
        [IN_HBM] * 2 + [IN_VMEM],
        scratch + [pltpu.SemaphoreType.DMA((11,))],
        carried,
        partial,
    )


def back_time(block, carried, partial, parts, places, frames, x, small, small_other, own, other, g1, qkv, attn, proj, probs, normed):
    total, width = x.shape
    count = width // places
    wide, full, triple = struct((total, width)), struct((total, width), F32), struct((total, 3 * width))
    few = struct((total, PAIR))
    result, low = struct((parts, 5 * count // parts, width)), struct((LOW, width), F32)
    scratch = held(*own) + small_held(small)
    scratch += held(full, triple, wide, wide, probs, wide, wide, wide, wide, triple, wide, few, few, full, full)
    scratch += held(struct((count + 16, total)), result, struct((16, width), F32), struct((count, width)))
    scratch += held(struct((width, PAIR)), struct((PAIR, width)))
    return call(
        functools.partial(back_time_kernel, block, carried, places, frames),
        f"block{block}_time_backward",
        24 * total * width * width,
        [IN_VMEM] * 7 + [IN_HBM] * 12,
        (x, *small, *small_other, *own, *other, g1, qkv, attn, proj, probs, normed),
        [wide, result, low],
        [IN_HBM] * 2 + [IN_VMEM],
        scratch + [pltpu.SemaphoreType.DMA((13,))],
        carried,
        partial,
    )


def begin_kernel(tokens, cotangent, *refs):
    own, refs = refs[:6], refs[6:]
    x_out, cot_out, refs = refs[0], refs[1], refs[2:]
    other, refs = refs[:6], refs[6:]
    frame, cot, send, recv, local = refs
    count = lax.axis_size("seq")
    me = lax.axis_index("seq")
    section = lax.axis_index("section")
    first = section == 0
    patches = tokens.shape[2]
    whole = patches // 16 * 16

    def pad_into(source, target):
        mine = jnp.where(first, source[0, 0], source[1, 0])
        target[0:whole, :] = mine[:whole]
        if target.shape[0] > whole:
            rest = jnp.zeros((target.shape[0] - patches, mine.shape[1]), BF)
            target[whole:, :] = jnp.concatenate([mine[whole:], rest], axis=0)

    pad_into(tokens, frame)
    barrier = pltpu.get_barrier_semaphore()
    mate = {"section": 1 - section}
    pl.semaphore_signal(barrier, inc=1, device_id=mate, device_id_type=MESH)
    for step in range(1, count):
        pl.semaphore_signal(barrier, inc=1, device_id={"seq": lax.rem(me + step, count)}, device_id_type=MESH)
    pl.semaphore_wait(barrier, count)
    copies = [pltpu.make_async_copy(frame, x_out.at[me], local.at[0])]
    for step in range(1, count):
        copies.append(
            pltpu.make_async_remote_copy(
                frame,
                x_out.at[me],
                send.at[step - 1],
                recv.at[step - 1],
                device_id={"seq": lax.rem(me + step, count)},
                device_id_type=MESH,
            )
        )
    for at, (source, target) in enumerate(zip(own, other)):
        copies.append(
            pltpu.make_async_remote_copy(
                source, target, send.at[count - 1 + at], recv.at[count - 1 + at], device_id=mate, device_id_type=MESH
            )
        )
    for copy in copies:
        copy.start()
    pad_into(cotangent, cot)
    last = pltpu.make_async_copy(cot, cot_out, local.at[1])
    last.start()
    for copy in copies:
        copy.wait()
    last.wait()


def begin(tokens, cotangent, own, rows):
    count = lax.axis_size("seq")
    width = tokens.shape[-1]
    pad = struct((rows, width))
    outs = [struct((count, rows, width)), pad] + [struct(a.shape, a.dtype) for a in own]
    copies = count - 1 + len(own)
    return pl.pallas_call(
        begin_kernel,
        out_shape=outs,
        in_specs=[IN_VMEM] * 2 + [IN_HBM] * len(own),
        out_specs=[IN_HBM] * len(outs),
        scratch_shapes=held(pad, pad)
        + [pltpu.SemaphoreType.DMA((copies,)), pltpu.SemaphoreType.DMA((copies,)), pltpu.SemaphoreType.DMA((2,))],
        compiler_params=pltpu.CompilerParams(collective_id=0, has_side_effects=True, vmem_limit_bytes=VMEM_BYTES),
        name="gather_frames",
    )(tokens, cotangent, *own)


def finish_kernel(partial, low, total_out, low_out, mates, taken, lows, send, recv, send_low, recv_low):
    count = lax.axis_size("dp")
    z = lax.axis_index("dp")
    section = lax.axis_index("section")
    mate = 1 - section
    spots = [(section, lax.rem(z + step, count)) for step in range(1, count)]
    spots += [(mate, lax.rem(z + step, count)) for step in range(count)]
    barrier = pltpu.get_barrier_semaphore()
    for s, d in spots:
        pl.semaphore_signal(barrier, inc=1, device_id={"section": s, "dp": d}, device_id_type=MESH)
    pl.semaphore_wait(barrier, len(spots))

    def over(step):
        target = lax.rem(z + step, count)
        return target, pltpu.make_async_remote_copy(
            partial.at[target],
            mates.at[step],
            send.at[step],
            recv.at[step],
            device_id={"section": mate},
            device_id_type=MESH,
        )

    def along(step):
        target = lax.rem(z + step, count)
        return pltpu.make_async_remote_copy(
            mates.at[step],
            taken.at[step - 1],
            send.at[count + step],
            recv.at[count + step],
            device_id={"dp": target},
            device_id_type=MESH,
        )

    order = list(range(1, count)) + [0]

    @pl.when(section == 1)
    def _():
        for step in order:
            over(step)[1].start()

    small = []
    for at, (s, d) in enumerate(spots):
        small.append(
            pltpu.make_async_remote_copy(
                low.at[s],
                lows.at[at],
                send_low.at[at],
                recv_low.at[at],
                device_id={"section": s, "dp": d},
                device_id_type=MESH,
            )
        )
    for copy in small:
        copy.start()

    @pl.when(section == 0)
    def _():
        for step in range(1, count):
            target, copy = over(step)
            copy.wait_recv()
            mates[step] = (mates[step].astype(F32) + partial[target].astype(F32)).astype(BF)
            along(step).start()
        target, copy = over(0)
        copy.wait_recv()
        total_out[...] = mates[0].astype(F32) + partial[z].astype(F32)
        for step in range(1, count):
            along(step).wait()
            total_out[...] += taken[step - 1].astype(F32)

    @pl.when(section == 1)
    def _():
        total_out[...] = jnp.zeros_like(total_out)
        for step in order:
            over(step)[1].wait_send()

    for copy in small:
        copy.wait()
    result = jnp.where(section == 0, low[0], low[1])
    for at in range(len(spots)):
        result = result + lows[at]
    low_out[...] = result


def finish(partial, low):
    count, rows, width = partial.shape
    others = 2 * count - 1
    dma = pltpu.SemaphoreType.DMA
    return pl.pallas_call(
        finish_kernel,
        out_shape=[struct((rows, width), F32), struct(low.shape[1:], F32)],
        in_specs=[IN_VMEM] * 2,
        out_specs=[IN_VMEM] * 2,
        scratch_shapes=held(
            struct((count, rows, width)), struct((count - 1, rows, width)), struct((others, *low.shape[1:]), F32)
        )
        + [dma((2 * count,)), dma((2 * count,)), dma((others,)), dma((others,))],
        compiler_params=pltpu.CompilerParams(collective_id=1, has_side_effects=True, vmem_limit_bytes=VMEM_BYTES),
        name="finish_sums",
    )(partial, low)


def after(first, then):
    return lax.optimization_barrier((first, then))[1]


def shards(clip_ids, tokens, *rest):
    weights, small, cotangent = rest[:7], list(rest[7:10]), rest[10]
    NEXT_ID[:] = [1]
    section = lax.axis_index("section")
    place = lax.axis_index("seq")
    z = lax.axis_index("dp")
    n_dp, n_seq = lax.axis_size("dp"), lax.axis_size("seq")
    first = section == 0
    micro, own_frames, patches, width = tokens.shape
    hidden = weights[5].shape[2]
    frames = own_frames * n_seq
    places = n_dp * n_seq
    rows = -(-patches // 16) * 16
    swap = [(0, 1), (1, 0)]
    small[2] = small[2].reshape(1, 1, hidden)

    own = [array[0] for array in weights]
    inputs, cot, *swapped = begin(tokens, cotangent, own[:3] + small, rows)
    small_other = swapped[3:]
    later = after(inputs, own[3:])
    other = swapped[:3] + [lax.ppermute(array, "section", swap) for array in later]
    inputs = inputs.reshape(frames * rows, width)
    grad_top = lax.all_gather(after(inputs, cot), "seq", axis=0, tiled=True)
    where = jnp.stack([section, place])
    params = (small, small_other)

    kept, outputs = [], []
    for block in range(2):
        time = forward_time(block, frames, inputs, where, clip_ids, small, small_other, own[:3], other[:3])
        rest = forward_rest(block, frames, patches, time[3], where, small, small_other, own[3:], other[3:])
        kept.append((inputs, time, rest))
        inputs = rest[0]
        outputs.append(inputs)

    def home(pair):
        frame = [lax.dynamic_slice_in_dim(array, place * own_frames * rows, own_frames * rows) for array in pair]
        mine = jnp.where(first, frame[0], frame[1])
        mate = lax.ppermute(jnp.where(first, frame[1], frame[0]), "section", swap)
        both = jnp.stack([jnp.where(first, mine, mate), jnp.where(first, mate, mine)])
        return both.reshape(1, micro, own_frames, rows, width)[:, :, :, :patches]

    input_grads, lows, sums = [None] * 2, [None] * 2, []
    carried = partial = None
    sizes = (n_dp, n_seq)
    for block in (1, 0):
        x, (qkv_t, attn_t, proj, x1, probs, normed_t), (_, qkv_s, attn_s, x2, act, slope, normed_s, normed_m, logs) = kept[block]
        g2, mlp, low_mlp, *total = back_mlp(
            block, carried, partial, *sizes, grad_top, *params, own[5:], other[5:], act, slope, x2, normed_m
        )
        sums += total
        g1, space, low_space, *total = back_space(
            block, block, mlp, *sizes, frames, patches, *params, own[3:5], other[3:5], g2, qkv_s, attn_s, x1, normed_s, logs
        )
        sums += total
        grad_top, time, low_time, *total = back_time(
            block, block, space, *sizes, frames, x, *params, own[:3], other[:3], g1, qkv_t, attn_t, proj, probs, normed_t
        )
        sums += total
        carried, partial = block, time
        input_grads[block] = grad_top
        lows[block] = low_time + low_space + low_mlp
    total, low = finish(partial, jnp.stack(lows))
    mlp1, space1, time1, mlp0, space0 = sums
    sums = ((total, time1), (space0, space1), (mlp0, mlp1))
    time, space, mlp = (jnp.where(first, *pair) for pair in sums)
    each = width // places
    deep = hidden // width

    def turn(part, count):
        return part.reshape(count, each, width).transpose(1, 0, 2).reshape(1, -1)

    shares = [
        turn(time[: 3 * each], 3),
        time[3 * each : 4 * each].reshape(1, -1),
        time[4 * each :].reshape(1, -1),
        turn(space[: 3 * each], 3),
        space[3 * each :].reshape(1, -1),
        turn(mlp[: deep * each], deep),
        mlp[deep * each :].reshape(1, -1),
    ]
    low = low.reshape(-1)
    for start, end in ((0, BIAS), (BIAS, UP), (UP, UP + deep)):
        size = (end - start) * width // places
        shares.append(lax.dynamic_slice_in_dim(low, start * width + (z * n_seq + place) * size, size)[None])
    return (home(outputs), home(input_grads), *shares)


def relay_from_behind(value, axis, steps):
    count = lax.axis_size(axis)
    leading, last = (max(0, -steps), min(count, count - steps))
    return lax.ppermute(value, axis, [(source, source + steps) for source in range(leading, last)])


def relay_norm_rows(values, gain, shift):
    centre = values - jnp.mean(values, axis=-1, keepdims=True)
    spread = jnp.mean(centre * centre, axis=-1, keepdims=True)
    return centre * lax.rsqrt(spread + eps_norm) * gain + shift


def relay_mixed_dot(left, right, form):
    return jnp.einsum(form, left, right, preferred_element_type=jnp.float32)


def relay_column_sum(grad_rows):
    return jnp.sum(grad_rows.astype(jnp.float32), axis=(0, 1))


def relay_flat_terms(terms):
    return tuple((term.reshape(-1) for term in terms))


def relay_masked_scores(queries, key_rows, allowed):
    scores = relay_mixed_dot(queries, key_rows, "bic,bjc->bij") * queries.shape[-1] ** (-0.5)
    if allowed is None:
        return scores
    return jnp.where(allowed[None], scores, far_below)


def relay_attend(queries, key_rows, values, allowed):
    scores = relay_masked_scores(queries, key_rows, allowed)
    top_score = jnp.max(scores, axis=-1, keepdims=True)
    total_exp = jnp.sum(jnp.exp(scores - top_score), axis=-1, keepdims=True)
    log_total = top_score + jnp.log(total_exp)
    weights_soft = jnp.exp(scores - log_total).astype(jnp.bfloat16)
    mixed = relay_mixed_dot(weights_soft, values, "bij,bjc->bic").astype(jnp.bfloat16)
    return (mixed, log_total)


def relay_attend_back(queries, key_rows, values, log_total, allowed, grad_out):
    scale = queries.shape[-1] ** (-0.5)
    weights_soft = jnp.exp(relay_masked_scores(queries, key_rows, allowed) - log_total)
    grad_values = relay_mixed_dot(weights_soft.astype(jnp.bfloat16), grad_out, "bij,bic->bjc")
    grad_soft = relay_mixed_dot(grad_out, values, "bic,bjc->bij")
    row_total = jnp.sum(grad_soft * weights_soft, axis=-1, keepdims=True)
    grad_scores = (weights_soft * (grad_soft - row_total)).astype(jnp.bfloat16)
    grad_queries = relay_mixed_dot(grad_scores, key_rows, "bij,bjc->bic") * scale
    grad_keys = relay_mixed_dot(grad_scores, queries, "bij,bic->bjc") * scale
    return (grad_queries, grad_keys, grad_values)


def relay_heads_first(rows):
    frames, patches, width = rows.shape
    return (
        rows.reshape(frames, patches, H, width // H)
        .transpose(0, 2, 1, 3)
        .reshape(frames * H, patches, width // H)
    )


def relay_heads_last(rows, frames):
    batch, patches, head_size = rows.shape
    return (
        rows.reshape(frames, batch // frames, patches, head_size)
        .transpose(0, 2, 1, 3)
        .reshape(frames, patches, batch // frames * head_size)
    )


def relay_time_mix(normed_time, time_qkv, time_out, bias_rows, allowed):
    frames, patches, width = normed_time.shape
    zero_row = jnp.zeros((width,), jnp.float32)
    bias_time = jnp.stack([bias_rows[1], zero_row, bias_rows[2]])
    proj_time = relay_mixed_dot(normed_time, time_qkv.reshape(width, 3, width), "fpd,dke->fkpe")
    proj_time = (proj_time + bias_time[None, :, None, :]).astype(jnp.bfloat16)
    proj_time = proj_time.reshape(frames, 3, patches * H, HD)
    by_patch = lax.all_to_all(proj_time, "seq", split_axis=2, concat_axis=0, tiled=True)
    query_time = by_patch[:, 0].transpose(1, 0, 2)
    key_time = by_patch[:, 1].transpose(1, 0, 2)
    value_time = by_patch[:, 2].transpose(1, 0, 2)
    mixed_time, total_time = relay_attend(query_time, key_time, value_time, allowed)
    back_frames = lax.all_to_all(
        mixed_time.transpose(1, 0, 2), "seq", split_axis=0, concat_axis=1, tiled=True
    )
    attn_time = back_frames.reshape(frames, patches, width)
    proj_out = (relay_mixed_dot(attn_time, time_out, "fpd,de->fpe") + bias_rows[3]).astype(jnp.bfloat16)
    return (proj_out, (normed_time, query_time, key_time, value_time, total_time, attn_time))


def relay_time_mix_back(grad_proj_out, time_qkv, time_out, time_kept, allowed):
    normed_rows, query_time, key_time, value_time, total_time, attn_time = time_kept
    frames, patches, width = grad_proj_out.shape
    grad_time_out = relay_mixed_dot(attn_time, grad_proj_out, "fpd,fpe->de")
    grad_attn_time = relay_mixed_dot(grad_proj_out, time_out, "fpe,de->fpd").astype(jnp.bfloat16)
    grad_attn_time = grad_attn_time.reshape(frames, patches * H, HD)
    grad_by_patch = lax.all_to_all(
        grad_attn_time, "seq", split_axis=1, concat_axis=0, tiled=True
    ).transpose(1, 0, 2)
    grads_time = relay_attend_back(query_time, key_time, value_time, total_time, allowed, grad_by_patch)
    grad_mixed = jnp.stack(grads_time, axis=0).transpose(2, 0, 1, 3).astype(jnp.bfloat16)
    grad_frames = lax.all_to_all(
        grad_mixed, "seq", split_axis=0, concat_axis=2, tiled=True
    ).reshape(frames, 3, patches, width)
    grad_time_qkv = relay_mixed_dot(normed_rows, grad_frames, "fpd,fkpe->dke").reshape(width, 3 * width)
    grad_normed = relay_mixed_dot(grad_frames, time_qkv.reshape(width, 3, width), "fkpe,dke->fpd")
    return (
        grad_normed,
        grad_time_qkv,
        grad_time_out,
        relay_column_sum(grad_frames[:, 0]),
        relay_column_sum(grad_frames[:, 2]),
        relay_column_sum(grad_proj_out),
    )


def relay_layer_forward(inputs, params, allowed):
    (
        time_qkv,
        time_out,
        time_fc,
        space_qkv,
        space_out,
        up_weight,
        down_weight,
        norm_gains,
        bias_rows,
        up_bias,
    ) = params
    frames, patches, width = inputs.shape
    zero_row = jnp.zeros((width,), jnp.float32)
    normed_time = relay_norm_rows(inputs, norm_gains[0], bias_rows[0]).astype(jnp.bfloat16)
    proj_out, time_kept = relay_time_mix(normed_time, time_qkv, time_out, bias_rows, allowed)
    after_time = inputs + (relay_mixed_dot(proj_out, time_fc, "fpd,de->fpe") + bias_rows[4])
    normed_space = relay_norm_rows(after_time, norm_gains[1], bias_rows[5]).astype(jnp.bfloat16)
    bias_space = jnp.stack([bias_rows[6], zero_row, bias_rows[7]])
    proj_space = relay_mixed_dot(normed_space, space_qkv.reshape(width, 3, width), "fpd,dke->fkpe")
    proj_space = (proj_space + bias_space[None, :, None, :]).astype(jnp.bfloat16)
    query_space = relay_heads_first(proj_space[:, 0])
    key_space = relay_heads_first(proj_space[:, 1])
    value_space = relay_heads_first(proj_space[:, 2])
    mixed_space, total_space = relay_attend(query_space, key_space, value_space, None)
    attn_space = relay_heads_last(mixed_space, frames)
    after_space = after_time + (relay_mixed_dot(attn_space, space_out, "fpd,de->fpe") + bias_rows[8])
    normed_mlp = relay_norm_rows(after_space, norm_gains[2], bias_rows[9]).astype(jnp.bfloat16)
    hidden_pre = relay_mixed_dot(normed_mlp, up_weight, "fpd,de->fpe") + up_bias
    hidden_act = jax.nn.gelu(hidden_pre).astype(jnp.bfloat16)
    outputs = after_space + (relay_mixed_dot(hidden_act, down_weight, "fpe,ed->fpd") + bias_rows[10])
    kept = (
        inputs,
        time_kept,
        proj_out,
        after_time,
        normed_space,
        query_space,
        key_space,
        value_space,
        total_space,
        attn_space,
        after_space,
        normed_mlp,
        hidden_pre,
        hidden_act,
    )
    return (outputs, kept)


def relay_layer_backward(grad_top, params, kept, allowed):
    (
        time_qkv,
        time_out,
        time_fc,
        space_qkv,
        space_out,
        up_weight,
        down_weight,
        norm_gains,
        bias_rows,
        up_bias,
    ) = params
    (
        inputs,
        time_kept,
        proj_out,
        after_time,
        normed_space,
        query_space,
        key_space,
        value_space,
        total_space,
        attn_space,
        after_space,
        normed_mlp,
        hidden_pre,
        hidden_act,
    ) = kept
    frames, patches, width = inputs.shape
    grad_mlp = grad_top.astype(jnp.bfloat16)
    grad_down = relay_mixed_dot(hidden_act, grad_mlp, "fpe,fpd->ed")
    grad_act = relay_mixed_dot(grad_mlp, down_weight, "fpd,ed->fpe")
    gelu_back = jax.vjp(jax.nn.gelu, hidden_pre)[1]
    grad_pre = gelu_back(grad_act)[0].astype(jnp.bfloat16)
    grad_up = relay_mixed_dot(normed_mlp, grad_pre, "fpd,fpe->de")
    grad_normed = relay_mixed_dot(grad_pre, up_weight, "fpe,de->fpd")
    norm_back = jax.vjp(relay_norm_rows, after_space, norm_gains[2], bias_rows[9])[1]
    grad_into, gain_mlp, shift_mlp = norm_back(grad_normed)
    grad_space = grad_top + grad_into
    grad_branch = grad_space.astype(jnp.bfloat16)
    grad_space_out = relay_mixed_dot(attn_space, grad_branch, "fpd,fpe->de")
    grad_attn = relay_heads_first(relay_mixed_dot(grad_branch, space_out, "fpe,de->fpd").astype(jnp.bfloat16))
    grads_space = relay_attend_back(query_space, key_space, value_space, total_space, None, grad_attn)
    grad_proj = jnp.stack([relay_heads_last(piece, frames) for piece in grads_space], axis=1).astype(
        jnp.bfloat16
    )
    grad_space_qkv = relay_mixed_dot(normed_space, grad_proj, "fpd,fkpe->dke").reshape(width, 3 * width)
    grad_normed = relay_mixed_dot(grad_proj, space_qkv.reshape(width, 3, width), "fkpe,dke->fpd")
    norm_back = jax.vjp(relay_norm_rows, after_time, norm_gains[1], bias_rows[5])[1]
    grad_into, gain_space, shift_space = norm_back(grad_normed)
    grad_time = grad_space + grad_into
    grad_branch_time = grad_time.astype(jnp.bfloat16)
    grad_time_fc = relay_mixed_dot(proj_out, grad_branch_time, "fpd,fpe->de")
    grad_proj_out = relay_mixed_dot(grad_branch_time, time_fc, "fpe,de->fpd").astype(jnp.bfloat16)
    grad_normed, grad_time_qkv, grad_time_out, query_bias, value_bias, out_bias = relay_time_mix_back(
        grad_proj_out, time_qkv, time_out, time_kept, allowed
    )
    norm_back = jax.vjp(relay_norm_rows, inputs, norm_gains[0], bias_rows[0])[1]
    grad_into, gain_time, shift_time = norm_back(grad_normed)
    grad_inputs = grad_time + grad_into
    gain_grads = jnp.stack([gain_time, gain_space, gain_mlp])
    bias_grads = jnp.stack(
        [
            shift_time,
            query_bias,
            value_bias,
            out_bias,
            relay_column_sum(grad_branch_time),
            shift_space,
            relay_column_sum(grad_proj[:, 0]),
            relay_column_sum(grad_proj[:, 2]),
            relay_column_sum(grad_branch),
            shift_mlp,
            relay_column_sum(grad_mlp),
        ]
    )
    up_grad = relay_column_sum(grad_pre)
    return (
        grad_inputs,
        (
            grad_time_qkv,
            grad_time_out,
            grad_time_fc,
            grad_space_qkv,
            grad_space_out,
            grad_up,
            grad_down,
            gain_grads,
            bias_grads,
            up_grad,
        ),
    )


def relay_shards(
    clip_ids,
    tokens,
    time_qkv,
    time_out,
    time_fc,
    space_qkv,
    space_out,
    up_weight,
    down_weight,
    norm_gains,
    bias_rows,
    up_bias,
    cotangent,
):
    params = (
        time_qkv[0],
        time_out[0],
        time_fc[0],
        space_qkv[0],
        space_out[0],
        up_weight[0],
        down_weight[0],
        norm_gains[0],
        bias_rows[0],
        up_bias[0],
    )
    allowed = clip_ids[0][:, None] == clip_ids[0][None, :]
    first_section = lax.axis_index("section") == 0
    micro = tokens.shape[0]
    arriving = jnp.zeros_like(tokens[0])
    section_inputs = []
    section_outputs = []
    for moment in range(micro + 1):
        taken_rows = jnp.where(first_section, tokens[min(moment, micro - 1)], arriving)
        result = relay_layer_forward(taken_rows.astype(jnp.float32), params, allowed)[0].astype(
            jnp.bfloat16
        )
        section_inputs.append(taken_rows)
        section_outputs.append(result)
        if moment < micro:
            arriving = relay_from_behind(result, "section", 1)
    saved_inputs = [
        jnp.where(first_section, section_inputs[number], section_inputs[number + 1])
        for number in range(micro)
    ]
    layer_outputs = jnp.stack(
        [
            jnp.where(first_section, section_outputs[number], section_outputs[number + 1])
            for number in range(micro)
        ]
    )
    returning = jnp.zeros_like(tokens[0])
    back_results = []
    totals = None
    for moment in range(micro + 1):
        grad_given = jnp.where(first_section, returning, cotangent[min(moment, micro - 1)]).astype(
            jnp.float32
        )
        source_rows = jnp.where(
            first_section, saved_inputs[max(moment - 1, 0)], saved_inputs[min(moment, micro - 1)]
        )
        live_share = jnp.where(
            first_section, 1.0 if moment >= 1 else 0.0, 1.0 if moment < micro else 0.0
        )
        kept = relay_layer_forward(source_rows.astype(jnp.float32), params, allowed)[1]
        grad_inputs, weight_terms = relay_layer_backward(grad_given, params, kept, allowed)
        grad_inputs = grad_inputs.astype(jnp.bfloat16)
        back_results.append(grad_inputs)
        weight_terms = relay_flat_terms(jax.tree.map(lambda term: term * live_share, weight_terms))
        if totals is None:
            totals = tuple(weight_terms)
        else:
            totals = tuple((left + right for left, right in zip(totals, weight_terms)))
        if moment < micro:
            returning = relay_from_behind(grad_inputs, "section", -1)
    input_grads = jnp.stack(
        [
            jnp.where(first_section, back_results[number + 1], back_results[number])
            for number in range(micro)
        ]
    )
    shares = (
        lax.psum_scatter(totals[0], ("dp", "seq"), scatter_dimension=0, tiled=True),
        lax.psum_scatter(totals[1], ("dp", "seq"), scatter_dimension=0, tiled=True),
        lax.psum_scatter(totals[2], ("dp", "seq"), scatter_dimension=0, tiled=True),
        lax.psum_scatter(totals[3], ("dp", "seq"), scatter_dimension=0, tiled=True),
        lax.psum_scatter(totals[4], ("dp", "seq"), scatter_dimension=0, tiled=True),
        lax.psum_scatter(totals[5], ("dp", "seq"), scatter_dimension=0, tiled=True),
        lax.psum_scatter(totals[6], ("dp", "seq"), scatter_dimension=0, tiled=True),
        lax.psum_scatter(totals[7], ("dp", "seq"), scatter_dimension=0, tiled=True),
        lax.psum_scatter(totals[8], ("dp", "seq"), scatter_dimension=0, tiled=True),
        lax.psum_scatter(totals[9], ("dp", "seq"), scatter_dimension=0, tiled=True),
    )
    return (
        layer_outputs[None],
        input_grads[None],
        shares[0][None],
        shares[1][None],
        shares[2][None],
        shares[3][None],
        shares[4][None],
        shares[5][None],
        shares[6][None],
        shares[7][None],
        shares[8][None],
        shares[9][None],
    )


def solution(mesh):
    stacked = P("section", None, None)
    spread = P(None, ("dp", "seq"), None, None)
    in_specs = (P("dp", None), spread, *[stacked] * 9, P("section", None), spread)
    flat = P("section", ("dp", "seq"))
    out = P("section", None, ("dp", "seq"), None, None)
    relay = mesh.shape["seq"] > 4 or mesh.shape["section"] != 2
    return jax.shard_map(
        relay_shards if relay else shards, mesh=mesh, in_specs=in_specs, out_specs=(out, out, *[flat] * 10), check_vma=False
    )
```

```python
import functools

import jax
import jax.numpy as jnp
from jax import lax
from jax.experimental import pallas as pl
from jax.experimental.pallas import tpu as pltpu
from jax.sharding import PartitionSpec as P

H = 12
HD = 64
PAIR = 2 * HD
eps_norm = 1e-06
far_below = -1000000000.0
BF = jnp.bfloat16
F32 = jnp.float32
VMEM_BYTES = 62 << 20
NEXT_ID = [1]
GROUP = 6
CUT = 2
GROUP_BACK = 6
CHUNK = 208


def nn(left, right):
    return lax.dot_general(left, right, (((1,), (0,)), ((), ())), preferred_element_type=F32)


def nt(left, right):
    return lax.dot_general(left, right, (((1,), (1,)), ((), ())), preferred_element_type=F32)


def norm_stats(values):
    centre = values - jnp.mean(values, axis=-1, keepdims=True)
    scale = lax.rsqrt(jnp.mean(centre * centre, axis=-1, keepdims=True) + eps_norm)
    return centre * scale, scale


def rows_at(index, count):
    return pl.ds(pl.multiple_of(index * count, count), count)


def norm_into(source, target, gain, shift, chunk):
    @pl.loop(0, source.shape[0] // chunk)
    def _(step):
        at = rows_at(step, chunk)
        hat, _ = norm_stats(source[at, :].astype(F32))
        target[at, :] = (hat * gain[...] + shift[...]).astype(BF)


def gelu_both(pre):
    rate, cube = 0.7978845608028654, 0.044715
    square = pre * pre
    tanh = jnp.tanh(pre * (rate + rate * cube * square))
    half = 0.5 + 0.5 * tanh
    act = pre * half
    slope = half + act * (1.0 - tanh) * (rate + 3.0 * rate * cube * square)
    return act, slope


class Copies:
    def __init__(self, sems):
        self.sems, self.used, self.open = sems, 0, []

    def fetch(self, own, other, target, mine):
        sem = self.sems.at[self.used]
        self.used += 1

        @pl.when(mine)
        def _():
            pltpu.make_async_copy(own, target, sem).start()

        @pl.when(jnp.logical_not(mine))
        def _():
            pltpu.make_async_copy(other, target, sem).start()

        return pltpu.make_async_copy(own, target, sem)

    def start(self, source, target):
        copy = pltpu.make_async_copy(source, target, self.sems.at[self.used])
        self.used += 1
        copy.start()
        return copy

    def store(self, source, target):
        self.open.append(self.start(source, target))

    def finish(self):
        for copy in self.open:
            copy.wait()


def time_attention(qkv, attn, probs, stage, soft, heads, heads_t, clips, frames, rows, width):
    @pl.loop(0, frames)
    def _(i):
        own = rows_at(i, rows)
        for j in range(frames):
            stage[pl.ds(j * rows, rows), :] = qkv[own, 0:width] * qkv[pl.ds(j * rows, rows), width : 2 * width]
        scores = nn(stage[...], heads[...])
        parts = []
        for j in range(frames):
            open_pair = clips[0, i] == clips[0, j]
            parts.append(scores[j * rows : (j + 1) * rows] + jnp.where(open_pair, 0.0, far_below))
        top = functools.reduce(jnp.maximum, parts)
        parts = [jnp.exp(part - top) for part in parts]
        inverse = 1.0 / sum(parts)
        for j in range(frames):
            prob = parts[j] * inverse
            probs[i, pl.ds(j * rows, rows), :] = prob
            soft[pl.ds(j * rows, rows), :] = prob.astype(BF)
        total = None
        for j in range(frames):
            at = pl.ds(j * rows, rows)
            term = nn(soft[at, :], heads_t[...]) * qkv[at, 2 * width : 3 * width].astype(F32)
            total = term if total is None else total + term
        attn[own, :] = total.astype(BF)


def fill_units(unit, pair_unit):
    for target in (unit, pair_unit):
        row = lax.broadcasted_iota(jnp.int32, target.shape, 0)
        column = lax.broadcasted_iota(jnp.int32, target.shape, 1)
        target[...] = jnp.where(row == column, 1.0, 0.0).astype(BF)


def split_patches(scores, patches):
    whole = patches // 16 * 16
    if whole == scores.shape[0]:
        return [scores]
    rest = scores[whole:]
    row = lax.broadcasted_iota(jnp.int32, rest.shape, 0)
    return [scores[:whole], jnp.where(row < patches - whole, rest, far_below)]


def space_attention(qkv, attn, logs, values_t, mixed_t, unit, pair_unit, frames, rows, patches, width):
    low_lane = lax.broadcasted_iota(jnp.int32, (rows, PAIR), 1) < HD
    deep = HD + 16
    values_t[...] = jnp.ones_like(values_t)

    @pl.loop(0, frames)
    def _(f):
        at = rows_at(f, rows)
        for pair in range(width // PAIR):
            turned = nt(pair_unit[...], qkv[at, 2 * width + pair * PAIR : 2 * width + (pair + 1) * PAIR]).astype(BF)
            for half in range(2):
                head = 2 * pair + half
                values_t[head * deep : head * deep + HD, :] = turned[half * HD : (half + 1) * HD]

        @pl.loop(0, width // PAIR // GROUP)
        def _(group):
            scores = []
            for member in range(GROUP):
                pair = group * GROUP + member

                def lanes(which):
                    return pl.ds(pl.multiple_of(which * width + pair * PAIR, PAIR), PAIR)

                query, key = qkv[at, lanes(0)] * BF(HD**-0.5), qkv[at, lanes(1)]
                for half in range(2):
                    scores.append(nt(jnp.where(low_lane if half == 0 else ~low_lane, key, BF(0)), query))
            expos, tops = [], []
            for score in scores:
                parts = split_patches(score, patches)
                top = functools.reduce(jnp.maximum, [jnp.max(part, axis=0, keepdims=True) for part in parts])
                expos.append(jnp.concatenate([jnp.exp(part - top).astype(BF) for part in parts], axis=0))
                tops.append(top)
            for member, (expo, top) in enumerate(zip(expos, tops)):
                head = group * (2 * GROUP) + member
                both = nn(values_t[pl.ds(pl.multiple_of(head * deep, 16), deep), :], expo)
                total = both[HD : HD + 1]
                logs[pl.ds(f * H + head, 1), :] = top + jnp.log(total)
                mixed_t[pl.ds(pl.multiple_of(head * HD, HD), HD), :] = (both[:HD] * (1.0 / total)).astype(BF)

        attn[at, :] = nt(unit[...], mixed_t[...]).astype(BF)


class Smalls:
    def __init__(self, own, other, held, mine):
        for which, refs in ((mine, own), (jnp.logical_not(mine), other)):

            @pl.when(which)
            def _(refs=refs):
                for source, target in zip(refs, held):
                    target[...] = source[...].reshape(target.shape)

        self.gains, self.biases, self.up_bias = held

    def gain(self, row):
        return self.gains.at[row : row + 1]

    def bias(self, row):
        return self.biases.at[row : row + 1]


def fill_heads(heads, heads_t):
    lane = lax.broadcasted_iota(jnp.int32, heads.shape, 0) // HD
    head = lax.broadcasted_iota(jnp.int32, heads.shape, 1)
    heads[...] = jnp.where(lane == head, HD**-0.5, 0.0).astype(BF)
    lane = lax.broadcasted_iota(jnp.int32, heads_t.shape, 1) // HD
    head = lax.broadcasted_iota(jnp.int32, heads_t.shape, 0)
    heads_t[...] = jnp.where(lane == head, 1.0, 0.0).astype(BF)


def fill_pick(pick, outer, place, count):
    each = pick.shape[0] // outer
    row = lax.broadcasted_iota(jnp.int32, pick.shape, 0)
    column = lax.broadcasted_iota(jnp.int32, pick.shape, 1)
    pick[...] = jnp.where(column == (row // each * count + place) * each + row % each, 1.0, 0.0).astype(BF)


def project(source, weight, biases, target):
    width = source.shape[1]
    for part in range(3):
        at = slice(part * width, (part + 1) * width)
        result = nn(source[...], weight[:, at])
        if biases[part] is not None:
            result = result + biases[part][...]
        target[:, at] = result.astype(BF)


def forward_time_kernel(block, frames, x, where, clips, *refs):
    small, small_other, own, other, refs = refs[:3], refs[3:6], refs[6:9], refs[9:12], refs[12:]
    (qkv_out, attn_out, proj_out, x1_out, probs_out, normed_out), refs = refs[:6], refs[6:]
    (time_qkv, time_out, time_fc), small_held, refs = refs[:3], refs[3:6], refs[6:]
    (normed, stage, qkv, attn, proj, x1, probs, soft, heads, heads_t, sems) = refs
    total, width = x.shape
    copies = Copies(sems)
    mine = where[0] == block
    loads = [copies.fetch(own[0], other[0], time_qkv, mine)]
    smalls = Smalls(small, small_other, small_held, mine)
    fill_heads(heads, heads_t)
    norm_into(x, normed, smalls.gain(0), smalls.bias(0), CHUNK)
    loads[0].wait()
    loads += [copies.fetch(a, b, c, mine) for a, b, c in zip(own[1:], other[1:], (time_out, time_fc))]
    copies.store(normed, normed_out)
    project(normed, time_qkv, (smalls.bias(1), None, smalls.bias(2)), qkv)
    copies.store(qkv, qkv_out)
    time_attention(qkv, attn, probs, stage, soft, heads, heads_t, clips, frames, total // frames, width)
    copies.store(attn, attn_out)
    copies.store(probs, probs_out)
    loads[1].wait()
    proj[...] = (nn(attn[...], time_out[...]) + smalls.bias(3)[...]).astype(BF)
    copies.store(proj, proj_out)
    loads[2].wait()
    x1[...] = x[...].astype(F32) + nn(proj[...], time_fc[...]) + smalls.bias(4)[...]
    copies.store(x1, x1_out)
    copies.finish()


def forward_rest_kernel(block, frames, patches, x1, where, *refs):
    small, small_other, own, other, refs = refs[:3], refs[3:6], refs[6:10], refs[10:14], refs[14:]
    (y_out, qkv_out, attn_out, x2_out, act_out, slope_out, normed_out, normed_mlp_out, logs_out), refs = refs[:9], refs[9:]
    (space_qkv, space_out, up_weight, down_weight), small_held, refs = refs[:4], refs[4:7], refs[7:]
    (normed, normed_mlp, y, qkv, attn, x2, act, slope, logs, values_t, mixed_t, unit, pair_unit, sems) = refs
    total, width = x1.shape
    copies = Copies(sems)
    mine = where[0] == block
    loads = [copies.fetch(own[0], other[0], space_qkv, mine)]
    smalls = Smalls(small, small_other, small_held, mine)
    fill_units(unit, pair_unit)
    norm_into(x1, normed, smalls.gain(1), smalls.bias(5), CHUNK)
    loads[0].wait()
    rest = (space_out, up_weight, down_weight)
    loads += [copies.fetch(a, b, c, mine) for a, b, c in zip(own[1:], other[1:], rest)]
    copies.store(normed, normed_out)
    project(normed, space_qkv, (smalls.bias(6), None, smalls.bias(7)), qkv)
    copies.store(qkv, qkv_out)
    space_attention(
        qkv, attn, logs, values_t, mixed_t, unit, pair_unit, frames, total // frames, patches, width
    )
    copies.store(attn, attn_out)
    copies.store(logs, logs_out)
    loads[1].wait()
    x2[...] = x1[...] + nn(attn[...], space_out[...]) + smalls.bias(8)[...]
    copies.store(x2, x2_out)
    norm_into(x2, normed_mlp, smalls.gain(2), smalls.bias(9), CHUNK)
    copies.store(normed_mlp, normed_mlp_out)
    loads[2].wait()

    @pl.loop(0, up_weight.shape[1] // width)
    def _(tile):
        at = rows_at(tile, width)
        pre = nn(normed_mlp[...], up_weight[:, at]) + smalls.up_bias[:, at]
        both = gelu_both(pre)
        act[:, at] = both[0].astype(BF)
        slope[:, at] = both[1].astype(BF)

    copies.store(act, act_out)
    copies.store(slope, slope_out)
    loads[3].wait()

    @pl.loop(0, 3)
    def _(tile):
        at = rows_at(tile, width // 3)
        y_at = nn(act[...], down_weight[:, at]) + smalls.biases[10:11, at] + x2[:, at]
        y[:, at] = y_at.astype(BF)

    copies.store(y, y_out)
    copies.finish()


def struct(shape, dtype=BF):
    return jax.ShapeDtypeStruct(shape, dtype)


def held(*structs):
    return [pltpu.VMEM(s.shape, s.dtype) for s in structs]


IN_VMEM = pl.BlockSpec(memory_space=pltpu.VMEM)
IN_SMEM = pl.BlockSpec(memory_space=pltpu.SMEM)
IN_HBM = pl.BlockSpec(memory_space=pl.ANY)


def small_held(small):
    return held(*[struct((array.size // array.shape[-1], array.shape[-1]), F32) for array in small])


def call(kernel, name, flops, specs, args, outs, out_specs, scratch, carried=None):
    remote = {}
    if carried is not None and carried.on:
        specs, args = specs + carried.arg_specs(), (*args, *carried.args())
        out_specs = out_specs + [IN_VMEM] * len(carried.outs())
        outs, scratch = outs + carried.outs(), scratch + carried.scratch()
        NEXT_ID.append(NEXT_ID[-1] + 1)
        remote = dict(collective_id=NEXT_ID[-1], has_side_effects=True)
    return pl.pallas_call(
        kernel,
        out_shape=outs,
        in_specs=specs,
        out_specs=out_specs,
        scratch_shapes=scratch,
        compiler_params=pltpu.CompilerParams(vmem_limit_bytes=VMEM_BYTES, **remote),
        cost_estimate=pl.CostEstimate(flops=flops, bytes_accessed=30 << 20, transcendentals=0),
        name=name,
    )(*args)


def forward_time(block, frames, x, where, clips, small, small_other, own, other):
    total, width = x.shape
    wide, full, triple = struct((total, width)), struct((total, width), F32), struct((total, 3 * width))
    probs = struct((frames, total, PAIR), F32)
    scratch = held(*own) + small_held(small)
    scratch += held(wide, wide, triple, wide, wide, full, probs, struct((total, PAIR)), struct((width, PAIR)), struct((PAIR, width)))
    return call(
        functools.partial(forward_time_kernel, block, frames),
        f"block{block}_forward_time",
        10 * total * width * width,
        [IN_VMEM, IN_SMEM, IN_SMEM] + [IN_VMEM] * 6 + [IN_HBM] * 6,
        (x, where, clips, *small, *small_other, *own, *other),
        [triple, wide, wide, full, probs, wide],
        [IN_HBM] * 6,
        scratch + [pltpu.SemaphoreType.DMA((9,))],
    )


def forward_rest(block, frames, patches, x1, where, small, small_other, own, other):
    total, width = x1.shape
    wide, full, triple = struct((total, width)), struct((total, width), F32), struct((total, 3 * width))
    deep = struct((total, own[2].shape[1]))
    rows = total // frames
    logs = struct((frames * H, rows), F32)
    scratch = held(*own) + small_held(small) + held(wide, wide, wide, triple, wide, full, deep, deep, logs)
    scratch += held(struct((H * (HD + 16), rows)), struct((width, rows)), struct((rows, rows)), struct((PAIR, PAIR)))
    return call(
        functools.partial(forward_rest_kernel, block, frames, patches),
        f"block{block}_forward_rest",
        24 * total * width * width,
        [IN_VMEM, IN_SMEM] + [IN_VMEM] * 6 + [IN_HBM] * 8,
        (x1, where, *small, *small_other, *own, *other),
        [wide, triple, wide, full, deep, deep, wide, wide, logs],
        [IN_HBM] * 9,
        scratch + [pltpu.SemaphoreType.DMA((13,))],
    )

MESH = pl.DeviceIdType.MESH


def beside(z):
    return z + 1 - 2 * lax.rem(z, 2), lax.rem(z + 2, 4)


def greet():
    barrier = pltpu.get_barrier_semaphore()
    near, far = beside(lax.axis_index("dp"))
    pl.semaphore_signal(barrier, inc=1, device_id={"section": 1 - lax.axis_index("section")}, device_id_type=MESH)
    pl.semaphore_signal(barrier, inc=1, device_id={"dp": near}, device_id_type=MESH)
    pl.semaphore_signal(barrier, inc=1, device_id={"dp": far}, device_id_type=MESH)
    pl.semaphore_wait(barrier, 3)


class Relay:
    def __init__(self, block, fetched, partial, out, scratch):
        self.partial, self.out, self.fetched = partial, out, fetched
        if fetched:
            self.mine, scratch = scratch[0], scratch[1:]
        else:
            self.mine = partial
        self.mates, self.taken, self.send, self.recv = scratch
        self.z = lax.axis_index("dp")
        self.near, self.far = beside(self.z)
        self.section = lax.axis_index("section")
        self.home = self.section == block
        self.away = self.section != block

    def over(self):
        return pltpu.make_async_remote_copy(
            self.partial,
            self.mates,
            self.send.at[0],
            self.recv.at[0],
            device_id={"section": 1 - self.section},
            device_id_type=MESH,
        )

    def local(self):
        return pltpu.make_async_copy(self.partial, self.mine, self.send.at[4])

    def along(self, step):
        part = (lax.rem(self.near + 2, 4), self.near, self.far)[step]
        return pltpu.make_async_remote_copy(
            self.mine.at[part],
            self.taken.at[step],
            self.send.at[1 + step],
            self.recv.at[1 + step],
            device_id={"dp": self.far if step == 2 else self.near},
            device_id_type=MESH,
        )

    def begin(self):
        @pl.when(self.away)
        def _():
            self.over().start()

        if self.fetched:

            @pl.when(self.home)
            def _():
                self.local().start()

    def middle(self):
        @pl.when(self.home)
        def _():
            if self.fetched:
                self.local().wait()
            self.over().wait_recv()
            for step, part in enumerate((lax.rem(self.near + 2, 4), self.near)):
                self.mine[part] = (self.mine[part].astype(F32) + self.mates[part].astype(F32)).astype(BF)
                self.along(step).start()

        @pl.when(self.away)
        def _():
            self.over().wait_send()

    def second(self):
        @pl.when(self.home)
        def _():
            far = self.far
            self.along(0).wait()
            total = self.mine[far].astype(F32) + self.mates[far].astype(F32) + self.taken[0].astype(F32)
            self.mine[far] = total.astype(BF)
            self.along(2).start()

    def end(self):
        @pl.when(self.home)
        def _():
            self.along(1).wait()
            total = self.mine[self.z].astype(F32) + self.mates[self.z].astype(F32) + self.taken[1].astype(F32)
            self.along(2).wait()
            self.out[...] = total + self.taken[2].astype(F32)

        @pl.when(self.away)
        def _():
            self.out[...] = jnp.zeros_like(self.out)


class LowRelay:
    def __init__(self, lows, out, scratch):
        self.lows, self.out = lows, out
        self.mine, self.mate, self.taken, self.send, self.recv = scratch
        self.places = beside(lax.axis_index("dp"))
        self.section = lax.axis_index("section")

    def over(self, low):
        return pltpu.make_async_remote_copy(
            low,
            self.mate,
            self.send.at[0],
            self.recv.at[0],
            device_id={"section": 1 - self.section},
            device_id_type=MESH,
        )

    def along(self, step):
        return pltpu.make_async_remote_copy(
            self.mine.at[step],
            self.taken.at[step],
            self.send.at[1 + step],
            self.recv.at[1 + step],
            device_id={"dp": self.places[step]},
            device_id_type=MESH,
        )

    def begin(self):
        for block, low in enumerate(self.lows):

            @pl.when(self.section != block)
            def _(low=low):
                self.over(low).start()

    def at_home(self, act):
        if len(self.lows) == 2:
            act()
        else:
            pl.when(self.section == 0)(act)

    def middle(self):
        for block, low in enumerate(self.lows):

            @pl.when(self.section == block)
            def _(low=low):
                self.over(low).wait_recv()
                self.mine[0] = low[...] + self.mate[...]
                self.along(0).start()

            @pl.when(self.section != block)
            def _(low=low):
                self.over(low).wait_send()

    def second(self):
        def _():
            self.along(0).wait()
            self.mine[1] = self.mine[0] + self.taken[0]
            self.along(1).start()

        self.at_home(_)

    def end(self):
        def _():
            self.along(1).wait()
            self.out[...] = self.mine[1] + self.taken[1]

        self.at_home(_)
        if len(self.lows) == 1:

            @pl.when(self.section != 0)
            def _():
                self.out[...] = jnp.zeros_like(self.out)


class Carried:
    def __init__(self, block, pieces, own=None, lows=()):
        self.block, self.pieces, self.own, self.lows = block, pieces, own, lows
        self.on = bool(pieces)

    def args(self):
        return [piece[0] for piece in self.pieces] + list(self.lows)

    def arg_specs(self):
        return [IN_HBM] * len(self.pieces) + [IN_VMEM] * len(self.lows)

    def sizes(self):
        sizes = [(piece[0].shape[0], piece[2], piece[0].shape[2], True) for piece in self.pieces]
        return sizes + ([(sizes[0][0], self.own[1], sizes[0][2], False)] if self.own else [])

    def outs(self):
        outs = [struct((rows, width), F32) for _, rows, width, _ in self.sizes()]
        return outs + [struct(low.shape, F32) for low in self.lows[:1]]

    def scratch(self):
        dma = pltpu.SemaphoreType.DMA
        scratch = []
        for count, rows, width, fetched in self.sizes():
            full = struct((count, rows, width))
            scratch += held(*[full] * (2 if fetched else 1), struct((3, rows, width)))
            scratch += [dma((5,)), dma((4,))]
        if self.lows:
            low = struct(self.lows[0].shape, F32)
            two = struct((2, *low.shape), F32)
            scratch += held(two, low, two) + [dma((3,)), dma((3,))]
        return scratch

    def split(self, refs, outs):
        n_lows, n_pieces = len(self.lows), len(self.pieces)
        partials, lows, refs = refs[:n_pieces], refs[n_pieces : n_pieces + n_lows], refs[n_pieces + n_lows :]
        results, refs = refs[:outs], refs[outs:]
        n_outs = len(self.outs())
        sums, refs = refs[:n_outs], refs[n_outs:]
        refs, scratch = list(refs), []
        self.relays, self.own_relay = [], None
        lengths = [5 if fetched else 4 for *_, fetched in self.sizes()] + ([5] if self.lows else [])
        scratch = refs[len(refs) - sum(lengths) :]
        refs = refs[: len(refs) - sum(lengths)]
        groups = []
        for length in lengths:
            groups.append(scratch[:length])
            scratch = scratch[length:]
        for (_, start, rows), partial, out, group in zip(self.pieces, partials, sums, groups):
            source = partial.at[:, start : start + rows]
            self.relays.append(Relay(self.block, True, source, out, group))
        self.left = (sums[n_pieces:], groups[n_pieces:])
        if self.lows:
            self.relays.append(LowRelay(lows, sums[-1], groups[-1]))
        return results, refs

    def begin(self):
        if self.on:
            greet()
            for relay in self.relays:
                relay.begin()

    def begin_own(self, result):
        if self.own:
            sums, groups = self.left
            source = result.at[:, self.own[0] : self.own[0] + self.own[1]]
            self.own_relay = Relay(self.block, False, source, sums[0], groups[0])
            self.own_relay.begin()

    def middle(self):
        for relay in self.relays:
            relay.middle()

    def second(self):
        for relay in self.relays:
            relay.second()

    def middle_own(self):
        if self.own:
            self.own_relay.middle()

    def second_own(self):
        if self.own:
            self.own_relay.second()

    def end(self):
        for relay in self.relays + ([self.own_relay] if self.own else []):
            relay.end()


BIAS, UP, LOW = 3, 14, 24


def norm_back(hidden, grads, gain, above, target, sums, chunk):
    width = hidden.shape[1]
    sums[...] = jnp.zeros_like(sums)

    def fold(rows):
        return jnp.sum(rows.reshape(chunk // 8, 8, width), axis=0)

    @pl.loop(0, hidden.shape[0] // chunk)
    def _(step):
        at = rows_at(step, chunk)
        hat, scale = norm_stats(hidden[at, :].astype(F32))
        grad = grads[at, :]
        sums[0:8, :] += fold(grad * hat)
        sums[8:16, :] += fold(grad)
        inner = grad * gain[...]
        mean = jnp.mean(inner, axis=-1, keepdims=True)
        slant = jnp.mean(inner * hat, axis=-1, keepdims=True)
        result = above[at, :].astype(F32) + scale * (inner - mean - hat * slant)
        target[at, :] = result.astype(target.dtype)


def norm_sums(sums, low, gain_row, bias_row):
    low[gain_row : gain_row + 1, :] = jnp.sum(sums[0:8, :], axis=0, keepdims=True)
    low[BIAS + bias_row : BIAS + bias_row + 1, :] = jnp.sum(sums[8:16, :], axis=0, keepdims=True)


def fill_ones(turned, count):
    turned[pl.ds(count, 16), :] = jnp.ones((16, turned.shape[1]), BF)


def weight_grad(turned, count, grads, result, row, low, *low_rows):
    width = low.shape[1]
    parts = result.shape[0]
    each = count // parts

    for step, low_row in enumerate(low_rows):
        both = nn(turned[0 : count + 16, :], grads[:, step * width : (step + 1) * width])
        at = slice(row + step * each, row + (step + 1) * each)
        for part in range(parts):
            result[part, at, :] = both[part * each : (part + 1) * each].astype(BF)
        if low_row is not None:
            low[low_row : low_row + 1, :] = both[count : count + 1, :]


def tiled_nt(left, right, target, tile):
    @pl.loop(0, right.shape[0] // tile)
    def _(step):
        at = rows_at(step, tile)
        target[:, at] = nt(left[...], right[at, :])


def back_mlp_kernel(block, carried, places, gy, *refs):
    small, small_other, own, other, refs = refs[:3], refs[3:6], refs[6:8], refs[8:10], refs[10:]
    act_in, slope_in, x2_in, normed_in, refs = refs[0], refs[1], refs[2], refs[3], refs[4:]
    (g2_out, grads_out, low), refs = carried.split(refs, 3)
    (up_weight, down_weight), small_held, refs = refs[:2], refs[2:5], refs[5:]
    (act, slope, x2, normed, gpre, gnm, g2, turned, result, sums, pick, pick_wide, sems) = refs
    total, width = gy.shape
    chunk = CHUNK
    copies = Copies(sems)
    carried.begin()
    mine = lax.axis_index("section") == block
    tiles = down_weight.shape[0] // width
    load_tiles = []
    for tile in range(tiles):
        at = pl.ds(tile * width, width)
        load_tiles.append(copies.fetch(own[1].at[at], other[1].at[at], down_weight.at[at], mine))
        load_tiles.append(copies.start(slope_in.at[:, at], slope.at[:, at]))
    smalls = Smalls(small, small_other, small_held, mine)
    fill_pick(pick, result.shape[0], lax.axis_index("seq"), places)
    fill_pick(pick_wide, 1, lax.axis_index("seq"), places)
    low[...] = jnp.zeros_like(low)
    for tile in range(tiles):
        at = slice(tile * width, (tile + 1) * width)
        load_tiles[2 * tile].wait()
        load_tiles[2 * tile + 1].wait()
        if tile == 1:
            load_up = copies.fetch(own[0], other[0], up_weight, mine)
            load_x2 = copies.start(x2_in, x2)
            load_normed = copies.start(normed_in, normed)
            load_act = copies.start(act_in, act)
        gpre[:, at] = (nt(gy[...], down_weight[at, :]) * slope[:, at].astype(F32)).astype(BF)

    carried.middle()
    load_up.wait()
    tiled_nt(gpre, up_weight, gnm, width // 3)
    load_x2.wait()
    carried.second()
    norm_back(x2, gnm, smalls.gain(2), gy, g2, sums, chunk)
    copies.store(g2, g2_out)
    norm_sums(sums, low, 2, 9)
    load_normed.wait()
    count = pick.shape[0]
    turned[0:count, :] = nt(pick[...], normed[...]).astype(BF)
    fill_ones(turned, count)
    weight_grad(turned, count, gpre, result, 0, low, *range(UP, UP + gpre.shape[1] // width))
    load_act.wait()
    wide = pick_wide.shape[0]
    parts = act.shape[1] // pick_wide.shape[1]

    @pl.loop(0, parts)
    def _(part):
        turned[rows_at(part, wide), :] = nt(pick_wide[...], act[:, rows_at(part, pick_wide.shape[1])]).astype(BF)

    fill_ones(turned, parts * wide)
    weight_grad(turned, parts * wide, gy, result, result.shape[1] - parts * wide // result.shape[0], low, BIAS + 10)
    copies.store(result, grads_out)
    carried.end()
    copies.finish()


def space_attention_back(
    qkv, grads, logs, result, keys_t, turned_t, unit, pair_unit, frames, rows, patches, width
):
    low_lane = lax.broadcasted_iota(jnp.int32, (rows, PAIR), 1) < HD

    @pl.loop(0, frames)
    def _(f):
        at = rows_at(f, rows)
        for pair in range(width // PAIR):
            lanes = slice(width + pair * PAIR, width + (pair + 1) * PAIR)
            keys_t[pair * PAIR : (pair + 1) * PAIR, :] = nt(pair_unit[...], qkv[at, lanes]).astype(BF)

        @pl.loop(0, width // PAIR // GROUP_BACK)
        def _(group):
            def lanes(which, member):
                pair = group * GROUP_BACK + member
                return pl.ds(pl.multiple_of(which * width + pair * PAIR, PAIR), PAIR)

            scores, grad_softs = [], []
            for member in range(GROUP_BACK):
                query = qkv[at, lanes(0, member)] * BF(HD**-0.5)
                key, value, grad = qkv[at, lanes(1, member)], qkv[at, lanes(2, member)], grads[at, lanes(0, member)]
                for half in range(2):
                    mine = low_lane if half == 0 else ~low_lane
                    scores.append(nt(jnp.where(mine, key, BF(0)), query))
                    grad_softs.append(nt(jnp.where(mine, value, BF(0)), grad))
            softs, grad_scores = [], []
            for member, (score, grad_soft) in enumerate(zip(scores, grad_softs)):
                head = group * (2 * GROUP_BACK) + member
                log = logs[pl.ds(f * H + head, 1), :]
                soft = [jnp.exp(part - log) for part in split_patches(score, patches)]
                cut = soft[0].shape[0]
                changes = [grad_soft[:cut], grad_soft[cut:]][: len(soft)]
                slant = sum(jnp.sum(part * change, axis=0, keepdims=True) for part, change in zip(soft, changes))
                changes = [change - slant for change in changes]
                softs.append(jnp.concatenate([part.astype(BF) for part in soft], axis=0))
                grad_scores.append(
                    jnp.concatenate([(part * change).astype(BF) for part, change in zip(soft, changes)], axis=0)
                )
            for member in range(GROUP_BACK):
                query = qkv[at, lanes(0, member)] * BF(HD**-0.5)
                grad = grads[at, lanes(0, member)]
                pair = 2 * member
                grad_key = [nn(grad_scores[pair + half], query) for half in range(2)]
                grad_value = [nn(softs[pair + half], grad) for half in range(2)]
                result[at, lanes(1, member)] = jnp.where(low_lane, *grad_key).astype(BF)
                result[at, lanes(2, member)] = jnp.where(low_lane, *grad_value).astype(BF)
                for half in range(2):
                    head = group * (2 * GROUP_BACK) + pair + half
                    own = pl.ds(pl.multiple_of(head * HD, HD), HD)
                    turned_t[own, :] = (nn(keys_t[own, :], grad_scores[pair + half]) * HD**-0.5).astype(BF)

        result[at, 0:width] = nt(unit[...], turned_t[...]).astype(BF)


def back_space_kernel(block, carried, places, frames, patches, *refs):
    small, small_other, own, other, refs = refs[:3], refs[3:6], refs[6:8], refs[8:10], refs[10:]
    (g2_in, qkv_in, attn_in, x1_in, normed_in, logs_in), refs = refs[:6], refs[6:]
    (g1_out, grads_out, low), refs = carried.split(refs, 3)
    (space_qkv, space_out), small_held, refs = refs[:2], refs[2:5], refs[5:]
    (g2, qkv, attn, x1, normed, logs, g2_low, gattn, gqkv, gnorm, g1, turned, result, sums, pick), refs = refs[:15], refs[15:]
    (keys_t, turned_t, unit, pair_unit, sems) = refs
    total, width = g2.shape
    chunk = CHUNK
    copies = Copies(sems)
    carried.begin()
    mine = lax.axis_index("section") == block
    load_g2 = copies.start(g2_in, g2)
    load_out = copies.fetch(own[1], other[1], space_out, mine)
    load_qkv = copies.start(qkv_in, qkv)
    load_logs = copies.start(logs_in, logs)
    load_weight = copies.fetch(own[0], other[0], space_qkv, mine)
    load_x1 = copies.start(x1_in, x1)
    load_attn = copies.start(attn_in, attn)
    load_normed = copies.start(normed_in, normed)
    smalls = Smalls(small, small_other, small_held, mine)
    fill_pick(pick, result.shape[0], lax.axis_index("seq"), places)
    fill_units(unit, pair_unit)
    low[...] = jnp.zeros_like(low)
    load_g2.wait()
    g2_low[...] = g2[...].astype(BF)
    load_out.wait()
    gattn[...] = nt(g2_low[...], space_out[...]).astype(BF)
    carried.middle()
    load_qkv.wait()
    load_logs.wait()
    space_attention_back(
        qkv, gattn, logs, gqkv, keys_t, turned_t, unit, pair_unit, frames, total // frames, patches, width
    )
    carried.second()
    load_weight.wait()
    tiled_nt(gqkv, space_qkv, gnorm, width // 3)
    load_x1.wait()
    norm_back(x1, gnorm, smalls.gain(1), g2, g1, sums, chunk)
    copies.store(g1, g1_out)
    norm_sums(sums, low, 1, 5)
    load_attn.wait()
    count = pick.shape[0]
    turned[0:count, :] = nt(pick[...], attn[...]).astype(BF)
    fill_ones(turned, count)
    each = count // result.shape[0]
    weight_grad(turned, count, g2_low, result, 3 * each, low, BIAS + 8)
    load_normed.wait()
    turned[0:count, :] = nt(pick[...], normed[...]).astype(BF)
    weight_grad(turned, count, gqkv, result, 0, low, BIAS + 6, None, BIAS + 7)
    copies.store(result, grads_out)
    carried.end()
    copies.finish()


def time_attention_back(qkv, grads, probs, result, stage, soft, soft_grad, grad_key, grad_value, heads, heads_t, frames, rows, width, between):
    grad_key[...] = jnp.zeros_like(grad_key)
    grad_value[...] = jnp.zeros_like(grad_value)

    @pl.loop(0, frames)
    def _(i):
        between(i)
        own = rows_at(i, rows)
        for j in range(frames):
            stage[pl.ds(j * rows, rows), :] = grads[own, :] * qkv[pl.ds(j * rows, rows), 2 * width : 3 * width]
        grad_soft = nn(stage[...], heads[...]) * HD**0.5
        parts = [probs[i, pl.ds(j * rows, rows), :] for j in range(frames)]
        changes = [grad_soft[j * rows : (j + 1) * rows] for j in range(frames)]
        total = sum(part * change for part, change in zip(parts, changes))
        for j in range(frames):
            at = pl.ds(j * rows, rows)
            soft[at, :] = parts[j].astype(BF)
            soft_grad[at, :] = (parts[j] * (changes[j] - total)).astype(BF)
        grad_query = None
        for j in range(frames):
            at = pl.ds(j * rows, rows)
            wide = nn(soft_grad[at, :], heads_t[...])
            term = wide * qkv[at, width : 2 * width].astype(F32)
            grad_query = term if grad_query is None else grad_query + term
            grad_key[at, :] += wide * qkv[own, 0:width].astype(F32)
            grad_value[at, :] += nn(soft[at, :], heads_t[...]) * grads[own, :].astype(F32)
        result[own, 0:width] = (grad_query * HD**-0.5).astype(BF)

    result[:, width : 2 * width] = (grad_key[...] * HD**-0.5).astype(BF)
    result[:, 2 * width : 3 * width] = grad_value[...].astype(BF)


def back_time_kernel(block, carried, places, frames, x, *refs):
    small, small_other, own, other, refs = refs[:3], refs[3:6], refs[6:9], refs[9:12], refs[12:]
    (g1_in, qkv_in, attn_in, proj_in, probs_in, normed_in), refs = refs[:6], refs[6:]
    (gx_out, grads_out, low), refs = carried.split(refs, 3)
    (time_qkv, time_out, time_fc), small_held, refs = refs[:3], refs[3:6], refs[6:]
    (g1, qkv, attn, proj, probs, normed, g1_low, gproj, gattn, gqkv, stage, soft, soft_grad), refs = refs[:13], refs[13:]
    (grad_key, grad_value, turned, result, sums, pick, heads, heads_t, sems) = refs
    total, width = x.shape
    chunk = CHUNK
    copies = Copies(sems)
    carried.begin()
    mine = lax.axis_index("section") == block
    load_g1 = copies.start(g1_in, g1)
    load_fc = copies.fetch(own[2], other[2], time_fc, mine)
    load_out = copies.fetch(own[1], other[1], time_out, mine)
    smalls = Smalls(small, small_other, small_held, mine)
    fill_pick(pick, result.shape[0], lax.axis_index("seq"), places)
    fill_heads(heads, heads_t)
    low[...] = jnp.zeros_like(low)
    load_g1.wait()
    load_fc.wait()
    load_proj = copies.start(proj_in, proj)
    load_attn = copies.start(attn_in, attn)
    load_qkv = copies.start(qkv_in, qkv)
    load_probs = copies.start(probs_in, probs)
    load_weight = copies.fetch(own[0], other[0], time_qkv, mine)
    load_normed = copies.start(normed_in, normed)
    g1_low[...] = g1[...].astype(BF)
    gproj[...] = nt(g1_low[...], time_fc[...]).astype(BF)
    load_out.wait()
    gattn[...] = nt(gproj[...], time_out[...]).astype(BF)
    carried.middle()
    count = pick.shape[0]
    each = count // result.shape[0]
    load_proj.wait()
    turned[0:count, :] = nt(pick[...], proj[...]).astype(BF)
    fill_ones(turned, count)
    weight_grad(turned, count, g1_low, result, 4 * each, low, BIAS + 4)
    load_attn.wait()
    turned[0:count, :] = nt(pick[...], attn[...]).astype(BF)
    weight_grad(turned, count, gproj, result, 3 * each, low, BIAS + 3)
    carried.begin_own(result)
    load_qkv.wait()
    load_probs.wait()

    def between(step):
        pl.when(step == 1)(carried.middle_own)
        pl.when(step == 3)(carried.second)

    time_attention_back(
        qkv, gattn, probs, gqkv, stage, soft, soft_grad, grad_key, grad_value, heads, heads_t, frames, total // frames, width, between
    )
    carried.second_own()
    load_weight.wait()
    gnorm = grad_key
    tiled_nt(gqkv, time_qkv, gnorm, width // 3)
    norm_back(x, gnorm, smalls.gain(0), g1, gattn, sums, chunk)
    copies.store(gattn, gx_out)
    norm_sums(sums, low, 0, 0)
    load_normed.wait()
    turned[0:count, :] = nt(pick[...], normed[...]).astype(BF)
    weight_grad(turned, count, gqkv, result, 0, low, BIAS + 1, None, BIAS + 2)
    copies.store(result, grads_out)
    carried.end()
    copies.finish()


def back_mlp(block, carried, parts, places, gy, small, small_other, own, other, act, slope, x2, normed):
    total, width = gy.shape
    hidden = act.shape[1]
    count, many = width // places, hidden // places
    wide, full, low = struct((total, width)), struct((total, width), F32), struct((LOW, width), F32)
    result = struct((parts, (count * (hidden // width) + many) // parts, width))
    deep = struct((total, hidden))
    scratch = held(*own) + small_held(small)
    scratch += held(deep, deep, full, wide, deep, full, full, struct((many + 16, total)), result, struct((16, width), F32))
    scratch += held(struct((count, width)), struct((hidden // parts // places, hidden // parts)))
    return call(
        functools.partial(back_mlp_kernel, block, carried, places),
        f"block{block}_mlp_backward",
        24 * total * width * width,
        [IN_VMEM] * 7 + [IN_HBM] * 8,
        (gy, *small, *small_other, *own, *other, act, slope, x2, normed),
        [full, result, low],
        [IN_HBM] * 2 + [IN_VMEM],
        scratch + [pltpu.SemaphoreType.DMA((4 + 2 * hidden // width + 3,))],
        carried,
    )


def back_space(block, carried, parts, places, frames, patches, small, small_other, own, other, g2, qkv, attn, x1, normed, logs):
    total, width = g2.shape
    count = width // places
    wide, full, triple = struct((total, width)), struct((total, width), F32), struct((total, 3 * width))
    result, low = struct((parts, 4 * count // parts, width)), struct((LOW, width), F32)
    scratch = held(*own) + small_held(small) + held(full, triple, wide, full, wide, logs, wide, wide, triple, full, full)
    scratch += held(struct((count + 16, total)), result, struct((16, width), F32), struct((count, width)))
    rows = total // frames
    scratch += held(struct((width, rows)), struct((width, rows)), struct((rows, rows)), struct((PAIR, PAIR)))
    return call(
        functools.partial(back_space_kernel, block, carried, places, frames, patches),
        f"block{block}_space_backward",
        30 * total * width * width,
        [IN_VMEM] * 6 + [IN_HBM] * 10,
        (*small, *small_other, *own, *other, g2, qkv, attn, x1, normed, logs),
        [full, result, low],
        [IN_HBM] * 2 + [IN_VMEM],
        scratch + [pltpu.SemaphoreType.DMA((11,))],
        carried,
    )


def back_time(block, carried, parts, places, frames, x, small, small_other, own, other, g1, qkv, attn, proj, probs, normed):
    total, width = x.shape
    count = width // places
    wide, full, triple = struct((total, width)), struct((total, width), F32), struct((total, 3 * width))
    few = struct((total, PAIR))
    result, low = struct((parts, 5 * count // parts, width)), struct((LOW, width), F32)
    scratch = held(*own) + small_held(small)
    scratch += held(full, triple, wide, wide, probs, wide, wide, wide, wide, triple, wide, few, few, full, full)
    scratch += held(struct((count + 16, total)), result, struct((16, width), F32), struct((count, width)))
    scratch += held(struct((width, PAIR)), struct((PAIR, width)))
    return call(
        functools.partial(back_time_kernel, block, carried, places, frames),
        f"block{block}_time_backward",
        24 * total * width * width,
        [IN_VMEM] * 7 + [IN_HBM] * 12,
        (x, *small, *small_other, *own, *other, g1, qkv, attn, proj, probs, normed),
        [wide, result, low],
        [IN_HBM] * 2 + [IN_VMEM],
        scratch + [pltpu.SemaphoreType.DMA((13,))],
        carried,
    )


def begin_kernel(tokens, cotangent, *refs):
    n = (len(refs) - 2 - 8) // 2
    own, refs = refs[:n], refs[n:]
    x_out, cot_out, refs = refs[0], refs[1], refs[2:]
    other, refs = refs[:n], refs[n:]
    raw, raw_cot, frame, cot, send, recv, local = refs[:7]
    count = lax.axis_size("seq")
    me = lax.axis_index("seq")
    section = lax.axis_index("section")
    patches = raw.shape[0]
    whole = patches // 16 * 16
    load = pltpu.make_async_copy(tokens.at[section, 0], raw, local.at[0])
    load_cot = pltpu.make_async_copy(cotangent.at[section, 0], raw_cot, local.at[1])
    load.start()
    load_cot.start()

    def pad_into(source, target):
        target[0:whole, :] = source[0:whole, :]
        if target.shape[0] > whole:
            rest = jnp.zeros((target.shape[0] - patches, source.shape[1]), BF)
            target[whole:, :] = jnp.concatenate([source[whole:, :], rest], axis=0)

    barrier = pltpu.get_barrier_semaphore()
    mate = {"section": 1 - section}
    pl.semaphore_signal(barrier, inc=1, device_id=mate, device_id_type=MESH)
    for step in range(1, count):
        pl.semaphore_signal(barrier, inc=1, device_id={"seq": lax.rem(me + step, count)}, device_id_type=MESH)
    load.wait()
    pad_into(raw, frame)
    pl.semaphore_wait(barrier, count)
    copies = []
    for step in range(1, count):
        copies.append(
            pltpu.make_async_remote_copy(
                frame,
                x_out.at[me],
                send.at[step - 1],
                recv.at[step - 1],
                device_id={"seq": lax.rem(me + step, count)},
                device_id_type=MESH,
            )
        )
    for at, (source, target) in enumerate(zip(own, other)):
        copies.append(
            pltpu.make_async_remote_copy(
                source, target, send.at[count - 1 + at], recv.at[count - 1 + at], device_id=mate, device_id_type=MESH
            )
        )
    copies.append(pltpu.make_async_copy(frame, x_out.at[me], local.at[2]))
    for copy in copies:
        copy.start()
    load_cot.wait()
    pad_into(raw_cot, cot)
    last = pltpu.make_async_copy(cot, cot_out, local.at[3])
    last.start()
    for copy in copies:
        copy.wait()
    last.wait()


def begin(tokens, cotangent, own, rows):
    count = lax.axis_size("seq")
    patches, width = tokens.shape[-2:]
    pad, raw = struct((rows, width)), struct((patches, width))
    outs = [struct((count, rows, width)), pad] + [struct(a.shape, a.dtype) for a in own]
    copies = count - 1 + len(own)
    dma = pltpu.SemaphoreType.DMA
    return pl.pallas_call(
        begin_kernel,
        out_shape=outs,
        in_specs=[IN_HBM] * (2 + len(own)),
        out_specs=[IN_HBM] * len(outs),
        scratch_shapes=held(raw, raw, pad, pad) + [dma((copies,)), dma((copies,)), dma((4,)), dma((1,))],
        compiler_params=pltpu.CompilerParams(collective_id=0, has_side_effects=True, vmem_limit_bytes=VMEM_BYTES),
        name="gather_frames",
    )(tokens, cotangent, *own)


def finish_kernel(carried, shares, *refs):
    results, refs = refs[:4], refs[4:]
    (swapped,), refs = carried.split(refs, 1)
    send, recv = refs
    section = lax.axis_index("section")
    rows = swapped.shape[1]
    own = rows_at(lax.axis_index("seq"), rows)
    carried.begin()

    def over(which, block):
        return pltpu.make_async_remote_copy(
            results[2 * which + block].at[own],
            swapped.at[which],
            send.at[which],
            recv.at[which],
            device_id={"section": 1 - section},
            device_id_type=MESH,
        )

    for which in range(2):
        for block in range(2):

            @pl.when(section != block)
            def _(which=which, block=block):
                over(which, block).start()

    carried.middle()
    for which in range(2):
        over(which, 0).wait()
    carried.second()
    carried.end()


def finish(carried, rows, results):
    width = results[0].shape[1]
    return call(
        functools.partial(finish_kernel, carried, rows),
        "finish_sums",
        1 << 20,
        [IN_HBM] * 4,
        tuple(results),
        [struct((2, rows, width))],
        [IN_HBM],
        [pltpu.SemaphoreType.DMA((2,)), pltpu.SemaphoreType.DMA((2,))],
        carried,
    )


def layout_kernel(places, patches, pieces, rows_each, low_a, low_b, *refs):
    n = len(pieces)
    sums, refs = (refs[:n], refs[n : 2 * n]), refs[2 * n :]
    results, swapped, refs = refs[:4], refs[4], refs[5:]
    weights, lows, frames, refs = refs[:7], refs[7:10], refs[10:12], refs[12:]
    total, mine, sems = refs
    section = lax.axis_index("section")
    z, place = lax.axis_index("dp"), lax.axis_index("seq")
    rows, width = mine.shape[1:]
    loads = []
    for at, (start, count) in enumerate(pieces):
        for block in range(2):

            @pl.when(section == block)
            def _(at=at, block=block, start=start, count=count):
                pltpu.make_async_copy(sums[block][at], total.at[start : start + count], sems.at[at]).start()

        loads.append(pltpu.make_async_copy(sums[0][at], total.at[start : start + count], sems.at[at]))
    for which in range(2):
        own = rows_at(place, rows)
        for block in range(2):

            @pl.when(section == block)
            def _(which=which, block=block):
                pltpu.make_async_copy(results[2 * which + block].at[own], mine.at[which], sems.at[n + which]).start()

        loads.append(pltpu.make_async_copy(results[2 * which].at[own], mine.at[which], sems.at[n + which]))
        loads.append(pltpu.make_async_copy(swapped.at[which], mine.at[2 + which], sems.at[n + 2 + which]))
        loads[-1].start()
    low = low_a[...]
    low = jnp.concatenate([low[0:8] + low_b[...], low[8:]], axis=0)
    part = z * lax.axis_size("seq") + place
    for target, first, count in zip(lows, (0, BIAS, UP), (BIAS, UP - BIAS, target_rows(lows[2], places, width))):
        flat = jnp.concatenate([low[first + at : first + at + 1] for at in range(count)], axis=1)
        size = target.shape[1]
        flat = jnp.broadcast_to(flat, (8, flat.shape[1]))
        target[...] = pltpu.roll(flat, lax.rem(count * width - part * size, count * width), 1)[0:1, :size]
    for load in loads:
        load.wait()
    for which, target in enumerate(frames):
        for block in range(2):

            @pl.when(section == block)
            def _(which=which, target=target, block=block):
                target[0, block, 0] = mine[which, 0:patches]
                target[0, 1 - block, 0] = mine[2 + which, 0:patches]

    start = 0
    lanes = width // PAIR
    for target, count in zip(weights, rows_each):
        each = target.shape[0] // (count * lanes)
        for at in range(count):
            for lane in range(lanes):
                target[pl.ds(at * lanes + lane, each, stride=count * lanes), :] = total[
                    start + at * each : start + (at + 1) * each, lane * PAIR : (lane + 1) * PAIR
                ]
        start += count * each


def target_rows(target, places, width):
    return target.shape[1] * places // width


def layout(patches, places, width, hidden, pieces, sums, low_a, low_b, results, swapped):
    each = width // places
    deep = hidden // width
    rows_each = (3, 1, 1, 3, 1, deep, 1)
    heights = (each, each, each, each, each, each, hidden // places)
    outs = [struct((h * r * width // PAIR, PAIR), F32) for h, r in zip(heights, rows_each)]
    outs += [struct((1, rows * width // places), F32) for rows in (BIAS, UP - BIAS, deep)]
    outs += [struct((1, 2, 1, patches, width))] * 2
    rows = swapped.shape[1]
    n = len(pieces)
    total = sum(count for _, count in pieces)
    scratch = held(struct((total, width), F32), struct((4, rows, width))) + [pltpu.SemaphoreType.DMA((n + 4,))]
    return call(
        functools.partial(layout_kernel, places, patches, pieces, rows_each),
        "lay_out",
        1 << 20,
        [IN_VMEM] * 2 + [IN_HBM] * (2 * n + 5),
        (low_a, low_b, *sums[0], *sums[1], *results, swapped),
        outs,
        [IN_VMEM] * len(outs),
        scratch,
    )


def after(first, then):
    return lax.optimization_barrier((first, then))[1]


def shards(clip_ids, tokens, *rest):
    weights, small, cotangent = rest[:7], list(rest[7:10]), rest[10]
    NEXT_ID[:] = [1]
    section = lax.axis_index("section")
    n_dp, n_seq = lax.axis_size("dp"), lax.axis_size("seq")
    patches, width = tokens.shape[2:]
    hidden = weights[5].shape[2]
    places = n_dp * n_seq
    rows = -(-patches // 16) * 16
    swap = [(0, 1), (1, 0)]
    small[2] = small[2].reshape(1, 1, hidden)

    own = [array[0] for array in weights]
    inputs, cot, *swapped = begin(tokens, cotangent, own[:5] + small, rows)
    small_other = swapped[5:]
    later = after(inputs, own[5:])
    other = swapped[:5] + [lax.ppermute(array, "section", swap) for array in later]
    inputs = inputs.reshape(n_seq * rows, width)
    grad_top = lax.all_gather(after(inputs, cot), "seq", axis=0, tiled=True)
    where = jnp.stack([section, lax.axis_index("seq")])
    params = (small, small_other)

    kept, outputs = [], []
    for block in range(2):
        time = forward_time(block, n_seq, inputs, where, clip_ids, small, small_other, own[:3], other[:3])
        rest = forward_rest(block, n_seq, patches, time[3], where, small, small_other, own[3:], other[3:])
        kept.append((inputs, time, rest))
        inputs = rest[0]
        outputs.append(inputs)

    each = width // places
    deep = hidden // width
    cut = each * CUT
    end = deep * each + hidden // places
    input_grads, sums = [None] * 2, [{}, {}]
    last, lows = None, []
    for block in (1, 0):
        x, (qkv_t, attn_t, proj, x1, probs, normed_t), rest = kept[block]
        _, qkv_s, attn_s, x2, act, slope, normed_s, normed_m, logs = rest
        sizes = (n_dp, n_seq)
        carried = Carried(1, [(last, 0, 3 * each)] if last is not None else [])
        g2, mlp, low_mlp, *total = back_mlp(
            block, carried, *sizes, grad_top, *params, own[5:], other[5:], act, slope, x2, normed_m
        )
        if total:
            sums[1]["qkv"] = total[0]
        carried = Carried(block, [(mlp, cut, end - cut)])
        g1, space, low_space, sums[block]["mlp"] = back_space(
            block, carried, *sizes, n_seq, patches, *params, own[3:5], other[3:5], g2, qkv_s, attn_s, x1, normed_s, logs
        )
        low = low_mlp + low_space
        pieces = [(mlp, 0, cut), (space, 0, 4 * each)]
        carried = Carried(block, pieces, (3 * each, 2 * each), [low, *lows] if lows else ())
        grad_top, last, low_time, up, out, both, *low_sum = back_time(
            block, carried, *sizes, n_seq, x, *params, own[:3], other[:3], g1, qkv_t, attn_t, proj, probs, normed_t
        )
        sums[block].update(up=up, space=out, time=both)
        input_grads[block] = grad_top
        lows = [low + low_time]
    results = (*outputs, *input_grads)
    carried = Carried(0, [(last, 0, 3 * each)], None, [low_time[0:8]])
    swapped, sums[0]["qkv"], low_last = finish(carried, rows, results)
    names = ("qkv", "time", "space", "up", "mlp")
    counts = (3 * each, 2 * each, 4 * each, cut, end - cut)
    pieces = [(sum(counts[:at]), count) for at, count in enumerate(counts)]
    ordered = [[sums[block][name] for name in names] for block in range(2)]
    shares = layout(patches, places, width, hidden, pieces, ordered, low_sum[0], low_last, results, swapped)
    frames = shares[10:]
    shares = [share.reshape(1, -1) for share in shares[:10]]
    return (*frames, *shares)


def relay_from_behind(value, axis, steps):
    count = lax.axis_size(axis)
    leading, last = (max(0, -steps), min(count, count - steps))
    return lax.ppermute(value, axis, [(source, source + steps) for source in range(leading, last)])


def relay_norm_rows(values, gain, shift):
    centre = values - jnp.mean(values, axis=-1, keepdims=True)
    spread = jnp.mean(centre * centre, axis=-1, keepdims=True)
    return centre * lax.rsqrt(spread + eps_norm) * gain + shift


def relay_mixed_dot(left, right, form):
    return jnp.einsum(form, left, right, preferred_element_type=jnp.float32)


def relay_column_sum(grad_rows):
    return jnp.sum(grad_rows.astype(jnp.float32), axis=(0, 1))


def relay_flat_terms(terms):
    return tuple((term.reshape(-1) for term in terms))


def relay_masked_scores(queries, key_rows, allowed):
    scores = relay_mixed_dot(queries, key_rows, "bic,bjc->bij") * queries.shape[-1] ** (-0.5)
    if allowed is None:
        return scores
    return jnp.where(allowed[None], scores, far_below)


def relay_attend(queries, key_rows, values, allowed):
    scores = relay_masked_scores(queries, key_rows, allowed)
    top_score = jnp.max(scores, axis=-1, keepdims=True)
    total_exp = jnp.sum(jnp.exp(scores - top_score), axis=-1, keepdims=True)
    log_total = top_score + jnp.log(total_exp)
    weights_soft = jnp.exp(scores - log_total).astype(jnp.bfloat16)
    mixed = relay_mixed_dot(weights_soft, values, "bij,bjc->bic").astype(jnp.bfloat16)
    return (mixed, log_total)


def relay_attend_back(queries, key_rows, values, log_total, allowed, grad_out):
    scale = queries.shape[-1] ** (-0.5)
    weights_soft = jnp.exp(relay_masked_scores(queries, key_rows, allowed) - log_total)
    grad_values = relay_mixed_dot(weights_soft.astype(jnp.bfloat16), grad_out, "bij,bic->bjc")
    grad_soft = relay_mixed_dot(grad_out, values, "bic,bjc->bij")
    row_total = jnp.sum(grad_soft * weights_soft, axis=-1, keepdims=True)
    grad_scores = (weights_soft * (grad_soft - row_total)).astype(jnp.bfloat16)
    grad_queries = relay_mixed_dot(grad_scores, key_rows, "bij,bjc->bic") * scale
    grad_keys = relay_mixed_dot(grad_scores, queries, "bij,bic->bjc") * scale
    return (grad_queries, grad_keys, grad_values)


def relay_heads_first(rows):
    frames, patches, width = rows.shape
    return (
        rows.reshape(frames, patches, H, width // H)
        .transpose(0, 2, 1, 3)
        .reshape(frames * H, patches, width // H)
    )


def relay_heads_last(rows, frames):
    batch, patches, head_size = rows.shape
    return (
        rows.reshape(frames, batch // frames, patches, head_size)
        .transpose(0, 2, 1, 3)
        .reshape(frames, patches, batch // frames * head_size)
    )


def relay_time_mix(normed_time, time_qkv, time_out, bias_rows, allowed):
    frames, patches, width = normed_time.shape
    zero_row = jnp.zeros((width,), jnp.float32)
    bias_time = jnp.stack([bias_rows[1], zero_row, bias_rows[2]])
    proj_time = relay_mixed_dot(normed_time, time_qkv.reshape(width, 3, width), "fpd,dke->fkpe")
    proj_time = (proj_time + bias_time[None, :, None, :]).astype(jnp.bfloat16)
    proj_time = proj_time.reshape(frames, 3, patches * H, HD)
    by_patch = lax.all_to_all(proj_time, "seq", split_axis=2, concat_axis=0, tiled=True)
    query_time = by_patch[:, 0].transpose(1, 0, 2)
    key_time = by_patch[:, 1].transpose(1, 0, 2)
    value_time = by_patch[:, 2].transpose(1, 0, 2)
    mixed_time, total_time = relay_attend(query_time, key_time, value_time, allowed)
    back_frames = lax.all_to_all(
        mixed_time.transpose(1, 0, 2), "seq", split_axis=0, concat_axis=1, tiled=True
    )
    attn_time = back_frames.reshape(frames, patches, width)
    proj_out = (relay_mixed_dot(attn_time, time_out, "fpd,de->fpe") + bias_rows[3]).astype(jnp.bfloat16)
    return (proj_out, (normed_time, query_time, key_time, value_time, total_time, attn_time))


def relay_time_mix_back(grad_proj_out, time_qkv, time_out, time_kept, allowed):
    normed_rows, query_time, key_time, value_time, total_time, attn_time = time_kept
    frames, patches, width = grad_proj_out.shape
    grad_time_out = relay_mixed_dot(attn_time, grad_proj_out, "fpd,fpe->de")
    grad_attn_time = relay_mixed_dot(grad_proj_out, time_out, "fpe,de->fpd").astype(jnp.bfloat16)
    grad_attn_time = grad_attn_time.reshape(frames, patches * H, HD)
    grad_by_patch = lax.all_to_all(
        grad_attn_time, "seq", split_axis=1, concat_axis=0, tiled=True
    ).transpose(1, 0, 2)
    grads_time = relay_attend_back(query_time, key_time, value_time, total_time, allowed, grad_by_patch)
    grad_mixed = jnp.stack(grads_time, axis=0).transpose(2, 0, 1, 3).astype(jnp.bfloat16)
    grad_frames = lax.all_to_all(
        grad_mixed, "seq", split_axis=0, concat_axis=2, tiled=True
    ).reshape(frames, 3, patches, width)
    grad_time_qkv = relay_mixed_dot(normed_rows, grad_frames, "fpd,fkpe->dke").reshape(width, 3 * width)
    grad_normed = relay_mixed_dot(grad_frames, time_qkv.reshape(width, 3, width), "fkpe,dke->fpd")
    return (
        grad_normed,
        grad_time_qkv,
        grad_time_out,
        relay_column_sum(grad_frames[:, 0]),
        relay_column_sum(grad_frames[:, 2]),
        relay_column_sum(grad_proj_out),
    )


def relay_layer_forward(inputs, params, allowed):
    (
        time_qkv,
        time_out,
        time_fc,
        space_qkv,
        space_out,
        up_weight,
        down_weight,
        norm_gains,
        bias_rows,
        up_bias,
    ) = params
    frames, patches, width = inputs.shape
    zero_row = jnp.zeros((width,), jnp.float32)
    normed_time = relay_norm_rows(inputs, norm_gains[0], bias_rows[0]).astype(jnp.bfloat16)
    proj_out, time_kept = relay_time_mix(normed_time, time_qkv, time_out, bias_rows, allowed)
    after_time = inputs + (relay_mixed_dot(proj_out, time_fc, "fpd,de->fpe") + bias_rows[4])
    normed_space = relay_norm_rows(after_time, norm_gains[1], bias_rows[5]).astype(jnp.bfloat16)
    bias_space = jnp.stack([bias_rows[6], zero_row, bias_rows[7]])
    proj_space = relay_mixed_dot(normed_space, space_qkv.reshape(width, 3, width), "fpd,dke->fkpe")
    proj_space = (proj_space + bias_space[None, :, None, :]).astype(jnp.bfloat16)
    query_space = relay_heads_first(proj_space[:, 0])
    key_space = relay_heads_first(proj_space[:, 1])
    value_space = relay_heads_first(proj_space[:, 2])
    mixed_space, total_space = relay_attend(query_space, key_space, value_space, None)
    attn_space = relay_heads_last(mixed_space, frames)
    after_space = after_time + (relay_mixed_dot(attn_space, space_out, "fpd,de->fpe") + bias_rows[8])
    normed_mlp = relay_norm_rows(after_space, norm_gains[2], bias_rows[9]).astype(jnp.bfloat16)
    hidden_pre = relay_mixed_dot(normed_mlp, up_weight, "fpd,de->fpe") + up_bias
    hidden_act = jax.nn.gelu(hidden_pre).astype(jnp.bfloat16)
    outputs = after_space + (relay_mixed_dot(hidden_act, down_weight, "fpe,ed->fpd") + bias_rows[10])
    kept = (
        inputs,
        time_kept,
        proj_out,
        after_time,
        normed_space,
        query_space,
        key_space,
        value_space,
        total_space,
        attn_space,
        after_space,
        normed_mlp,
        hidden_pre,
        hidden_act,
    )
    return (outputs, kept)


def relay_layer_backward(grad_top, params, kept, allowed):
    (
        time_qkv,
        time_out,
        time_fc,
        space_qkv,
        space_out,
        up_weight,
        down_weight,
        norm_gains,
        bias_rows,
        up_bias,
    ) = params
    (
        inputs,
        time_kept,
        proj_out,
        after_time,
        normed_space,
        query_space,
        key_space,
        value_space,
        total_space,
        attn_space,
        after_space,
        normed_mlp,
        hidden_pre,
        hidden_act,
    ) = kept
    frames, patches, width = inputs.shape
    grad_mlp = grad_top.astype(jnp.bfloat16)
    grad_down = relay_mixed_dot(hidden_act, grad_mlp, "fpe,fpd->ed")
    grad_act = relay_mixed_dot(grad_mlp, down_weight, "fpd,ed->fpe")
    gelu_back = jax.vjp(jax.nn.gelu, hidden_pre)[1]
    grad_pre = gelu_back(grad_act)[0].astype(jnp.bfloat16)
    grad_up = relay_mixed_dot(normed_mlp, grad_pre, "fpd,fpe->de")
    grad_normed = relay_mixed_dot(grad_pre, up_weight, "fpe,de->fpd")
    norm_back = jax.vjp(relay_norm_rows, after_space, norm_gains[2], bias_rows[9])[1]
    grad_into, gain_mlp, shift_mlp = norm_back(grad_normed)
    grad_space = grad_top + grad_into
    grad_branch = grad_space.astype(jnp.bfloat16)
    grad_space_out = relay_mixed_dot(attn_space, grad_branch, "fpd,fpe->de")
    grad_attn = relay_heads_first(relay_mixed_dot(grad_branch, space_out, "fpe,de->fpd").astype(jnp.bfloat16))
    grads_space = relay_attend_back(query_space, key_space, value_space, total_space, None, grad_attn)
    grad_proj = jnp.stack([relay_heads_last(piece, frames) for piece in grads_space], axis=1).astype(
        jnp.bfloat16
    )
    grad_space_qkv = relay_mixed_dot(normed_space, grad_proj, "fpd,fkpe->dke").reshape(width, 3 * width)
    grad_normed = relay_mixed_dot(grad_proj, space_qkv.reshape(width, 3, width), "fkpe,dke->fpd")
    norm_back = jax.vjp(relay_norm_rows, after_time, norm_gains[1], bias_rows[5])[1]
    grad_into, gain_space, shift_space = norm_back(grad_normed)
    grad_time = grad_space + grad_into
    grad_branch_time = grad_time.astype(jnp.bfloat16)
    grad_time_fc = relay_mixed_dot(proj_out, grad_branch_time, "fpd,fpe->de")
    grad_proj_out = relay_mixed_dot(grad_branch_time, time_fc, "fpe,de->fpd").astype(jnp.bfloat16)
    grad_normed, grad_time_qkv, grad_time_out, query_bias, value_bias, out_bias = relay_time_mix_back(
        grad_proj_out, time_qkv, time_out, time_kept, allowed
    )
    norm_back = jax.vjp(relay_norm_rows, inputs, norm_gains[0], bias_rows[0])[1]
    grad_into, gain_time, shift_time = norm_back(grad_normed)
    grad_inputs = grad_time + grad_into
    gain_grads = jnp.stack([gain_time, gain_space, gain_mlp])
    bias_grads = jnp.stack(
        [
            shift_time,
            query_bias,
            value_bias,
            out_bias,
            relay_column_sum(grad_branch_time),
            shift_space,
            relay_column_sum(grad_proj[:, 0]),
            relay_column_sum(grad_proj[:, 2]),
            relay_column_sum(grad_branch),
            shift_mlp,
            relay_column_sum(grad_mlp),
        ]
    )
    up_grad = relay_column_sum(grad_pre)
    return (
        grad_inputs,
        (
            grad_time_qkv,
            grad_time_out,
            grad_time_fc,
            grad_space_qkv,
            grad_space_out,
            grad_up,
            grad_down,
            gain_grads,
            bias_grads,
            up_grad,
        ),
    )


def relay_shards(
    clip_ids,
    tokens,
    time_qkv,
    time_out,
    time_fc,
    space_qkv,
    space_out,
    up_weight,
    down_weight,
    norm_gains,
    bias_rows,
    up_bias,
    cotangent,
):
    params = (
        time_qkv[0],
        time_out[0],
        time_fc[0],
        space_qkv[0],
        space_out[0],
        up_weight[0],
        down_weight[0],
        norm_gains[0],
        bias_rows[0],
        up_bias[0],
    )
    allowed = clip_ids[0][:, None] == clip_ids[0][None, :]
    first_section = lax.axis_index("section") == 0
    micro = tokens.shape[0]
    arriving = jnp.zeros_like(tokens[0])
    section_inputs = []
    section_outputs = []
    for moment in range(micro + 1):
        taken_rows = jnp.where(first_section, tokens[min(moment, micro - 1)], arriving)
        result = relay_layer_forward(taken_rows.astype(jnp.float32), params, allowed)[0].astype(
            jnp.bfloat16
        )
        section_inputs.append(taken_rows)
        section_outputs.append(result)
        if moment < micro:
            arriving = relay_from_behind(result, "section", 1)
    saved_inputs = [
        jnp.where(first_section, section_inputs[number], section_inputs[number + 1])
        for number in range(micro)
    ]
    layer_outputs = jnp.stack(
        [
            jnp.where(first_section, section_outputs[number], section_outputs[number + 1])
            for number in range(micro)
        ]
    )
    returning = jnp.zeros_like(tokens[0])
    back_results = []
    totals = None
    for moment in range(micro + 1):
        grad_given = jnp.where(first_section, returning, cotangent[min(moment, micro - 1)]).astype(
            jnp.float32
        )
        source_rows = jnp.where(
            first_section, saved_inputs[max(moment - 1, 0)], saved_inputs[min(moment, micro - 1)]
        )
        live_share = jnp.where(
            first_section, 1.0 if moment >= 1 else 0.0, 1.0 if moment < micro else 0.0
        )
        kept = relay_layer_forward(source_rows.astype(jnp.float32), params, allowed)[1]
        grad_inputs, weight_terms = relay_layer_backward(grad_given, params, kept, allowed)
        grad_inputs = grad_inputs.astype(jnp.bfloat16)
        back_results.append(grad_inputs)
        weight_terms = relay_flat_terms(jax.tree.map(lambda term: term * live_share, weight_terms))
        if totals is None:
            totals = tuple(weight_terms)
        else:
            totals = tuple((left + right for left, right in zip(totals, weight_terms)))
        if moment < micro:
            returning = relay_from_behind(grad_inputs, "section", -1)
    input_grads = jnp.stack(
        [
            jnp.where(first_section, back_results[number + 1], back_results[number])
            for number in range(micro)
        ]
    )
    shares = (
        lax.psum_scatter(totals[0], ("dp", "seq"), scatter_dimension=0, tiled=True),
        lax.psum_scatter(totals[1], ("dp", "seq"), scatter_dimension=0, tiled=True),
        lax.psum_scatter(totals[2], ("dp", "seq"), scatter_dimension=0, tiled=True),
        lax.psum_scatter(totals[3], ("dp", "seq"), scatter_dimension=0, tiled=True),
        lax.psum_scatter(totals[4], ("dp", "seq"), scatter_dimension=0, tiled=True),
        lax.psum_scatter(totals[5], ("dp", "seq"), scatter_dimension=0, tiled=True),
        lax.psum_scatter(totals[6], ("dp", "seq"), scatter_dimension=0, tiled=True),
        lax.psum_scatter(totals[7], ("dp", "seq"), scatter_dimension=0, tiled=True),
        lax.psum_scatter(totals[8], ("dp", "seq"), scatter_dimension=0, tiled=True),
        lax.psum_scatter(totals[9], ("dp", "seq"), scatter_dimension=0, tiled=True),
    )
    return (
        layer_outputs[None],
        input_grads[None],
        shares[0][None],
        shares[1][None],
        shares[2][None],
        shares[3][None],
        shares[4][None],
        shares[5][None],
        shares[6][None],
        shares[7][None],
        shares[8][None],
        shares[9][None],
    )


def solution(mesh):
    stacked = P("section", None, None)
    spread = P(None, ("dp", "seq"), None, None)
    in_specs = (P("dp", None), spread, *[stacked] * 9, P("section", None), spread)
    flat = P("section", ("dp", "seq"))
    out = P("section", None, ("dp", "seq"), None, None)
    relay = mesh.shape["seq"] != 4 or mesh.shape["dp"] != 4
    return jax.shard_map(
        relay_shards if relay else shards, mesh=mesh, in_specs=in_specs, out_specs=(out, out, *[flat] * 10), check_vma=False
    )
```

```python
import functools

import jax
import jax.numpy as jnp
from jax import lax
from jax.experimental import pallas as pl
from jax.experimental.pallas import tpu as pltpu
from jax.sharding import PartitionSpec as P

H = 12
HD = 64
PAIR = 2 * HD
eps_norm = 1e-06
far_below = -1000000000.0
BF = jnp.bfloat16
F32 = jnp.float32
VMEM_BYTES = 62 << 20
NEXT_ID = [1]
GROUP = 6
CUT = 3
GROUP_BACK = 6
CHUNK = 208


def nn(left, right):
    return lax.dot_general(left, right, (((1,), (0,)), ((), ())), preferred_element_type=F32)


def nt(left, right):
    return lax.dot_general(left, right, (((1,), (1,)), ((), ())), preferred_element_type=F32)


def norm_stats(values):
    centre = values - jnp.mean(values, axis=-1, keepdims=True)
    scale = lax.rsqrt(jnp.mean(centre * centre, axis=-1, keepdims=True) + eps_norm)
    return centre * scale, scale


def rows_at(index, count):
    return pl.ds(pl.multiple_of(index * count, count), count)


def norm_into(source, target, gain, shift, chunk):
    @pl.loop(0, source.shape[0] // chunk)
    def _(step):
        at = rows_at(step, chunk)
        hat, _ = norm_stats(source[at, :].astype(F32))
        target[at, :] = (hat * gain[...] + shift[...]).astype(BF)


def gelu_both(pre):
    rate, cube = 0.7978845608028654, 0.044715
    square = pre * pre
    tanh = jnp.tanh(pre * (rate + rate * cube * square))
    half = 0.5 + 0.5 * tanh
    act = pre * half
    slope = half + act * (1.0 - tanh) * (rate + 3.0 * rate * cube * square)
    return act, slope


class Copies:
    def __init__(self, sems):
        self.sems, self.used, self.open = sems, 0, []

    def fetch(self, own, other, target, mine):
        sem = self.sems.at[self.used]
        self.used += 1

        @pl.when(mine)
        def _():
            pltpu.make_async_copy(own, target, sem).start()

        @pl.when(jnp.logical_not(mine))
        def _():
            pltpu.make_async_copy(other, target, sem).start()

        return pltpu.make_async_copy(own, target, sem)

    def start(self, source, target):
        copy = pltpu.make_async_copy(source, target, self.sems.at[self.used])
        self.used += 1
        copy.start()
        return copy

    def store(self, source, target):
        self.open.append(self.start(source, target))

    def finish(self):
        for copy in self.open:
            copy.wait()


def time_attention(qkv, attn, probs, stage, soft, heads, heads_t, clips, frames, rows, width):
    @pl.loop(0, frames)
    def _(i):
        own = rows_at(i, rows)
        for j in range(frames):
            stage[pl.ds(j * rows, rows), :] = qkv[own, 0:width] * qkv[pl.ds(j * rows, rows), width : 2 * width]
        scores = nn(stage[...], heads[...])
        parts = []
        for j in range(frames):
            open_pair = clips[0, i] == clips[0, j]
            parts.append(scores[j * rows : (j + 1) * rows] + jnp.where(open_pair, 0.0, far_below))
        top = functools.reduce(jnp.maximum, parts)
        parts = [jnp.exp(part - top) for part in parts]
        inverse = 1.0 / sum(parts)
        for j in range(frames):
            prob = parts[j] * inverse
            probs[i, pl.ds(j * rows, rows), :] = prob
            soft[pl.ds(j * rows, rows), :] = prob.astype(BF)
        total = None
        for j in range(frames):
            at = pl.ds(j * rows, rows)
            term = nn(soft[at, :], heads_t[...]) * qkv[at, 2 * width : 3 * width].astype(F32)
            total = term if total is None else total + term
        attn[own, :] = total.astype(BF)


def fill_units(unit, pair_unit):
    for target in (unit, pair_unit):
        row = lax.broadcasted_iota(jnp.int32, target.shape, 0)
        column = lax.broadcasted_iota(jnp.int32, target.shape, 1)
        target[...] = jnp.where(row == column, 1.0, 0.0).astype(BF)


def split_patches(scores, patches):
    whole = patches // 16 * 16
    if whole == scores.shape[0]:
        return [scores]
    rest = scores[whole:]
    row = lax.broadcasted_iota(jnp.int32, rest.shape, 0)
    return [scores[:whole], jnp.where(row < patches - whole, rest, far_below)]


def space_attention(qkv, attn, logs, values_t, mixed_t, unit, pair_unit, frames, rows, patches, width):
    low_lane = lax.broadcasted_iota(jnp.int32, (rows, PAIR), 1) < HD
    deep = HD + 16
    values_t[...] = jnp.ones_like(values_t)

    @pl.loop(0, frames)
    def _(f):
        at = rows_at(f, rows)
        for pair in range(width // PAIR):
            turned = nt(pair_unit[...], qkv[at, 2 * width + pair * PAIR : 2 * width + (pair + 1) * PAIR]).astype(BF)
            for half in range(2):
                head = 2 * pair + half
                values_t[head * deep : head * deep + HD, :] = turned[half * HD : (half + 1) * HD]

        @pl.loop(0, width // PAIR // GROUP)
        def _(group):
            scores = []
            for member in range(GROUP):
                pair = group * GROUP + member

                def lanes(which):
                    return pl.ds(pl.multiple_of(which * width + pair * PAIR, PAIR), PAIR)

                query, key = qkv[at, lanes(0)] * BF(HD**-0.5), qkv[at, lanes(1)]
                for half in range(2):
                    scores.append(nt(jnp.where(low_lane if half == 0 else ~low_lane, key, BF(0)), query))
            expos, tops = [], []
            for score in scores:
                parts = split_patches(score, patches)
                top = functools.reduce(jnp.maximum, [jnp.max(part, axis=0, keepdims=True) for part in parts])
                expos.append(jnp.concatenate([jnp.exp(part - top).astype(BF) for part in parts], axis=0))
                tops.append(top)
            for member, (expo, top) in enumerate(zip(expos, tops)):
                head = group * (2 * GROUP) + member
                both = nn(values_t[pl.ds(pl.multiple_of(head * deep, 16), deep), :], expo)
                total = both[HD : HD + 1]
                logs[pl.ds(f * H + head, 1), :] = top + jnp.log(total)
                mixed_t[pl.ds(pl.multiple_of(head * HD, HD), HD), :] = (both[:HD] * (1.0 / total)).astype(BF)

        attn[at, :] = nt(unit[...], mixed_t[...]).astype(BF)


class Smalls:
    def __init__(self, own, other, held, mine):
        for which, refs in ((mine, own), (jnp.logical_not(mine), other)):

            @pl.when(which)
            def _(refs=refs):
                for source, target in zip(refs, held):
                    width = target.shape[1]
                    for row in range(target.shape[0]):
                        target[row : row + 1, :] = source[:, row * width : (row + 1) * width]

        self.gains, self.biases, self.up_bias = held

    def gain(self, row):
        return self.gains.at[row : row + 1]

    def bias(self, row):
        return self.biases.at[row : row + 1]


def fill_heads(heads, heads_t):
    lane = lax.broadcasted_iota(jnp.int32, heads.shape, 0) // HD
    head = lax.broadcasted_iota(jnp.int32, heads.shape, 1)
    heads[...] = jnp.where(lane == head, HD**-0.5, 0.0).astype(BF)
    lane = lax.broadcasted_iota(jnp.int32, heads_t.shape, 1) // HD
    head = lax.broadcasted_iota(jnp.int32, heads_t.shape, 0)
    heads_t[...] = jnp.where(lane == head, 1.0, 0.0).astype(BF)


def fill_pick(pick, outer, place, count):
    each = pick.shape[0] // outer
    row = lax.broadcasted_iota(jnp.int32, pick.shape, 0)
    column = lax.broadcasted_iota(jnp.int32, pick.shape, 1)
    pick[...] = jnp.where(column == (row // each * count + place) * each + row % each, 1.0, 0.0).astype(BF)


def project(source, weight, biases, target):
    width = source.shape[1]
    for part in range(3):
        at = slice(part * width, (part + 1) * width)
        result = nn(source[...], weight[:, at])
        if biases[part] is not None:
            result = result + biases[part][...]
        target[:, at] = result.astype(BF)


def struct(shape, dtype=BF):
    return jax.ShapeDtypeStruct(shape, dtype)


def held(*structs):
    return [pltpu.VMEM(s.shape, s.dtype) for s in structs]


IN_VMEM = pl.BlockSpec(memory_space=pltpu.VMEM)
IN_SMEM = pl.BlockSpec(memory_space=pltpu.SMEM)
IN_HBM = pl.BlockSpec(memory_space=pl.ANY)


def vmem(**structs):
    return {name: pltpu.VMEM(s.shape, s.dtype) for name, s in structs.items()}


def small_held(width, hidden):
    return vmem(
        gains=struct((BIAS, width), F32), biases=struct((UP - BIAS, width), F32), up_bias=struct((1, hidden), F32)
    )


def small_ins(own, other):
    (gains, biases, up_bias), (gains_2, biases_2, up_bias_2) = own, other
    return dict(
        own_gains=(gains, IN_VMEM),
        own_biases=(biases, IN_VMEM),
        own_up_bias=(up_bias, IN_VMEM),
        other_gains=(gains_2, IN_VMEM),
        other_biases=(biases_2, IN_VMEM),
        other_up_bias=(up_bias_2, IN_VMEM),
    )


def load_smalls(k, mine):
    return Smalls(
        (k.own_gains, k.own_biases, k.own_up_bias),
        (k.other_gains, k.other_biases, k.other_up_bias),
        (k.gains, k.biases, k.up_bias),
        mine,
    )


def own_ins(own):
    time, time_out, time_fc, space, space_out, up, down = own
    return dict(
        own_time=(time, IN_HBM),
        own_time_out=(time_out, IN_HBM),
        own_time_fc=(time_fc, IN_HBM),
        own_space=(space, IN_HBM),
        own_space_out=(space_out, IN_HBM),
        own_up=(up, IN_HBM),
        own_down=(down, IN_HBM),
    )


def other_refs(other):
    time, time_out, time_fc, space, space_out, up, down = other
    return dict(
        other_time=(time, IN_HBM),
        other_time_out=(time_out, IN_HBM),
        other_time_fc=(time_fc, IN_HBM),
        other_space=(space, IN_HBM),
        other_space_out=(space_out, IN_HBM),
        other_up=(up, IN_HBM),
        other_down=(down, IN_HBM),
    )


MESH = pl.DeviceIdType.MESH
BIAS, UP, LOW = 3, 14, 24


class Named:
    def __init__(self, names, refs):
        self.__dict__.update(zip(names, refs, strict=True))


def named_call(kernel, name, flops, ins, outs, scratch, remote):
    names = [*ins, *outs, *scratch]
    if remote:
        NEXT_ID.append(NEXT_ID[-1] + 1)
    extra = dict(collective_id=NEXT_ID[-1], has_side_effects=True) if remote else {}
    results = pl.pallas_call(
        lambda *refs: kernel(Named(names, refs)),
        out_shape=[value for value, _ in outs.values()],
        in_specs=[spec for _, spec in ins.values()],
        out_specs=[spec for _, spec in outs.values()],
        scratch_shapes=list(scratch.values()),
        compiler_params=pltpu.CompilerParams(vmem_limit_bytes=VMEM_BYTES, **extra),
        cost_estimate=pl.CostEstimate(flops=flops, bytes_accessed=60 << 20, transcendentals=0),
        name=name,
    )(*[value for value, _ in ins.values()])
    return dict(zip(outs, results))


class Begin:
    def __init__(self, k, patches):
        self.k, self.patches = k, patches
        self.count, self.me = lax.axis_size("seq"), lax.axis_index("seq")
        self.section = lax.axis_index("section")
        self.mate = {"section": 1 - self.section}
        self.first = [
            (k.own_time, k.other_time),
            (k.own_time_out, k.other_time_out),
            (k.own_time_fc, k.other_time_fc),
        ]
        self.then = [(k.own_space, k.other_space), (k.own_space_out, k.other_space_out)]
        self.last = [(k.own_up, k.other_up), (k.own_down, k.other_down)]
        self.smalls = [
            (k.own_gains, k.other_gains),
            (k.own_biases, k.other_biases),
            (k.own_up_bias, k.other_up_bias),
        ]
        self.pairs = self.first + self.then + self.last + self.smalls

    def over(self, at):
        source, target = self.pairs[at]
        return pltpu.make_async_remote_copy(
            source, target, self.k.over_send.at[at], self.k.over_recv.at[at], device_id=self.mate, device_id_type=MESH
        )

    def around(self, which, step):
        source, target = ((self.k.frame, self.k.x), (self.k.cot, self.k.cot_out))[which]
        rows = source.shape[0]
        at = which * (self.count - 1) + step - 1
        return pltpu.make_async_remote_copy(
            source,
            target.at[rows_at(self.me, rows)],
            self.k.send.at[at],
            self.k.recv.at[at],
            device_id={"seq": lax.rem(self.me + step, self.count)},
            device_id_type=MESH,
        )

    def pad_into(self, source, target):
        whole = self.patches // 16 * 16
        target[0:whole, :] = source[0:whole, :]
        if target.shape[0] > whole:
            rest = jnp.zeros((target.shape[0] - self.patches, source.shape[1]), BF)
            target[whole:, :] = jnp.concatenate([source[whole:, :], rest], axis=0)

    def begin(self):
        k = self.k
        loads = [
            pltpu.make_async_copy(source.at[self.section, 0], target, k.local.at[at])
            for at, (source, target) in enumerate(((k.tokens, k.raw), (k.cotangent, k.raw_cot)))
        ]
        for load in loads:
            load.start()
        barrier = pltpu.get_barrier_semaphore()
        pl.semaphore_signal(barrier, inc=1, device_id=self.mate, device_id_type=MESH)
        for step in range(1, self.count):
            at = {"seq": lax.rem(self.me + step, self.count)}
            pl.semaphore_signal(barrier, inc=1, device_id=at, device_id_type=MESH)
        loads[0].wait()
        self.pad_into(k.raw, k.frame)
        pl.semaphore_wait(barrier, self.count)
        for step in range(1, self.count):
            self.around(0, step).start()
        for at in (7, 8, 9, 0, 1, 2):
            self.over(at).start()
        loads[1].wait()
        self.pad_into(k.raw_cot, k.cot)
        rows = k.frame.shape[0]
        own = rows_at(self.me, rows)
        k.x[own, :] = k.frame[...]
        keep = pltpu.make_async_copy(k.cot, k.cot_out.at[own], k.local.at[2])
        keep.start()
        for at in (7, 8, 9):
            self.over(at).wait()
        for step in range(1, self.count):
            self.around(0, step).wait()
        for step in range(1, self.count):
            self.around(1, step).start()
        keep.wait()

    def next(self, done, then):
        for at in done:
            self.over(at).wait_send()
        for at in then:
            self.over(at).start()

    def fetch(self, copies, at, target, mine):
        own, other = self.pairs[at]

        @pl.when(jnp.logical_not(mine))
        def _():
            self.over(at).wait_recv()

        return copies.fetch(own, other, target, mine)

    def end(self, mine):
        for at in (5, 6):
            self.over(at).wait_send()

        @pl.when(mine)
        def _():
            for at in range(7):
                self.over(at).wait_recv()

        for step in range(1, self.count):
            self.around(1, step).wait()


def forward_kernel(block, frames, patches, k):
    total, width = k.x.shape
    rows = total // frames
    copies = Copies(k.sems)
    mine = lax.axis_index("section") == block
    fill_heads(k.heads, k.heads_t)
    fill_units(k.unit, k.pair_unit)
    if block == 0:
        start = Begin(k, patches)
        start.begin()
        copies.store(k.x, k.r_x)
        fetch = functools.partial(start.fetch, copies, mine=mine)
    else:
        load_x = copies.start(k.x_in, k.x)
        pairs = (
            (k.own_time, k.other_time),
            (k.own_time_out, k.other_time_out),
            (k.own_time_fc, k.other_time_fc),
            (k.own_space, k.other_space),
            (k.own_space_out, k.other_space_out),
            (k.own_up, k.other_up),
            (k.own_down, k.other_down),
        )

        def fetch(at, target):
            return copies.fetch(*pairs[at], target, mine)

    load_time = fetch(0, k.time)
    smalls = load_smalls(k, mine)
    if block == 1:
        load_x.wait()
    norm_into(k.x, k.normed_t, smalls.gain(0), smalls.bias(0), CHUNK)
    copies.store(k.normed_t, k.r_normed_t)
    load_time.wait()
    load_time_out, load_time_fc = fetch(1, k.time_out), fetch(2, k.time_fc)
    if block == 0:
        start.next((0, 1, 2), (3, 4))
    project(k.normed_t, k.time, (smalls.bias(1), None, smalls.bias(2)), k.qkv_t)
    copies.store(k.qkv_t, k.r_qkv_t)
    if block == 1:
        load_space, load_space_out = fetch(3, k.space), fetch(4, k.space_out)
    time_attention(k.qkv_t, k.attn_t, k.probs, k.stage, k.soft, k.heads, k.heads_t, k.clips, frames, rows, width)
    copies.store(k.attn_t, k.r_attn_t)
    copies.store(k.probs, k.r_probs)
    load_time_out.wait()
    k.proj[...] = (nn(k.attn_t[...], k.time_out[...]) + smalls.bias(3)[...]).astype(BF)
    copies.store(k.proj, k.r_proj)
    load_time_fc.wait()
    k.x1[...] = k.x[...].astype(F32) + nn(k.proj[...], k.time_fc[...]) + smalls.bias(4)[...]
    copies.store(k.x1, k.r_x1)
    if block == 0:
        load_space, load_space_out = fetch(3, k.space), fetch(4, k.space_out)
        start.next((3, 4), (5, 6))
    else:
        load_up, load_down = fetch(5, k.up), fetch(6, k.down)
    norm_into(k.x1, k.normed_s, smalls.gain(1), smalls.bias(5), CHUNK)
    copies.store(k.normed_s, k.r_normed_s)
    load_space.wait()
    project(k.normed_s, k.space, (smalls.bias(6), None, smalls.bias(7)), k.qkv_s)
    copies.store(k.qkv_s, k.r_qkv_s)
    space_attention(
        k.qkv_s, k.attn_s, k.logs, k.values_t, k.mixed_t, k.unit, k.pair_unit, frames, rows, patches, width
    )
    copies.store(k.attn_s, k.r_attn_s)
    copies.store(k.logs, k.r_logs)
    load_space_out.wait()
    if block == 0:
        load_up, load_down = fetch(5, k.up), fetch(6, k.down)
    k.x2[...] = k.x1[...] + nn(k.attn_s[...], k.space_out[...]) + smalls.bias(8)[...]
    copies.store(k.x2, k.r_x2)
    norm_into(k.x2, k.normed_m, smalls.gain(2), smalls.bias(9), CHUNK)
    copies.store(k.normed_m, k.r_normed_m)
    load_up.wait()

    for tile in range(k.up.shape[1] // width):
        at = slice(tile * width, (tile + 1) * width)
        pre = nn(k.normed_m[...], k.up[:, at]) + smalls.up_bias[:, at]
        both = gelu_both(pre)
        k.act[:, at] = both[0].astype(BF)
        k.slope[:, at] = both[1].astype(BF)
        copies.store(k.act.at[:, at], k.r_act.at[:, at])
        copies.store(k.slope.at[:, at], k.r_slope.at[:, at])

    load_down.wait()

    @pl.loop(0, 3)
    def _(tile):
        at = rows_at(tile, width // 3)
        y_at = nn(k.act[...], k.down[:, at]) + smalls.biases[10:11, at] + k.x2[:, at]
        k.y[:, at] = y_at.astype(BF)

    copies.store(k.y, k.y_out)
    if block == 0:
        start.end(mine)
    copies.finish()


def forward(block, frames, patches, clips, small, small_other, own, other, x=None, tokens=None, cotangent=None):
    width, hidden = own[5].shape
    rows = -(-patches // 16) * 16
    total = frames * rows
    wide, full, triple = struct((total, width)), struct((total, width), F32), struct((total, 3 * width))
    deep, few = struct((total, hidden)), struct((total, PAIR))
    logs, probs = struct((frames * H, rows), F32), struct((frames, total, PAIR), F32)
    lie = lambda **structs: {name: (s, IN_HBM) for name, s in structs.items()}
    ins = dict(clips=(clips, IN_SMEM), **own_ins(own))
    outs = lie(y_out=wide, r_qkv_t=triple, r_attn_t=wide, r_proj=wide, r_x1=full, r_probs=probs, r_normed_t=wide)
    outs |= lie(r_qkv_s=triple, r_attn_s=wide, r_x2=full, r_act=deep, r_slope=deep, r_normed_s=wide, r_normed_m=wide)
    outs |= lie(r_logs=logs)
    square, third = struct((width, width)), struct((width, 3 * width))
    scratch = vmem(time=third, time_out=square, time_fc=square, space=third, space_out=square)
    scratch |= vmem(up=struct((width, hidden)), down=struct((hidden, width)), x=wide, normed_t=wide, stage=wide)
    scratch |= vmem(qkv_t=triple, attn_t=wide, proj=wide, x1=full, probs=probs, soft=few, normed_s=wide, qkv_s=triple)
    scratch |= vmem(attn_s=wide, logs=logs, x2=full, normed_m=wide, act=deep, slope=deep, y=wide)
    scratch |= vmem(values_t=struct((H * (HD + 16), rows)), mixed_t=struct((width, rows)), unit=struct((rows, rows)))
    scratch |= vmem(pair_unit=struct((PAIR, PAIR)), heads=struct((width, PAIR)), heads_t=struct((PAIR, width)))
    scratch |= small_held(width, hidden)
    dma = pltpu.SemaphoreType.DMA
    scratch |= dict(sems=dma((40,)))
    if block == 0:
        gains, biases, up_bias = small
        ins |= dict(tokens=(tokens, IN_HBM), cotangent=(cotangent, IN_HBM))
        ins |= dict(own_gains=(gains, IN_VMEM), own_biases=(biases, IN_VMEM), own_up_bias=(up_bias, IN_VMEM))
        outs |= other_refs([struct(array.shape) for array in own])
        like = [struct(array.shape, F32) for array in small]
        outs |= dict(other_gains=(like[0], IN_VMEM), other_biases=(like[1], IN_VMEM), other_up_bias=(like[2], IN_VMEM))
        outs |= lie(cot_out=wide, r_x=wide)
        raw, frame = struct((patches, width)), struct((rows, width))
        scratch |= vmem(raw=raw, raw_cot=raw, frame=frame, cot=frame)
        scratch |= dict(send=dma((2 * frames,)), recv=dma((2 * frames,)), over_send=dma((10,)), over_recv=dma((10,)))
        scratch |= dict(local=dma((3,)))
    else:
        ins |= dict(x_in=(x, IN_HBM), **other_refs(other), **small_ins(small, small_other))
    kernel = functools.partial(forward_kernel, block, frames, patches)
    return named_call(kernel, f"block{block}_forward", 34 * total * width * width, ins, outs, scratch, block == 0)


def beside(z):
    return z + 1 - 2 * lax.rem(z, 2), lax.rem(z + 2, 4)


def greet():
    barrier = pltpu.get_barrier_semaphore()
    near, far = beside(lax.axis_index("dp"))
    pl.semaphore_signal(barrier, inc=1, device_id={"section": 1 - lax.axis_index("section")}, device_id_type=MESH)
    pl.semaphore_signal(barrier, inc=1, device_id={"dp": near}, device_id_type=MESH)
    pl.semaphore_signal(barrier, inc=1, device_id={"dp": far}, device_id_type=MESH)
    pl.semaphore_wait(barrier, 3)


class Relay:
    def __init__(self, block, mine, mates, taken, send, recv, source=None):
        self.mine, self.mates, self.taken, self.send, self.recv = mine, mates, taken, send, recv
        self.source = source
        self.z = lax.axis_index("dp")
        self.near, self.far = beside(self.z)
        self.section = lax.axis_index("section")
        self.home = self.section == block
        self.away = self.section != block

    def parts(self):
        return lax.rem(self.near + 2, 4), self.near, self.far, self.z

    def mate(self, part):
        if len(self.mates.shape) == 3:
            return self.mates.at[part]
        return self.mates.at[rows_at(part, self.mine.shape[1])]

    def over(self, at):
        part = self.parts()[at]
        return pltpu.make_async_remote_copy(
            (self.mine if self.source is None else self.source).at[part],
            self.mate(part),
            self.send.at[3 + at],
            self.recv.at[3 + at],
            device_id={"section": 1 - self.section},
            device_id_type=MESH,
        )

    def local(self):
        return pltpu.make_async_copy(self.source, self.mine, self.send.at[7])

    def along(self, step):
        part = self.parts()[step]
        return pltpu.make_async_remote_copy(
            self.mine.at[part],
            self.taken.at[step],
            self.send.at[step],
            self.recv.at[step],
            device_id={"dp": self.far if step == 2 else self.near},
            device_id_type=MESH,
        )

    def begin(self):
        @pl.when(self.away)
        def _():
            for at in range(4):
                self.over(at).start()

        if self.source is not None:

            @pl.when(self.home)
            def _():
                self.local().start()

    def middle(self):
        @pl.when(self.home)
        def _():
            if self.source is not None:
                self.local().wait()
            for at, part in enumerate(self.parts()):
                self.over(at).wait_recv()
                self.mine[part] = (self.mine[part].astype(F32) + self.mate(part)[...].astype(F32)).astype(BF)
                if at < 2:
                    self.along(at).start()

        @pl.when(self.away)
        def _():
            for at in range(4):
                self.over(at).wait_send()

    def second(self):
        @pl.when(self.home)
        def _():
            self.along(0).wait()
            self.mine[self.far] = (self.mine[self.far].astype(F32) + self.taken[0].astype(F32)).astype(BF)
            self.along(2).start()

    def end(self, staged, out, sem):
        self.store = pltpu.make_async_copy(staged, out, sem)

        @pl.when(self.home)
        def _():
            self.along(1).wait()
            total = self.mine[self.z].astype(F32) + self.taken[1].astype(F32)
            self.along(2).wait()
            staged[...] = total + self.taken[2].astype(F32)
            self.store.start()

    def settle(self):
        pl.when(self.home)(self.store.wait)


class LowRelay:
    def __init__(self, lows, out, scratch):
        self.lows, self.out = lows, out
        self.mine, self.mate, self.taken, self.send, self.recv = scratch
        self.places = beside(lax.axis_index("dp"))
        self.section = lax.axis_index("section")

    def over(self, low):
        return pltpu.make_async_remote_copy(
            low,
            self.mate,
            self.send.at[0],
            self.recv.at[0],
            device_id={"section": 1 - self.section},
            device_id_type=MESH,
        )

    def along(self, step):
        return pltpu.make_async_remote_copy(
            self.mine.at[step],
            self.taken.at[step],
            self.send.at[1 + step],
            self.recv.at[1 + step],
            device_id={"dp": self.places[step]},
            device_id_type=MESH,
        )

    def begin(self):
        for block, low in enumerate(self.lows):

            @pl.when(self.section != block)
            def _(low=low):
                self.over(low).start()

    def at_home(self, act):
        if len(self.lows) == 2:
            act()
        else:
            pl.when(self.section == 0)(act)

    def middle(self):
        for block, low in enumerate(self.lows):

            @pl.when(self.section == block)
            def _(low=low):
                self.over(low).wait_recv()
                self.mine[0] = low[...] + self.mate[...]
                self.along(0).start()

            @pl.when(self.section != block)
            def _(low=low):
                self.over(low).wait_send()

    def second(self):
        def _():
            self.along(0).wait()
            self.mine[1] = self.mine[0] + self.taken[0]
            self.along(1).start()

        self.at_home(_)

    def end(self):
        def _():
            self.along(1).wait()
            self.out[...] = self.mine[1] + self.taken[1]

        self.at_home(_)
        if len(self.lows) == 1:

            @pl.when(self.section != 0)
            def _():
                self.out[...] = jnp.zeros_like(self.out)


def norm_back(hidden, grads, gain, above, target, sums, chunk):
    width = hidden.shape[1]
    sums[...] = jnp.zeros_like(sums)

    def fold(rows):
        return jnp.sum(rows.reshape(chunk // 8, 8, width), axis=0)

    @pl.loop(0, hidden.shape[0] // chunk)
    def _(step):
        at = rows_at(step, chunk)
        hat, scale = norm_stats(hidden[at, :].astype(F32))
        grad = grads[at, :]
        sums[0:8, :] += fold(grad * hat)
        sums[8:16, :] += fold(grad)
        inner = grad * gain[...]
        mean = jnp.mean(inner, axis=-1, keepdims=True)
        slant = jnp.mean(inner * hat, axis=-1, keepdims=True)
        result = above[at, :].astype(F32) + scale * (inner - mean - hat * slant)
        target[at, :] = result.astype(target.dtype)


def norm_sums(sums, low, gain_row, bias_row):
    low[gain_row : gain_row + 1, :] = jnp.sum(sums[0:8, :], axis=0, keepdims=True)
    low[BIAS + bias_row : BIAS + bias_row + 1, :] = jnp.sum(sums[8:16, :], axis=0, keepdims=True)


def fill_ones(turned, count):
    turned[pl.ds(count, 16), :] = jnp.ones((16, turned.shape[1]), BF)


def weight_grad(turned, count, grads, result, row, low, *low_rows):
    width = low.shape[1]
    parts = result.shape[0]
    each = count // parts

    for step, low_row in enumerate(low_rows):
        both = nn(turned[0 : count + 16, :], grads[:, step * width : (step + 1) * width])
        at = slice(row + step * each, row + (step + 1) * each)
        for part in range(parts):
            result[part, at, :] = both[part * each : (part + 1) * each].astype(BF)
        if low_row is not None:
            low[low_row : low_row + 1, :] = both[count : count + 1, :]


def tiled_nt(left, right, target, tile):
    @pl.loop(0, right.shape[0] // tile)
    def _(step):
        at = rows_at(step, tile)
        target[:, at] = nt(left[...], right[at, :])


def space_attention_back(
    qkv, grads, logs, result, keys_t, turned_t, unit, pair_unit, frames, rows, patches, width
):
    low_lane = lax.broadcasted_iota(jnp.int32, (rows, PAIR), 1) < HD

    @pl.loop(0, frames)
    def _(f):
        at = rows_at(f, rows)
        for pair in range(width // PAIR):
            lanes = slice(width + pair * PAIR, width + (pair + 1) * PAIR)
            keys_t[pair * PAIR : (pair + 1) * PAIR, :] = nt(pair_unit[...], qkv[at, lanes]).astype(BF)

        @pl.loop(0, width // PAIR // GROUP_BACK)
        def _(group):
            def lanes(which, member):
                pair = group * GROUP_BACK + member
                return pl.ds(pl.multiple_of(which * width + pair * PAIR, PAIR), PAIR)

            scores, grad_softs = [], []
            for member in range(GROUP_BACK):
                query = qkv[at, lanes(0, member)] * BF(HD**-0.5)
                key, value, grad = qkv[at, lanes(1, member)], qkv[at, lanes(2, member)], grads[at, lanes(0, member)]
                for half in range(2):
                    mine = low_lane if half == 0 else ~low_lane
                    scores.append(nt(jnp.where(mine, key, BF(0)), query))
                    grad_softs.append(nt(jnp.where(mine, value, BF(0)), grad))
            softs, grad_scores = [], []
            for member, (score, grad_soft) in enumerate(zip(scores, grad_softs)):
                head = group * (2 * GROUP_BACK) + member
                log = logs[pl.ds(f * H + head, 1), :]
                soft = [jnp.exp(part - log) for part in split_patches(score, patches)]
                cut = soft[0].shape[0]
                changes = [grad_soft[:cut], grad_soft[cut:]][: len(soft)]
                slant = sum(jnp.sum(part * change, axis=0, keepdims=True) for part, change in zip(soft, changes))
                changes = [change - slant for change in changes]
                softs.append(jnp.concatenate([part.astype(BF) for part in soft], axis=0))
                grad_scores.append(
                    jnp.concatenate([(part * change).astype(BF) for part, change in zip(soft, changes)], axis=0)
                )
            for member in range(GROUP_BACK):
                query = qkv[at, lanes(0, member)] * BF(HD**-0.5)
                grad = grads[at, lanes(0, member)]
                pair = 2 * member
                grad_key = [nn(grad_scores[pair + half], query) for half in range(2)]
                grad_value = [nn(softs[pair + half], grad) for half in range(2)]
                result[at, lanes(1, member)] = jnp.where(low_lane, *grad_key).astype(BF)
                result[at, lanes(2, member)] = jnp.where(low_lane, *grad_value).astype(BF)
                for half in range(2):
                    head = group * (2 * GROUP_BACK) + pair + half
                    own = pl.ds(pl.multiple_of(head * HD, HD), HD)
                    turned_t[own, :] = (nn(keys_t[own, :], grad_scores[pair + half]) * HD**-0.5).astype(BF)

        result[at, 0:width] = nt(unit[...], turned_t[...]).astype(BF)


def time_attention_back(qkv, grads, probs, result, stage, soft, soft_grad, grad_key, grad_value, heads, heads_t, frames, rows, width, between):
    grad_key[...] = jnp.zeros_like(grad_key)
    grad_value[...] = jnp.zeros_like(grad_value)

    @pl.loop(0, frames)
    def _(i):
        between(i)
        own = rows_at(i, rows)
        for j in range(frames):
            stage[pl.ds(j * rows, rows), :] = grads[own, :] * qkv[pl.ds(j * rows, rows), 2 * width : 3 * width]
        grad_soft = nn(stage[...], heads[...]) * HD**0.5
        parts = [probs[i, pl.ds(j * rows, rows), :] for j in range(frames)]
        changes = [grad_soft[j * rows : (j + 1) * rows] for j in range(frames)]
        total = sum(part * change for part, change in zip(parts, changes))
        for j in range(frames):
            at = pl.ds(j * rows, rows)
            soft[at, :] = parts[j].astype(BF)
            soft_grad[at, :] = (parts[j] * (changes[j] - total)).astype(BF)
        grad_query = None
        for j in range(frames):
            at = pl.ds(j * rows, rows)
            wide = nn(soft_grad[at, :], heads_t[...])
            term = wide * qkv[at, width : 2 * width].astype(F32)
            grad_query = term if grad_query is None else grad_query + term
            grad_key[at, :] += wide * qkv[own, 0:width].astype(F32)
            grad_value[at, :] += nn(soft[at, :], heads_t[...]) * grads[own, :].astype(F32)
        result[own, 0:width] = (grad_query * HD**-0.5).astype(BF)

    result[:, width : 2 * width] = (grad_key[...] * HD**-0.5).astype(BF)
    result[:, 2 * width : 3 * width] = grad_value[...].astype(BF)


def back_kernel(block, parts, places, patches, k):
    total, width = k.grads.shape
    hidden = k.act.shape[1]
    frames = k.probs.shape[0]
    rows = total // frames
    deep = hidden // width
    copies = Copies(k.sems)
    section, place = lax.axis_index("section"), lax.axis_index("seq")
    mine = section == block
    last = block == 0
    columns = lambda tile, count=1: slice(tile * width, (tile + count) * width)

    greet()
    load_gy = copies.start(k.gy_in, k.low_grads)
    tiles = []
    for tile in range(deep):
        at = pl.ds(tile * width, width)
        tiles.append(copies.fetch(k.own_down.at[at], k.other_down.at[at], k.down.at[at], mine))
        tiles.append(copies.start(k.r_slope.at[:, at], k.gpre.at[:, at]))
    carried = []
    if last:
        relay = Relay(1, k.last_mine, k.last_mates, k.last_taken, k.last_send, k.last_recv, k.last_in)
        relay.begin()
        carried.append(relay)
        swaps = Swaps(k)
        swaps.begin()
    smalls = load_smalls(k, mine)
    fill_pick(k.pick, parts, place, places)
    fill_pick(k.pick_wide, 1, place, places)
    fill_units(k.unit, k.pair_unit)
    fill_heads(k.heads, k.heads_t)
    low = k.low
    low[...] = jnp.zeros_like(low)
    count = k.pick.shape[0]
    each = count // parts
    wide = k.pick_wide.shape[0]

    def turn(source):
        k.turned[0:count, :] = nt(k.pick[...], source).astype(BF)

    load_gy.wait()
    for tile in range(deep):
        tiles[2 * tile].wait()
        tiles[2 * tile + 1].wait()
        if tile == 1:
            load_act = copies.start(k.r_act, k.act)
            load_up = copies.fetch(k.own_up, k.other_up, k.up, mine)
            load_normed = copies.start(k.r_normed_m, k.normed)
            load_x2 = copies.start(k.r_x2, k.hidden)
        at = columns(tile)
        k.gpre[:, at] = (nt(k.low_grads[...], k.down[at, :]) * k.gpre[:, at].astype(F32)).astype(BF)
    load_space_out = copies.fetch(k.own_space_out, k.other_space_out, k.down.at[columns(3)], mine)
    load_space = [
        copies.fetch(k.own_space.at[:, columns(part)], k.other_space.at[:, columns(part)], k.down.at[columns(part)], mine)
        for part in range(3)
    ]
    for relay in carried:
        relay.middle()
    load_act.wait()
    for part in range(parts):
        at = slice(part * wide, (part + 1) * wide)
        k.turned[at, :] = nt(k.pick_wide[...], k.act[:, part * (hidden // parts) : (part + 1) * (hidden // parts)]).astype(BF)
    fill_ones(k.turned, parts * wide)
    weight_grad(k.turned, parts * wide, k.low_grads, k.mlp, deep * each, low, BIAS + 10)
    load_qkv = copies.start(k.r_qkv_s, k.act.at[:, columns(0, 3)])
    load_logs = copies.start(k.r_logs, k.logs)
    load_up.wait()
    tiled_nt(k.gpre, k.up, k.gnorm, width // 3)
    load_time = copies.fetch(k.own_time, k.other_time, k.up.at[:, columns(0, 3)], mine)
    load_time_out = copies.fetch(k.own_time_out, k.other_time_out, k.up.at[:, columns(3)], mine)
    load_normed.wait()
    turn(k.normed[...])
    fill_ones(k.turned, count)
    weight_grad(k.turned, count, k.gpre, k.mlp, 0, low, *range(UP, UP + deep))
    load_normed = copies.start(k.r_normed_s, k.normed)
    mlp = Relay(block, k.mlp, k.spare, k.mlp_taken, k.mlp_send, k.mlp_recv)
    mlp.begin()
    load_attn = copies.start(k.r_attn_s, k.attn)
    for relay in carried:
        relay.second()
    load_x2.wait()
    norm_back(k.hidden, k.gnorm, smalls.gain(2), k.low_grads, k.grads, k.sums, CHUNK)
    load_x1 = copies.start(k.r_x1, k.hidden)
    norm_sums(k.sums, low, 2, 9)

    k.low_grads[...] = k.grads[...].astype(BF)
    load_space_out.wait()
    k.gattn[...] = nt(k.low_grads[...], k.down[columns(3), :]).astype(BF)
    load_time_fc = copies.fetch(k.own_time_fc, k.other_time_fc, k.down.at[columns(3)], mine)
    load_attn.wait()
    turn(k.attn[...])
    weight_grad(k.turned, count, k.low_grads, k.space, 3 * each, low, BIAS + 8)
    mlp.middle()
    load_attn = copies.start(k.r_attn_t, k.attn)
    proj, stage = k.spare.at[0:total], k.spare.at[total : 2 * total]
    load_proj = copies.start(k.r_proj, proj)
    load_qkv.wait()
    load_logs.wait()
    qkv, gqkv = k.act.at[:, columns(0, 3)], k.gpre.at[:, columns(0, 3)]
    space_attention_back(
        qkv, k.gattn, k.logs, gqkv, k.keys_t, k.turned_t, k.unit, k.pair_unit, frames, rows, patches, width
    )
    load_qkv = copies.start(k.r_qkv_t, qkv)
    load_probs = copies.start(k.r_probs, k.probs)
    mlp.second()
    for load in load_space:
        load.wait()
    load_normed.wait()
    turn(k.normed[...])
    weight_grad(k.turned, count, gqkv, k.space, 0, low, BIAS + 6, None, BIAS + 7)
    load_normed = copies.start(k.r_normed_t, k.normed)
    space = Relay(block, k.space, k.space_mates, k.space_taken, k.space_send, k.space_recv)
    space.begin()

    @pl.loop(0, 3)
    def _(tile):
        size = width // 3
        result = None
        for part in range(3):
            at = pl.ds(pl.multiple_of(part * width + tile * size, size), size)
            term = nt(gqkv[:, columns(part)], k.down[at, :])
            result = term if result is None else result + term
        k.gnorm[:, rows_at(tile, size)] = result

    load_x1.wait()
    norm_back(k.hidden, k.gnorm, smalls.gain(1), k.grads, k.grads, k.sums, CHUNK)
    load_x = copies.start(k.r_x, k.x)
    norm_sums(k.sums, low, 1, 5)

    k.low_grads[...] = k.grads[...].astype(BF)
    load_time_fc.wait()
    k.gproj[...] = nt(k.low_grads[...], k.down[columns(3), :]).astype(BF)
    space.middle()
    load_proj.wait()
    turn(proj[...])
    weight_grad(k.turned, count, k.low_grads, k.time, 4 * each, low, BIAS + 4)
    load_time_out.wait()
    k.gattn[...] = nt(k.gproj[...], k.up[:, columns(3)]).astype(BF)
    load_attn.wait()
    turn(k.attn[...])
    weight_grad(k.turned, count, k.gproj, k.time, 3 * each, low, BIAS + 3)
    outs = Relay(
        block, k.time.at[:, 3 * each : 5 * each], k.outs_mates, k.outs_taken, k.outs_send, k.outs_recv
    )
    outs.begin()
    load_qkv.wait()
    load_probs.wait()

    def between(step):
        pl.when(step == 1)(outs.middle)
        pl.when(step == 3)(space.second)

    time_attention_back(
        qkv, k.gattn, k.probs, gqkv, stage, k.soft, k.soft_grad, k.gnorm, k.hidden, k.heads, k.heads_t, frames, rows,
        width, between,
    )
    outs.second()
    load_normed.wait()
    turn(k.normed[...])
    weight_grad(k.turned, count, gqkv, k.time, 0, low, BIAS + 1, None, BIAS + 2)
    qkv_part = k.time.at[:, 0 : 3 * each]
    if last:
        final = Relay(0, qkv_part, k.qkv_mates, k.qkv_taken, k.qkv_send, k.qkv_recv)
        final.begin()
    else:
        copies.store(qkv_part, k.last_out)
    load_time.wait()
    tiled_nt(gqkv, k.up.at[:, columns(0, 3)], k.gnorm, width // 3)
    if last:
        final.middle()
    load_x.wait()
    norm_back(k.x, k.gnorm, smalls.gain(0), k.grads, k.gattn, k.sums, CHUNK)
    copies.store(k.gattn, k.gx_out)
    norm_sums(k.sums, low, 0, 0)
    relays = [(mlp, k.mlp_out), (space, k.space_out), (outs, k.outs_out)]
    if last:
        lows = LowRelay([low, k.low_in], k.low_sum, (k.low_mine, k.low_mate, k.low_taken, k.low_send, k.low_recv))
        lows.begin()
        swaps.late()
        relays.append((carried[0], k.last_out))
        final.second()
        lows.middle()
    start = 0
    for at, (relay, out) in enumerate(relays):
        size = out.shape[0]
        relay.end(k.hidden.at[start : start + size], out, k.end_sems.at[at])
        start += size
    if last:
        lows.second()
        swaps.end()
        size = 3 * each
        final.end(k.hidden.at[start - size : start], k.qkv_out, k.end_sems.at[len(relays)])
        lows.end()
        relays.append((final, k.qkv_out))
    for relay, _ in relays:
        relay.settle()
    copies.finish()


class Swaps:
    def __init__(self, k):
        self.k = k
        self.section = lax.axis_index("section")
        rows = k.swapped.shape[1]
        self.own = rows_at(lax.axis_index("seq"), rows)

    def over(self, which, source):
        return pltpu.make_async_remote_copy(
            source.at[self.own],
            self.k.swapped.at[which],
            self.k.swap_send.at[which],
            self.k.swap_recv.at[which],
            device_id={"section": 1 - self.section},
            device_id_type=MESH,
        )

    def begin(self):
        @pl.when(self.section == 0)
        def _():
            self.over(0, self.k.y1_in).start()
            self.over(1, self.k.gy_in).start()

        @pl.when(self.section == 1)
        def _():
            self.over(0, self.k.y0_in).start()

    def late(self):
        @pl.when(self.section == 1)
        def _():
            self.over(1, self.k.gattn).start()

    def end(self):
        self.over(0, self.k.y1_in).wait()
        self.over(1, self.k.gy_in).wait()


def back(block, parts, places, patches, gy, small, small_other, own, other, kept, last=None, low=None, outputs=None):
    total, width = gy.shape
    hidden = own[5].shape[1]
    logs, probs = kept["r_logs"], kept["r_probs"]
    rows = logs.shape[1]
    count = width // places
    each = count // parts
    deep = hidden // width
    dma = pltpu.SemaphoreType.DMA
    wide, full, deepest = struct((total, width)), struct((total, width), F32), struct((total, hidden))
    few, lowest = struct((total, PAIR)), struct((LOW, width), F32)
    piece = lambda height, n=parts: struct((n, height, width))
    mlp, space, time = deep * each + hidden // places // parts, 4 * each, 5 * each
    ins = dict(gy_in=(gy, IN_HBM), **small_ins(small, small_other), **own_ins(own), **other_refs(other))
    ins |= {name: (array, IN_HBM) for name, array in kept.items()}
    summed = lambda height: (struct((height, width), F32), IN_HBM)
    outs = dict(gx_out=(wide, IN_HBM), low=(lowest, IN_VMEM))
    outs |= dict(mlp_out=summed(mlp), space_out=summed(space), outs_out=summed(2 * each))
    scratch = vmem(up=struct((width, hidden)), down=struct((hidden, width)), gpre=deepest, act=deepest)
    scratch |= vmem(grads=full, hidden=full, gnorm=full, low_grads=wide, normed=wide, attn=wide, gattn=wide, gproj=wide)
    scratch |= vmem(x=wide, spare=struct((max(2 * total, parts * mlp), width)), soft=few, soft_grad=few)
    scratch |= vmem(probs=struct(probs.shape, F32), logs=struct(logs.shape, F32), unit=struct((rows, rows)))
    scratch |= vmem(pair_unit=struct((PAIR, PAIR)), keys_t=struct((width, rows)), turned_t=struct((width, rows)))
    scratch |= vmem(heads=struct((width, PAIR)), heads_t=struct((PAIR, width)), pick=struct((count, width)))
    scratch |= vmem(turned=struct((hidden // places + 16, total)), sums=struct((16, width), F32))
    scratch |= vmem(pick_wide=struct((hidden // parts // places, hidden // parts)))
    scratch |= vmem(mlp=piece(mlp), mlp_taken=piece(mlp, 3), space=piece(space), space_mates=piece(space))
    scratch |= vmem(space_taken=piece(space, 3), time=piece(time), outs_mates=piece(2 * each))
    scratch |= vmem(outs_taken=piece(2 * each, 3))
    scratch |= small_held(width, hidden)
    scratch |= dict(mlp_send=dma((8,)), mlp_recv=dma((7,)), space_send=dma((8,)), space_recv=dma((7,)))
    scratch |= dict(outs_send=dma((8,)), outs_recv=dma((7,)), sems=dma((40,)), end_sems=dma((8,)))
    if block == 1:
        outs |= dict(last_out=(piece(3 * each), IN_HBM))
    else:
        y_0, y_1 = outputs
        ins |= dict(last_in=(last, IN_HBM), low_in=(low, IN_VMEM), y0_in=(y_0, IN_HBM), y1_in=(y_1, IN_HBM))
        outs |= dict(last_out=summed(3 * each), qkv_out=summed(3 * each), low_sum=(lowest, IN_VMEM))
        outs |= dict(swapped=(struct((2, rows, width)), IN_HBM))
        low_two, part = struct((2, LOW, width), F32), piece(3 * each)
        scratch |= vmem(last_mine=part, last_mates=part, last_taken=piece(3 * each, 3), qkv_mates=part)
        scratch |= vmem(qkv_taken=piece(3 * each, 3), low_mine=low_two, low_mate=lowest, low_taken=low_two)
        scratch |= dict(low_send=dma((3,)), low_recv=dma((3,)), swap_send=dma((2,)), swap_recv=dma((2,)))
        scratch |= dict(last_send=dma((8,)), last_recv=dma((7,)), qkv_send=dma((8,)), qkv_recv=dma((7,)))
    kernel = functools.partial(back_kernel, block, parts, places, patches)
    return named_call(kernel, f"block{block}_backward", 70 * total * width * width, ins, outs, scratch, True)
def layout_kernel(places, patches, pieces, rows_each, low, *refs):
    n = len(pieces)
    sums, refs = (refs[:n], refs[n : 2 * n]), refs[2 * n :]
    results, swapped, refs = refs[:4], refs[4], refs[5:]
    weights, lows, frames, refs = refs[:7], refs[7:10], refs[10:12], refs[12:]
    total, mine, sems = refs
    section = lax.axis_index("section")
    z, place = lax.axis_index("dp"), lax.axis_index("seq")
    rows, width = mine.shape[1:]
    loads = []
    for at, (start, count) in enumerate(pieces):
        for block in range(2):

            @pl.when(section == block)
            def _(at=at, block=block, start=start, count=count):
                pltpu.make_async_copy(sums[block][at], total.at[start : start + count], sems.at[at]).start()

        loads.append(pltpu.make_async_copy(sums[0][at], total.at[start : start + count], sems.at[at]))
    for which in range(2):
        own = rows_at(place, rows)
        for block in range(2):

            @pl.when(section == block)
            def _(which=which, block=block):
                pltpu.make_async_copy(results[2 * which + block].at[own], mine.at[which], sems.at[n + which]).start()

        loads.append(pltpu.make_async_copy(results[2 * which].at[own], mine.at[which], sems.at[n + which]))
        loads.append(pltpu.make_async_copy(swapped.at[which], mine.at[2 + which], sems.at[n + 2 + which]))
        loads[-1].start()
    part = z * lax.axis_size("seq") + place
    for target, first, count in zip(lows, (0, BIAS, UP), (BIAS, UP - BIAS, target_rows(lows[2], places, width))):
        flat = jnp.concatenate([low[first + at : first + at + 1] for at in range(count)], axis=1)
        size = target.shape[1]
        flat = jnp.broadcast_to(flat, (8, flat.shape[1]))
        target[...] = pltpu.roll(flat, lax.rem(count * width - part * size, count * width), 1)[0:1, :size]
    for load in loads:
        load.wait()
    for which, target in enumerate(frames):
        for block in range(2):

            @pl.when(section == block)
            def _(which=which, target=target, block=block):
                target[0, block, 0] = mine[which, 0:patches]
                target[0, 1 - block, 0] = mine[2 + which, 0:patches]

    start = 0
    lanes = width // PAIR
    for target, count in zip(weights, rows_each):
        each = target.shape[0] // (count * lanes)
        for at in range(count):
            for lane in range(lanes):
                target[pl.ds(at * lanes + lane, each, stride=count * lanes), :] = total[
                    start + at * each : start + (at + 1) * each, lane * PAIR : (lane + 1) * PAIR
                ]
        start += count * each


def target_rows(target, places, width):
    return target.shape[1] * places // width


def layout(patches, places, width, hidden, pieces, sums, low, results, swapped):
    each = width // places
    deep = hidden // width
    rows_each = (3, 1, 1, 3, 1, deep, 1)
    heights = (each, each, each, each, each, each, hidden // places)
    outs = [struct((h * r * width // PAIR, PAIR), F32) for h, r in zip(heights, rows_each)]
    outs += [struct((1, rows * width // places), F32) for rows in (BIAS, UP - BIAS, deep)]
    outs += [struct((1, 2, 1, patches, width))] * 2
    rows = swapped.shape[1]
    n = len(pieces)
    total = sum(count for _, count in pieces)
    scratch = held(struct((total, width), F32), struct((4, rows, width))) + [pltpu.SemaphoreType.DMA((n + 4,))]
    return pl.pallas_call(
        functools.partial(layout_kernel, places, patches, pieces, rows_each),
        out_shape=outs,
        in_specs=[IN_VMEM] + [IN_HBM] * (2 * n + 5),
        out_specs=[IN_VMEM] * len(outs),
        scratch_shapes=scratch,
        compiler_params=pltpu.CompilerParams(vmem_limit_bytes=VMEM_BYTES),
        name="lay_out",
    )(low, *sums[0], *sums[1], *results, swapped)


def shards(clip_ids, tokens, *rest):
    weights, small, cotangent = rest[:7], rest[7:10], rest[10]
    NEXT_ID[:] = [1]
    n_dp, n_seq = lax.axis_size("dp"), lax.axis_size("seq")
    patches, width = tokens.shape[2:]
    hidden = weights[5].shape[2]
    places = n_dp * n_seq
    small = [array.reshape(1, -1) for array in small]
    own = [array[0] for array in weights]

    first = forward(0, n_seq, patches, clip_ids, small, None, own, None, None, tokens, cotangent)
    y_0, grad_top, x = first.pop("y_out"), first.pop("cot_out"), first["r_x"]
    small_other = [first.pop("other_gains"), first.pop("other_biases"), first.pop("other_up_bias")]
    other = [first.pop("other_time"), first.pop("other_time_out"), first.pop("other_time_fc"), first.pop("other_space")]
    other += [first.pop("other_space_out"), first.pop("other_up"), first.pop("other_down")]
    common = (small, small_other, own, other)
    second = forward(1, n_seq, patches, clip_ids, *common, y_0)
    y_1 = second.pop("y_out")
    second["r_x"] = y_0
    outputs = (y_0, y_1)

    each = width // places
    back_1 = back(1, n_dp, n_seq, patches, grad_top, *common, second)
    back_0 = back(
        0, n_dp, n_seq, patches, back_1["gx_out"], *common, first, back_1["last_out"], back_1["low"], outputs
    )
    results = (*outputs, back_0["gx_out"], back_1["gx_out"])
    counts = (3 * each, 2 * each, 4 * each, hidden // width * each + hidden // places)
    pieces = [(sum(counts[:at]), count) for at, count in enumerate(counts)]
    ordered = [
        [first, *(done[name] for name in ("outs_out", "space_out", "mlp_out"))]
        for first, done in ((back_0["qkv_out"], back_0), (back_0["last_out"], back_1))
    ]
    shares = layout(
        patches, places, width, hidden, pieces, ordered, back_0["low_sum"], results, back_0["swapped"]
    )
    frames = shares[10:]
    shares = [share.reshape(1, -1) for share in shares[:10]]
    return (*frames, *shares)


def relay_from_behind(value, axis, steps):
    count = lax.axis_size(axis)
    leading, last = (max(0, -steps), min(count, count - steps))
    return lax.ppermute(value, axis, [(source, source + steps) for source in range(leading, last)])


def relay_norm_rows(values, gain, shift):
    centre = values - jnp.mean(values, axis=-1, keepdims=True)
    spread = jnp.mean(centre * centre, axis=-1, keepdims=True)
    return centre * lax.rsqrt(spread + eps_norm) * gain + shift


def relay_mixed_dot(left, right, form):
    return jnp.einsum(form, left, right, preferred_element_type=jnp.float32)


def relay_column_sum(grad_rows):
    return jnp.sum(grad_rows.astype(jnp.float32), axis=(0, 1))


def relay_flat_terms(terms):
    return tuple((term.reshape(-1) for term in terms))


def relay_masked_scores(queries, key_rows, allowed):
    scores = relay_mixed_dot(queries, key_rows, "bic,bjc->bij") * queries.shape[-1] ** (-0.5)
    if allowed is None:
        return scores
    return jnp.where(allowed[None], scores, far_below)


def relay_attend(queries, key_rows, values, allowed):
    scores = relay_masked_scores(queries, key_rows, allowed)
    top_score = jnp.max(scores, axis=-1, keepdims=True)
    total_exp = jnp.sum(jnp.exp(scores - top_score), axis=-1, keepdims=True)
    log_total = top_score + jnp.log(total_exp)
    weights_soft = jnp.exp(scores - log_total).astype(jnp.bfloat16)
    mixed = relay_mixed_dot(weights_soft, values, "bij,bjc->bic").astype(jnp.bfloat16)
    return (mixed, log_total)


def relay_attend_back(queries, key_rows, values, log_total, allowed, grad_out):
    scale = queries.shape[-1] ** (-0.5)
    weights_soft = jnp.exp(relay_masked_scores(queries, key_rows, allowed) - log_total)
    grad_values = relay_mixed_dot(weights_soft.astype(jnp.bfloat16), grad_out, "bij,bic->bjc")
    grad_soft = relay_mixed_dot(grad_out, values, "bic,bjc->bij")
    row_total = jnp.sum(grad_soft * weights_soft, axis=-1, keepdims=True)
    grad_scores = (weights_soft * (grad_soft - row_total)).astype(jnp.bfloat16)
    grad_queries = relay_mixed_dot(grad_scores, key_rows, "bij,bjc->bic") * scale
    grad_keys = relay_mixed_dot(grad_scores, queries, "bij,bic->bjc") * scale
    return (grad_queries, grad_keys, grad_values)


def relay_heads_first(rows):
    frames, patches, width = rows.shape
    return (
        rows.reshape(frames, patches, H, width // H)
        .transpose(0, 2, 1, 3)
        .reshape(frames * H, patches, width // H)
    )


def relay_heads_last(rows, frames):
    batch, patches, head_size = rows.shape
    return (
        rows.reshape(frames, batch // frames, patches, head_size)
        .transpose(0, 2, 1, 3)
        .reshape(frames, patches, batch // frames * head_size)
    )


def relay_time_mix(normed_time, time_qkv, time_out, bias_rows, allowed):
    frames, patches, width = normed_time.shape
    zero_row = jnp.zeros((width,), jnp.float32)
    bias_time = jnp.stack([bias_rows[1], zero_row, bias_rows[2]])
    proj_time = relay_mixed_dot(normed_time, time_qkv.reshape(width, 3, width), "fpd,dke->fkpe")
    proj_time = (proj_time + bias_time[None, :, None, :]).astype(jnp.bfloat16)
    proj_time = proj_time.reshape(frames, 3, patches * H, HD)
    by_patch = lax.all_to_all(proj_time, "seq", split_axis=2, concat_axis=0, tiled=True)
    query_time = by_patch[:, 0].transpose(1, 0, 2)
    key_time = by_patch[:, 1].transpose(1, 0, 2)
    value_time = by_patch[:, 2].transpose(1, 0, 2)
    mixed_time, total_time = relay_attend(query_time, key_time, value_time, allowed)
    back_frames = lax.all_to_all(
        mixed_time.transpose(1, 0, 2), "seq", split_axis=0, concat_axis=1, tiled=True
    )
    attn_time = back_frames.reshape(frames, patches, width)
    proj_out = (relay_mixed_dot(attn_time, time_out, "fpd,de->fpe") + bias_rows[3]).astype(jnp.bfloat16)
    return (proj_out, (normed_time, query_time, key_time, value_time, total_time, attn_time))


def relay_time_mix_back(grad_proj_out, time_qkv, time_out, time_kept, allowed):
    normed_rows, query_time, key_time, value_time, total_time, attn_time = time_kept
    frames, patches, width = grad_proj_out.shape
    grad_time_out = relay_mixed_dot(attn_time, grad_proj_out, "fpd,fpe->de")
    grad_attn_time = relay_mixed_dot(grad_proj_out, time_out, "fpe,de->fpd").astype(jnp.bfloat16)
    grad_attn_time = grad_attn_time.reshape(frames, patches * H, HD)
    grad_by_patch = lax.all_to_all(
        grad_attn_time, "seq", split_axis=1, concat_axis=0, tiled=True
    ).transpose(1, 0, 2)
    grads_time = relay_attend_back(query_time, key_time, value_time, total_time, allowed, grad_by_patch)
    grad_mixed = jnp.stack(grads_time, axis=0).transpose(2, 0, 1, 3).astype(jnp.bfloat16)
    grad_frames = lax.all_to_all(
        grad_mixed, "seq", split_axis=0, concat_axis=2, tiled=True
    ).reshape(frames, 3, patches, width)
    grad_time_qkv = relay_mixed_dot(normed_rows, grad_frames, "fpd,fkpe->dke").reshape(width, 3 * width)
    grad_normed = relay_mixed_dot(grad_frames, time_qkv.reshape(width, 3, width), "fkpe,dke->fpd")
    return (
        grad_normed,
        grad_time_qkv,
        grad_time_out,
        relay_column_sum(grad_frames[:, 0]),
        relay_column_sum(grad_frames[:, 2]),
        relay_column_sum(grad_proj_out),
    )


def relay_layer_forward(inputs, params, allowed):
    (
        time_qkv,
        time_out,
        time_fc,
        space_qkv,
        space_out,
        up_weight,
        down_weight,
        norm_gains,
        bias_rows,
        up_bias,
    ) = params
    frames, patches, width = inputs.shape
    zero_row = jnp.zeros((width,), jnp.float32)
    normed_time = relay_norm_rows(inputs, norm_gains[0], bias_rows[0]).astype(jnp.bfloat16)
    proj_out, time_kept = relay_time_mix(normed_time, time_qkv, time_out, bias_rows, allowed)
    after_time = inputs + (relay_mixed_dot(proj_out, time_fc, "fpd,de->fpe") + bias_rows[4])
    normed_space = relay_norm_rows(after_time, norm_gains[1], bias_rows[5]).astype(jnp.bfloat16)
    bias_space = jnp.stack([bias_rows[6], zero_row, bias_rows[7]])
    proj_space = relay_mixed_dot(normed_space, space_qkv.reshape(width, 3, width), "fpd,dke->fkpe")
    proj_space = (proj_space + bias_space[None, :, None, :]).astype(jnp.bfloat16)
    query_space = relay_heads_first(proj_space[:, 0])
    key_space = relay_heads_first(proj_space[:, 1])
    value_space = relay_heads_first(proj_space[:, 2])
    mixed_space, total_space = relay_attend(query_space, key_space, value_space, None)
    attn_space = relay_heads_last(mixed_space, frames)
    after_space = after_time + (relay_mixed_dot(attn_space, space_out, "fpd,de->fpe") + bias_rows[8])
    normed_mlp = relay_norm_rows(after_space, norm_gains[2], bias_rows[9]).astype(jnp.bfloat16)
    hidden_pre = relay_mixed_dot(normed_mlp, up_weight, "fpd,de->fpe") + up_bias
    hidden_act = jax.nn.gelu(hidden_pre).astype(jnp.bfloat16)
    outputs = after_space + (relay_mixed_dot(hidden_act, down_weight, "fpe,ed->fpd") + bias_rows[10])
    kept = (
        inputs,
        time_kept,
        proj_out,
        after_time,
        normed_space,
        query_space,
        key_space,
        value_space,
        total_space,
        attn_space,
        after_space,
        normed_mlp,
        hidden_pre,
        hidden_act,
    )
    return (outputs, kept)


def relay_layer_backward(grad_top, params, kept, allowed):
    (
        time_qkv,
        time_out,
        time_fc,
        space_qkv,
        space_out,
        up_weight,
        down_weight,
        norm_gains,
        bias_rows,
        up_bias,
    ) = params
    (
        inputs,
        time_kept,
        proj_out,
        after_time,
        normed_space,
        query_space,
        key_space,
        value_space,
        total_space,
        attn_space,
        after_space,
        normed_mlp,
        hidden_pre,
        hidden_act,
    ) = kept
    frames, patches, width = inputs.shape
    grad_mlp = grad_top.astype(jnp.bfloat16)
    grad_down = relay_mixed_dot(hidden_act, grad_mlp, "fpe,fpd->ed")
    grad_act = relay_mixed_dot(grad_mlp, down_weight, "fpd,ed->fpe")
    gelu_back = jax.vjp(jax.nn.gelu, hidden_pre)[1]
    grad_pre = gelu_back(grad_act)[0].astype(jnp.bfloat16)
    grad_up = relay_mixed_dot(normed_mlp, grad_pre, "fpd,fpe->de")
    grad_normed = relay_mixed_dot(grad_pre, up_weight, "fpe,de->fpd")
    norm_back = jax.vjp(relay_norm_rows, after_space, norm_gains[2], bias_rows[9])[1]
    grad_into, gain_mlp, shift_mlp = norm_back(grad_normed)
    grad_space = grad_top + grad_into
    grad_branch = grad_space.astype(jnp.bfloat16)
    grad_space_out = relay_mixed_dot(attn_space, grad_branch, "fpd,fpe->de")
    grad_attn = relay_heads_first(relay_mixed_dot(grad_branch, space_out, "fpe,de->fpd").astype(jnp.bfloat16))
    grads_space = relay_attend_back(query_space, key_space, value_space, total_space, None, grad_attn)
    grad_proj = jnp.stack([relay_heads_last(piece, frames) for piece in grads_space], axis=1).astype(
        jnp.bfloat16
    )
    grad_space_qkv = relay_mixed_dot(normed_space, grad_proj, "fpd,fkpe->dke").reshape(width, 3 * width)
    grad_normed = relay_mixed_dot(grad_proj, space_qkv.reshape(width, 3, width), "fkpe,dke->fpd")
    norm_back = jax.vjp(relay_norm_rows, after_time, norm_gains[1], bias_rows[5])[1]
    grad_into, gain_space, shift_space = norm_back(grad_normed)
    grad_time = grad_space + grad_into
    grad_branch_time = grad_time.astype(jnp.bfloat16)
    grad_time_fc = relay_mixed_dot(proj_out, grad_branch_time, "fpd,fpe->de")
    grad_proj_out = relay_mixed_dot(grad_branch_time, time_fc, "fpe,de->fpd").astype(jnp.bfloat16)
    grad_normed, grad_time_qkv, grad_time_out, query_bias, value_bias, out_bias = relay_time_mix_back(
        grad_proj_out, time_qkv, time_out, time_kept, allowed
    )
    norm_back = jax.vjp(relay_norm_rows, inputs, norm_gains[0], bias_rows[0])[1]
    grad_into, gain_time, shift_time = norm_back(grad_normed)
    grad_inputs = grad_time + grad_into
    gain_grads = jnp.stack([gain_time, gain_space, gain_mlp])
    bias_grads = jnp.stack(
        [
            shift_time,
            query_bias,
            value_bias,
            out_bias,
            relay_column_sum(grad_branch_time),
            shift_space,
            relay_column_sum(grad_proj[:, 0]),
            relay_column_sum(grad_proj[:, 2]),
            relay_column_sum(grad_branch),
            shift_mlp,
            relay_column_sum(grad_mlp),
        ]
    )
    up_grad = relay_column_sum(grad_pre)
    return (
        grad_inputs,
        (
            grad_time_qkv,
            grad_time_out,
            grad_time_fc,
            grad_space_qkv,
            grad_space_out,
            grad_up,
            grad_down,
            gain_grads,
            bias_grads,
            up_grad,
        ),
    )


def relay_shards(
    clip_ids,
    tokens,
    time_qkv,
    time_out,
    time_fc,
    space_qkv,
    space_out,
    up_weight,
    down_weight,
    norm_gains,
    bias_rows,
    up_bias,
    cotangent,
):
    params = (
        time_qkv[0],
        time_out[0],
        time_fc[0],
        space_qkv[0],
        space_out[0],
        up_weight[0],
        down_weight[0],
        norm_gains[0],
        bias_rows[0],
        up_bias[0],
    )
    allowed = clip_ids[0][:, None] == clip_ids[0][None, :]
    first_section = lax.axis_index("section") == 0
    micro = tokens.shape[0]
    arriving = jnp.zeros_like(tokens[0])
    section_inputs = []
    section_outputs = []
    for moment in range(micro + 1):
        taken_rows = jnp.where(first_section, tokens[min(moment, micro - 1)], arriving)
        result = relay_layer_forward(taken_rows.astype(jnp.float32), params, allowed)[0].astype(
            jnp.bfloat16
        )
        section_inputs.append(taken_rows)
        section_outputs.append(result)
        if moment < micro:
            arriving = relay_from_behind(result, "section", 1)
    saved_inputs = [
        jnp.where(first_section, section_inputs[number], section_inputs[number + 1])
        for number in range(micro)
    ]
    layer_outputs = jnp.stack(
        [
            jnp.where(first_section, section_outputs[number], section_outputs[number + 1])
            for number in range(micro)
        ]
    )
    returning = jnp.zeros_like(tokens[0])
    back_results = []
    totals = None
    for moment in range(micro + 1):
        grad_given = jnp.where(first_section, returning, cotangent[min(moment, micro - 1)]).astype(
            jnp.float32
        )
        source_rows = jnp.where(
            first_section, saved_inputs[max(moment - 1, 0)], saved_inputs[min(moment, micro - 1)]
        )
        live_share = jnp.where(
            first_section, 1.0 if moment >= 1 else 0.0, 1.0 if moment < micro else 0.0
        )
        kept = relay_layer_forward(source_rows.astype(jnp.float32), params, allowed)[1]
        grad_inputs, weight_terms = relay_layer_backward(grad_given, params, kept, allowed)
        grad_inputs = grad_inputs.astype(jnp.bfloat16)
        back_results.append(grad_inputs)
        weight_terms = relay_flat_terms(jax.tree.map(lambda term: term * live_share, weight_terms))
        if totals is None:
            totals = tuple(weight_terms)
        else:
            totals = tuple((left + right for left, right in zip(totals, weight_terms)))
        if moment < micro:
            returning = relay_from_behind(grad_inputs, "section", -1)
    input_grads = jnp.stack(
        [
            jnp.where(first_section, back_results[number + 1], back_results[number])
            for number in range(micro)
        ]
    )
    shares = (
        lax.psum_scatter(totals[0], ("dp", "seq"), scatter_dimension=0, tiled=True),
        lax.psum_scatter(totals[1], ("dp", "seq"), scatter_dimension=0, tiled=True),
        lax.psum_scatter(totals[2], ("dp", "seq"), scatter_dimension=0, tiled=True),
        lax.psum_scatter(totals[3], ("dp", "seq"), scatter_dimension=0, tiled=True),
        lax.psum_scatter(totals[4], ("dp", "seq"), scatter_dimension=0, tiled=True),
        lax.psum_scatter(totals[5], ("dp", "seq"), scatter_dimension=0, tiled=True),
        lax.psum_scatter(totals[6], ("dp", "seq"), scatter_dimension=0, tiled=True),
        lax.psum_scatter(totals[7], ("dp", "seq"), scatter_dimension=0, tiled=True),
        lax.psum_scatter(totals[8], ("dp", "seq"), scatter_dimension=0, tiled=True),
        lax.psum_scatter(totals[9], ("dp", "seq"), scatter_dimension=0, tiled=True),
    )
    return (
        layer_outputs[None],
        input_grads[None],
        shares[0][None],
        shares[1][None],
        shares[2][None],
        shares[3][None],
        shares[4][None],
        shares[5][None],
        shares[6][None],
        shares[7][None],
        shares[8][None],
        shares[9][None],
    )


def solution(mesh):
    stacked = P("section", None, None)
    spread = P(None, ("dp", "seq"), None, None)
    in_specs = (P("dp", None), spread, *[stacked] * 9, P("section", None), spread)
    flat = P("section", ("dp", "seq"))
    out = P("section", None, ("dp", "seq"), None, None)
    relay = mesh.shape["seq"] != 4 or mesh.shape["dp"] != 4
    return jax.shard_map(
        relay_shards if relay else shards, mesh=mesh, in_specs=in_specs, out_specs=(out, out, *[flat] * 10), check_vma=False
    )
```

```python
import functools

import jax
import jax.numpy as jnp
from jax import lax
from jax.experimental import pallas as pl
from jax.experimental.pallas import tpu as pltpu
from jax.sharding import PartitionSpec as P

H = 12
HD = 64
PAIR = 2 * HD
eps_norm = 1e-06
far_below = -1000000000.0
BF = jnp.bfloat16
F32 = jnp.float32
VMEM_BYTES = 62 << 20
NEXT_ID = [1]
GROUP = 6
GROUP_BACK = 6
CHUNK = 416


def nn(left, right):
    return lax.dot_general(left, right, (((1,), (0,)), ((), ())), preferred_element_type=F32)


def nt(left, right):
    return lax.dot_general(left, right, (((1,), (1,)), ((), ())), preferred_element_type=F32)


def norm_stats(values):
    centre = values - jnp.mean(values, axis=-1, keepdims=True)
    scale = lax.rsqrt(jnp.mean(centre * centre, axis=-1, keepdims=True) + eps_norm)
    return centre * scale, scale


def rows_at(index, count):
    return pl.ds(pl.multiple_of(index * count, count), count)


def norm_into(source, target, gain, shift, chunk):
    @pl.loop(0, source.shape[0] // chunk)
    def _(step):
        at = rows_at(step, chunk)
        hat, _ = norm_stats(source[at, :].astype(F32))
        target[at, :] = (hat * gain[...] + shift[...]).astype(BF)


def gelu_both(pre):
    rate, cube = 0.7978845608028654, 0.044715
    square = pre * pre
    tanh = jnp.tanh(pre * (rate + rate * cube * square))
    half = 0.5 + 0.5 * tanh
    act = pre * half
    slope = half + act * (1.0 - tanh) * (rate + 3.0 * rate * cube * square)
    return act, slope


class Copies:
    def __init__(self, sems):
        self.sems, self.used, self.open = sems, 0, []

    def fetch(self, own, other, target, mine):
        sem = self.sems.at[self.used]
        self.used += 1

        @pl.when(mine)
        def _():
            pltpu.make_async_copy(own, target, sem).start()

        @pl.when(jnp.logical_not(mine))
        def _():
            pltpu.make_async_copy(other, target, sem).start()

        return pltpu.make_async_copy(own, target, sem)

    def start(self, source, target):
        copy = pltpu.make_async_copy(source, target, self.sems.at[self.used])
        self.used += 1
        copy.start()
        return copy

    def store(self, source, target):
        self.open.append(self.start(source, target))

    def finish(self):
        for copy in self.open:
            copy.wait()


def time_attention(qkv, attn, probs, stage, soft, heads, heads_t, clips, frames, rows, width):
    @pl.loop(0, frames)
    def _(i):
        own = rows_at(i, rows)
        for j in range(frames):
            stage[pl.ds(j * rows, rows), :] = qkv[own, 0:width] * qkv[pl.ds(j * rows, rows), width : 2 * width]
        scores = nn(stage[...], heads[...])
        parts = []
        for j in range(frames):
            open_pair = clips[0, i] == clips[0, j]
            parts.append(scores[j * rows : (j + 1) * rows] + jnp.where(open_pair, 0.0, far_below))
        top = functools.reduce(jnp.maximum, parts)
        parts = [jnp.exp(part - top) for part in parts]
        inverse = 1.0 / sum(parts)
        for j in range(frames):
            prob = parts[j] * inverse
            probs[i, pl.ds(j * rows, rows), :] = prob
            soft[pl.ds(j * rows, rows), :] = prob.astype(BF)
        total = None
        for j in range(frames):
            at = pl.ds(j * rows, rows)
            term = nn(soft[at, :], heads_t[...]) * qkv[at, 2 * width : 3 * width].astype(F32)
            total = term if total is None else total + term
        attn[own, :] = total.astype(BF)


def fill_units(unit, pair_unit):
    for target in (unit, pair_unit):
        row = lax.broadcasted_iota(jnp.int32, target.shape, 0)
        column = lax.broadcasted_iota(jnp.int32, target.shape, 1)
        target[...] = jnp.where(row == column, 1.0, 0.0).astype(BF)


def split_patches(scores, patches):
    whole = patches // 16 * 16
    if whole == scores.shape[0]:
        return [scores]
    rest = scores[whole:]
    row = lax.broadcasted_iota(jnp.int32, rest.shape, 0)
    return [scores[:whole], jnp.where(row < patches - whole, rest, far_below)]


def space_attention(qkv, attn, logs, values_t, mixed_t, unit, pair_unit, frames, rows, patches, width):
    low_lane = lax.broadcasted_iota(jnp.int32, (rows, PAIR), 1) < HD
    deep = HD + 16
    values_t[...] = jnp.ones_like(values_t)

    @pl.loop(0, frames)
    def _(f):
        at = rows_at(f, rows)
        for pair in range(width // PAIR):
            turned = nt(pair_unit[...], qkv[at, 2 * width + pair * PAIR : 2 * width + (pair + 1) * PAIR]).astype(BF)
            for half in range(2):
                head = 2 * pair + half
                values_t[head * deep : head * deep + HD, :] = turned[half * HD : (half + 1) * HD]

        @pl.loop(0, width // PAIR // GROUP)
        def _(group):
            scores = []
            for member in range(GROUP):
                pair = group * GROUP + member

                def lanes(which):
                    return pl.ds(pl.multiple_of(which * width + pair * PAIR, PAIR), PAIR)

                query, key = qkv[at, lanes(0)] * BF(HD**-0.5), qkv[at, lanes(1)]
                for half in range(2):
                    scores.append(nt(jnp.where(low_lane if half == 0 else ~low_lane, key, BF(0)), query))
            expos, tops = [], []
            for score in scores:
                parts = split_patches(score, patches)
                top = functools.reduce(jnp.maximum, [jnp.max(part, axis=0, keepdims=True) for part in parts])
                expos.append(jnp.concatenate([jnp.exp(part - top).astype(BF) for part in parts], axis=0))
                tops.append(top)
            for member, (expo, top) in enumerate(zip(expos, tops)):
                head = group * (2 * GROUP) + member
                both = nn(values_t[pl.ds(pl.multiple_of(head * deep, 16), deep), :], expo)
                total = both[HD : HD + 1]
                logs[pl.ds(f * H + head, 1), :] = top + jnp.log(total)
                mixed_t[pl.ds(pl.multiple_of(head * HD, HD), HD), :] = (both[:HD] * (1.0 / total)).astype(BF)

        attn[at, :] = nt(unit[...], mixed_t[...]).astype(BF)


class Smalls:
    def __init__(self, own, other, held, mine):
        for which, refs in ((mine, own), (jnp.logical_not(mine), other)):

            @pl.when(which)
            def _(refs=refs):
                for source, target in zip(refs, held):
                    width = target.shape[1]
                    for row in range(target.shape[0]):
                        target[row : row + 1, :] = source[:, row * width : (row + 1) * width]

        self.gains, self.biases, self.up_bias = held

    def gain(self, row):
        return self.gains.at[row : row + 1]

    def bias(self, row):
        return self.biases.at[row : row + 1]


def fill_heads(heads, heads_t):
    lane = lax.broadcasted_iota(jnp.int32, heads.shape, 0) // HD
    head = lax.broadcasted_iota(jnp.int32, heads.shape, 1)
    heads[...] = jnp.where(lane == head, HD**-0.5, 0.0).astype(BF)
    lane = lax.broadcasted_iota(jnp.int32, heads_t.shape, 1) // HD
    head = lax.broadcasted_iota(jnp.int32, heads_t.shape, 0)
    heads_t[...] = jnp.where(lane == head, 1.0, 0.0).astype(BF)


def fill_pick(pick, outer, place, count):
    each = pick.shape[0] // outer
    row = lax.broadcasted_iota(jnp.int32, pick.shape, 0)
    column = lax.broadcasted_iota(jnp.int32, pick.shape, 1)
    pick[...] = jnp.where(column == (row // each * count + place) * each + row % each, 1.0, 0.0).astype(BF)


def project(source, weight, biases, target):
    width = source.shape[1]
    for part in range(3):
        at = slice(part * width, (part + 1) * width)
        result = nn(source[...], weight[:, at])
        if biases[part] is not None:
            result = result + biases[part][...]
        target[:, at] = result.astype(BF)


def struct(shape, dtype=BF):
    return jax.ShapeDtypeStruct(shape, dtype)


def held(*structs):
    return [pltpu.VMEM(s.shape, s.dtype) for s in structs]


IN_VMEM = pl.BlockSpec(memory_space=pltpu.VMEM)
IN_SMEM = pl.BlockSpec(memory_space=pltpu.SMEM)
IN_HBM = pl.BlockSpec(memory_space=pl.ANY)


def vmem(**structs):
    return {name: pltpu.VMEM(s.shape, s.dtype) for name, s in structs.items()}


def small_held(width, hidden):
    return vmem(
        gains=struct((BIAS, width), F32), biases=struct((UP - BIAS, width), F32), up_bias=struct((1, hidden), F32)
    )


def small_ins(own, other):
    (gains, biases, up_bias), (gains_2, biases_2, up_bias_2) = own, other
    return dict(
        own_gains=(gains, IN_VMEM),
        own_biases=(biases, IN_VMEM),
        own_up_bias=(up_bias, IN_VMEM),
        other_gains=(gains_2, IN_VMEM),
        other_biases=(biases_2, IN_VMEM),
        other_up_bias=(up_bias_2, IN_VMEM),
    )


def load_smalls(k, mine):
    return Smalls(
        (k.own_gains, k.own_biases, k.own_up_bias),
        (k.other_gains, k.other_biases, k.other_up_bias),
        (k.gains, k.biases, k.up_bias),
        mine,
    )


def own_ins(own):
    time, time_out, time_fc, space, space_out, up, down = own
    return dict(
        own_time=(time, IN_HBM),
        own_time_out=(time_out, IN_HBM),
        own_time_fc=(time_fc, IN_HBM),
        own_space=(space, IN_HBM),
        own_space_out=(space_out, IN_HBM),
        own_up=(up, IN_HBM),
        own_down=(down, IN_HBM),
    )


def other_refs(other):
    time, time_out, time_fc, space, space_out, up, down = other
    return dict(
        other_time=(time, IN_HBM),
        other_time_out=(time_out, IN_HBM),
        other_time_fc=(time_fc, IN_HBM),
        other_space=(space, IN_HBM),
        other_space_out=(space_out, IN_HBM),
        other_up=(up, IN_HBM),
        other_down=(down, IN_HBM),
    )


MESH = pl.DeviceIdType.MESH
BIAS, UP, LOW = 3, 14, 24


class Named:
    def __init__(self, names, refs):
        self.__dict__.update(zip(names, refs, strict=True))


def named_call(kernel, name, flops, ins, outs, scratch, remote):
    names = [*ins, *outs, *scratch]
    if remote:
        NEXT_ID.append(NEXT_ID[-1] + 1)
    extra = dict(collective_id=NEXT_ID[-1], has_side_effects=True) if remote else {}
    results = pl.pallas_call(
        lambda *refs: kernel(Named(names, refs)),
        out_shape=[value for value, _ in outs.values()],
        in_specs=[spec for _, spec in ins.values()],
        out_specs=[spec for _, spec in outs.values()],
        scratch_shapes=list(scratch.values()),
        compiler_params=pltpu.CompilerParams(vmem_limit_bytes=VMEM_BYTES, **extra),
        cost_estimate=pl.CostEstimate(flops=flops, bytes_accessed=60 << 20, transcendentals=0),
        name=name,
    )(*[value for value, _ in ins.values()])
    return dict(zip(outs, results))


class Begin:
    def __init__(self, k, patches):
        self.k, self.patches = k, patches
        self.count, self.me = lax.axis_size("seq"), lax.axis_index("seq")
        self.section = lax.axis_index("section")
        self.mate = {"section": 1 - self.section}
        self.first = [
            (k.own_time, k.other_time),
            (k.own_time_out, k.other_time_out),
            (k.own_time_fc, k.other_time_fc),
        ]
        self.then = [(k.own_space, k.other_space), (k.own_space_out, k.other_space_out)]
        self.last = [(k.own_up, k.other_up), (k.own_down, k.other_down)]
        self.smalls = [
            (k.own_gains, k.other_gains),
            (k.own_biases, k.other_biases),
            (k.own_up_bias, k.other_up_bias),
        ]
        self.pairs = self.first + self.then + self.last + self.smalls

    def over(self, at):
        source, target = self.pairs[at]
        return pltpu.make_async_remote_copy(
            source, target, self.k.over_send.at[at], self.k.over_recv.at[at], device_id=self.mate, device_id_type=MESH
        )

    def around(self, which, step):
        source, target = ((self.k.frame, self.k.x), (self.k.cot, self.k.cot_out))[which]
        rows = source.shape[0]
        at = which * (self.count - 1) + step - 1
        return pltpu.make_async_remote_copy(
            source,
            target.at[rows_at(self.me, rows)],
            self.k.send.at[at],
            self.k.recv.at[at],
            device_id={"seq": lax.rem(self.me + step, self.count)},
            device_id_type=MESH,
        )

    def pad_into(self, source, target):
        whole = self.patches // 16 * 16
        target[0:whole, :] = source[0:whole, :]
        if target.shape[0] > whole:
            rest = jnp.zeros((target.shape[0] - self.patches, source.shape[1]), BF)
            target[whole:, :] = jnp.concatenate([source[whole:, :], rest], axis=0)

    def begin(self, copies, mine):
        k = self.k
        loads = [
            pltpu.make_async_copy(source.at[self.section, 0], target, k.local.at[at])
            for at, (source, target) in enumerate(((k.tokens, k.raw), (k.cotangent, k.raw_cot)))
        ]
        for load in loads:
            load.start()
        barrier = pltpu.get_barrier_semaphore()
        pl.semaphore_signal(barrier, inc=1, device_id=self.mate, device_id_type=MESH)
        for step in range(1, self.count):
            at = {"seq": lax.rem(self.me + step, self.count)}
            pl.semaphore_signal(barrier, inc=1, device_id=at, device_id_type=MESH)
        loads[0].wait()
        self.pad_into(k.raw, k.frame)
        pl.semaphore_wait(barrier, self.count)
        for step in range(1, self.count):
            self.around(0, step).start()
        for at in (7, 8, 9, 0, 1, 2):
            self.over(at).start()
        loads[1].wait()
        self.pad_into(k.raw_cot, k.cot)
        rows = k.frame.shape[0]
        own = rows_at(self.me, rows)
        k.x[own, :] = k.frame[...]
        keep = pltpu.make_async_copy(k.cot, k.cot_out.at[own], k.local.at[2])
        keep.start()
        loads = [self.fetch(copies, at, target, mine) for at, target in enumerate((k.time, k.time_out, k.time_fc))]
        self.next((0, 1, 2), (3, 4))
        for at in (7, 8, 9):
            self.over(at).wait()
        for step in range(1, self.count):
            self.around(0, step).wait()
        for step in range(1, self.count):
            self.around(1, step).start()
        keep.wait()
        return loads

    def next(self, done, then):
        for at in done:
            self.over(at).wait_send()
        for at in then:
            self.over(at).start()

    def fetch(self, copies, at, target, mine):
        own, other = self.pairs[at]

        @pl.when(jnp.logical_not(mine))
        def _():
            self.over(at).wait_recv()

        return copies.fetch(own, other, target, mine)

    def end(self, mine):
        for at in (5, 6):
            self.over(at).wait_send()

        @pl.when(mine)
        def _():
            for at in range(7):
                self.over(at).wait_recv()

        for step in range(1, self.count):
            self.around(1, step).wait()


def forward_kernel(block, frames, patches, k):
    total, width = k.x.shape
    rows = total // frames
    copies = Copies(k.sems)
    mine = lax.axis_index("section") == block
    fill_heads(k.heads, k.heads_t)
    fill_units(k.unit, k.pair_unit)
    if block == 0:
        start = Begin(k, patches)
        load_time, load_time_out, load_time_fc = start.begin(copies, mine)
        copies.store(k.x, k.r_x)
        fetch = functools.partial(start.fetch, copies, mine=mine)
    else:
        load_x = copies.start(k.x_in, k.x)
        pairs = (
            (k.own_time, k.other_time),
            (k.own_time_out, k.other_time_out),
            (k.own_time_fc, k.other_time_fc),
            (k.own_space, k.other_space),
            (k.own_space_out, k.other_space_out),
            (k.own_up, k.other_up),
            (k.own_down, k.other_down),
        )

        def fetch(at, target):
            return copies.fetch(*pairs[at], target, mine)

    if block == 1:
        load_time = fetch(0, k.time)
    smalls = load_smalls(k, mine)
    if block == 1:
        load_x.wait()
    norm_into(k.x, k.normed_t, smalls.gain(0), smalls.bias(0), CHUNK)
    copies.store(k.normed_t, k.r_normed_t)
    load_time.wait()
    if block == 1:
        load_time_out, load_time_fc = fetch(1, k.time_out), fetch(2, k.time_fc)
    project(k.normed_t, k.time, (smalls.bias(1), None, smalls.bias(2)), k.qkv_t)
    copies.store(k.qkv_t, k.r_qkv_t)
    load_space, load_space_out = fetch(3, k.space), fetch(4, k.space_out)
    if block == 0:
        start.next((3, 4), (5, 6))
    time_attention(k.qkv_t, k.attn_t, k.probs, k.stage, k.soft, k.heads, k.heads_t, k.clips, frames, rows, width)
    copies.store(k.attn_t, k.r_attn_t)
    copies.store(k.probs, k.r_probs)
    load_time_out.wait()
    k.proj[...] = (nn(k.attn_t[...], k.time_out[...]) + smalls.bias(3)[...]).astype(BF)
    copies.store(k.proj, k.r_proj)
    load_time_fc.wait()
    k.x1[...] = k.x[...].astype(F32) + nn(k.proj[...], k.time_fc[...]) + smalls.bias(4)[...]
    copies.store(k.x1, k.r_x1)
    if block == 1:
        load_up, load_down = fetch(5, k.up), fetch(6, k.down)
    norm_into(k.x1, k.normed_s, smalls.gain(1), smalls.bias(5), CHUNK)
    copies.store(k.normed_s, k.r_normed_s)
    load_space.wait()
    project(k.normed_s, k.space, (smalls.bias(6), None, smalls.bias(7)), k.qkv_s)
    copies.store(k.qkv_s, k.r_qkv_s)
    space_attention(
        k.qkv_s, k.attn_s, k.logs, k.values_t, k.mixed_t, k.unit, k.pair_unit, frames, rows, patches, width
    )
    copies.store(k.attn_s, k.r_attn_s)
    copies.store(k.logs, k.r_logs)
    load_space_out.wait()
    if block == 0:
        load_up, load_down = fetch(5, k.up), fetch(6, k.down)
    k.x2[...] = k.x1[...] + nn(k.attn_s[...], k.space_out[...]) + smalls.bias(8)[...]
    copies.store(k.x2, k.r_x2)
    norm_into(k.x2, k.normed_m, smalls.gain(2), smalls.bias(9), CHUNK)
    copies.store(k.normed_m, k.r_normed_m)
    load_up.wait()

    for tile in range(k.up.shape[1] // width):
        at = slice(tile * width, (tile + 1) * width)
        pre = nn(k.normed_m[...], k.up[:, at]) + smalls.up_bias[:, at]
        both = gelu_both(pre)
        k.act[:, at] = both[0].astype(BF)
        k.slope[:, at] = both[1].astype(BF)
        copies.store(k.act.at[:, at], k.r_act.at[:, at])
        copies.store(k.slope.at[:, at], k.r_slope.at[:, at])

    load_down.wait()

    @pl.loop(0, 3)
    def _(tile):
        at = rows_at(tile, width // 3)
        y_at = nn(k.act[...], k.down[:, at]) + smalls.biases[10:11, at] + k.x2[:, at]
        k.y[:, at] = y_at.astype(BF)

    copies.store(k.y, k.y_out)
    if block == 0:
        start.end(mine)
    copies.finish()


def forward(block, frames, patches, clips, small, small_other, own, other, x=None, tokens=None, cotangent=None):
    width, hidden = own[5].shape
    rows = -(-patches // 16) * 16
    total = frames * rows
    wide, full, triple = struct((total, width)), struct((total, width), F32), struct((total, 3 * width))
    deep, few = struct((total, hidden)), struct((total, PAIR))
    logs, probs = struct((frames * H, rows), F32), struct((frames, total, PAIR), F32)
    lie = lambda **structs: {name: (s, IN_HBM) for name, s in structs.items()}
    ins = dict(clips=(clips, IN_SMEM), **own_ins(own))
    outs = lie(y_out=wide, r_qkv_t=triple, r_attn_t=wide, r_proj=wide, r_x1=full, r_probs=probs, r_normed_t=wide)
    outs |= lie(r_qkv_s=triple, r_attn_s=wide, r_x2=full, r_act=deep, r_slope=deep, r_normed_s=wide, r_normed_m=wide)
    outs |= lie(r_logs=logs)
    square, third = struct((width, width)), struct((width, 3 * width))
    scratch = vmem(time=third, time_out=square, time_fc=square, space=third, space_out=square)
    scratch |= vmem(up=struct((width, hidden)), down=struct((hidden, width)), x=wide, normed_t=wide, stage=wide)
    scratch |= vmem(qkv_t=triple, attn_t=wide, proj=wide, x1=full, probs=probs, soft=few, normed_s=wide, qkv_s=triple)
    scratch |= vmem(attn_s=wide, logs=logs, x2=full, normed_m=wide, act=deep, slope=deep, y=wide)
    scratch |= vmem(values_t=struct((H * (HD + 16), rows)), mixed_t=struct((width, rows)), unit=struct((rows, rows)))
    scratch |= vmem(pair_unit=struct((PAIR, PAIR)), heads=struct((width, PAIR)), heads_t=struct((PAIR, width)))
    scratch |= small_held(width, hidden)
    dma = pltpu.SemaphoreType.DMA
    scratch |= dict(sems=dma((40,)))
    if block == 0:
        gains, biases, up_bias = small
        ins |= dict(tokens=(tokens, IN_HBM), cotangent=(cotangent, IN_HBM))
        ins |= dict(own_gains=(gains, IN_VMEM), own_biases=(biases, IN_VMEM), own_up_bias=(up_bias, IN_VMEM))
        outs |= other_refs([struct(array.shape) for array in own])
        like = [struct(array.shape, F32) for array in small]
        outs |= dict(other_gains=(like[0], IN_VMEM), other_biases=(like[1], IN_VMEM), other_up_bias=(like[2], IN_VMEM))
        outs |= lie(cot_out=wide, r_x=wide)
        raw, frame = struct((patches, width)), struct((rows, width))
        scratch |= vmem(raw=raw, raw_cot=raw, frame=frame, cot=frame)
        scratch |= dict(send=dma((2 * frames,)), recv=dma((2 * frames,)), over_send=dma((10,)), over_recv=dma((10,)))
        scratch |= dict(local=dma((3,)))
    else:
        ins |= dict(x_in=(x, IN_HBM), **other_refs(other), **small_ins(small, small_other))
    kernel = functools.partial(forward_kernel, block, frames, patches)
    return named_call(kernel, f"block{block}_forward", 34 * total * width * width, ins, outs, scratch, block == 0)


def beside(z):
    return z + 1 - 2 * lax.rem(z, 2), lax.rem(z + 2, 4)


def greet():
    barrier = pltpu.get_barrier_semaphore()
    z = lax.axis_index("dp")
    pl.semaphore_signal(barrier, inc=1, device_id={"section": 1 - lax.axis_index("section")}, device_id_type=MESH)
    for step in range(1, 4):
        pl.semaphore_signal(barrier, inc=1, device_id={"dp": lax.rem(z + step, 4)}, device_id_type=MESH)
    pl.semaphore_wait(barrier, 4)


class Relay:
    def __init__(self, block, mine, mates, taken, send, recv, source=None, direct=False):
        self.mine, self.mates, self.taken, self.send, self.recv = mine, mates, taken, send, recv
        self.source, self.direct = source, direct
        self.z = lax.axis_index("dp")
        self.near, self.far = beside(self.z)
        self.section = lax.axis_index("section")
        self.home = self.section == block
        self.away = self.section != block

    def parts(self):
        if self.direct:
            return tuple(lax.rem(self.z + step, 4) for step in (2, 1, 3, 0))
        return lax.rem(self.near + 2, 4), self.near, self.far, self.z

    def mate(self, part):
        if len(self.mates.shape) == 3:
            return self.mates.at[part]
        return self.mates.at[rows_at(part, self.mine.shape[1])]

    def over(self, at):
        part = self.parts()[at]
        return pltpu.make_async_remote_copy(
            (self.mine if self.source is None else self.source).at[part],
            self.mate(part),
            self.send.at[3 + at],
            self.recv.at[3 + at],
            device_id={"section": 1 - self.section},
            device_id_type=MESH,
        )

    def local(self):
        return pltpu.make_async_copy(self.source, self.mine, self.send.at[7])

    def along(self, step):
        part = self.parts()[step]
        return pltpu.make_async_remote_copy(
            self.mine.at[part],
            self.taken.at[step],
            self.send.at[step],
            self.recv.at[step],
            device_id={"dp": part if self.direct else self.far if step == 2 else self.near},
            device_id_type=MESH,
        )

    def begin(self):
        @pl.when(self.away)
        def _():
            for at in range(4):
                self.over(at).start()

        if self.source is not None:

            @pl.when(self.home)
            def _():
                self.local().start()

    def middle(self):
        @pl.when(self.home)
        def _():
            if self.source is not None:
                self.local().wait()
            for at, part in enumerate(self.parts()):
                self.over(at).wait_recv()
                self.mine[part] = (self.mine[part].astype(F32) + self.mate(part)[...].astype(F32)).astype(BF)
                if at < (3 if self.direct else 2):
                    self.along(at).start()

        @pl.when(self.away)
        def _():
            for at in range(4):
                self.over(at).wait_send()

    def second(self):
        @pl.when(self.home)
        def _():
            self.along(0).wait()
            self.mine[self.far] = (self.mine[self.far].astype(F32) + self.taken[0].astype(F32)).astype(BF)
            self.along(2).start()

    def end(self, staged, out, sem):
        self.store = pltpu.make_async_copy(staged, out, sem)

        @pl.when(self.home)
        def _():
            self.along(1).wait()
            total = self.mine[self.z].astype(F32) + self.taken[1].astype(F32)
            if self.direct:
                self.along(0).wait()
                total = total + self.taken[0].astype(F32)
            self.along(2).wait()
            staged[...] = total + self.taken[2].astype(F32)
            self.store.start()

    def settle(self):
        pl.when(self.home)(self.store.wait)


class LowRelay:
    def __init__(self, lows, out, scratch):
        self.lows, self.out = lows, out
        self.mine, self.mate, self.taken, self.send, self.recv = scratch
        self.places = beside(lax.axis_index("dp"))
        self.section = lax.axis_index("section")

    def over(self, low):
        return pltpu.make_async_remote_copy(
            low,
            self.mate,
            self.send.at[0],
            self.recv.at[0],
            device_id={"section": 1 - self.section},
            device_id_type=MESH,
        )

    def along(self, step):
        return pltpu.make_async_remote_copy(
            self.mine.at[step],
            self.taken.at[step],
            self.send.at[1 + step],
            self.recv.at[1 + step],
            device_id={"dp": self.places[step]},
            device_id_type=MESH,
        )

    def begin(self):
        for block, low in enumerate(self.lows):

            @pl.when(self.section != block)
            def _(low=low):
                self.over(low).start()

    def at_home(self, act):
        if len(self.lows) == 2:
            act()
        else:
            pl.when(self.section == 0)(act)

    def middle(self):
        for block, low in enumerate(self.lows):

            @pl.when(self.section == block)
            def _(low=low):
                self.over(low).wait_recv()
                self.mine[0] = low[...] + self.mate[...]
                self.along(0).start()

            @pl.when(self.section != block)
            def _(low=low):
                self.over(low).wait_send()

    def second(self):
        def _():
            self.along(0).wait()
            self.mine[1] = self.mine[0] + self.taken[0]
            self.along(1).start()

        self.at_home(_)

    def end(self):
        def _():
            self.along(1).wait()
            self.out[...] = self.mine[1] + self.taken[1]

        self.at_home(_)
        if len(self.lows) == 1:

            @pl.when(self.section != 0)
            def _():
                self.out[...] = jnp.zeros_like(self.out)


class LateRelay:
    def __init__(self, low, out, mine, mate, taken, send, recv):
        self.low, self.out, self.mine, self.mate, self.taken, self.send, self.recv = low, out, mine, mate, taken, send, recv
        self.z = lax.axis_index("dp")
        self.section = lax.axis_index("section")

    def over(self):
        return pltpu.make_async_remote_copy(
            self.low,
            self.mate,
            self.send.at[3],
            self.recv.at[3],
            device_id={"section": 1 - self.section},
            device_id_type=MESH,
        )

    def along(self, step):
        return pltpu.make_async_remote_copy(
            self.mine,
            self.taken.at[step],
            self.send.at[step],
            self.recv.at[step],
            device_id={"dp": lax.rem(self.z + 1 + step, 4)},
            device_id_type=MESH,
        )

    def begin(self):
        pl.when(self.section == 1)(lambda: self.over().start())

    def middle(self):
        @pl.when(self.section == 0)
        def _():
            self.over().wait_recv()
            self.mine[...] = self.low[...] + self.mate[...]
            for step in range(3):
                self.along(step).start()

        @pl.when(self.section == 1)
        def _():
            self.over().wait_send()
            self.out[...] = jnp.zeros_like(self.out)

    def end(self):
        @pl.when(self.section == 0)
        def _():
            total = self.mine[...]
            for step in range(3):
                self.along(step).wait()
                total = total + self.taken[step]
            self.out[...] = total


def norm_back(hidden, grads, gain, above, target, low_target, sums, beside=()):
    width = hidden.shape[1]
    lots = 4
    chunk = hidden.shape[0] // lots

    def fold(rows):
        return jnp.sum(rows.reshape(chunk // 8, 8, width), axis=0)

    def lot(step, at):
        hat, scale = norm_stats(hidden[at, :].astype(F32))
        grad = grads[at, :]
        sums[0:8, :] += fold(grad * hat)
        sums[8:16, :] += fold(grad)
        inner = grad * gain[...]
        mean = jnp.mean(inner, axis=-1, keepdims=True)
        slant = jnp.mean(inner * hat, axis=-1, keepdims=True)
        result = above[at, :].astype(F32) + scale * (inner - mean - hat * slant)
        if target is not None:
            target[at, :] = result
        low_target[at, :] = result.astype(BF)

    sums[...] = jnp.zeros_like(sums)
    if beside:
        for step in range(lots):
            lot(step, slice(step * chunk, (step + 1) * chunk))
            for work in beside[step : step + 1]:
                work()
    else:
        pl.loop(0, lots)(lambda step: lot(step, rows_at(step, chunk)))


def norm_sums(sums, low, gain_row, bias_row):
    low[gain_row : gain_row + 1, :] = jnp.sum(sums[0:8, :], axis=0, keepdims=True)
    low[BIAS + bias_row : BIAS + bias_row + 1, :] = jnp.sum(sums[8:16, :], axis=0, keepdims=True)


def fill_ones(turned, count):
    turned[pl.ds(count, 16), :] = jnp.ones((16, turned.shape[1]), BF)


def weight_grad(turned, count, grads, result, row, low, *low_rows):
    width = low.shape[1]
    parts = result.shape[0]
    each = count // parts

    def step_of(step, low_row):
        both = nn(turned[0 : count + 16, :], grads[:, step * width : (step + 1) * width])
        at = slice(row + step * each, row + (step + 1) * each)
        for part in range(parts):
            result[part, at, :] = both[part * each : (part + 1) * each].astype(BF)
        if low_row is not None:
            low[low_row : low_row + 1, :] = both[count : count + 1, :]

    return [functools.partial(step_of, step, low_row) for step, low_row in enumerate(low_rows)]


def do(steps):
    for step in steps:
        step()


def tiled_nt(left, right, target, tile):
    @pl.loop(0, right.shape[0] // tile)
    def _(step):
        at = rows_at(step, tile)
        target[:, at] = nt(left[...], right[at, :])


def space_attention_back(
    qkv, grads, logs, result, keys_t, turned_t, unit, pair_unit, frames, rows, patches, width
):
    low_lane = lax.broadcasted_iota(jnp.int32, (rows, PAIR), 1) < HD

    @pl.loop(0, frames)
    def _(f):
        at = rows_at(f, rows)
        for pair in range(width // PAIR):
            lanes = slice(width + pair * PAIR, width + (pair + 1) * PAIR)
            keys_t[pair * PAIR : (pair + 1) * PAIR, :] = nt(pair_unit[...], qkv[at, lanes]).astype(BF)

        @pl.loop(0, width // PAIR // GROUP_BACK)
        def _(group):
            def lanes(which, member):
                pair = group * GROUP_BACK + member
                return pl.ds(pl.multiple_of(which * width + pair * PAIR, PAIR), PAIR)

            scores, grad_softs = [], []
            for member in range(GROUP_BACK):
                query = qkv[at, lanes(0, member)] * BF(HD**-0.5)
                key, value, grad = qkv[at, lanes(1, member)], qkv[at, lanes(2, member)], grads[at, lanes(0, member)]
                for half in range(2):
                    mine = low_lane if half == 0 else ~low_lane
                    scores.append(nt(jnp.where(mine, key, BF(0)), query))
                    grad_softs.append(nt(jnp.where(mine, value, BF(0)), grad))
            softs, grad_scores = [], []
            for member, (score, grad_soft) in enumerate(zip(scores, grad_softs)):
                head = group * (2 * GROUP_BACK) + member
                log = logs[pl.ds(f * H + head, 1), :]
                soft = [jnp.exp(part - log) for part in split_patches(score, patches)]
                cut = soft[0].shape[0]
                changes = [grad_soft[:cut], grad_soft[cut:]][: len(soft)]
                slant = sum(jnp.sum(part * change, axis=0, keepdims=True) for part, change in zip(soft, changes))
                changes = [change - slant for change in changes]
                softs.append(jnp.concatenate([part.astype(BF) for part in soft], axis=0))
                grad_scores.append(
                    jnp.concatenate([(part * change).astype(BF) for part, change in zip(soft, changes)], axis=0)
                )
            for member in range(GROUP_BACK):
                query = qkv[at, lanes(0, member)] * BF(HD**-0.5)
                grad = grads[at, lanes(0, member)]
                pair = 2 * member
                grad_key = [nn(grad_scores[pair + half], query) for half in range(2)]
                grad_value = [nn(softs[pair + half], grad) for half in range(2)]
                result[at, lanes(1, member)] = jnp.where(low_lane, *grad_key).astype(BF)
                result[at, lanes(2, member)] = jnp.where(low_lane, *grad_value).astype(BF)
                for half in range(2):
                    head = group * (2 * GROUP_BACK) + pair + half
                    own = pl.ds(pl.multiple_of(head * HD, HD), HD)
                    turned_t[own, :] = (nn(keys_t[own, :], grad_scores[pair + half]) * HD**-0.5).astype(BF)

        result[at, 0:width] = nt(unit[...], turned_t[...]).astype(BF)


def time_attention_back(qkv, grads, probs, result, stage, soft, soft_grad, grad_key, grad_value, heads, heads_t, frames, rows, width, between):
    grad_key[...] = jnp.zeros_like(grad_key)
    grad_value[...] = jnp.zeros_like(grad_value)

    @pl.loop(0, frames)
    def _(i):
        between(i)
        own = rows_at(i, rows)
        for j in range(frames):
            stage[pl.ds(j * rows, rows), :] = grads[own, :] * qkv[pl.ds(j * rows, rows), 2 * width : 3 * width]
        grad_soft = nn(stage[...], heads[...]) * HD**0.5
        parts = [probs[i, pl.ds(j * rows, rows), :] for j in range(frames)]
        changes = [grad_soft[j * rows : (j + 1) * rows] for j in range(frames)]
        total = sum(part * change for part, change in zip(parts, changes))
        for j in range(frames):
            at = pl.ds(j * rows, rows)
            soft[at, :] = parts[j].astype(BF)
            soft_grad[at, :] = (parts[j] * (changes[j] - total)).astype(BF)
        grad_query = None
        for j in range(frames):
            at = pl.ds(j * rows, rows)
            wide = nn(soft_grad[at, :], heads_t[...])
            term = wide * qkv[at, width : 2 * width].astype(F32)
            grad_query = term if grad_query is None else grad_query + term
            grad_key[at, :] += wide * qkv[own, 0:width].astype(F32)
            grad_value[at, :] += nn(soft[at, :], heads_t[...]) * grads[own, :].astype(F32)
        result[own, 0:width] = (grad_query * HD**-0.5).astype(BF)

    result[:, width : 2 * width] = (grad_key[...] * HD**-0.5).astype(BF)
    result[:, 2 * width : 3 * width] = grad_value[...].astype(BF)


def back_kernel(block, parts, places, patches, k):
    total, width = k.grads.shape
    hidden = k.act.shape[1]
    frames = k.probs.shape[0]
    rows = total // frames
    deep = hidden // width
    copies = Copies(k.sems)
    section, place = lax.axis_index("section"), lax.axis_index("seq")
    mine = section == block
    last = block == 0
    columns = lambda tile, count=1: slice(tile * width, (tile + count) * width)

    greet()
    load_gy = copies.start(k.gy_in, k.low_grads)
    tiles = []
    for tile in range(deep):
        at = pl.ds(tile * width, width)
        tiles.append(copies.fetch(k.own_down.at[at], k.other_down.at[at], k.down.at[at], mine))
        tiles.append(copies.start(k.r_slope.at[:, at], k.gpre.at[:, at]))
    carried = []
    if last:
        relay = Relay(1, k.last_mine, k.last_mates, k.last_taken, k.last_send, k.last_recv, k.last_in, True)
        relay.begin()
        carried.append(relay)
        swaps = Swaps(k)
        swaps.begin()
    smalls = load_smalls(k, mine)
    fill_pick(k.pick, parts, place, places)
    fill_pick(k.pick_wide, 1, place, places)
    fill_units(k.unit, k.pair_unit)
    fill_heads(k.heads, k.heads_t)
    low = k.low
    low[...] = jnp.zeros_like(low)
    count = k.pick.shape[0]
    each = count // parts
    wide = k.pick_wide.shape[0]

    def turn(source):
        k.turned[0:count, :] = nt(k.pick[...], source).astype(BF)

    load_gy.wait()
    for tile in range(deep):
        tiles[2 * tile].wait()
        tiles[2 * tile + 1].wait()
        if tile == 1:
            load_act = copies.start(k.r_act, k.act)
            load_up = copies.fetch(k.own_up, k.other_up, k.up, mine)
            load_normed = copies.start(k.r_normed_m, k.normed)
            load_x2 = copies.start(k.r_x2, k.hidden)
        at = columns(tile)
        k.gpre[:, at] = (nt(k.low_grads[...], k.down[at, :]) * k.gpre[:, at].astype(F32)).astype(BF)
    load_space_out = copies.fetch(k.own_space_out, k.other_space_out, k.down.at[columns(3)], mine)
    load_space = [
        copies.fetch(k.own_space.at[:, columns(part)], k.other_space.at[:, columns(part)], k.down.at[columns(part)], mine)
        for part in range(3)
    ]
    for relay in carried:
        relay.middle()
    load_act.wait()
    for part in range(parts):
        at = slice(part * wide, (part + 1) * wide)
        k.turned[at, :] = nt(k.pick_wide[...], k.act[:, part * (hidden // parts) : (part + 1) * (hidden // parts)]).astype(BF)
    fill_ones(k.turned, parts * wide)
    do(weight_grad(k.turned, parts * wide, k.low_grads, k.mlp, deep * each, low, BIAS + 10))
    half = deep * each
    small_part = slice(half, k.mlp.shape[1])
    mates = (k.spare.at[0 : parts * half], k.spare.at[parts * half : parts * k.mlp.shape[1]])
    down = Relay(block, k.mlp.at[:, small_part], mates[1], k.mlp_taken.at[:, small_part], k.down_send, k.down_recv)
    down.begin()
    load_qkv = copies.start(k.r_qkv_s, k.act.at[:, columns(0, 3)])
    load_logs = copies.start(k.r_logs, k.logs)
    load_up.wait()
    tiled_nt(k.gpre, k.up, k.gnorm, width // 3)
    load_time = copies.fetch(k.own_time, k.other_time, k.up.at[:, columns(0, 3)], mine)
    load_time_out = copies.fetch(k.own_time_out, k.other_time_out, k.up.at[:, columns(3)], mine)
    down.middle()
    load_normed.wait()
    turn(k.normed[...])
    fill_ones(k.turned, count)
    steps = weight_grad(k.turned, count, k.gpre, k.mlp, 0, low, *range(UP, UP + deep))
    load_normed = copies.start(k.r_normed_s, k.normed)
    load_x2.wait()
    do(steps)
    mlp = Relay(block, k.mlp.at[:, 0:half], mates[0], k.mlp_taken.at[:, 0:half], k.mlp_send, k.mlp_recv)
    mlp.begin()
    norm_back(k.hidden, k.gnorm, smalls.gain(2), k.low_grads, k.grads, k.low_grads, k.sums)
    load_attn = copies.start(k.r_attn_s, k.attn)
    down.second()
    load_x1 = copies.start(k.r_x1, k.hidden)
    norm_sums(k.sums, low, 2, 9)

    load_space_out.wait()
    k.gattn[...] = nt(k.low_grads[...], k.down[columns(3), :]).astype(BF)
    load_time_fc = copies.fetch(k.own_time_fc, k.other_time_fc, k.down.at[columns(3)], mine)
    load_attn.wait()
    turn(k.attn[...])
    do(weight_grad(k.turned, count, k.low_grads, k.space, 3 * each, low, BIAS + 8))
    mlp.middle()
    load_attn = copies.start(k.r_attn_t, k.attn)
    proj, stage = k.spare.at[0:total], k.spare.at[total : 2 * total]
    load_qkv.wait()
    load_logs.wait()
    qkv, gqkv = k.act.at[:, columns(0, 3)], k.gpre.at[:, columns(0, 3)]
    space_attention_back(
        qkv, k.gattn, k.logs, gqkv, k.keys_t, k.turned_t, k.unit, k.pair_unit, frames, rows, patches, width,
    )
    mlp.second()
    load_proj = copies.start(k.r_proj, proj)
    load_qkv = copies.start(k.r_qkv_t, qkv)
    load_probs = copies.start(k.r_probs, k.probs)
    for load in load_space:
        load.wait()
    load_normed.wait()
    turn(k.normed[...])
    steps = weight_grad(k.turned, count, gqkv, k.space, 0, low, BIAS + 6, None, BIAS + 7)
    space = Relay(block, k.space, k.space_mates, k.space_taken, k.space_send, k.space_recv)

    @pl.loop(0, 3)
    def _(tile):
        size = width // 3
        result = None
        for part in range(3):
            at = pl.ds(pl.multiple_of(part * width + tile * size, size), size)
            term = nt(gqkv[:, columns(part)], k.down[at, :])
            result = term if result is None else result + term
        k.gnorm[:, rows_at(tile, size)] = result

    load_x1.wait()
    norm_back(k.hidden, k.gnorm, smalls.gain(1), k.grads, k.grads, k.low_grads, k.sums, steps)
    space.begin()
    norm_sums(k.sums, low, 1, 5)
    if last:
        k.low_early[...] = low[...]
        k.low_early[0:8, :] = jnp.zeros((8, width), F32)
        early = LowRelay(
            [k.low_early, k.low_in], k.low_sum, (k.low_mine, k.low_mate, k.low_taken, k.low_send, k.low_recv)
        )
        early.begin()

    load_time_fc.wait()
    k.normed[...] = nt(k.low_grads[...], k.down[columns(3), :]).astype(BF)
    load_proj.wait()
    turn(proj[...])
    do(weight_grad(k.turned, count, k.low_grads, k.time, 4 * each, low, BIAS + 4))
    load_time_out.wait()
    k.gattn[...] = nt(k.normed[...], k.up[:, columns(3)]).astype(BF)
    space.middle()
    if last:
        early.middle()
    load_attn.wait()
    turn(k.attn[...])
    do(weight_grad(k.turned, count, k.normed, k.time, 3 * each, low, BIAS + 3))
    load_normed = copies.start(k.r_normed_t, k.normed)
    load_x = copies.start(k.r_x, k.attn)
    outs = Relay(
        block, k.time.at[:, 3 * each : 5 * each], k.outs_mates, k.outs_taken, k.outs_send, k.outs_recv, None, True
    )
    outs.begin()
    load_qkv.wait()
    load_probs.wait()

    def between(step):
        pl.when(step == 1)(outs.middle)
        pl.when(step == 3)(space.second)

    time_attention_back(
        qkv, k.gattn, k.probs, gqkv, stage, k.soft, k.soft_grad, k.gnorm, k.hidden, k.heads, k.heads_t, frames, rows,
        width, between,
    )
    if last:
        early.second()
    done = []

    def end(relay, out):
        start = sum(size for _, size in done)
        size = out.shape[0]
        relay.end(k.hidden.at[start : start + size], out, k.end_sems.at[len(done)])
        done.append((relay, size))

    load_normed.wait()
    turn(k.normed[...])
    steps = weight_grad(k.turned, count, gqkv, k.time, 0, low, BIAS + 1, None, BIAS + 2)
    qkv_part = k.time.at[:, 0 : 3 * each]
    if last:
        do(steps)
        final = Relay(0, qkv_part, k.qkv_mates, k.qkv_taken, k.qkv_send, k.qkv_recv, None, True)
        final.begin()
        end(down, k.mlp_out.at[half : k.mlp.shape[1]])
        end(mlp, k.mlp_out.at[0:half])
        final.middle()
    load_time.wait()
    tiled_nt(gqkv, k.up.at[:, columns(0, 3)], k.gnorm, width // 3)
    load_x.wait()
    norm_back(k.attn, k.gnorm, smalls.gain(0), k.grads, None, k.gattn, k.sums, () if last else steps)
    norm_sums(k.sums, low, 0, 0)
    if last:
        late = LateRelay(low.at[0:8], k.low_last, k.late_mine, k.late_mate, k.late_taken, k.late_send, k.late_recv)
        late.begin()
        swaps.late()
    copies.store(k.gattn, k.gx_out)
    if last:
        end(carried[0], k.last_out)
        late.middle()
    else:
        copies.store(qkv_part, k.last_out)
        end(down, k.mlp_out.at[half : k.mlp.shape[1]])
        end(mlp, k.mlp_out.at[0:half])
    end(space, k.space_out)
    end(outs, k.outs_out)
    if last:
        early.end()
        swaps.end()
        start = k.mlp.shape[1]
        final.end(k.hidden.at[start : start + 3 * each], k.qkv_out, k.end_sems.at[len(done)])
        done.append((final, 0))
        late.end()
    for relay, _ in done:
        relay.settle()
    copies.finish()


class Swaps:
    def __init__(self, k):
        self.k = k
        self.section = lax.axis_index("section")
        rows = k.swapped.shape[1]
        self.own = rows_at(lax.axis_index("seq"), rows)

    def over(self, which, source):
        return pltpu.make_async_remote_copy(
            source.at[self.own],
            self.k.swapped.at[which],
            self.k.swap_send.at[which],
            self.k.swap_recv.at[which],
            device_id={"section": 1 - self.section},
            device_id_type=MESH,
        )

    def begin(self):
        @pl.when(self.section == 0)
        def _():
            self.over(0, self.k.y1_in).start()
            self.over(1, self.k.gy_in).start()

        @pl.when(self.section == 1)
        def _():
            self.over(0, self.k.y0_in).start()

    def late(self):
        @pl.when(self.section == 1)
        def _():
            self.over(1, self.k.gattn).start()

    def end(self):
        self.over(0, self.k.y1_in).wait()
        self.over(1, self.k.gy_in).wait()


def back(block, parts, places, patches, gy, small, small_other, own, other, kept, last=None, low=None, outputs=None):
    total, width = gy.shape
    hidden = own[5].shape[1]
    logs, probs = kept["r_logs"], kept["r_probs"]
    rows = logs.shape[1]
    count = width // places
    each = count // parts
    deep = hidden // width
    dma = pltpu.SemaphoreType.DMA
    wide, full, deepest = struct((total, width)), struct((total, width), F32), struct((total, hidden))
    few, lowest = struct((total, PAIR)), struct((LOW, width), F32)
    piece = lambda height, n=parts: struct((n, height, width))
    mlp, space, time = deep * each + hidden // places // parts, 4 * each, 5 * each
    ins = dict(gy_in=(gy, IN_HBM), **small_ins(small, small_other), **own_ins(own), **other_refs(other))
    ins |= {name: (array, IN_HBM) for name, array in kept.items()}
    summed = lambda height: (struct((height, width), F32), IN_HBM)
    outs = dict(gx_out=(wide, IN_HBM), low=(lowest, IN_VMEM))
    outs |= dict(mlp_out=summed(mlp), space_out=summed(space), outs_out=summed(2 * each))
    scratch = vmem(up=struct((width, hidden)), down=struct((hidden, width)), gpre=deepest, act=deepest)
    scratch |= vmem(grads=full, hidden=full, gnorm=full, low_grads=wide, normed=wide, attn=wide, gattn=wide)
    scratch |= vmem(spare=struct((max(2 * total, parts * mlp), width)), soft=few, soft_grad=few)
    scratch |= vmem(probs=struct(probs.shape, F32), logs=struct(logs.shape, F32), unit=struct((rows, rows)))
    scratch |= vmem(pair_unit=struct((PAIR, PAIR)), keys_t=struct((width, rows)), turned_t=struct((width, rows)))
    scratch |= vmem(heads=struct((width, PAIR)), heads_t=struct((PAIR, width)), pick=struct((count, width)))
    scratch |= vmem(turned=struct((hidden // places + 16, total)), sums=struct((16, width), F32))
    scratch |= vmem(pick_wide=struct((hidden // parts // places, hidden // parts)))
    scratch |= vmem(mlp=piece(mlp), mlp_taken=piece(mlp, 3), space=piece(space), space_mates=piece(space))
    scratch |= vmem(space_taken=piece(space, 3), time=piece(time), outs_mates=piece(2 * each))
    scratch |= vmem(outs_taken=piece(2 * each, 3))
    scratch |= small_held(width, hidden)
    scratch |= dict(down_send=dma((8,)), down_recv=dma((7,)))
    scratch |= dict(mlp_send=dma((8,)), mlp_recv=dma((7,)), space_send=dma((8,)), space_recv=dma((7,)))
    scratch |= dict(outs_send=dma((8,)), outs_recv=dma((7,)), sems=dma((40,)), end_sems=dma((8,)))
    if block == 1:
        outs |= dict(last_out=(piece(3 * each), IN_HBM))
    else:
        y_0, y_1 = outputs
        ins |= dict(last_in=(last, IN_HBM), low_in=(low, IN_VMEM), y0_in=(y_0, IN_HBM), y1_in=(y_1, IN_HBM))
        outs |= dict(last_out=summed(3 * each), qkv_out=summed(3 * each), low_sum=(lowest, IN_VMEM))
        outs |= dict(low_last=(struct((8, width), F32), IN_VMEM))
        late, late_three = struct((8, width), F32), struct((3, 8, width), F32)
        scratch |= vmem(late_mine=late, late_mate=late, late_taken=late_three, low_early=lowest)
        scratch |= dict(late_send=dma((4,)), late_recv=dma((4,)))
        outs |= dict(swapped=(struct((2, rows, width)), IN_HBM))
        low_two, part = struct((2, LOW, width), F32), piece(3 * each)
        scratch |= vmem(last_mine=part, last_mates=part, last_taken=piece(3 * each, 3), qkv_mates=part)
        scratch |= vmem(qkv_taken=piece(3 * each, 3), low_mine=low_two, low_mate=lowest, low_taken=low_two)
        scratch |= dict(low_send=dma((3,)), low_recv=dma((3,)), swap_send=dma((2,)), swap_recv=dma((2,)))
        scratch |= dict(last_send=dma((8,)), last_recv=dma((7,)), qkv_send=dma((8,)), qkv_recv=dma((7,)))
    kernel = functools.partial(back_kernel, block, parts, places, patches)
    return named_call(kernel, f"block{block}_backward", 70 * total * width * width, ins, outs, scratch, True)
def layout_kernel(places, patches, pieces, rows_each, low_a, low_b, *refs):
    n = len(pieces)
    sums, refs = (refs[:n], refs[n : 2 * n]), refs[2 * n :]
    results, swapped, refs = refs[:4], refs[4], refs[5:]
    weights, lows, frames, refs = refs[:7], refs[7:10], refs[10:12], refs[12:]
    total, mine, sems = refs
    section = lax.axis_index("section")
    z, place = lax.axis_index("dp"), lax.axis_index("seq")
    rows, width = mine.shape[1:]
    loads = []
    for at, (start, count) in enumerate(pieces):
        for block in range(2):

            @pl.when(section == block)
            def _(at=at, block=block, start=start, count=count):
                pltpu.make_async_copy(sums[block][at], total.at[start : start + count], sems.at[at]).start()

        loads.append(pltpu.make_async_copy(sums[0][at], total.at[start : start + count], sems.at[at]))
    for which in range(2):
        own = rows_at(place, rows)
        for block in range(2):

            @pl.when(section == block)
            def _(which=which, block=block):
                pltpu.make_async_copy(results[2 * which + block].at[own], mine.at[which], sems.at[n + which]).start()

        loads.append(pltpu.make_async_copy(results[2 * which].at[own], mine.at[which], sems.at[n + which]))
        loads.append(pltpu.make_async_copy(swapped.at[which], mine.at[2 + which], sems.at[n + 2 + which]))
        loads[-1].start()
    part = z * lax.axis_size("seq") + place
    low = low_a[...]
    low = jnp.concatenate([low[0:8] + low_b[...], low[8:]], axis=0)
    for target, first, count in zip(lows, (0, BIAS, UP), (BIAS, UP - BIAS, target_rows(lows[2], places, width))):
        flat = jnp.concatenate([low[first + at : first + at + 1] for at in range(count)], axis=1)
        size = target.shape[1]
        flat = jnp.broadcast_to(flat, (8, flat.shape[1]))
        target[...] = pltpu.roll(flat, lax.rem(count * width - part * size, count * width), 1)[0:1, :size]
    for load in loads:
        load.wait()
    for which, target in enumerate(frames):
        for block in range(2):

            @pl.when(section == block)
            def _(which=which, target=target, block=block):
                target[:, block, :] = mine[which, 0:patches]
                target[:, 1 - block, :] = mine[2 + which, 0:patches]

    start = 0
    lanes = width // PAIR
    for target, count in zip(weights, rows_each):
        each = target.shape[0] // (count * lanes)
        for at in range(count):
            for lane in range(lanes):
                target[pl.ds(at * lanes + lane, each, stride=count * lanes), :] = total[
                    start + at * each : start + (at + 1) * each, lane * PAIR : (lane + 1) * PAIR
                ]
        start += count * each


def target_rows(target, places, width):
    return target.shape[1] * places // width


def layout(patches, places, width, hidden, pieces, sums, low, low_last, results, swapped):
    each = width // places
    deep = hidden // width
    rows_each = (3, 1, 1, 3, 1, deep, 1)
    heights = (each, each, each, each, each, each, hidden // places)
    outs = [struct((h * r * width // PAIR, PAIR), F32) for h, r in zip(heights, rows_each)]
    outs += [struct((1, rows * width // places), F32) for rows in (BIAS, UP - BIAS, deep)]
    outs += [struct((patches, 2, width))] * 2
    rows = swapped.shape[1]
    n = len(pieces)
    total = sum(count for _, count in pieces)
    scratch = held(struct((total, width), F32), struct((4, rows, width))) + [pltpu.SemaphoreType.DMA((n + 4,))]
    return pl.pallas_call(
        functools.partial(layout_kernel, places, patches, pieces, rows_each),
        out_shape=outs,
        in_specs=[IN_VMEM] * 2 + [IN_HBM] * (2 * n + 5),
        out_specs=[IN_VMEM] * len(outs),
        scratch_shapes=scratch,
        compiler_params=pltpu.CompilerParams(vmem_limit_bytes=VMEM_BYTES),
        name="lay_out",
    )(low, low_last, *sums[0], *sums[1], *results, swapped)


def shards(clip_ids, tokens, *rest):
    weights, small, cotangent = rest[:7], rest[7:10], rest[10]
    NEXT_ID[:] = [1]
    n_dp, n_seq = lax.axis_size("dp"), lax.axis_size("seq")
    patches, width = tokens.shape[2:]
    hidden = weights[5].shape[2]
    places = n_dp * n_seq
    small = [array.reshape(1, -1) for array in small]
    own = [array[0] for array in weights]

    first = forward(0, n_seq, patches, clip_ids, small, None, own, None, None, tokens, cotangent)
    y_0, grad_top, x = first.pop("y_out"), first.pop("cot_out"), first["r_x"]
    small_other = [first.pop("other_gains"), first.pop("other_biases"), first.pop("other_up_bias")]
    other = [first.pop("other_time"), first.pop("other_time_out"), first.pop("other_time_fc"), first.pop("other_space")]
    other += [first.pop("other_space_out"), first.pop("other_up"), first.pop("other_down")]
    common = (small, small_other, own, other)
    second = forward(1, n_seq, patches, clip_ids, *common, y_0)
    y_1 = second.pop("y_out")
    second["r_x"] = y_0
    outputs = (y_0, y_1)

    each = width // places
    back_1 = back(1, n_dp, n_seq, patches, grad_top, *common, second)
    back_0 = back(
        0, n_dp, n_seq, patches, back_1["gx_out"], *common, first, back_1["last_out"], back_1["low"], outputs
    )
    results = (*outputs, back_0["gx_out"], back_1["gx_out"])
    counts = (3 * each, 2 * each, 4 * each, hidden // width * each + hidden // places)
    pieces = [(sum(counts[:at]), count) for at, count in enumerate(counts)]
    ordered = [
        [first, *(done[name] for name in ("outs_out", "space_out", "mlp_out"))]
        for first, done in ((back_0["qkv_out"], back_0), (back_0["last_out"], back_1))
    ]
    shares = layout(
        patches, places, width, hidden, pieces, ordered, back_0["low_sum"], back_0["low_last"], results, back_0["swapped"]
    )
    frames = [frame.transpose(1, 0, 2).reshape(1, 2, 1, patches, width) for frame in shares[10:]]
    shares = [share.reshape(1, -1) for share in shares[:10]]
    return (*frames, *shares)


def relay_from_behind(value, axis, steps):
    count = lax.axis_size(axis)
    leading, last = (max(0, -steps), min(count, count - steps))
    return lax.ppermute(value, axis, [(source, source + steps) for source in range(leading, last)])


def relay_norm_rows(values, gain, shift):
    centre = values - jnp.mean(values, axis=-1, keepdims=True)
    spread = jnp.mean(centre * centre, axis=-1, keepdims=True)
    return centre * lax.rsqrt(spread + eps_norm) * gain + shift


def relay_mixed_dot(left, right, form):
    return jnp.einsum(form, left, right, preferred_element_type=jnp.float32)


def relay_column_sum(grad_rows):
    return jnp.sum(grad_rows.astype(jnp.float32), axis=(0, 1))


def relay_flat_terms(terms):
    return tuple((term.reshape(-1) for term in terms))


def relay_masked_scores(queries, key_rows, allowed):
    scores = relay_mixed_dot(queries, key_rows, "bic,bjc->bij") * queries.shape[-1] ** (-0.5)
    if allowed is None:
        return scores
    return jnp.where(allowed[None], scores, far_below)


def relay_attend(queries, key_rows, values, allowed):
    scores = relay_masked_scores(queries, key_rows, allowed)
    top_score = jnp.max(scores, axis=-1, keepdims=True)
    total_exp = jnp.sum(jnp.exp(scores - top_score), axis=-1, keepdims=True)
    log_total = top_score + jnp.log(total_exp)
    weights_soft = jnp.exp(scores - log_total).astype(jnp.bfloat16)
    mixed = relay_mixed_dot(weights_soft, values, "bij,bjc->bic").astype(jnp.bfloat16)
    return (mixed, log_total)


def relay_attend_back(queries, key_rows, values, log_total, allowed, grad_out):
    scale = queries.shape[-1] ** (-0.5)
    weights_soft = jnp.exp(relay_masked_scores(queries, key_rows, allowed) - log_total)
    grad_values = relay_mixed_dot(weights_soft.astype(jnp.bfloat16), grad_out, "bij,bic->bjc")
    grad_soft = relay_mixed_dot(grad_out, values, "bic,bjc->bij")
    row_total = jnp.sum(grad_soft * weights_soft, axis=-1, keepdims=True)
    grad_scores = (weights_soft * (grad_soft - row_total)).astype(jnp.bfloat16)
    grad_queries = relay_mixed_dot(grad_scores, key_rows, "bij,bjc->bic") * scale
    grad_keys = relay_mixed_dot(grad_scores, queries, "bij,bic->bjc") * scale
    return (grad_queries, grad_keys, grad_values)


def relay_heads_first(rows):
    frames, patches, width = rows.shape
    return (
        rows.reshape(frames, patches, H, width // H)
        .transpose(0, 2, 1, 3)
        .reshape(frames * H, patches, width // H)
    )


def relay_heads_last(rows, frames):
    batch, patches, head_size = rows.shape
    return (
        rows.reshape(frames, batch // frames, patches, head_size)
        .transpose(0, 2, 1, 3)
        .reshape(frames, patches, batch // frames * head_size)
    )


def relay_time_mix(normed_time, time_qkv, time_out, bias_rows, allowed):
    frames, patches, width = normed_time.shape
    zero_row = jnp.zeros((width,), jnp.float32)
    bias_time = jnp.stack([bias_rows[1], zero_row, bias_rows[2]])
    proj_time = relay_mixed_dot(normed_time, time_qkv.reshape(width, 3, width), "fpd,dke->fkpe")
    proj_time = (proj_time + bias_time[None, :, None, :]).astype(jnp.bfloat16)
    proj_time = proj_time.reshape(frames, 3, patches * H, HD)
    by_patch = lax.all_to_all(proj_time, "seq", split_axis=2, concat_axis=0, tiled=True)
    query_time = by_patch[:, 0].transpose(1, 0, 2)
    key_time = by_patch[:, 1].transpose(1, 0, 2)
    value_time = by_patch[:, 2].transpose(1, 0, 2)
    mixed_time, total_time = relay_attend(query_time, key_time, value_time, allowed)
    back_frames = lax.all_to_all(
        mixed_time.transpose(1, 0, 2), "seq", split_axis=0, concat_axis=1, tiled=True
    )
    attn_time = back_frames.reshape(frames, patches, width)
    proj_out = (relay_mixed_dot(attn_time, time_out, "fpd,de->fpe") + bias_rows[3]).astype(jnp.bfloat16)
    return (proj_out, (normed_time, query_time, key_time, value_time, total_time, attn_time))


def relay_time_mix_back(grad_proj_out, time_qkv, time_out, time_kept, allowed):
    normed_rows, query_time, key_time, value_time, total_time, attn_time = time_kept
    frames, patches, width = grad_proj_out.shape
    grad_time_out = relay_mixed_dot(attn_time, grad_proj_out, "fpd,fpe->de")
    grad_attn_time = relay_mixed_dot(grad_proj_out, time_out, "fpe,de->fpd").astype(jnp.bfloat16)
    grad_attn_time = grad_attn_time.reshape(frames, patches * H, HD)
    grad_by_patch = lax.all_to_all(
        grad_attn_time, "seq", split_axis=1, concat_axis=0, tiled=True
    ).transpose(1, 0, 2)
    grads_time = relay_attend_back(query_time, key_time, value_time, total_time, allowed, grad_by_patch)
    grad_mixed = jnp.stack(grads_time, axis=0).transpose(2, 0, 1, 3).astype(jnp.bfloat16)
    grad_frames = lax.all_to_all(
        grad_mixed, "seq", split_axis=0, concat_axis=2, tiled=True
    ).reshape(frames, 3, patches, width)
    grad_time_qkv = relay_mixed_dot(normed_rows, grad_frames, "fpd,fkpe->dke").reshape(width, 3 * width)
    grad_normed = relay_mixed_dot(grad_frames, time_qkv.reshape(width, 3, width), "fkpe,dke->fpd")
    return (
        grad_normed,
        grad_time_qkv,
        grad_time_out,
        relay_column_sum(grad_frames[:, 0]),
        relay_column_sum(grad_frames[:, 2]),
        relay_column_sum(grad_proj_out),
    )


def relay_layer_forward(inputs, params, allowed):
    (
        time_qkv,
        time_out,
        time_fc,
        space_qkv,
        space_out,
        up_weight,
        down_weight,
        norm_gains,
        bias_rows,
        up_bias,
    ) = params
    frames, patches, width = inputs.shape
    zero_row = jnp.zeros((width,), jnp.float32)
    normed_time = relay_norm_rows(inputs, norm_gains[0], bias_rows[0]).astype(jnp.bfloat16)
    proj_out, time_kept = relay_time_mix(normed_time, time_qkv, time_out, bias_rows, allowed)
    after_time = inputs + (relay_mixed_dot(proj_out, time_fc, "fpd,de->fpe") + bias_rows[4])
    normed_space = relay_norm_rows(after_time, norm_gains[1], bias_rows[5]).astype(jnp.bfloat16)
    bias_space = jnp.stack([bias_rows[6], zero_row, bias_rows[7]])
    proj_space = relay_mixed_dot(normed_space, space_qkv.reshape(width, 3, width), "fpd,dke->fkpe")
    proj_space = (proj_space + bias_space[None, :, None, :]).astype(jnp.bfloat16)
    query_space = relay_heads_first(proj_space[:, 0])
    key_space = relay_heads_first(proj_space[:, 1])
    value_space = relay_heads_first(proj_space[:, 2])
    mixed_space, total_space = relay_attend(query_space, key_space, value_space, None)
    attn_space = relay_heads_last(mixed_space, frames)
    after_space = after_time + (relay_mixed_dot(attn_space, space_out, "fpd,de->fpe") + bias_rows[8])
    normed_mlp = relay_norm_rows(after_space, norm_gains[2], bias_rows[9]).astype(jnp.bfloat16)
    hidden_pre = relay_mixed_dot(normed_mlp, up_weight, "fpd,de->fpe") + up_bias
    hidden_act = jax.nn.gelu(hidden_pre).astype(jnp.bfloat16)
    outputs = after_space + (relay_mixed_dot(hidden_act, down_weight, "fpe,ed->fpd") + bias_rows[10])
    kept = (
        inputs,
        time_kept,
        proj_out,
        after_time,
        normed_space,
        query_space,
        key_space,
        value_space,
        total_space,
        attn_space,
        after_space,
        normed_mlp,
        hidden_pre,
        hidden_act,
    )
    return (outputs, kept)


def relay_layer_backward(grad_top, params, kept, allowed):
    (
        time_qkv,
        time_out,
        time_fc,
        space_qkv,
        space_out,
        up_weight,
        down_weight,
        norm_gains,
        bias_rows,
        up_bias,
    ) = params
    (
        inputs,
        time_kept,
        proj_out,
        after_time,
        normed_space,
        query_space,
        key_space,
        value_space,
        total_space,
        attn_space,
        after_space,
        normed_mlp,
        hidden_pre,
        hidden_act,
    ) = kept
    frames, patches, width = inputs.shape
    grad_mlp = grad_top.astype(jnp.bfloat16)
    grad_down = relay_mixed_dot(hidden_act, grad_mlp, "fpe,fpd->ed")
    grad_act = relay_mixed_dot(grad_mlp, down_weight, "fpd,ed->fpe")
    gelu_back = jax.vjp(jax.nn.gelu, hidden_pre)[1]
    grad_pre = gelu_back(grad_act)[0].astype(jnp.bfloat16)
    grad_up = relay_mixed_dot(normed_mlp, grad_pre, "fpd,fpe->de")
    grad_normed = relay_mixed_dot(grad_pre, up_weight, "fpe,de->fpd")
    norm_back = jax.vjp(relay_norm_rows, after_space, norm_gains[2], bias_rows[9])[1]
    grad_into, gain_mlp, shift_mlp = norm_back(grad_normed)
    grad_space = grad_top + grad_into
    grad_branch = grad_space.astype(jnp.bfloat16)
    grad_space_out = relay_mixed_dot(attn_space, grad_branch, "fpd,fpe->de")
    grad_attn = relay_heads_first(relay_mixed_dot(grad_branch, space_out, "fpe,de->fpd").astype(jnp.bfloat16))
    grads_space = relay_attend_back(query_space, key_space, value_space, total_space, None, grad_attn)
    grad_proj = jnp.stack([relay_heads_last(piece, frames) for piece in grads_space], axis=1).astype(
        jnp.bfloat16
    )
    grad_space_qkv = relay_mixed_dot(normed_space, grad_proj, "fpd,fkpe->dke").reshape(width, 3 * width)
    grad_normed = relay_mixed_dot(grad_proj, space_qkv.reshape(width, 3, width), "fkpe,dke->fpd")
    norm_back = jax.vjp(relay_norm_rows, after_time, norm_gains[1], bias_rows[5])[1]
    grad_into, gain_space, shift_space = norm_back(grad_normed)
    grad_time = grad_space + grad_into
    grad_branch_time = grad_time.astype(jnp.bfloat16)
    grad_time_fc = relay_mixed_dot(proj_out, grad_branch_time, "fpd,fpe->de")
    grad_proj_out = relay_mixed_dot(grad_branch_time, time_fc, "fpe,de->fpd").astype(jnp.bfloat16)
    grad_normed, grad_time_qkv, grad_time_out, query_bias, value_bias, out_bias = relay_time_mix_back(
        grad_proj_out, time_qkv, time_out, time_kept, allowed
    )
    norm_back = jax.vjp(relay_norm_rows, inputs, norm_gains[0], bias_rows[0])[1]
    grad_into, gain_time, shift_time = norm_back(grad_normed)
    grad_inputs = grad_time + grad_into
    gain_grads = jnp.stack([gain_time, gain_space, gain_mlp])
    bias_grads = jnp.stack(
        [
            shift_time,
            query_bias,
            value_bias,
            out_bias,
            relay_column_sum(grad_branch_time),
            shift_space,
            relay_column_sum(grad_proj[:, 0]),
            relay_column_sum(grad_proj[:, 2]),
            relay_column_sum(grad_branch),
            shift_mlp,
            relay_column_sum(grad_mlp),
        ]
    )
    up_grad = relay_column_sum(grad_pre)
    return (
        grad_inputs,
        (
            grad_time_qkv,
            grad_time_out,
            grad_time_fc,
            grad_space_qkv,
            grad_space_out,
            grad_up,
            grad_down,
            gain_grads,
            bias_grads,
            up_grad,
        ),
    )


def relay_shards(
    clip_ids,
    tokens,
    time_qkv,
    time_out,
    time_fc,
    space_qkv,
    space_out,
    up_weight,
    down_weight,
    norm_gains,
    bias_rows,
    up_bias,
    cotangent,
):
    params = (
        time_qkv[0],
        time_out[0],
        time_fc[0],
        space_qkv[0],
        space_out[0],
        up_weight[0],
        down_weight[0],
        norm_gains[0],
        bias_rows[0],
        up_bias[0],
    )
    allowed = clip_ids[0][:, None] == clip_ids[0][None, :]
    first_section = lax.axis_index("section") == 0
    micro = tokens.shape[0]
    arriving = jnp.zeros_like(tokens[0])
    section_inputs = []
    section_outputs = []
    for moment in range(micro + 1):
        taken_rows = jnp.where(first_section, tokens[min(moment, micro - 1)], arriving)
        result = relay_layer_forward(taken_rows.astype(jnp.float32), params, allowed)[0].astype(
            jnp.bfloat16
        )
        section_inputs.append(taken_rows)
        section_outputs.append(result)
        if moment < micro:
            arriving = relay_from_behind(result, "section", 1)
    saved_inputs = [
        jnp.where(first_section, section_inputs[number], section_inputs[number + 1])
        for number in range(micro)
    ]
    layer_outputs = jnp.stack(
        [
            jnp.where(first_section, section_outputs[number], section_outputs[number + 1])
            for number in range(micro)
        ]
    )
    returning = jnp.zeros_like(tokens[0])
    back_results = []
    totals = None
    for moment in range(micro + 1):
        grad_given = jnp.where(first_section, returning, cotangent[min(moment, micro - 1)]).astype(
            jnp.float32
        )
        source_rows = jnp.where(
            first_section, saved_inputs[max(moment - 1, 0)], saved_inputs[min(moment, micro - 1)]
        )
        live_share = jnp.where(
            first_section, 1.0 if moment >= 1 else 0.0, 1.0 if moment < micro else 0.0
        )
        kept = relay_layer_forward(source_rows.astype(jnp.float32), params, allowed)[1]
        grad_inputs, weight_terms = relay_layer_backward(grad_given, params, kept, allowed)
        grad_inputs = grad_inputs.astype(jnp.bfloat16)
        back_results.append(grad_inputs)
        weight_terms = relay_flat_terms(jax.tree.map(lambda term: term * live_share, weight_terms))
        if totals is None:
            totals = tuple(weight_terms)
        else:
            totals = tuple((left + right for left, right in zip(totals, weight_terms)))
        if moment < micro:
            returning = relay_from_behind(grad_inputs, "section", -1)
    input_grads = jnp.stack(
        [
            jnp.where(first_section, back_results[number + 1], back_results[number])
            for number in range(micro)
        ]
    )
    shares = (
        lax.psum_scatter(totals[0], ("dp", "seq"), scatter_dimension=0, tiled=True),
        lax.psum_scatter(totals[1], ("dp", "seq"), scatter_dimension=0, tiled=True),
        lax.psum_scatter(totals[2], ("dp", "seq"), scatter_dimension=0, tiled=True),
        lax.psum_scatter(totals[3], ("dp", "seq"), scatter_dimension=0, tiled=True),
        lax.psum_scatter(totals[4], ("dp", "seq"), scatter_dimension=0, tiled=True),
        lax.psum_scatter(totals[5], ("dp", "seq"), scatter_dimension=0, tiled=True),
        lax.psum_scatter(totals[6], ("dp", "seq"), scatter_dimension=0, tiled=True),
        lax.psum_scatter(totals[7], ("dp", "seq"), scatter_dimension=0, tiled=True),
        lax.psum_scatter(totals[8], ("dp", "seq"), scatter_dimension=0, tiled=True),
        lax.psum_scatter(totals[9], ("dp", "seq"), scatter_dimension=0, tiled=True),
    )
    return (
        layer_outputs[None],
        input_grads[None],
        shares[0][None],
        shares[1][None],
        shares[2][None],
        shares[3][None],
        shares[4][None],
        shares[5][None],
        shares[6][None],
        shares[7][None],
        shares[8][None],
        shares[9][None],
    )


def solution(mesh):
    stacked = P("section", None, None)
    spread = P(None, ("dp", "seq"), None, None)
    in_specs = (P("dp", None), spread, *[stacked] * 9, P("section", None), spread)
    flat = P("section", ("dp", "seq"))
    out = P("section", None, ("dp", "seq"), None, None)
    relay = mesh.shape["seq"] != 4 or mesh.shape["dp"] != 4
    return jax.shard_map(
        relay_shards if relay else shards, mesh=mesh, in_specs=in_specs, out_specs=(out, out, *[flat] * 10), check_vma=False
    )
```

```python
import functools

import jax
import jax.numpy as jnp
from jax import lax
from jax.experimental import pallas as pl
from jax.experimental.pallas import tpu as pltpu
from jax.sharding import PartitionSpec as P

H = 12
HD = 64
PAIR = 2 * HD
eps_norm = 1e-06
far_below = -1000000000.0
BF = jnp.bfloat16
F32 = jnp.float32
VMEM_BYTES = 62 << 20
NEXT_ID = [1]
GROUP = 6
GROUP_BACK = 6
CHUNK = 416


def nn(left, right):
    return lax.dot_general(left, right, (((1,), (0,)), ((), ())), preferred_element_type=F32)


def nt(left, right):
    return lax.dot_general(left, right, (((1,), (1,)), ((), ())), preferred_element_type=F32)


def norm_stats(values):
    centre = values - jnp.mean(values, axis=-1, keepdims=True)
    scale = lax.rsqrt(jnp.mean(centre * centre, axis=-1, keepdims=True) + eps_norm)
    return centre * scale, scale


def rows_at(index, count):
    return pl.ds(pl.multiple_of(index * count, count), count)


def norm_into(source, target, gain, shift, chunk):
    @pl.loop(0, source.shape[0] // chunk)
    def _(step):
        at = rows_at(step, chunk)
        hat, _ = norm_stats(source[at, :].astype(F32))
        target[at, :] = (hat * gain[...] + shift[...]).astype(BF)


def gelu_both(pre):
    rate, cube = 0.7978845608028654, 0.044715
    square = pre * pre
    tanh = jnp.tanh(pre * (rate + rate * cube * square))
    half = 0.5 + 0.5 * tanh
    act = pre * half
    slope = half + act * (1.0 - tanh) * (rate + 3.0 * rate * cube * square)
    return act, slope


class Copies:
    def __init__(self, sems):
        self.sems, self.used, self.open = sems, 0, []

    def fetch(self, own, other, target, mine):
        sem = self.sems.at[self.used]
        self.used += 1

        @pl.when(mine)
        def _():
            pltpu.make_async_copy(own, target, sem).start()

        @pl.when(jnp.logical_not(mine))
        def _():
            pltpu.make_async_copy(other, target, sem).start()

        return pltpu.make_async_copy(own, target, sem)

    def start(self, source, target):
        copy = pltpu.make_async_copy(source, target, self.sems.at[self.used])
        self.used += 1
        copy.start()
        return copy

    def store(self, source, target):
        self.open.append(self.start(source, target))

    def finish(self):
        for copy in self.open:
            copy.wait()


def time_attention(qkv, attn, probs, stage, soft, heads, heads_t, clips, frames, rows, width):
    @pl.loop(0, frames, unroll=2)
    def _(i):
        own = rows_at(i, rows)
        for j in range(frames):
            stage[pl.ds(j * rows, rows), :] = qkv[own, 0:width] * qkv[pl.ds(j * rows, rows), width : 2 * width]
        scores = nn(stage[...], heads[...])
        parts = []
        for j in range(frames):
            open_pair = clips[0, i] == clips[0, j]
            parts.append(scores[j * rows : (j + 1) * rows] + jnp.where(open_pair, 0.0, far_below))
        top = functools.reduce(jnp.maximum, parts)
        parts = [jnp.exp(part - top) for part in parts]
        inverse = 1.0 / sum(parts)
        for j in range(frames):
            prob = parts[j] * inverse
            probs[i, pl.ds(j * rows, rows), :] = prob
            soft[pl.ds(j * rows, rows), :] = prob.astype(BF)
        total = None
        for j in range(frames):
            at = pl.ds(j * rows, rows)
            term = nn(soft[at, :], heads_t[...]) * qkv[at, 2 * width : 3 * width].astype(F32)
            total = term if total is None else total + term
        attn[own, :] = total.astype(BF)


def fill_units(unit, pair_unit):
    for target in (unit, pair_unit):
        row = lax.broadcasted_iota(jnp.int32, target.shape, 0)
        column = lax.broadcasted_iota(jnp.int32, target.shape, 1)
        target[...] = jnp.where(row == column, 1.0, 0.0).astype(BF)


def split_patches(scores, patches):
    whole = patches // 16 * 16
    if whole == scores.shape[0]:
        return [scores]
    rest = scores[whole:]
    row = lax.broadcasted_iota(jnp.int32, rest.shape, 0)
    return [scores[:whole], jnp.where(row < patches - whole, rest, far_below)]


def space_attention(qkv, attn, logs, values_t, mixed_t, unit, pair_unit, frames, rows, patches, width):
    low_lane = lax.broadcasted_iota(jnp.int32, (rows, PAIR), 1) < HD
    deep = HD + 16
    values_t[...] = jnp.ones_like(values_t)

    @pl.loop(0, frames, unroll=2)
    def _(f):
        at = rows_at(f, rows)
        for pair in range(width // PAIR):
            turned = nt(pair_unit[...], qkv[at, 2 * width + pair * PAIR : 2 * width + (pair + 1) * PAIR]).astype(BF)
            for half in range(2):
                head = 2 * pair + half
                values_t[head * deep : head * deep + HD, :] = turned[half * HD : (half + 1) * HD]

        @pl.loop(0, width // PAIR // GROUP)
        def _(group):
            scores = []
            for member in range(GROUP):
                pair = group * GROUP + member

                def lanes(which):
                    return pl.ds(pl.multiple_of(which * width + pair * PAIR, PAIR), PAIR)

                query, key = qkv[at, lanes(0)] * BF(HD**-0.5), qkv[at, lanes(1)]
                for half in range(2):
                    scores.append(nt(jnp.where(low_lane if half == 0 else ~low_lane, key, BF(0)), query))
            expos, tops = [], []
            for score in scores:
                parts = split_patches(score, patches)
                top = functools.reduce(jnp.maximum, [jnp.max(part, axis=0, keepdims=True) for part in parts])
                expos.append(jnp.concatenate([jnp.exp(part - top).astype(BF) for part in parts], axis=0))
                tops.append(top)
            for member, (expo, top) in enumerate(zip(expos, tops)):
                head = group * (2 * GROUP) + member
                both = nn(values_t[pl.ds(pl.multiple_of(head * deep, 16), deep), :], expo)
                total = both[HD : HD + 1]
                logs[pl.ds(f * H + head, 1), :] = top + jnp.log(total)
                mixed_t[pl.ds(pl.multiple_of(head * HD, HD), HD), :] = (both[:HD] * (1.0 / total)).astype(BF)

        attn[at, :] = nt(unit[...], mixed_t[...]).astype(BF)


class Smalls:
    def __init__(self, own, other, held, mine):
        for which, refs in ((mine, own), (jnp.logical_not(mine), other)):

            @pl.when(which)
            def _(refs=refs):
                for source, target in zip(refs, held):
                    width = target.shape[1]
                    for row in range(target.shape[0]):
                        target[row : row + 1, :] = source[:, row * width : (row + 1) * width]

        self.gains, self.biases, self.up_bias = held

    def gain(self, row):
        return self.gains.at[row : row + 1]

    def bias(self, row):
        return self.biases.at[row : row + 1]


def fill_heads(heads, heads_t):
    lane = lax.broadcasted_iota(jnp.int32, heads.shape, 0) // HD
    head = lax.broadcasted_iota(jnp.int32, heads.shape, 1)
    heads[...] = jnp.where(lane == head, HD**-0.5, 0.0).astype(BF)
    lane = lax.broadcasted_iota(jnp.int32, heads_t.shape, 1) // HD
    head = lax.broadcasted_iota(jnp.int32, heads_t.shape, 0)
    heads_t[...] = jnp.where(lane == head, 1.0, 0.0).astype(BF)


def fill_pick(pick, outer, place, count):
    each = pick.shape[0] // outer
    row = lax.broadcasted_iota(jnp.int32, pick.shape, 0)
    column = lax.broadcasted_iota(jnp.int32, pick.shape, 1)
    pick[...] = jnp.where(column == (row // each * count + place) * each + row % each, 1.0, 0.0).astype(BF)


def project(source, weight, biases, target):
    width = source.shape[1]
    for part in range(3):
        at = slice(part * width, (part + 1) * width)
        result = nn(source[...], weight[:, at])
        if biases[part] is not None:
            result = result + biases[part][...]
        target[:, at] = result.astype(BF)


def struct(shape, dtype=BF):
    return jax.ShapeDtypeStruct(shape, dtype)


def held(*structs):
    return [pltpu.VMEM(s.shape, s.dtype) for s in structs]


IN_VMEM = pl.BlockSpec(memory_space=pltpu.VMEM)
IN_SMEM = pl.BlockSpec(memory_space=pltpu.SMEM)
IN_HBM = pl.BlockSpec(memory_space=pl.ANY)


def vmem(**structs):
    return {name: pltpu.VMEM(s.shape, s.dtype) for name, s in structs.items()}


def small_held(width, hidden):
    return vmem(
        gains=struct((BIAS, width), F32), biases=struct((UP - BIAS, width), F32), up_bias=struct((1, hidden), F32)
    )


def small_ins(own, other):
    (gains, biases, up_bias), (gains_2, biases_2, up_bias_2) = own, other
    return dict(
        own_gains=(gains, IN_VMEM),
        own_biases=(biases, IN_VMEM),
        own_up_bias=(up_bias, IN_VMEM),
        other_gains=(gains_2, IN_VMEM),
        other_biases=(biases_2, IN_VMEM),
        other_up_bias=(up_bias_2, IN_VMEM),
    )


def load_smalls(k, mine):
    return Smalls(
        (k.own_gains, k.own_biases, k.own_up_bias),
        (k.other_gains, k.other_biases, k.other_up_bias),
        (k.gains, k.biases, k.up_bias),
        mine,
    )


def own_ins(own):
    time, time_out, time_fc, space, space_out, up, down = own
    return dict(
        own_time=(time, IN_HBM),
        own_time_out=(time_out, IN_HBM),
        own_time_fc=(time_fc, IN_HBM),
        own_space=(space, IN_HBM),
        own_space_out=(space_out, IN_HBM),
        own_up=(up, IN_HBM),
        own_down=(down, IN_HBM),
    )


def other_refs(other):
    time, time_out, time_fc, space, space_out, up, down = other
    return dict(
        other_time=(time, IN_HBM),
        other_time_out=(time_out, IN_HBM),
        other_time_fc=(time_fc, IN_HBM),
        other_space=(space, IN_HBM),
        other_space_out=(space_out, IN_HBM),
        other_up=(up, IN_HBM),
        other_down=(down, IN_HBM),
    )


MESH = pl.DeviceIdType.MESH
BIAS, UP, LOW = 3, 14, 24


class Named:
    def __init__(self, names, refs):
        self.__dict__.update(zip(names, refs, strict=True))


def named_call(kernel, name, flops, ins, outs, scratch, remote):
    names = [*ins, *outs, *scratch]
    if remote:
        NEXT_ID.append(NEXT_ID[-1] + 1)
    extra = dict(collective_id=NEXT_ID[-1], has_side_effects=True) if remote else {}
    results = pl.pallas_call(
        lambda *refs: kernel(Named(names, refs)),
        out_shape=[value for value, _ in outs.values()],
        in_specs=[spec for _, spec in ins.values()],
        out_specs=[spec for _, spec in outs.values()],
        scratch_shapes=list(scratch.values()),
        compiler_params=pltpu.CompilerParams(vmem_limit_bytes=VMEM_BYTES, **extra),
        cost_estimate=pl.CostEstimate(flops=flops, bytes_accessed=60 << 20, transcendentals=0),
        name=name,
    )(*[value for value, _ in ins.values()])
    return dict(zip(outs, results))


class Begin:
    def __init__(self, k, patches):
        self.k, self.patches = k, patches
        self.count, self.me = lax.axis_size("seq"), lax.axis_index("seq")
        self.section = lax.axis_index("section")
        self.mate = {"section": 1 - self.section}
        self.first = [
            (k.own_time, k.other_time),
            (k.own_time_out, k.other_time_out),
            (k.own_time_fc, k.other_time_fc),
        ]
        self.then = [(k.own_space, k.other_space), (k.own_space_out, k.other_space_out)]
        self.last = [(k.own_up, k.other_up), (k.own_down, k.other_down)]
        self.smalls = [
            (k.own_gains, k.other_gains),
            (k.own_biases, k.other_biases),
            (k.own_up_bias, k.other_up_bias),
        ]
        self.pairs = self.first + self.then + self.last + self.smalls

    def over(self, at):
        source, target = self.pairs[at]
        return pltpu.make_async_remote_copy(
            source, target, self.k.over_send.at[at], self.k.over_recv.at[at], device_id=self.mate, device_id_type=MESH
        )

    def around(self, which, step):
        source, target = ((self.k.frame, self.k.x), (self.k.cot, self.k.cot_out))[which]
        rows = source.shape[0]
        at = which * (self.count - 1) + step - 1
        return pltpu.make_async_remote_copy(
            source,
            target.at[rows_at(self.me, rows)],
            self.k.send.at[at],
            self.k.recv.at[at],
            device_id={"seq": lax.rem(self.me + step, self.count)},
            device_id_type=MESH,
        )

    def pad_into(self, source, target):
        whole = self.patches // 16 * 16
        target[0:whole, :] = source[0:whole, :]
        if target.shape[0] > whole:
            rest = jnp.zeros((target.shape[0] - self.patches, source.shape[1]), BF)
            target[whole:, :] = jnp.concatenate([source[whole:, :], rest], axis=0)

    def begin(self, copies, mine):
        k = self.k
        loads = [
            pltpu.make_async_copy(source.at[self.section, 0], target, k.local.at[at])
            for at, (source, target) in enumerate(((k.tokens, k.raw), (k.cotangent, k.raw_cot)))
        ]
        for load in loads:
            load.start()
        barrier = pltpu.get_barrier_semaphore()
        pl.semaphore_signal(barrier, inc=1, device_id=self.mate, device_id_type=MESH)
        for step in range(1, self.count):
            at = {"seq": lax.rem(self.me + step, self.count)}
            pl.semaphore_signal(barrier, inc=1, device_id=at, device_id_type=MESH)
        loads[0].wait()
        self.pad_into(k.raw, k.frame)
        pl.semaphore_wait(barrier, self.count)
        for step in range(1, self.count):
            self.around(0, step).start()
        for at in (7, 8, 9, 0, 1, 2):
            self.over(at).start()
        loads[1].wait()
        self.pad_into(k.raw_cot, k.cot)
        rows = k.frame.shape[0]
        own = rows_at(self.me, rows)
        k.x[own, :] = k.frame[...]
        keep = pltpu.make_async_copy(k.cot, k.cot_out.at[own], k.local.at[2])
        keep.start()
        loads = [self.fetch(copies, at, target, mine) for at, target in enumerate((k.time, k.time_out, k.time_fc))]
        self.next((0, 1, 2), (3, 4))
        for at in (7, 8, 9):
            self.over(at).wait()
        for step in range(1, self.count):
            self.around(0, step).wait()
        for step in range(1, self.count):
            self.around(1, step).start()
        keep.wait()
        return loads

    def next(self, done, then):
        for at in done:
            self.over(at).wait_send()
        for at in then:
            self.over(at).start()

    def fetch(self, copies, at, target, mine):
        own, other = self.pairs[at]

        @pl.when(jnp.logical_not(mine))
        def _():
            self.over(at).wait_recv()

        return copies.fetch(own, other, target, mine)

    def end(self, mine):
        for at in (5, 6):
            self.over(at).wait_send()

        @pl.when(mine)
        def _():
            for at in range(7):
                self.over(at).wait_recv()

        for step in range(1, self.count):
            self.around(1, step).wait()


def forward_kernel(block, frames, patches, k):
    total, width = k.x.shape
    rows = total // frames
    copies = Copies(k.sems)
    mine = lax.axis_index("section") == block
    fill_heads(k.heads, k.heads_t)
    fill_units(k.unit, k.pair_unit)
    if block == 0:
        start = Begin(k, patches)
        load_time, load_time_out, load_time_fc = start.begin(copies, mine)
        copies.store(k.x, k.r_x)
        fetch = functools.partial(start.fetch, copies, mine=mine)
    else:
        load_x = copies.start(k.x_in, k.x)
        pairs = (
            (k.own_time, k.other_time),
            (k.own_time_out, k.other_time_out),
            (k.own_time_fc, k.other_time_fc),
            (k.own_space, k.other_space),
            (k.own_space_out, k.other_space_out),
            (k.own_up, k.other_up),
            (k.own_down, k.other_down),
        )

        def fetch(at, target):
            return copies.fetch(*pairs[at], target, mine)

    if block == 1:
        load_time = fetch(0, k.time)
    smalls = load_smalls(k, mine)
    if block == 1:
        load_x.wait()
    norm_into(k.x, k.normed_t, smalls.gain(0), smalls.bias(0), CHUNK)
    copies.store(k.normed_t, k.r_normed_t)
    load_time.wait()
    if block == 1:
        load_time_out, load_time_fc = fetch(1, k.time_out), fetch(2, k.time_fc)
    project(k.normed_t, k.time, (smalls.bias(1), None, smalls.bias(2)), k.qkv_t)
    copies.store(k.qkv_t, k.r_qkv_t)
    load_space, load_space_out = fetch(3, k.space), fetch(4, k.space_out)
    if block == 0:
        start.next((3, 4), (5, 6))
    time_attention(k.qkv_t, k.attn_t, k.probs, k.stage, k.soft, k.heads, k.heads_t, k.clips, frames, rows, width)
    copies.store(k.attn_t, k.r_attn_t)
    copies.store(k.probs, k.r_probs)
    load_time_out.wait()
    k.proj[...] = (nn(k.attn_t[...], k.time_out[...]) + smalls.bias(3)[...]).astype(BF)
    copies.store(k.proj, k.r_proj)
    load_time_fc.wait()
    k.x1[...] = k.x[...].astype(F32) + nn(k.proj[...], k.time_fc[...]) + smalls.bias(4)[...]
    copies.store(k.x1, k.r_x1)
    if block == 1:
        load_up, load_down = fetch(5, k.up), fetch(6, k.down)
    norm_into(k.x1, k.normed_s, smalls.gain(1), smalls.bias(5), CHUNK)
    copies.store(k.normed_s, k.r_normed_s)
    load_space.wait()
    project(k.normed_s, k.space, (smalls.bias(6), None, smalls.bias(7)), k.qkv_s)
    copies.store(k.qkv_s, k.r_qkv_s)
    space_attention(
        k.qkv_s, k.attn_s, k.logs, k.values_t, k.mixed_t, k.unit, k.pair_unit, frames, rows, patches, width
    )
    copies.store(k.attn_s, k.r_attn_s)
    copies.store(k.logs, k.r_logs)
    load_space_out.wait()
    if block == 0:
        load_up, load_down = fetch(5, k.up), fetch(6, k.down)
    k.x2[...] = k.x1[...] + nn(k.attn_s[...], k.space_out[...]) + smalls.bias(8)[...]
    copies.store(k.x2, k.r_x2)
    norm_into(k.x2, k.normed_m, smalls.gain(2), smalls.bias(9), CHUNK)
    copies.store(k.normed_m, k.r_normed_m)
    load_up.wait()

    for tile in range(k.up.shape[1] // width):
        at = slice(tile * width, (tile + 1) * width)
        pre = nn(k.normed_m[...], k.up[:, at]) + smalls.up_bias[:, at]
        both = gelu_both(pre)
        k.act[:, at] = both[0].astype(BF)
        k.slope[:, at] = both[1].astype(BF)
        copies.store(k.act.at[:, at], k.r_act.at[:, at])
        copies.store(k.slope.at[:, at], k.r_slope.at[:, at])

    load_down.wait()

    @pl.loop(0, 3)
    def _(tile):
        at = rows_at(tile, width // 3)
        y_at = nn(k.act[...], k.down[:, at]) + smalls.biases[10:11, at] + k.x2[:, at]
        k.y[:, at] = y_at.astype(BF)

    copies.store(k.y, k.y_out)
    if block == 0:
        start.end(mine)
    copies.finish()


def forward(block, frames, patches, clips, small, small_other, own, other, x=None, tokens=None, cotangent=None):
    width, hidden = own[5].shape
    rows = -(-patches // 16) * 16
    total = frames * rows
    wide, full, triple = struct((total, width)), struct((total, width), F32), struct((total, 3 * width))
    deep, few = struct((total, hidden)), struct((total, PAIR))
    logs, probs = struct((frames * H, rows), F32), struct((frames, total, PAIR), F32)
    lie = lambda **structs: {name: (s, IN_HBM) for name, s in structs.items()}
    ins = dict(clips=(clips, IN_SMEM), **own_ins(own))
    outs = lie(y_out=wide, r_qkv_t=triple, r_attn_t=wide, r_proj=wide, r_x1=full, r_probs=probs, r_normed_t=wide)
    outs |= lie(r_qkv_s=triple, r_attn_s=wide, r_x2=full, r_act=deep, r_slope=deep, r_normed_s=wide, r_normed_m=wide)
    outs |= lie(r_logs=logs)
    square, third = struct((width, width)), struct((width, 3 * width))
    scratch = vmem(time=third, time_out=square, time_fc=square, space=third, space_out=square)
    scratch |= vmem(up=struct((width, hidden)), down=struct((hidden, width)), x=wide, normed_t=wide, stage=wide)
    scratch |= vmem(qkv_t=triple, attn_t=wide, proj=wide, x1=full, probs=probs, soft=few, normed_s=wide, qkv_s=triple)
    scratch |= vmem(attn_s=wide, logs=logs, x2=full, normed_m=wide, act=deep, slope=deep, y=wide)
    scratch |= vmem(values_t=struct((H * (HD + 16), rows)), mixed_t=struct((width, rows)), unit=struct((rows, rows)))
    scratch |= vmem(pair_unit=struct((PAIR, PAIR)), heads=struct((width, PAIR)), heads_t=struct((PAIR, width)))
    scratch |= small_held(width, hidden)
    dma = pltpu.SemaphoreType.DMA
    scratch |= dict(sems=dma((40,)))
    if block == 0:
        gains, biases, up_bias = small
        ins |= dict(tokens=(tokens, IN_HBM), cotangent=(cotangent, IN_HBM))
        ins |= dict(own_gains=(gains, IN_VMEM), own_biases=(biases, IN_VMEM), own_up_bias=(up_bias, IN_VMEM))
        outs |= other_refs([struct(array.shape) for array in own])
        like = [struct(array.shape, F32) for array in small]
        outs |= dict(other_gains=(like[0], IN_VMEM), other_biases=(like[1], IN_VMEM), other_up_bias=(like[2], IN_VMEM))
        outs |= lie(cot_out=wide, r_x=wide)
        raw, frame = struct((patches, width)), struct((rows, width))
        scratch |= vmem(raw=raw, raw_cot=raw, frame=frame, cot=frame)
        scratch |= dict(send=dma((2 * frames,)), recv=dma((2 * frames,)), over_send=dma((10,)), over_recv=dma((10,)))
        scratch |= dict(local=dma((3,)))
    else:
        ins |= dict(x_in=(x, IN_HBM), **other_refs(other), **small_ins(small, small_other))
    kernel = functools.partial(forward_kernel, block, frames, patches)
    return named_call(kernel, f"block{block}_forward", 34 * total * width * width, ins, outs, scratch, block == 0)


def beside(z):
    return z + 1 - 2 * lax.rem(z, 2), lax.rem(z + 2, 4)


def greet():
    barrier = pltpu.get_barrier_semaphore()
    z = lax.axis_index("dp")
    pl.semaphore_signal(barrier, inc=1, device_id={"section": 1 - lax.axis_index("section")}, device_id_type=MESH)
    for step in range(1, 4):
        pl.semaphore_signal(barrier, inc=1, device_id={"dp": lax.rem(z + step, 4)}, device_id_type=MESH)
    pl.semaphore_wait(barrier, 4)


class Relay:
    def __init__(self, block, mine, mates, taken, send, recv, source=None, direct=False):
        self.mine, self.mates, self.taken, self.send, self.recv = mine, mates, taken, send, recv
        self.source, self.direct = source, direct
        self.z = lax.axis_index("dp")
        self.near, self.far = beside(self.z)
        self.section = lax.axis_index("section")
        self.home = self.section == block
        self.away = self.section != block

    def parts(self):
        if self.direct:
            return tuple(lax.rem(self.z + step, 4) for step in (2, 1, 3, 0))
        return lax.rem(self.near + 2, 4), self.near, self.far, self.z

    def mate(self, part):
        if len(self.mates.shape) == 3:
            return self.mates.at[part]
        return self.mates.at[rows_at(part, self.mine.shape[1])]

    def over(self, at):
        part = self.parts()[at]
        return pltpu.make_async_remote_copy(
            (self.mine if self.source is None else self.source).at[part],
            self.mate(part),
            self.send.at[3 + at],
            self.recv.at[3 + at],
            device_id={"section": 1 - self.section},
            device_id_type=MESH,
        )

    def local(self):
        return pltpu.make_async_copy(self.source, self.mine, self.send.at[7])

    def along(self, step):
        part = self.parts()[step]
        return pltpu.make_async_remote_copy(
            self.mine.at[part],
            self.taken.at[step],
            self.send.at[step],
            self.recv.at[step],
            device_id={"dp": part if self.direct else self.far if step == 2 else self.near},
            device_id_type=MESH,
        )

    def begin(self):
        @pl.when(self.away)
        def _():
            for at in range(4):
                self.over(at).start()

        if self.source is not None:

            @pl.when(self.home)
            def _():
                self.local().start()

    def middle(self):
        @pl.when(self.home)
        def _():
            if self.source is not None:
                self.local().wait()
            for at, part in enumerate(self.parts()):
                self.over(at).wait_recv()
                self.mine[part] = (self.mine[part].astype(F32) + self.mate(part)[...].astype(F32)).astype(BF)
                if at < (3 if self.direct else 2):
                    self.along(at).start()

        @pl.when(self.away)
        def _():
            for at in range(4):
                self.over(at).wait_send()

    def second(self):
        @pl.when(self.home)
        def _():
            self.along(0).wait()
            self.mine[self.far] = (self.mine[self.far].astype(F32) + self.taken[0].astype(F32)).astype(BF)
            self.along(2).start()

    def end(self, staged, out, sem):
        self.store = pltpu.make_async_copy(staged, out, sem)

        @pl.when(self.home)
        def _():
            self.along(1).wait()
            total = self.mine[self.z].astype(F32) + self.taken[1].astype(F32)
            if self.direct:
                self.along(0).wait()
                total = total + self.taken[0].astype(F32)
            self.along(2).wait()
            staged[...] = total + self.taken[2].astype(F32)
            self.store.start()

    def settle(self):
        pl.when(self.home)(self.store.wait)


class LowRelay:
    def __init__(self, lows, out, scratch):
        self.lows, self.out = lows, out
        self.mine, self.mate, self.taken, self.send, self.recv = scratch
        self.places = beside(lax.axis_index("dp"))
        self.section = lax.axis_index("section")

    def over(self, low):
        return pltpu.make_async_remote_copy(
            low,
            self.mate,
            self.send.at[0],
            self.recv.at[0],
            device_id={"section": 1 - self.section},
            device_id_type=MESH,
        )

    def along(self, step):
        return pltpu.make_async_remote_copy(
            self.mine.at[step],
            self.taken.at[step],
            self.send.at[1 + step],
            self.recv.at[1 + step],
            device_id={"dp": self.places[step]},
            device_id_type=MESH,
        )

    def begin(self):
        for block, low in enumerate(self.lows):

            @pl.when(self.section != block)
            def _(low=low):
                self.over(low).start()

    def at_home(self, act):
        if len(self.lows) == 2:
            act()
        else:
            pl.when(self.section == 0)(act)

    def middle(self):
        for block, low in enumerate(self.lows):

            @pl.when(self.section == block)
            def _(low=low):
                self.over(low).wait_recv()
                self.mine[0] = low[...] + self.mate[...]
                self.along(0).start()

            @pl.when(self.section != block)
            def _(low=low):
                self.over(low).wait_send()

    def second(self):
        def _():
            self.along(0).wait()
            self.mine[1] = self.mine[0] + self.taken[0]
            self.along(1).start()

        self.at_home(_)

    def end(self):
        def _():
            self.along(1).wait()
            self.out[...] = self.mine[1] + self.taken[1]

        self.at_home(_)
        if len(self.lows) == 1:

            @pl.when(self.section != 0)
            def _():
                self.out[...] = jnp.zeros_like(self.out)


class LateRelay:
    def __init__(self, low, out, mine, mate, taken, send, recv):
        self.low, self.out, self.mine, self.mate, self.taken, self.send, self.recv = low, out, mine, mate, taken, send, recv
        self.z = lax.axis_index("dp")
        self.section = lax.axis_index("section")

    def over(self):
        return pltpu.make_async_remote_copy(
            self.low,
            self.mate,
            self.send.at[3],
            self.recv.at[3],
            device_id={"section": 1 - self.section},
            device_id_type=MESH,
        )

    def along(self, step):
        return pltpu.make_async_remote_copy(
            self.mine,
            self.taken.at[step],
            self.send.at[step],
            self.recv.at[step],
            device_id={"dp": lax.rem(self.z + 1 + step, 4)},
            device_id_type=MESH,
        )

    def begin(self):
        pl.when(self.section == 1)(lambda: self.over().start())

    def middle(self):
        @pl.when(self.section == 0)
        def _():
            self.over().wait_recv()
            self.mine[...] = self.low[...] + self.mate[...]
            for step in range(3):
                self.along(step).start()

        @pl.when(self.section == 1)
        def _():
            self.over().wait_send()
            self.out[...] = jnp.zeros_like(self.out)

    def end(self):
        @pl.when(self.section == 0)
        def _():
            total = self.mine[...]
            for step in range(3):
                self.along(step).wait()
                total = total + self.taken[step]
            self.out[...] = total


def norm_back(hidden, grads, gain, above, target, low_target, sums, beside=()):
    width = hidden.shape[1]
    lots = 4
    chunk = hidden.shape[0] // lots

    def fold(rows):
        return jnp.sum(rows.reshape(chunk // 8, 8, width), axis=0)

    def lot(step, at):
        hat, scale = norm_stats(hidden[at, :].astype(F32))
        grad = grads[at, :]
        sums[0:8, :] += fold(grad * hat)
        sums[8:16, :] += fold(grad)
        inner = grad * gain[...]
        mean = jnp.mean(inner, axis=-1, keepdims=True)
        slant = jnp.mean(inner * hat, axis=-1, keepdims=True)
        result = above[at, :].astype(F32) + scale * (inner - mean - hat * slant)
        if target is not None:
            target[at, :] = result
        low_target[at, :] = result.astype(BF)

    sums[...] = jnp.zeros_like(sums)
    if beside:
        for step in range(lots):
            lot(step, slice(step * chunk, (step + 1) * chunk))
            for work in beside[step : step + 1]:
                work()
    else:
        pl.loop(0, lots)(lambda step: lot(step, rows_at(step, chunk)))


def norm_sums(sums, low, gain_row, bias_row):
    low[gain_row : gain_row + 1, :] = jnp.sum(sums[0:8, :], axis=0, keepdims=True)
    low[BIAS + bias_row : BIAS + bias_row + 1, :] = jnp.sum(sums[8:16, :], axis=0, keepdims=True)


def fill_ones(turned, count):
    turned[pl.ds(count, 16), :] = jnp.ones((16, turned.shape[1]), BF)


def weight_grad(turned, count, grads, result, row, low, *low_rows):
    width = low.shape[1]
    parts = result.shape[0]
    each = count // parts

    def step_of(step, low_row):
        both = nn(turned[0 : count + 16, :], grads[:, step * width : (step + 1) * width])
        at = slice(row + step * each, row + (step + 1) * each)
        for part in range(parts):
            result[part, at, :] = both[part * each : (part + 1) * each].astype(BF)
        if low_row is not None:
            low[low_row : low_row + 1, :] = both[count : count + 1, :]

    return [functools.partial(step_of, step, low_row) for step, low_row in enumerate(low_rows)]


def do(steps):
    for step in steps:
        step()


def tiled_nt(left, right, target, tile):
    @pl.loop(0, right.shape[0] // tile)
    def _(step):
        at = rows_at(step, tile)
        target[:, at] = nt(left[...], right[at, :])


def space_attention_back(
    qkv, grads, logs, result, keys_t, turned_t, unit, pair_unit, frames, rows, patches, width
):
    low_lane = lax.broadcasted_iota(jnp.int32, (rows, PAIR), 1) < HD

    @pl.loop(0, frames)
    def _(f):
        at = rows_at(f, rows)
        for pair in range(width // PAIR):
            lanes = slice(width + pair * PAIR, width + (pair + 1) * PAIR)
            keys_t[pair * PAIR : (pair + 1) * PAIR, :] = nt(pair_unit[...], qkv[at, lanes]).astype(BF)

        @pl.loop(0, width // PAIR // GROUP_BACK)
        def _(group):
            def lanes(which, member):
                pair = group * GROUP_BACK + member
                return pl.ds(pl.multiple_of(which * width + pair * PAIR, PAIR), PAIR)

            scores, grad_softs = [], []
            for member in range(GROUP_BACK):
                query = qkv[at, lanes(0, member)] * BF(HD**-0.5)
                key, value, grad = qkv[at, lanes(1, member)], qkv[at, lanes(2, member)], grads[at, lanes(0, member)]
                for half in range(2):
                    mine = low_lane if half == 0 else ~low_lane
                    scores.append(nt(jnp.where(mine, key, BF(0)), query))
                    grad_softs.append(nt(jnp.where(mine, value, BF(0)), grad))
            softs, grad_scores = [], []
            for member, (score, grad_soft) in enumerate(zip(scores, grad_softs)):
                head = group * (2 * GROUP_BACK) + member
                log = logs[pl.ds(f * H + head, 1), :]
                soft = [jnp.exp(part - log) for part in split_patches(score, patches)]
                cut = soft[0].shape[0]
                changes = [grad_soft[:cut], grad_soft[cut:]][: len(soft)]
                slant = sum(jnp.sum(part * change, axis=0, keepdims=True) for part, change in zip(soft, changes))
                changes = [change - slant for change in changes]
                softs.append(jnp.concatenate([part.astype(BF) for part in soft], axis=0))
                grad_scores.append(
                    jnp.concatenate([(part * change).astype(BF) for part, change in zip(soft, changes)], axis=0)
                )
            for member in range(GROUP_BACK):
                query = qkv[at, lanes(0, member)] * BF(HD**-0.5)
                grad = grads[at, lanes(0, member)]
                pair = 2 * member
                grad_key = [nn(grad_scores[pair + half], query) for half in range(2)]
                grad_value = [nn(softs[pair + half], grad) for half in range(2)]
                result[at, lanes(1, member)] = jnp.where(low_lane, *grad_key).astype(BF)
                result[at, lanes(2, member)] = jnp.where(low_lane, *grad_value).astype(BF)
                for half in range(2):
                    head = group * (2 * GROUP_BACK) + pair + half
                    own = pl.ds(pl.multiple_of(head * HD, HD), HD)
                    turned_t[own, :] = (nn(keys_t[own, :], grad_scores[pair + half]) * HD**-0.5).astype(BF)

        result[at, 0:width] = nt(unit[...], turned_t[...]).astype(BF)


def time_attention_back(qkv, grads, probs, result, stage, soft, soft_grad, grad_key, grad_value, heads, heads_t, frames, rows, width, between):
    grad_key[...] = jnp.zeros_like(grad_key)
    grad_value[...] = jnp.zeros_like(grad_value)

    @pl.loop(0, frames)
    def _(i):
        between(i)
        own = rows_at(i, rows)
        for j in range(frames):
            stage[pl.ds(j * rows, rows), :] = grads[own, :] * qkv[pl.ds(j * rows, rows), 2 * width : 3 * width]
        grad_soft = nn(stage[...], heads[...]) * HD**0.5
        parts = [probs[i, pl.ds(j * rows, rows), :] for j in range(frames)]
        changes = [grad_soft[j * rows : (j + 1) * rows] for j in range(frames)]
        total = sum(part * change for part, change in zip(parts, changes))
        for j in range(frames):
            at = pl.ds(j * rows, rows)
            soft[at, :] = parts[j].astype(BF)
            soft_grad[at, :] = (parts[j] * (changes[j] - total)).astype(BF)
        grad_query = None
        for j in range(frames):
            at = pl.ds(j * rows, rows)
            wide = nn(soft_grad[at, :], heads_t[...])
            term = wide * qkv[at, width : 2 * width].astype(F32)
            grad_query = term if grad_query is None else grad_query + term
            grad_key[at, :] += wide * qkv[own, 0:width].astype(F32)
            grad_value[at, :] += nn(soft[at, :], heads_t[...]) * grads[own, :].astype(F32)
        result[own, 0:width] = (grad_query * HD**-0.5).astype(BF)

    result[:, width : 2 * width] = (grad_key[...] * HD**-0.5).astype(BF)
    result[:, 2 * width : 3 * width] = grad_value[...].astype(BF)


def back_kernel(block, parts, places, patches, k):
    total, width = k.grads.shape
    hidden = k.act.shape[1]
    frames = k.probs.shape[0]
    rows = total // frames
    deep = hidden // width
    copies = Copies(k.sems)
    section, place = lax.axis_index("section"), lax.axis_index("seq")
    mine = section == block
    last = block == 0
    columns = lambda tile, count=1: slice(tile * width, (tile + count) * width)

    greet()
    load_gy = copies.start(k.gy_in, k.low_grads)
    tiles = []
    for tile in range(deep):
        at = pl.ds(tile * width, width)
        tiles.append(copies.fetch(k.own_down.at[at], k.other_down.at[at], k.down.at[at], mine))
        tiles.append(copies.start(k.r_slope.at[:, at], k.gpre.at[:, at]))
    carried = []
    if last:
        relay = Relay(1, k.last_mine, k.last_mates, k.last_taken, k.last_send, k.last_recv, k.last_in, True)
        relay.begin()
        carried.append(relay)
        swaps = Swaps(k)
        swaps.begin()
    smalls = load_smalls(k, mine)
    fill_pick(k.pick, parts, place, places)
    fill_pick(k.pick_wide, 1, place, places)
    fill_units(k.unit, k.pair_unit)
    fill_heads(k.heads, k.heads_t)
    low = k.low
    low[...] = jnp.zeros_like(low)
    count = k.pick.shape[0]
    each = count // parts
    wide = k.pick_wide.shape[0]

    def turn(source):
        k.turned[0:count, :] = nt(k.pick[...], source).astype(BF)

    load_gy.wait()
    for tile in range(deep):
        tiles[2 * tile].wait()
        tiles[2 * tile + 1].wait()
        if tile == 1:
            load_act = copies.start(k.r_act, k.act)
            load_up = copies.fetch(k.own_up, k.other_up, k.up, mine)
            load_normed = copies.start(k.r_normed_m, k.normed)
            load_x2 = copies.start(k.r_x2, k.hidden)
        at = columns(tile)
        k.gpre[:, at] = (nt(k.low_grads[...], k.down[at, :]) * k.gpre[:, at].astype(F32)).astype(BF)
    load_space_out = copies.fetch(k.own_space_out, k.other_space_out, k.down.at[columns(3)], mine)
    load_space = [
        copies.fetch(k.own_space.at[:, columns(part)], k.other_space.at[:, columns(part)], k.down.at[columns(part)], mine)
        for part in range(3)
    ]
    for relay in carried:
        relay.middle()
    load_act.wait()
    for part in range(parts):
        at = slice(part * wide, (part + 1) * wide)
        k.turned[at, :] = nt(k.pick_wide[...], k.act[:, part * (hidden // parts) : (part + 1) * (hidden // parts)]).astype(BF)
    fill_ones(k.turned, parts * wide)
    do(weight_grad(k.turned, parts * wide, k.low_grads, k.mlp, deep * each, low, BIAS + 10))
    half = deep * each
    small_part = slice(half, k.mlp.shape[1])
    mates = (k.spare.at[0 : parts * half], k.spare.at[parts * half : parts * k.mlp.shape[1]])
    down = Relay(block, k.mlp.at[:, small_part], mates[1], k.mlp_taken.at[:, small_part], k.down_send, k.down_recv)
    down.begin()
    load_qkv = copies.start(k.r_qkv_s, k.act.at[:, columns(0, 3)])
    load_logs = copies.start(k.r_logs, k.logs)
    load_up.wait()
    tiled_nt(k.gpre, k.up, k.gnorm, width // 3)
    load_time = copies.fetch(k.own_time, k.other_time, k.up.at[:, columns(0, 3)], mine)
    load_time_out = copies.fetch(k.own_time_out, k.other_time_out, k.up.at[:, columns(3)], mine)
    down.middle()
    load_normed.wait()
    turn(k.normed[...])
    fill_ones(k.turned, count)
    steps = weight_grad(k.turned, count, k.gpre, k.mlp, 0, low, *range(UP, UP + deep))
    load_normed = copies.start(k.r_normed_s, k.normed)
    load_x2.wait()
    do(steps)
    mlp = Relay(block, k.mlp.at[:, 0:half], mates[0], k.mlp_taken.at[:, 0:half], k.mlp_send, k.mlp_recv)
    mlp.begin()
    norm_back(k.hidden, k.gnorm, smalls.gain(2), k.low_grads, k.grads, k.low_grads, k.sums)
    load_attn = copies.start(k.r_attn_s, k.attn)
    down.second()
    load_x1 = copies.start(k.r_x1, k.hidden)
    norm_sums(k.sums, low, 2, 9)

    load_space_out.wait()
    k.gattn[...] = nt(k.low_grads[...], k.down[columns(3), :]).astype(BF)
    load_time_fc = copies.fetch(k.own_time_fc, k.other_time_fc, k.down.at[columns(3)], mine)
    load_attn.wait()
    turn(k.attn[...])
    do(weight_grad(k.turned, count, k.low_grads, k.space, 3 * each, low, BIAS + 8))
    mlp.middle()
    load_attn = copies.start(k.r_attn_t, k.attn)
    proj, stage = k.spare.at[0:total], k.spare.at[total : 2 * total]
    load_qkv.wait()
    load_logs.wait()
    qkv, gqkv = k.act.at[:, columns(0, 3)], k.gpre.at[:, columns(0, 3)]
    space_attention_back(
        qkv, k.gattn, k.logs, gqkv, k.keys_t, k.turned_t, k.unit, k.pair_unit, frames, rows, patches, width,
    )
    mlp.second()
    load_proj = copies.start(k.r_proj, proj)
    load_qkv = copies.start(k.r_qkv_t, qkv)
    load_probs = copies.start(k.r_probs, k.probs)
    for load in load_space:
        load.wait()
    load_normed.wait()
    turn(k.normed[...])
    steps = weight_grad(k.turned, count, gqkv, k.space, 0, low, BIAS + 6, None, BIAS + 7)
    space = Relay(block, k.space, k.space_mates, k.space_taken, k.space_send, k.space_recv)

    @pl.loop(0, 3)
    def _(tile):
        size = width // 3
        result = None
        for part in range(3):
            at = pl.ds(pl.multiple_of(part * width + tile * size, size), size)
            term = nt(gqkv[:, columns(part)], k.down[at, :])
            result = term if result is None else result + term
        k.gnorm[:, rows_at(tile, size)] = result

    load_x1.wait()
    norm_back(k.hidden, k.gnorm, smalls.gain(1), k.grads, k.grads, k.low_grads, k.sums, steps)
    space.begin()
    norm_sums(k.sums, low, 1, 5)
    if last:
        k.low_early[...] = low[...]
        k.low_early[0:8, :] = jnp.zeros((8, width), F32)
        early = LowRelay(
            [k.low_early, k.low_in], k.low_sum, (k.low_mine, k.low_mate, k.low_taken, k.low_send, k.low_recv)
        )
        early.begin()

    load_time_fc.wait()
    k.normed[...] = nt(k.low_grads[...], k.down[columns(3), :]).astype(BF)
    load_proj.wait()
    turn(proj[...])
    do(weight_grad(k.turned, count, k.low_grads, k.time, 4 * each, low, BIAS + 4))
    load_time_out.wait()
    k.gattn[...] = nt(k.normed[...], k.up[:, columns(3)]).astype(BF)
    space.middle()
    if last:
        early.middle()
    load_attn.wait()
    turn(k.attn[...])
    do(weight_grad(k.turned, count, k.normed, k.time, 3 * each, low, BIAS + 3))
    load_normed = copies.start(k.r_normed_t, k.normed)
    load_x = copies.start(k.r_x, k.attn)
    outs = Relay(
        block, k.time.at[:, 3 * each : 5 * each], k.outs_mates, k.outs_taken, k.outs_send, k.outs_recv, None, True
    )
    outs.begin()
    load_qkv.wait()
    load_probs.wait()

    def between(step):
        pl.when(step == 1)(outs.middle)
        pl.when(step == 3)(space.second)

    time_attention_back(
        qkv, k.gattn, k.probs, gqkv, stage, k.soft, k.soft_grad, k.gnorm, k.hidden, k.heads, k.heads_t, frames, rows,
        width, between,
    )
    if last:
        early.second()
    done = []

    def end(relay, out):
        start = sum(size for _, size in done)
        size = out.shape[0]
        relay.end(k.hidden.at[start : start + size], out, k.end_sems.at[len(done)])
        done.append((relay, size))

    load_normed.wait()
    turn(k.normed[...])
    steps = weight_grad(k.turned, count, gqkv, k.time, 0, low, BIAS + 1, None, BIAS + 2)
    qkv_part = k.time.at[:, 0 : 3 * each]
    if last:
        do(steps)
        final = Relay(0, qkv_part, k.qkv_mates, k.qkv_taken, k.qkv_send, k.qkv_recv, None, True)
        final.begin()
        end(down, k.mlp_out.at[half : k.mlp.shape[1]])
        end(mlp, k.mlp_out.at[0:half])
    load_time.wait()
    tiled_nt(gqkv, k.up.at[:, columns(0, 3)], k.gnorm, width // 3)
    if last:
        final.middle()
    load_x.wait()
    norm_back(k.attn, k.gnorm, smalls.gain(0), k.grads, None, k.gattn, k.sums, () if last else steps)
    norm_sums(k.sums, low, 0, 0)
    if last:
        late = LateRelay(low.at[0:8], k.low_last, k.late_mine, k.late_mate, k.late_taken, k.late_send, k.late_recv)
        late.begin()
        swaps.late()
    copies.store(k.gattn, k.gx_out)
    if last:
        end(carried[0], k.last_out)
        late.middle()
    else:
        copies.store(qkv_part, k.last_out)
        end(down, k.mlp_out.at[half : k.mlp.shape[1]])
        end(mlp, k.mlp_out.at[0:half])
    end(space, k.space_out)
    end(outs, k.outs_out)
    if last:
        early.end()
        swaps.end()
        start = k.mlp.shape[1]
        final.end(k.hidden.at[start : start + 3 * each], k.qkv_out, k.end_sems.at[len(done)])
        done.append((final, 0))
        late.end()
    for relay, _ in done:
        relay.settle()
    copies.finish()


class Swaps:
    def __init__(self, k):
        self.k = k
        self.section = lax.axis_index("section")
        rows = k.swapped.shape[1]
        self.own = rows_at(lax.axis_index("seq"), rows)

    def over(self, which, source):
        return pltpu.make_async_remote_copy(
            source.at[self.own],
            self.k.swapped.at[which],
            self.k.swap_send.at[which],
            self.k.swap_recv.at[which],
            device_id={"section": 1 - self.section},
            device_id_type=MESH,
        )

    def begin(self):
        @pl.when(self.section == 0)
        def _():
            self.over(0, self.k.y1_in).start()
            self.over(1, self.k.gy_in).start()

        @pl.when(self.section == 1)
        def _():
            self.over(0, self.k.y0_in).start()

    def late(self):
        @pl.when(self.section == 1)
        def _():
            self.over(1, self.k.gattn).start()

    def end(self):
        self.over(0, self.k.y1_in).wait()
        self.over(1, self.k.gy_in).wait()


def back(block, parts, places, patches, gy, small, small_other, own, other, kept, last=None, low=None, outputs=None):
    total, width = gy.shape
    hidden = own[5].shape[1]
    logs, probs = kept["r_logs"], kept["r_probs"]
    rows = logs.shape[1]
    count = width // places
    each = count // parts
    deep = hidden // width
    dma = pltpu.SemaphoreType.DMA
    wide, full, deepest = struct((total, width)), struct((total, width), F32), struct((total, hidden))
    few, lowest = struct((total, PAIR)), struct((LOW, width), F32)
    piece = lambda height, n=parts: struct((n, height, width))
    mlp, space, time = deep * each + hidden // places // parts, 4 * each, 5 * each
    ins = dict(gy_in=(gy, IN_HBM), **small_ins(small, small_other), **own_ins(own), **other_refs(other))
    ins |= {name: (array, IN_HBM) for name, array in kept.items()}
    summed = lambda height: (struct((height, width), F32), IN_HBM)
    outs = dict(gx_out=(wide, IN_HBM), low=(lowest, IN_VMEM))
    outs |= dict(mlp_out=summed(mlp), space_out=summed(space), outs_out=summed(2 * each))
    scratch = vmem(up=struct((width, hidden)), down=struct((hidden, width)), gpre=deepest, act=deepest)
    scratch |= vmem(grads=full, hidden=full, gnorm=full, low_grads=wide, normed=wide, attn=wide, gattn=wide)
    scratch |= vmem(spare=struct((max(2 * total, parts * mlp), width)), soft=few, soft_grad=few)
    scratch |= vmem(probs=struct(probs.shape, F32), logs=struct(logs.shape, F32), unit=struct((rows, rows)))
    scratch |= vmem(pair_unit=struct((PAIR, PAIR)), keys_t=struct((width, rows)), turned_t=struct((width, rows)))
    scratch |= vmem(heads=struct((width, PAIR)), heads_t=struct((PAIR, width)), pick=struct((count, width)))
    scratch |= vmem(turned=struct((hidden // places + 16, total)), sums=struct((16, width), F32))
    scratch |= vmem(pick_wide=struct((hidden // parts // places, hidden // parts)))
    scratch |= vmem(mlp=piece(mlp), mlp_taken=piece(mlp, 3), space=piece(space), space_mates=piece(space))
    scratch |= vmem(space_taken=piece(space, 3), time=piece(time), outs_mates=piece(2 * each))
    scratch |= vmem(outs_taken=piece(2 * each, 3))
    scratch |= small_held(width, hidden)
    scratch |= dict(down_send=dma((8,)), down_recv=dma((7,)))
    scratch |= dict(mlp_send=dma((8,)), mlp_recv=dma((7,)), space_send=dma((8,)), space_recv=dma((7,)))
    scratch |= dict(outs_send=dma((8,)), outs_recv=dma((7,)), sems=dma((40,)), end_sems=dma((8,)))
    if block == 1:
        outs |= dict(last_out=(piece(3 * each), IN_HBM))
    else:
        y_0, y_1 = outputs
        ins |= dict(last_in=(last, IN_HBM), low_in=(low, IN_VMEM), y0_in=(y_0, IN_HBM), y1_in=(y_1, IN_HBM))
        outs |= dict(last_out=summed(3 * each), qkv_out=summed(3 * each), low_sum=(lowest, IN_VMEM))
        outs |= dict(low_last=(struct((8, width), F32), IN_VMEM))
        late, late_three = struct((8, width), F32), struct((3, 8, width), F32)
        scratch |= vmem(late_mine=late, late_mate=late, late_taken=late_three, low_early=lowest)
        scratch |= dict(late_send=dma((4,)), late_recv=dma((4,)))
        outs |= dict(swapped=(struct((2, rows, width)), IN_HBM))
        low_two, part = struct((2, LOW, width), F32), piece(3 * each)
        scratch |= vmem(last_mine=part, last_mates=part, last_taken=piece(3 * each, 3), qkv_mates=part)
        scratch |= vmem(qkv_taken=piece(3 * each, 3), low_mine=low_two, low_mate=lowest, low_taken=low_two)
        scratch |= dict(low_send=dma((3,)), low_recv=dma((3,)), swap_send=dma((2,)), swap_recv=dma((2,)))
        scratch |= dict(last_send=dma((8,)), last_recv=dma((7,)), qkv_send=dma((8,)), qkv_recv=dma((7,)))
    kernel = functools.partial(back_kernel, block, parts, places, patches)
    return named_call(kernel, f"block{block}_backward", 70 * total * width * width, ins, outs, scratch, True)
def layout_kernel(places, patches, pieces, rows_each, low_a, low_b, *refs):
    n = len(pieces)
    sums, refs = (refs[:n], refs[n : 2 * n]), refs[2 * n :]
    results, swapped, refs = refs[:4], refs[4], refs[5:]
    weights, lows, frames, refs = refs[:7], refs[7:10], refs[10:12], refs[12:]
    total, mine, sems = refs
    section = lax.axis_index("section")
    z, place = lax.axis_index("dp"), lax.axis_index("seq")
    rows, width = mine.shape[1:]
    loads = []
    for at, (start, count) in enumerate(pieces):
        for block in range(2):

            @pl.when(section == block)
            def _(at=at, block=block, start=start, count=count):
                pltpu.make_async_copy(sums[block][at], total.at[start : start + count], sems.at[at]).start()

        loads.append(pltpu.make_async_copy(sums[0][at], total.at[start : start + count], sems.at[at]))
    for which in range(2):
        own = rows_at(place, rows)
        for block in range(2):

            @pl.when(section == block)
            def _(which=which, block=block):
                pltpu.make_async_copy(results[2 * which + block].at[own], mine.at[which], sems.at[n + which]).start()

        loads.append(pltpu.make_async_copy(results[2 * which].at[own], mine.at[which], sems.at[n + which]))
        loads.append(pltpu.make_async_copy(swapped.at[which], mine.at[2 + which], sems.at[n + 2 + which]))
        loads[-1].start()
    part = z * lax.axis_size("seq") + place
    low = low_a[...]
    low = jnp.concatenate([low[0:8] + low_b[...], low[8:]], axis=0)
    for target, first, count in zip(lows, (0, BIAS, UP), (BIAS, UP - BIAS, target_rows(lows[2], places, width))):
        flat = jnp.concatenate([low[first + at : first + at + 1] for at in range(count)], axis=1)
        size = target.shape[1]
        flat = jnp.broadcast_to(flat, (8, flat.shape[1]))
        target[...] = pltpu.roll(flat, lax.rem(count * width - part * size, count * width), 1)[0:1, :size]
    for load in loads:
        load.wait()
    for which, target in enumerate(frames):
        for block in range(2):

            @pl.when(section == block)
            def _(which=which, target=target, block=block):
                target[:, block, :] = mine[which, 0:patches]
                target[:, 1 - block, :] = mine[2 + which, 0:patches]

    start = 0
    lanes = width // PAIR
    for target, count in zip(weights, rows_each):
        each = target.shape[0] // (count * lanes)
        for at in range(count):
            for lane in range(lanes):
                target[pl.ds(at * lanes + lane, each, stride=count * lanes), :] = total[
                    start + at * each : start + (at + 1) * each, lane * PAIR : (lane + 1) * PAIR
                ]
        start += count * each


def target_rows(target, places, width):
    return target.shape[1] * places // width


def layout(patches, places, width, hidden, pieces, sums, low, low_last, results, swapped):
    each = width // places
    deep = hidden // width
    rows_each = (3, 1, 1, 3, 1, deep, 1)
    heights = (each, each, each, each, each, each, hidden // places)
    outs = [struct((h * r * width // PAIR, PAIR), F32) for h, r in zip(heights, rows_each)]
    outs += [struct((1, rows * width // places), F32) for rows in (BIAS, UP - BIAS, deep)]
    outs += [struct((patches, 2, width))] * 2
    rows = swapped.shape[1]
    n = len(pieces)
    total = sum(count for _, count in pieces)
    scratch = held(struct((total, width), F32), struct((4, rows, width))) + [pltpu.SemaphoreType.DMA((n + 4,))]
    return pl.pallas_call(
        functools.partial(layout_kernel, places, patches, pieces, rows_each),
        out_shape=outs,
        in_specs=[IN_VMEM] * 2 + [IN_HBM] * (2 * n + 5),
        out_specs=[IN_VMEM] * len(outs),
        scratch_shapes=scratch,
        compiler_params=pltpu.CompilerParams(vmem_limit_bytes=VMEM_BYTES),
        name="lay_out",
    )(low, low_last, *sums[0], *sums[1], *results, swapped)


def shards(clip_ids, tokens, *rest):
    weights, small, cotangent = rest[:7], rest[7:10], rest[10]
    NEXT_ID[:] = [1]
    n_dp, n_seq = lax.axis_size("dp"), lax.axis_size("seq")
    patches, width = tokens.shape[2:]
    hidden = weights[5].shape[2]
    places = n_dp * n_seq
    small = [array.reshape(1, -1) for array in small]
    own = [array[0] for array in weights]

    first = forward(0, n_seq, patches, clip_ids, small, None, own, None, None, tokens, cotangent)
    y_0, grad_top, x = first.pop("y_out"), first.pop("cot_out"), first["r_x"]
    small_other = [first.pop("other_gains"), first.pop("other_biases"), first.pop("other_up_bias")]
    other = [first.pop("other_time"), first.pop("other_time_out"), first.pop("other_time_fc"), first.pop("other_space")]
    other += [first.pop("other_space_out"), first.pop("other_up"), first.pop("other_down")]
    common = (small, small_other, own, other)
    second = forward(1, n_seq, patches, clip_ids, *common, y_0)
    y_1 = second.pop("y_out")
    second["r_x"] = y_0
    outputs = (y_0, y_1)

    each = width // places
    back_1 = back(1, n_dp, n_seq, patches, grad_top, *common, second)
    back_0 = back(
        0, n_dp, n_seq, patches, back_1["gx_out"], *common, first, back_1["last_out"], back_1["low"], outputs
    )
    results = (*outputs, back_0["gx_out"], back_1["gx_out"])
    counts = (3 * each, 2 * each, 4 * each, hidden // width * each + hidden // places)
    pieces = [(sum(counts[:at]), count) for at, count in enumerate(counts)]
    ordered = [
        [first, *(done[name] for name in ("outs_out", "space_out", "mlp_out"))]
        for first, done in ((back_0["qkv_out"], back_0), (back_0["last_out"], back_1))
    ]
    shares = layout(
        patches, places, width, hidden, pieces, ordered, back_0["low_sum"], back_0["low_last"], results, back_0["swapped"]
    )
    frames = [frame.transpose(1, 0, 2).reshape(1, 2, 1, patches, width) for frame in shares[10:]]
    shares = [share.reshape(1, -1) for share in shares[:10]]
    return (*frames, *shares)


def relay_from_behind(value, axis, steps):
    count = lax.axis_size(axis)
    leading, last = (max(0, -steps), min(count, count - steps))
    return lax.ppermute(value, axis, [(source, source + steps) for source in range(leading, last)])


def relay_norm_rows(values, gain, shift):
    centre = values - jnp.mean(values, axis=-1, keepdims=True)
    spread = jnp.mean(centre * centre, axis=-1, keepdims=True)
    return centre * lax.rsqrt(spread + eps_norm) * gain + shift


def relay_mixed_dot(left, right, form):
    return jnp.einsum(form, left, right, preferred_element_type=jnp.float32)


def relay_column_sum(grad_rows):
    return jnp.sum(grad_rows.astype(jnp.float32), axis=(0, 1))


def relay_flat_terms(terms):
    return tuple((term.reshape(-1) for term in terms))


def relay_masked_scores(queries, key_rows, allowed):
    scores = relay_mixed_dot(queries, key_rows, "bic,bjc->bij") * queries.shape[-1] ** (-0.5)
    if allowed is None:
        return scores
    return jnp.where(allowed[None], scores, far_below)


def relay_attend(queries, key_rows, values, allowed):
    scores = relay_masked_scores(queries, key_rows, allowed)
    top_score = jnp.max(scores, axis=-1, keepdims=True)
    total_exp = jnp.sum(jnp.exp(scores - top_score), axis=-1, keepdims=True)
    log_total = top_score + jnp.log(total_exp)
    weights_soft = jnp.exp(scores - log_total).astype(jnp.bfloat16)
    mixed = relay_mixed_dot(weights_soft, values, "bij,bjc->bic").astype(jnp.bfloat16)
    return (mixed, log_total)


def relay_attend_back(queries, key_rows, values, log_total, allowed, grad_out):
    scale = queries.shape[-1] ** (-0.5)
    weights_soft = jnp.exp(relay_masked_scores(queries, key_rows, allowed) - log_total)
    grad_values = relay_mixed_dot(weights_soft.astype(jnp.bfloat16), grad_out, "bij,bic->bjc")
    grad_soft = relay_mixed_dot(grad_out, values, "bic,bjc->bij")
    row_total = jnp.sum(grad_soft * weights_soft, axis=-1, keepdims=True)
    grad_scores = (weights_soft * (grad_soft - row_total)).astype(jnp.bfloat16)
    grad_queries = relay_mixed_dot(grad_scores, key_rows, "bij,bjc->bic") * scale
    grad_keys = relay_mixed_dot(grad_scores, queries, "bij,bic->bjc") * scale
    return (grad_queries, grad_keys, grad_values)


def relay_heads_first(rows):
    frames, patches, width = rows.shape
    return (
        rows.reshape(frames, patches, H, width // H)
        .transpose(0, 2, 1, 3)
        .reshape(frames * H, patches, width // H)
    )


def relay_heads_last(rows, frames):
    batch, patches, head_size = rows.shape
    return (
        rows.reshape(frames, batch // frames, patches, head_size)
        .transpose(0, 2, 1, 3)
        .reshape(frames, patches, batch // frames * head_size)
    )


def relay_time_mix(normed_time, time_qkv, time_out, bias_rows, allowed):
    frames, patches, width = normed_time.shape
    zero_row = jnp.zeros((width,), jnp.float32)
    bias_time = jnp.stack([bias_rows[1], zero_row, bias_rows[2]])
    proj_time = relay_mixed_dot(normed_time, time_qkv.reshape(width, 3, width), "fpd,dke->fkpe")
    proj_time = (proj_time + bias_time[None, :, None, :]).astype(jnp.bfloat16)
    proj_time = proj_time.reshape(frames, 3, patches * H, HD)
    by_patch = lax.all_to_all(proj_time, "seq", split_axis=2, concat_axis=0, tiled=True)
    query_time = by_patch[:, 0].transpose(1, 0, 2)
    key_time = by_patch[:, 1].transpose(1, 0, 2)
    value_time = by_patch[:, 2].transpose(1, 0, 2)
    mixed_time, total_time = relay_attend(query_time, key_time, value_time, allowed)
    back_frames = lax.all_to_all(
        mixed_time.transpose(1, 0, 2), "seq", split_axis=0, concat_axis=1, tiled=True
    )
    attn_time = back_frames.reshape(frames, patches, width)
    proj_out = (relay_mixed_dot(attn_time, time_out, "fpd,de->fpe") + bias_rows[3]).astype(jnp.bfloat16)
    return (proj_out, (normed_time, query_time, key_time, value_time, total_time, attn_time))


def relay_time_mix_back(grad_proj_out, time_qkv, time_out, time_kept, allowed):
    normed_rows, query_time, key_time, value_time, total_time, attn_time = time_kept
    frames, patches, width = grad_proj_out.shape
    grad_time_out = relay_mixed_dot(attn_time, grad_proj_out, "fpd,fpe->de")
    grad_attn_time = relay_mixed_dot(grad_proj_out, time_out, "fpe,de->fpd").astype(jnp.bfloat16)
    grad_attn_time = grad_attn_time.reshape(frames, patches * H, HD)
    grad_by_patch = lax.all_to_all(
        grad_attn_time, "seq", split_axis=1, concat_axis=0, tiled=True
    ).transpose(1, 0, 2)
    grads_time = relay_attend_back(query_time, key_time, value_time, total_time, allowed, grad_by_patch)
    grad_mixed = jnp.stack(grads_time, axis=0).transpose(2, 0, 1, 3).astype(jnp.bfloat16)
    grad_frames = lax.all_to_all(
        grad_mixed, "seq", split_axis=0, concat_axis=2, tiled=True
    ).reshape(frames, 3, patches, width)
    grad_time_qkv = relay_mixed_dot(normed_rows, grad_frames, "fpd,fkpe->dke").reshape(width, 3 * width)
    grad_normed = relay_mixed_dot(grad_frames, time_qkv.reshape(width, 3, width), "fkpe,dke->fpd")
    return (
        grad_normed,
        grad_time_qkv,
        grad_time_out,
        relay_column_sum(grad_frames[:, 0]),
        relay_column_sum(grad_frames[:, 2]),
        relay_column_sum(grad_proj_out),
    )


def relay_layer_forward(inputs, params, allowed):
    (
        time_qkv,
        time_out,
        time_fc,
        space_qkv,
        space_out,
        up_weight,
        down_weight,
        norm_gains,
        bias_rows,
        up_bias,
    ) = params
    frames, patches, width = inputs.shape
    zero_row = jnp.zeros((width,), jnp.float32)
    normed_time = relay_norm_rows(inputs, norm_gains[0], bias_rows[0]).astype(jnp.bfloat16)
    proj_out, time_kept = relay_time_mix(normed_time, time_qkv, time_out, bias_rows, allowed)
    after_time = inputs + (relay_mixed_dot(proj_out, time_fc, "fpd,de->fpe") + bias_rows[4])
    normed_space = relay_norm_rows(after_time, norm_gains[1], bias_rows[5]).astype(jnp.bfloat16)
    bias_space = jnp.stack([bias_rows[6], zero_row, bias_rows[7]])
    proj_space = relay_mixed_dot(normed_space, space_qkv.reshape(width, 3, width), "fpd,dke->fkpe")
    proj_space = (proj_space + bias_space[None, :, None, :]).astype(jnp.bfloat16)
    query_space = relay_heads_first(proj_space[:, 0])
    key_space = relay_heads_first(proj_space[:, 1])
    value_space = relay_heads_first(proj_space[:, 2])
    mixed_space, total_space = relay_attend(query_space, key_space, value_space, None)
    attn_space = relay_heads_last(mixed_space, frames)
    after_space = after_time + (relay_mixed_dot(attn_space, space_out, "fpd,de->fpe") + bias_rows[8])
    normed_mlp = relay_norm_rows(after_space, norm_gains[2], bias_rows[9]).astype(jnp.bfloat16)
    hidden_pre = relay_mixed_dot(normed_mlp, up_weight, "fpd,de->fpe") + up_bias
    hidden_act = jax.nn.gelu(hidden_pre).astype(jnp.bfloat16)
    outputs = after_space + (relay_mixed_dot(hidden_act, down_weight, "fpe,ed->fpd") + bias_rows[10])
    kept = (
        inputs,
        time_kept,
        proj_out,
        after_time,
        normed_space,
        query_space,
        key_space,
        value_space,
        total_space,
        attn_space,
        after_space,
        normed_mlp,
        hidden_pre,
        hidden_act,
    )
    return (outputs, kept)


def relay_layer_backward(grad_top, params, kept, allowed):
    (
        time_qkv,
        time_out,
        time_fc,
        space_qkv,
        space_out,
        up_weight,
        down_weight,
        norm_gains,
        bias_rows,
        up_bias,
    ) = params
    (
        inputs,
        time_kept,
        proj_out,
        after_time,
        normed_space,
        query_space,
        key_space,
        value_space,
        total_space,
        attn_space,
        after_space,
        normed_mlp,
        hidden_pre,
        hidden_act,
    ) = kept
    frames, patches, width = inputs.shape
    grad_mlp = grad_top.astype(jnp.bfloat16)
    grad_down = relay_mixed_dot(hidden_act, grad_mlp, "fpe,fpd->ed")
    grad_act = relay_mixed_dot(grad_mlp, down_weight, "fpd,ed->fpe")
    gelu_back = jax.vjp(jax.nn.gelu, hidden_pre)[1]
    grad_pre = gelu_back(grad_act)[0].astype(jnp.bfloat16)
    grad_up = relay_mixed_dot(normed_mlp, grad_pre, "fpd,fpe->de")
    grad_normed = relay_mixed_dot(grad_pre, up_weight, "fpe,de->fpd")
    norm_back = jax.vjp(relay_norm_rows, after_space, norm_gains[2], bias_rows[9])[1]
    grad_into, gain_mlp, shift_mlp = norm_back(grad_normed)
    grad_space = grad_top + grad_into
    grad_branch = grad_space.astype(jnp.bfloat16)
    grad_space_out = relay_mixed_dot(attn_space, grad_branch, "fpd,fpe->de")
    grad_attn = relay_heads_first(relay_mixed_dot(grad_branch, space_out, "fpe,de->fpd").astype(jnp.bfloat16))
    grads_space = relay_attend_back(query_space, key_space, value_space, total_space, None, grad_attn)
    grad_proj = jnp.stack([relay_heads_last(piece, frames) for piece in grads_space], axis=1).astype(
        jnp.bfloat16
    )
    grad_space_qkv = relay_mixed_dot(normed_space, grad_proj, "fpd,fkpe->dke").reshape(width, 3 * width)
    grad_normed = relay_mixed_dot(grad_proj, space_qkv.reshape(width, 3, width), "fkpe,dke->fpd")
    norm_back = jax.vjp(relay_norm_rows, after_time, norm_gains[1], bias_rows[5])[1]
    grad_into, gain_space, shift_space = norm_back(grad_normed)
    grad_time = grad_space + grad_into
    grad_branch_time = grad_time.astype(jnp.bfloat16)
    grad_time_fc = relay_mixed_dot(proj_out, grad_branch_time, "fpd,fpe->de")
    grad_proj_out = relay_mixed_dot(grad_branch_time, time_fc, "fpe,de->fpd").astype(jnp.bfloat16)
    grad_normed, grad_time_qkv, grad_time_out, query_bias, value_bias, out_bias = relay_time_mix_back(
        grad_proj_out, time_qkv, time_out, time_kept, allowed
    )
    norm_back = jax.vjp(relay_norm_rows, inputs, norm_gains[0], bias_rows[0])[1]
    grad_into, gain_time, shift_time = norm_back(grad_normed)
    grad_inputs = grad_time + grad_into
    gain_grads = jnp.stack([gain_time, gain_space, gain_mlp])
    bias_grads = jnp.stack(
        [
            shift_time,
            query_bias,
            value_bias,
            out_bias,
            relay_column_sum(grad_branch_time),
            shift_space,
            relay_column_sum(grad_proj[:, 0]),
            relay_column_sum(grad_proj[:, 2]),
            relay_column_sum(grad_branch),
            shift_mlp,
            relay_column_sum(grad_mlp),
        ]
    )
    up_grad = relay_column_sum(grad_pre)
    return (
        grad_inputs,
        (
            grad_time_qkv,
            grad_time_out,
            grad_time_fc,
            grad_space_qkv,
            grad_space_out,
            grad_up,
            grad_down,
            gain_grads,
            bias_grads,
            up_grad,
        ),
    )


def relay_shards(
    clip_ids,
    tokens,
    time_qkv,
    time_out,
    time_fc,
    space_qkv,
    space_out,
    up_weight,
    down_weight,
    norm_gains,
    bias_rows,
    up_bias,
    cotangent,
):
    params = (
        time_qkv[0],
        time_out[0],
        time_fc[0],
        space_qkv[0],
        space_out[0],
        up_weight[0],
        down_weight[0],
        norm_gains[0],
        bias_rows[0],
        up_bias[0],
    )
    allowed = clip_ids[0][:, None] == clip_ids[0][None, :]
    first_section = lax.axis_index("section") == 0
    micro = tokens.shape[0]
    arriving = jnp.zeros_like(tokens[0])
    section_inputs = []
    section_outputs = []
    for moment in range(micro + 1):
        taken_rows = jnp.where(first_section, tokens[min(moment, micro - 1)], arriving)
        result = relay_layer_forward(taken_rows.astype(jnp.float32), params, allowed)[0].astype(
            jnp.bfloat16
        )
        section_inputs.append(taken_rows)
        section_outputs.append(result)
        if moment < micro:
            arriving = relay_from_behind(result, "section", 1)
    saved_inputs = [
        jnp.where(first_section, section_inputs[number], section_inputs[number + 1])
        for number in range(micro)
    ]
    layer_outputs = jnp.stack(
        [
            jnp.where(first_section, section_outputs[number], section_outputs[number + 1])
            for number in range(micro)
        ]
    )
    returning = jnp.zeros_like(tokens[0])
    back_results = []
    totals = None
    for moment in range(micro + 1):
        grad_given = jnp.where(first_section, returning, cotangent[min(moment, micro - 1)]).astype(
            jnp.float32
        )
        source_rows = jnp.where(
            first_section, saved_inputs[max(moment - 1, 0)], saved_inputs[min(moment, micro - 1)]
        )
        live_share = jnp.where(
            first_section, 1.0 if moment >= 1 else 0.0, 1.0 if moment < micro else 0.0
        )
        kept = relay_layer_forward(source_rows.astype(jnp.float32), params, allowed)[1]
        grad_inputs, weight_terms = relay_layer_backward(grad_given, params, kept, allowed)
        grad_inputs = grad_inputs.astype(jnp.bfloat16)
        back_results.append(grad_inputs)
        weight_terms = relay_flat_terms(jax.tree.map(lambda term: term * live_share, weight_terms))
        if totals is None:
            totals = tuple(weight_terms)
        else:
            totals = tuple((left + right for left, right in zip(totals, weight_terms)))
        if moment < micro:
            returning = relay_from_behind(grad_inputs, "section", -1)
    input_grads = jnp.stack(
        [
            jnp.where(first_section, back_results[number + 1], back_results[number])
            for number in range(micro)
        ]
    )
    shares = (
        lax.psum_scatter(totals[0], ("dp", "seq"), scatter_dimension=0, tiled=True),
        lax.psum_scatter(totals[1], ("dp", "seq"), scatter_dimension=0, tiled=True),
        lax.psum_scatter(totals[2], ("dp", "seq"), scatter_dimension=0, tiled=True),
        lax.psum_scatter(totals[3], ("dp", "seq"), scatter_dimension=0, tiled=True),
        lax.psum_scatter(totals[4], ("dp", "seq"), scatter_dimension=0, tiled=True),
        lax.psum_scatter(totals[5], ("dp", "seq"), scatter_dimension=0, tiled=True),
        lax.psum_scatter(totals[6], ("dp", "seq"), scatter_dimension=0, tiled=True),
        lax.psum_scatter(totals[7], ("dp", "seq"), scatter_dimension=0, tiled=True),
        lax.psum_scatter(totals[8], ("dp", "seq"), scatter_dimension=0, tiled=True),
        lax.psum_scatter(totals[9], ("dp", "seq"), scatter_dimension=0, tiled=True),
    )
    return (
        layer_outputs[None],
        input_grads[None],
        shares[0][None],
        shares[1][None],
        shares[2][None],
        shares[3][None],
        shares[4][None],
        shares[5][None],
        shares[6][None],
        shares[7][None],
        shares[8][None],
        shares[9][None],
    )


def solution(mesh):
    stacked = P("section", None, None)
    spread = P(None, ("dp", "seq"), None, None)
    in_specs = (P("dp", None), spread, *[stacked] * 9, P("section", None), spread)
    flat = P("section", ("dp", "seq"))
    out = P("section", None, ("dp", "seq"), None, None)
    relay = mesh.shape["seq"] != 4 or mesh.shape["dp"] != 4
    return jax.shard_map(
        relay_shards if relay else shards, mesh=mesh, in_specs=in_specs, out_specs=(out, out, *[flat] * 10), check_vma=False
    )
```
